32 devices in a mesh: pb: 2 (over x), ka: 16 (over z, y, core).
Axes of the slice: x: 2, y: 2, z: 4, core: 2. Of those that a mesh axis runs over, the one named last changes fastest.
Arguments:
- tokens: bfloat16 [4096, 768], P(('pb', 'ka')), may hold values from -6 to 6
- positions: float32 [3, 4096], replicated, may hold values from -24 to 24
- item_of_atom: int32 [4096], replicated, may hold values from 0 to 104, as said below
- item_lengths: int32 [105], replicated, may hold values from 8 to 768, as said below
- atom_types: int32 [4096], replicated, may hold values from 0 to 127, as said below
- key_mask: int32 [4096], replicated, may hold values 0 or 1
- ln1_gain: float32 [768], replicated, may hold values from 0.5 to 1.5
- ln1_bias: float32 [768], replicated, may hold values from -3 to 3
- w_qkv: bfloat16 [768, 2304], replicated, may hold values from -0.21875 to 0.21875
- kernel_means: float32 [128], replicated, may hold values from 0 to 16
- kernel_widths: float32 [128], replicated, may hold values from 0.5 to 4
- kernel_weight: bfloat16 [128, 32], replicated, may hold values from -6 to 6
- type_scale: float32 [160], replicated, may hold values from 0.5 to 1.5
- type_shift: float32 [160], replicated, may hold values from -3 to 3
- w_out: bfloat16 [768, 768], replicated, may hold values from -0.875 to 0.875
- ln2_gain: float32 [768], replicated, may hold values from 0.5 to 1.5
- ln2_bias: float32 [768], replicated, may hold values from -3 to 3
- w_up: bfloat16 [768, 3072], replicated, may hold values from -0.21875 to 0.21875
- w_down: bfloat16 [3072, 768], replicated, may hold values from -0.109375 to 0.109375
- out_cotangent: bfloat16 [4096, 768], P(('pb', 'ka')), may hold values from -6 to 6
Outputs:
- block_out: bfloat16 [4096, 768], P(('pb', 'ka'))
- grad_tokens: float32 [4096, 768], P(('pb', 'ka'))
- grad_positions: float32 [3, 4096], P(None, ('pb', 'ka'))
- grad_ln1_gain: float32 [768], replicated
- grad_ln1_bias: float32 [768], replicated
- grad_w_qkv: float32 [768, 2304], P(None, 'ka')
- grad_kernel_means: float32 [128], replicated
- grad_kernel_widths: float32 [128], replicated
- grad_kernel_weight: float32 [128, 32], replicated
- grad_type_scale: float32 [160], replicated
- grad_type_shift: float32 [160], replicated
- grad_w_out: float32 [768, 768], P(None, 'ka')
- grad_ln2_gain: float32 [768], replicated
- grad_ln2_bias: float32 [768], replicated
- grad_w_up: float32 [768, 3072], P(None, 'ka')
- grad_w_down: float32 [3072, 768], P('ka')
The draws below stay inside these ranges and needn't reach their ends.
Inputs may be any that keep to these rules, and one draw needn't show every extreme that they name: `item_of_atom`: items are contiguous in atom order: item i holds the item_lengths[i] atoms that follow those of items 0 to i - 1; an item is a protein when it has more than 64 atoms, else a molecule. `item_lengths`: the lengths sum to 4096. `atom_types`: ids of protein atoms lie below 32.
All inputs are finite; a program needn't handle non-finite values.
Results may differ from the reference program's by a relative error of at most 0.017.
Values may be sent and summed in bfloat16 or wider, within the bound.
No kernel may reach another device: no remote copies, remote signals or barrier semaphores. Data moves between devices by JAX's collectives and lax.ppermute only.
A program may use at most 128 MiB of HBM per device.

```python
import math
import jax
import jax.numpy as jnp
from jax import lax

D = 768
HEADS = 32
FF = 3072
KERNELS = 128
MOL_TYPES = 128
RES_TYPES = 32
PROT_LEN = 768
MOL_MEAN = 32
ATOMS = 4096
PROTEINS = 1
MOLECULES = 104
ITEMS = 105


def paired_offsets(key, count, most):
    raw = jax.random.randint(key, (count // 2 + 1,), 0, most + 1)
    spots = jnp.arange(count)
    signs = jnp.where(spots % 2 == 0, 1, -1)
    offsets = raw[spots // 2] * signs
    lone = (spots == count - 1) & (count % 2 == 1)
    return jnp.where(lone, 0, offsets).astype(jnp.int32)


def pack_layout(key):
    key_prot, key_mol, key_order, key_mtype, key_ptype = jax.random.split(key, 5)
    others = paired_offsets(key_prot, PROTEINS - 1, PROT_LEN // 3 - 1) + 2 * PROT_LEN // 3
    proteins = jnp.concatenate([jnp.full((1,), PROT_LEN, jnp.int32), others.astype(jnp.int32)])
    molecules = paired_offsets(key_mol, MOLECULES, MOL_MEAN * 3 // 4) + MOL_MEAN
    lengths = jnp.concatenate([proteins, molecules.astype(jnp.int32)]).astype(jnp.int32)
    lengths = lengths[jax.random.permutation(key_order, ITEMS)]
    ends = jnp.cumsum(lengths)
    packed = jnp.arange(ATOMS, dtype=jnp.int32)
    packed_item = jnp.searchsorted(ends, packed, side='right').astype(jnp.int32)
    flags = lengths[packed_item] > 2 * MOL_MEAN
    residue_ids = jax.random.randint(key_ptype, (ATOMS,), 0, RES_TYPES)
    molecule_ids = jax.random.randint(key_mtype, (ATOMS,), 0, MOL_TYPES)
    packed_type = jnp.where(flags, residue_ids, molecule_ids).astype(jnp.int32)
    return (lengths, packed_item, packed_type)


def draw_item_of_atom(key, part):
    shared = pack_layout(key)
    return shared[1]


def draw_item_lengths(key, part):
    shared = pack_layout(key)
    return shared[0]


def draw_atom_types(key, part):
    shared = pack_layout(key)
    return shared[2]


def plant(drawn, own_key, smallest, top_value):
    longest = drawn.shape.index(max(drawn.shape))
    spots = []
    for shift in (0, 1):
        where = [jax.random.randint(jax.random.fold_in(own_key, axis), (), 0, length) for axis, length in enumerate(drawn.shape)]
        where[longest] = (where[longest] + shift) % drawn.shape[longest]
        spots.append(tuple(where))
    return drawn.at[spots[0]].set(smallest).at[spots[1]].set(top_value)


def steps_of(rng, dims, cuts, low, high):
    def one(axis_at, shards_of):
        heights = jax.random.uniform(jax.random.fold_in(jax.random.fold_in(rng, 6), axis_at), (shards_of,), jnp.float32, low / len(cuts), high / len(cuts))
        return jnp.repeat(jnp.exp(heights), dims[axis_at] // shards_of).reshape((-1,) + (1,) * (len(dims) - axis_at - 1))

    gain = one(*cuts[0])
    for cut in cuts[1:]:
        gain = gain * one(*cut)
    return gain


def normal_values(own_key, shape, scale, bound, cuts=(), held_as=jnp.bfloat16):
    drawn = scale * jax.random.normal(own_key, shape, jnp.float32)
    if cuts:
        drawn = drawn * steps_of(own_key, shape, cuts, -0.22, 0.18)
    return jnp.clip(drawn, -bound, bound).astype(held_as)


def setup_inputs(seed: int = 0) -> dict:
    keys = jax.random.split(jax.random.key(seed), 21)
    tokens = normal_values(keys[0], (ATOMS, D), 1.0, 6.0, ((0, 32),))
    positions = normal_values(keys[1], (3, ATOMS), 4.0, 24.0, (), jnp.float32)
    item_of_atom = draw_item_of_atom(jax.random.fold_in(keys[20], 71), 0)
    item_lengths = draw_item_lengths(jax.random.fold_in(keys[20], 71), 0)
    atom_types = draw_atom_types(jax.random.fold_in(keys[20], 71), 0)
    key_mask = plant((jax.random.randint(keys[5], (ATOMS,), 0, 8) < 7).astype(jnp.int32), jax.random.fold_in(keys[5], 1), 0, 1)
    ln1_gain = jnp.clip(1.0 + 0.1 * jax.random.normal(keys[6], (D,), jnp.float32), 0.5, 1.5)
    ln1_bias = normal_values(keys[7], (D,), 0.5, 3.0, (), jnp.float32)
    w_qkv = normal_values(keys[8], (D, 3 * D), D ** -0.5, 0.21875)
    kernel_means = jnp.clip(jax.random.uniform(keys[9], (KERNELS,), jnp.float32, 0.0, 16.0), 0.0, 16.0)
    kernel_widths = jnp.clip(jnp.exp(jax.random.uniform(keys[10], (KERNELS,), jnp.float32, math.log(0.5), math.log(4.0))), 0.5, 4.0)
    kernel_weight = normal_values(keys[11], (KERNELS, HEADS), 1.0, 6.0)
    type_scale = jnp.clip(1.0 + 0.1 * jax.random.normal(keys[12], (MOL_TYPES + RES_TYPES,), jnp.float32), 0.5, 1.5)
    type_shift = normal_values(keys[13], (MOL_TYPES + RES_TYPES,), 0.5, 3.0, (), jnp.float32)
    w_out = normal_values(keys[14], (D, D), (D // 16) ** -0.5, 0.875)
    ln2_gain = jnp.clip(1.0 + 0.1 * jax.random.normal(keys[15], (D,), jnp.float32), 0.5, 1.5)
    ln2_bias = normal_values(keys[16], (D,), 0.5, 3.0, (), jnp.float32)
    w_up = normal_values(keys[17], (D, FF), D ** -0.5, 0.21875)
    w_down = normal_values(keys[18], (FF, D), FF ** -0.5, 0.109375)
    out_cotangent = normal_values(keys[19], (ATOMS, D), 1.0, 6.0, ((0, 32),))
    return dict(tokens=tokens, positions=positions, item_of_atom=item_of_atom, item_lengths=item_lengths, atom_types=atom_types, key_mask=key_mask, ln1_gain=ln1_gain, ln1_bias=ln1_bias, w_qkv=w_qkv, kernel_means=kernel_means, kernel_widths=kernel_widths, kernel_weight=kernel_weight, type_scale=type_scale, type_shift=type_shift, w_out=w_out, ln2_gain=ln2_gain, ln2_bias=ln2_bias, w_up=w_up, w_down=w_down, out_cotangent=out_cotangent)


@jax.custom_vjp
def low(v):
    return lax.optimization_barrier(v.astype(jnp.bfloat16)).astype(jnp.float32)

@jax.custom_vjp
def low_back(v):
    return v

def low_keep(v):
    return (low(v), None)

def low_pass(kept, grad):
    return (grad,)

def back_keep(v):
    return (v, None)

def back_low(kept, grad):
    return (low(grad),)
low.defvjp(low_keep, low_pass)
low_back.defvjp(back_keep, back_low)
LN_EPS = 1e-05
MASKED = -1e+30
ROOT_TWO_PI = math.sqrt(2.0 * math.pi)

def layer_norm(values, ln_gain, ln_shift):
    centre = lax.optimization_barrier(jnp.mean(values, axis=-1, keepdims=True))
    offsets = values - centre
    spread = lax.optimization_barrier(jnp.mean(offsets * offsets, axis=-1, keepdims=True))
    return offsets * lax.rsqrt(spread + LN_EPS) * ln_gain + ln_shift

def pair_geometry(query_pos, key_pos, query_scale, key_scale, query_shift, key_shift, centres, widths):
    displace = query_pos[:, :, None] - key_pos[:, None, :]
    length = jnp.sqrt(lax.optimization_barrier(jnp.sum(displace * displace, axis=0)) + 1.0)
    stretched = query_scale[:, None] * key_scale[None, :] * length + query_shift[:, None] + key_shift[None, :]
    normed = (stretched[:, :, None] - centres) / widths
    return jnp.exp(-0.5 * normed * normed) / (ROOT_TWO_PI * widths)

def pair_allowed(query_item, key_item, key_open, query_global, key_global):
    same_item = query_item[:, None] == key_item[None, :]
    visible = (key_open[None, :] > 0) | (query_global[:, None] == key_global[None, :])
    return same_item & visible

def matmul_high(left, right):
    return jnp.dot(left, right, precision=lax.Precision.HIGHEST)

def reference(tokens, positions, item_of_atom, item_lengths, atom_types, key_mask, ln1_gain, ln1_bias, w_qkv, kernel_means, kernel_widths, kernel_weight, type_scale, type_shift, w_out, ln2_gain, ln2_bias, w_up, w_down, out_cotangent):
    atoms_total = tokens.shape[0]
    model_width = tokens.shape[1]
    heads_count = kernel_weight.shape[1]
    head_size = model_width // heads_count
    head_scale = head_size ** (-0.5)
    item_flags = (item_lengths > 2 * MOL_MEAN).astype(jnp.int32)
    table_index = (atom_types + MOL_TYPES * item_flags[item_of_atom]).astype(jnp.int32)
    global_ids = jnp.arange(atoms_total, dtype=jnp.int32)
    block_rows = math.gcd(atoms_total, 64)
    block_count = atoms_total // block_rows
    key_span = min(atoms_total, block_rows + 2 * PROT_LEN)

    def forward(tokens_wide, positions_wide, gain_first, shift_first, qkv_weight, centres, widths, kernel_wide, scale_table, shift_table, out_weight, gain_second, shift_second, up_weight, down_weight):
        normed_first = layer_norm(tokens_wide, gain_first, shift_first)
        projected = low(low_back(matmul_high(low(normed_first), qkv_weight)))
        query = projected[:, :model_width].reshape(atoms_total, heads_count, head_size)
        key_heads = projected[:, model_width:2 * model_width].reshape(atoms_total, heads_count, head_size)
        value_heads = projected[:, 2 * model_width:].reshape(atoms_total, heads_count, head_size)
        atom_scale = scale_table[table_index]
        atom_shift = shift_table[table_index]

        def attend(block):
            query_block, query_pos, query_scale, query_shift, query_item, query_global = block
            key_start = jnp.clip(query_global[0] - PROT_LEN, 0, atoms_total - key_span).astype(jnp.int32)
            key_pos = lax.dynamic_slice_in_dim(positions_wide, key_start, key_span, 1)
            key_scale = lax.dynamic_slice_in_dim(atom_scale, key_start, key_span, 0)
            key_shift = lax.dynamic_slice_in_dim(atom_shift, key_start, key_span, 0)
            key_items = lax.dynamic_slice_in_dim(item_of_atom, key_start, key_span, 0)
            key_open = lax.dynamic_slice_in_dim(key_mask, key_start, key_span, 0)
            key_global = lax.dynamic_slice_in_dim(global_ids, key_start, key_span, 0)
            key_part = lax.dynamic_slice_in_dim(key_heads, key_start, key_span, 0)
            value_part = lax.dynamic_slice_in_dim(value_heads, key_start, key_span, 0)
            phi = pair_geometry(query_pos, key_pos, query_scale, key_scale, query_shift, key_shift, centres, widths)
            phi_low = low(phi)
            dots = jnp.einsum('qhd,khd->hqk', query_block, key_part, precision=lax.Precision.HIGHEST)
            bias_terms = jnp.einsum('qkc,ch->hqk', phi_low, kernel_wide, precision=lax.Precision.HIGHEST)
            allowed = pair_allowed(query_item, key_items, key_open, query_global, key_global)
            scores = low_back(jnp.where(allowed[None], dots * head_scale + bias_terms, MASKED))
            log_total = jax.nn.logsumexp(scores, axis=-1, keepdims=True)
            probs = low(jnp.exp(scores - log_total))
            summed = jnp.einsum('hqk,khd->qhd', probs, value_part, precision=lax.Precision.HIGHEST)
            return summed.reshape(block_rows, model_width)
        blocks = (query.reshape(block_count, block_rows, heads_count, head_size), positions_wide.reshape(3, block_count, block_rows).transpose(1, 0, 2), atom_scale.reshape(block_count, block_rows), atom_shift.reshape(block_count, block_rows), item_of_atom.reshape(block_count, block_rows), global_ids.reshape(block_count, block_rows))
        attended = lax.map(jax.checkpoint(attend), blocks).reshape(atoms_total, model_width)
        attended_low = low(low_back(attended))
        mixed = tokens_wide + low_back(matmul_high(attended_low, out_weight))
        normed_second = layer_norm(mixed, gain_second, shift_second)
        up_proj = low_back(matmul_high(low(normed_second), up_weight))
        hidden = low(jax.nn.gelu(up_proj))
        return mixed + matmul_high(hidden, down_weight)
    primals = (tokens.astype(jnp.float32), positions, ln1_gain, ln1_bias, w_qkv.astype(jnp.float32), kernel_means, kernel_widths, kernel_weight.astype(jnp.float32), type_scale, type_shift, w_out.astype(jnp.float32), ln2_gain, ln2_bias, w_up.astype(jnp.float32), w_down.astype(jnp.float32))
    output, backward = jax.vjp(forward, *primals)
    grads = backward(out_cotangent.astype(jnp.float32))
    return (output.astype(jnp.bfloat16), grads[0], grads[1], grads[2], grads[3], grads[4], grads[5], grads[6], grads[7], grads[8], grads[9], grads[10], grads[11], grads[12], grads[13], grads[14])
```

```python
import functools
import math

import jax
import jax.numpy as jnp
from jax import lax
from jax.experimental import pallas as pl
from jax.experimental.pallas import tpu as pltpu
from jax.sharding import PartitionSpec as P

MOL_TYPES = 128
PROT_LEN = 768
MOL_MEAN = 32

LN_EPS = 1e-05
MASKED = -1e30
ROOT_TWO_PI = math.sqrt(2.0 * math.pi)
LOG2E = math.log2(math.e)
KAPPA = math.sqrt(0.5 * LOG2E)

PAD = 32
GROUP = 8
SPAN = PAD * GROUP
PIECES = 3
CHUNK = 32
MESH = ("pb", "ka")

BF = jnp.bfloat16
F32 = jnp.float32


def shifted(block, axis, distance):
    devices = range(lax.axis_size(axis))
    route = [(i - distance, i) for i in devices if i - distance in devices]
    return lax.ppermute(block, axis, route)


def core_flip(block):
    devices = range(lax.axis_size(MESH))
    return lax.ppermute(block, MESH, [(i, i ^ 1) for i in devices])


def window_of(block, chips):
    pieces = [
        block if step == 0 else shifted(block, MESH, -2 * step) for step in range(-chips, chips + 1)
    ]
    mine = jnp.stack(pieces, axis=0)
    return mine, core_flip(mine)


def layer_norm(values, ln_gain, ln_shift):
    centre = jnp.mean(values, axis=-1, keepdims=True)
    offsets = values - centre
    spread = jnp.mean(offsets * offsets, axis=-1, keepdims=True)
    return offsets * lax.rsqrt(spread + LN_EPS) * ln_gain + ln_shift


def dot_nn(left, right):
    return lax.dot_general(left, right, (((1,), (0,)), ((), ())), preferred_element_type=F32)


def dot_nt(left, right):
    return lax.dot_general(left, right, (((1,), (1,)), ((), ())), preferred_element_type=F32)


def stretched_of(own, other):
    delta = [own[:, i : i + 1] - other[i : i + 1, :] for i in range(3)]
    square = delta[0] * delta[0] + delta[1] * delta[1] + delta[2] * delta[2]
    dist = jnp.sqrt(square + 1.0)
    scales = own[:, 3:4] * other[3:4, :]
    stretched = scales * dist + own[:, 4:5] + other[4:5, :]
    return delta, dist, scales, stretched


def mask_of(own, other, key_is_own):
    same = own[:, 5:6] == other[5:6, :]
    itself = own[:, 7:8] == other[7:8, :]
    is_open = (own[:, 6:7] > 0.5) if key_is_own else (other[6:7, :] > 0.5)
    return jnp.where(same & (is_open | itself), 0.0, MASKED)


def head_mask():
    head = lax.broadcasted_iota(jnp.int32, (GROUP, SPAN), 0)
    column = lax.broadcasted_iota(jnp.int32, (GROUP, SPAN), 1)
    return jnp.where(column // PAD == head, 1.0, 0.0)


def expand_into(out_ref, padded, groups):
    rows = padded.shape[0]
    keep = head_mask()
    for g in range(groups):
        part = padded[:, g * SPAN : (g + 1) * SPAN].astype(F32)
        wide = jnp.broadcast_to(part[:, None, :], (rows, GROUP, SPAN)) * keep[None]
        out_ref[g] = wide.reshape(rows * GROUP, SPAN).astype(BF)


def collapse(values):
    rows = values.shape[0] // GROUP
    return jnp.sum(values.reshape(rows, GROUP, SPAN) * head_mask()[None], axis=1)


def spread_mask(mask_ref, mask):
    mask_ref[...] = jnp.broadcast_to(mask[:, None, :], mask_ref.shape)


def bias_kernel(span_ref, own_ref, other_ref, tab_ref, kwt_ref, out_ref, str_ref):
    rows, keys = str_ref.shape
    kernels = tab_ref.shape[1]
    str_ref[...] = stretched_of(own_ref[...], other_ref[...])[3]

    def step(i, carry):
        block = str_ref[pl.ds(i * 8, 8), :]
        for r in range(8):
            parts = []
            for half in range(keys // 128):
                line = jnp.broadcast_to(
                    block[r : r + 1, half * 128 : (half + 1) * 128], (kernels, 128)
                )
                z = (line - tab_ref[0]) * tab_ref[1]
                parts.append(jnp.exp2(tab_ref[2] - z * z).astype(BF))
            phi = jnp.concatenate(parts, axis=1)
            out_ref[0, i * 8 + r] = dot_nn(kwt_ref[...], phi) * LOG2E
        return carry

    lax.fori_loop(0, rows // 8, step, 0)


def forward_kernel(
    scale2,
    groups,
    span_ref,
    own_ref,
    other_ref,
    mine_ref,
    sib_ref,
    tok_ref,
    ln_ref,
    w_ref,
    ones_ref,
    place_ref,
    bias_ref,
    att_ref,
    qaug_ref,
    lse_ref,
    now_ref,
    kvq_ref,
    qexp_ref,
    mask_ref,
    max_ref,
    sum_ref,
    acc_ref,
    lane_ref,
):
    step = pl.program_id(0)
    width = groups * SPAN
    rows = tok_ref.shape[0]
    gain, shift = ln_ref[0:1, :], ln_ref[1:2, :]

    @pl.when(step == 0)
    def _():
        normed = layer_norm(tok_ref[...].astype(F32), gain, shift).astype(BF)
        now_ref[...] = normed
        query = dot_nn(normed, w_ref[:, 2 * width :]).astype(BF)
        qaug_ref[...] = query
        expand_into(qexp_ref, query, groups)
        max_ref[...] = jnp.full(max_ref.shape, 2.0 * MASKED, F32)
        sum_ref[...] = jnp.zeros(sum_ref.shape, F32)
        acc_ref[...] = jnp.zeros(acc_ref.shape, F32)

    tokens = jnp.concatenate([mine_ref[0], sib_ref[0]], axis=0).astype(F32)
    normed = layer_norm(tokens, gain, shift).astype(BF)
    for part in range(3):
        value = dot_nn(normed, w_ref[:, part * width : (part + 1) * width])
        if part < 2:
            value = value + ones_ref[...]
        kvq_ref[0, :, part * width : (part + 1) * width] = value.astype(BF)
    spread_mask(mask_ref, mask_of(own_ref[...], other_ref[...], False))

    def chunk_step(i, carry):
        at = pl.multiple_of(i * CHUNK, CHUNK)
        lines = pl.ds(pl.multiple_of(i * CHUNK * GROUP, CHUNK * GROUP), CHUNK * GROUP)
        mask = mask_ref[pl.ds(at, CHUNK)]
        for g in range(groups):
            columns = slice(g * SPAN, (g + 1) * SPAN)
            dots = dot_nt(qexp_ref[g, lines, :], kvq_ref[0, :, columns])
            bias = bias_ref[0, pl.ds(at, CHUNK), g * GROUP : (g + 1) * GROUP, :] + mask
            scores = dots * scale2 + bias.reshape(dots.shape)
            old = max_ref[g, lines, :]
            top = jnp.maximum(scores[:, :128], scores[:, 128:])
            new = jnp.maximum(old, jnp.max(top, axis=1, keepdims=True))
            alpha = jnp.exp2(old - new)
            low = jnp.exp2(scores[:, :128] - new)
            high = jnp.exp2(scores[:, 128:] - new)
            max_ref[g, lines, :] = new
            sum_ref[g, lines, :] = sum_ref[g, lines, :] * alpha + (low + high)
            probs = jnp.concatenate([low, high], axis=1).astype(BF)
            values = dot_nn(probs, kvq_ref[0, :, width + g * SPAN : width + (g + 1) * SPAN])
            wide = jnp.concatenate([alpha, alpha], axis=1)
            acc_ref[g, lines, :] = acc_ref[g, lines, :] * wide + values
        return carry

    lax.fori_loop(0, rows // CHUNK, chunk_step, 0)

    @pl.when(step == span_ref[1] - span_ref[0])
    def _():
        lane = lax.broadcasted_iota(jnp.int32, (GROUP, 128), 1)
        head = lax.broadcasted_iota(jnp.int32, (GROUP, 128), 0)

        def finish(i, carry):
            at = pl.multiple_of(i * CHUNK, CHUNK)
            lines = pl.ds(pl.multiple_of(i * CHUNK * GROUP, CHUNK * GROUP), CHUNK * GROUP)
            lanes = jnp.zeros((CHUNK, 128), F32)
            for g in range(groups):
                total = jnp.sum(sum_ref[g, lines, :], axis=1, keepdims=True)
                attended = collapse(acc_ref[g, lines, :] / total)
                att_ref[pl.ds(at, CHUNK), g * SPAN : (g + 1) * SPAN] = attended
                lse = max_ref[g, lines, :] + jnp.log(total) * LOG2E
                own_lane = jnp.where(lane == head + g * GROUP, 1.0, 0.0)
                lanes = lanes + jnp.sum(
                    lse.reshape(CHUNK, GROUP, 128) * own_lane[None], axis=1
                )
            lane_ref[pl.ds(at, CHUNK), :] = lanes
            return carry

        lax.fori_loop(0, rows // CHUNK, finish, 0)
        rest = lane_ref[...] * (-1.0 / scale2)
        query = qaug_ref[...].astype(F32)
        for p in range(PIECES):
            piece = rest.astype(BF)
            rest = rest - piece.astype(F32)
            lse_ref[p] = piece
            query = query + dot_nn(piece, place_ref[p])
        qaug_ref[...] = query.astype(BF)


def query_grad_kernel(
    scale2,
    head_scale,
    groups,
    span_ref,
    own_ref,
    other_ref,
    qaug_ref,
    doaug_ref,
    kv_ref,
    bias_ref,
    tab_ref,
    kw_ref,
    dq_ref,
    gkw_ref,
    moment_ref,
    atom_ref,
    key_ref,
    qexp_ref,
    doexp_ref,
    mask_ref,
    str_ref,
    ds_ref,
    dqacc_ref,
    dphi_ref,
    phi_ref,
    gs_ref,
    own_acc_ref,
):
    step = pl.program_id(0)
    width = groups * SPAN
    rows, keys = str_ref.shape
    kernels = tab_ref.shape[1]

    @pl.when(step == 0)
    def _():
        expand_into(qexp_ref, qaug_ref[...], groups)
        expand_into(doexp_ref, doaug_ref[...], groups)
        dqacc_ref[...] = jnp.zeros(dqacc_ref.shape, F32)
        gkw_ref[...] = jnp.zeros(gkw_ref.shape, F32)
        moment_ref[...] = jnp.zeros(moment_ref.shape, F32)
        own_acc_ref[...] = jnp.zeros(own_acc_ref.shape, F32)

    own, other = own_ref[...], other_ref[...]
    str_ref[...] = stretched_of(own, other)[3]
    spread_mask(mask_ref, mask_of(own, other, False))

    def chunk_step(i, carry):
        at = pl.multiple_of(i * CHUNK, CHUNK)
        lines = pl.ds(pl.multiple_of(i * CHUNK * GROUP, CHUNK * GROUP), CHUNK * GROUP)
        mask = mask_ref[pl.ds(at, CHUNK)]
        for g in range(groups):
            key_block = kv_ref[0, :, g * SPAN : (g + 1) * SPAN]
            value_block = kv_ref[0, :, width + g * SPAN : width + (g + 1) * SPAN]
            dots = dot_nt(qexp_ref[g, lines, :], key_block)
            grads = dot_nt(doexp_ref[g, lines, :], value_block)
            bias = bias_ref[0, pl.ds(at, CHUNK), g * GROUP : (g + 1) * GROUP, :] + mask
            probs = jnp.exp2(dots * scale2 + bias.reshape(dots.shape))
            grad_scores = probs * grads
            ds_ref[pl.ds(at, CHUNK), g * GROUP : (g + 1) * GROUP, :] = grad_scores.reshape(
                CHUNK, GROUP, keys
            )
            dqacc_ref[g, lines, :] += dot_nn(grad_scores.astype(BF), key_block)
        return carry

    lax.fori_loop(0, rows // CHUNK, chunk_step, 0)

    tile = 32

    def pair_step(i, carry):
        block = str_ref[pl.ds(pl.multiple_of(i * 8, 8), 8), :]
        lows = []
        for r in range(8):
            low = ds_ref[i * 8 + r].astype(BF)
            lows.append(low)
            dphi_ref[:, r * keys : (r + 1) * keys] = dot_nn(kw_ref[...], low)
        halves = keys // 128
        partial = [[None] * halves for _ in range(8)]
        for c in range(kernels // tile):
            cs = slice(c * tile, (c + 1) * tile)
            first = jnp.zeros((tile, 128), F32)
            second = jnp.zeros((tile, 128), F32)
            for r in range(8):
                for half in range(halves):
                    line = jnp.broadcast_to(
                        block[r : r + 1, half * 128 : (half + 1) * 128], (tile, 128)
                    )
                    columns = slice(r * keys + half * 128, r * keys + (half + 1) * 128)
                    z = (line - tab_ref[0, cs, :]) * tab_ref[1, cs, :]
                    phi = jnp.exp2(tab_ref[2, cs, :] - z * z)
                    phi_ref[cs, columns] = phi.astype(BF)
                    ez = dphi_ref[cs, columns] * phi * z
                    first = first + ez
                    second = second + ez * z
                    term = jnp.sum((ez * tab_ref[3, cs, :]).reshape(tile // 8, 8, 128), axis=0)
                    partial[r][half] = term if c == 0 else partial[r][half] + term
            moment_ref[0, cs, :] += first
            moment_ref[1, cs, :] += second
        lines = [
            jnp.concatenate(
                [jnp.sum(partial[r][half], axis=0, keepdims=True) for half in range(halves)], axis=1
            )
            for r in range(8)
        ]
        gs_ref[pl.ds(pl.multiple_of(i * 8, 8), 8), :] = jnp.concatenate(lines, axis=0)
        gkw_ref[...] += dot_nt(phi_ref[...], jnp.concatenate(lows, axis=1))
        return carry

    lax.fori_loop(0, rows // 8, pair_step, 0)

    delta, dist, scales, _ = stretched_of(own, other)
    grad = -gs_ref[...]
    by_scale = grad * dist
    pull = grad * scales / dist
    terms = [pull * delta[0], pull * delta[1], pull * delta[2], by_scale * other[3:4, :], grad]
    for k, term in enumerate(terms):
        own_acc_ref[k] += term[:, :128] + term[:, 128:]
    lines = [-jnp.sum(terms[k], axis=0, keepdims=True) for k in range(3)]
    lines.append(jnp.sum(by_scale * own[:, 3:4], axis=0, keepdims=True))
    lines.append(jnp.sum(grad, axis=0, keepdims=True))
    lines.append(jnp.zeros((3, keys), F32))
    key_ref[...] = jnp.concatenate(lines, axis=0)

    @pl.when(step == span_ref[1] - span_ref[0])
    def _():
        lane = lax.broadcasted_iota(jnp.int32, (rows, 128), 1)
        total = jnp.zeros((rows, 128), F32)
        for k in range(5):
            column = jnp.sum(own_acc_ref[k], axis=1, keepdims=True)
            total = total + jnp.where(lane == k, column, 0.0)
        atom_ref[...] = total

        def finish(i, carry):
            at = pl.multiple_of(i * CHUNK, CHUNK)
            lines = pl.ds(pl.multiple_of(i * CHUNK * GROUP, CHUNK * GROUP), CHUNK * GROUP)
            for g in range(groups):
                value = collapse(dqacc_ref[g, lines, :]) * head_scale
                dq_ref[pl.ds(at, CHUNK), g * SPAN : (g + 1) * SPAN] = value.astype(BF)
            return carry

        lax.fori_loop(0, rows // CHUNK, finish, 0)


def key_grad_kernel(
    scale2,
    head_scale,
    groups,
    model_width,
    span_ref,
    own_ref,
    other_ref,
    kv_ref,
    q_ref,
    mine_ref,
    sib_ref,
    wout_ref,
    place_ref,
    bias_ref,
    dkv_ref,
    kexp_ref,
    vexp_ref,
    mask_ref,
    qb_ref,
    dob_ref,
    dk_ref,
    dv_ref,
):
    step = pl.program_id(0)
    width = groups * SPAN
    rows = own_ref.shape[0]

    @pl.when(step == 0)
    def _():
        expand_into(kexp_ref, kv_ref[0, :, :width], groups)
        expand_into(vexp_ref, kv_ref[0, :, width:], groups)
        dk_ref[...] = jnp.zeros(dk_ref.shape, F32)
        dv_ref[...] = jnp.zeros(dv_ref.shape, F32)

    payload = jnp.concatenate([mine_ref[0], sib_ref[0]], axis=0)
    tail = payload[:, model_width:]
    grads = dot_nt(payload[:, :model_width], wout_ref[...]).astype(BF).astype(F32)
    dob_ref[...] = (grads + dot_nn(tail, place_ref[1])).astype(BF)
    qb_ref[...] = (q_ref[0].astype(F32) + dot_nn(tail, place_ref[0])).astype(BF)
    spread_mask(mask_ref, mask_of(own_ref[...], other_ref[...], True))

    def chunk_step(i, carry):
        at = pl.multiple_of(i * CHUNK, CHUNK)
        lines = pl.ds(pl.multiple_of(i * CHUNK * GROUP, CHUNK * GROUP), CHUNK * GROUP)
        mask = mask_ref[pl.ds(at, CHUNK)]
        for g in range(groups):
            query_block = qb_ref[:, g * SPAN : (g + 1) * SPAN]
            grad_block = dob_ref[:, g * SPAN : (g + 1) * SPAN]
            dots = dot_nt(kexp_ref[g, lines, :], query_block)
            grads = dot_nt(vexp_ref[g, lines, :], grad_block)
            bias = bias_ref[0, pl.ds(at, CHUNK), g * GROUP : (g + 1) * GROUP, :] + mask
            probs = jnp.exp2(dots * scale2 + bias.reshape(dots.shape))
            grad_scores = (probs * grads).astype(BF)
            dk_ref[g, lines, :] += dot_nn(grad_scores, query_block)
            dv_ref[g, lines, :] += dot_nn(probs.astype(BF), grad_block)
        return carry

    lax.fori_loop(0, rows // CHUNK, chunk_step, 0)

    @pl.when(step == span_ref[1] - span_ref[0])
    def _():
        def finish(i, carry):
            at = pl.multiple_of(i * CHUNK, CHUNK)
            lines = pl.ds(pl.multiple_of(i * CHUNK * GROUP, CHUNK * GROUP), CHUNK * GROUP)
            for g in range(groups):
                key = collapse(dk_ref[g, lines, :]) * head_scale
                value = collapse(dv_ref[g, lines, :])
                dkv_ref[pl.ds(at, CHUNK), g * SPAN : (g + 1) * SPAN] = key.astype(BF)
                dkv_ref[pl.ds(at, CHUNK), width + g * SPAN : width + (g + 1) * SPAN] = (
                    value.astype(BF)
                )
            return carry

        lax.fori_loop(0, rows // CHUNK, finish, 0)


def fixed(shape, *index):
    at = index or (0,) * len(shape)
    return pl.BlockSpec(shape, lambda j, span: at, pipeline_mode=pl.Buffered(1))


def moving(shape, rank_at=0, last=0):
    def index(j, span):
        at = [0] * len(shape)
        at[rank_at] = jnp.minimum(span[0] + j, span[1])
        if last:
            at[-1] = last
        return tuple(at)

    return pl.BlockSpec(shape, index)


def while_inside(kernel):
    def body(span_ref, *refs):
        @pl.when(pl.program_id(0) <= span_ref[1] - span_ref[0])
        def _():
            kernel(span_ref, *refs)

    return body


def call(kernel, steps, in_specs, out_specs, out_shapes, scratch, flops, name):
    return pl.pallas_call(
        while_inside(kernel),
        grid_spec=pltpu.PrefetchScalarGridSpec(
            num_scalar_prefetch=1,
            grid=(steps,),
            in_specs=in_specs,
            out_specs=out_specs,
            scratch_shapes=scratch,
        ),
        out_shape=out_shapes,
        compiler_params=pltpu.CompilerParams(
            dimension_semantics=("arbitrary",), vmem_limit_bytes=60 * 1024 * 1024
        ),
        cost_estimate=pl.CostEstimate(flops=flops, bytes_accessed=20_000_000, transcendentals=0),
        name=name,
    )


def shape_of(shape, dtype=F32):
    return jax.ShapeDtypeStruct(shape, dtype)


def pad_heads(values, heads, size):
    rows = values.shape[0]
    wide = jnp.pad(values.reshape(rows, heads, size), ((0, 0), (0, 0), (0, PAD - size)))
    return wide.reshape(rows, heads * PAD)


def drop_pad(values, heads, size):
    rows = values.shape[0]
    return values.reshape(rows, heads, PAD)[:, :, :size].reshape(rows, heads * size)


def pieces_of(values):
    rest, out = values, []
    for _ in range(PIECES):
        piece = rest.astype(BF)
        rest = rest - piece.astype(F32)
        out.append(piece)
    return out


def on_device(
    tokens,
    positions,
    item_of_atom,
    item_lengths,
    atom_types,
    key_mask,
    ln1_gain,
    ln1_bias,
    w_qkv,
    kernel_means,
    kernel_widths,
    kernel_weight,
    type_scale,
    type_shift,
    w_out,
    ln2_gain,
    ln2_bias,
    w_up,
    w_down,
    out_cotangent,
):
    own_rows, model_width = tokens.shape
    kernels, heads = kernel_weight.shape
    head_size = model_width // heads
    head_scale = head_size ** (-0.5)
    scale2 = head_scale * LOG2E
    groups = heads // GROUP
    width = groups * SPAN
    ka_count = lax.axis_size("ka")
    flat = lax.axis_index("pb") * ka_count + lax.axis_index("ka")
    core = flat % 2
    reach = (PROT_LEN + own_rows - 2) // own_rows
    chips = (reach + 1) // 2
    pairs = 2 * chips + 1
    keys = 2 * own_rows
    atoms = positions.shape[1]
    chip_start = (flat // 2) * keys
    margin = chips * keys

    table = jnp.concatenate(
        [
            positions,
            item_of_atom.astype(F32)[None],
            key_mask.astype(F32)[None],
            jnp.arange(atoms, dtype=jnp.int32).astype(F32)[None],
            atom_types.astype(F32)[None],
        ],
        axis=0,
    )
    table = jnp.pad(table, ((0, 0), (margin, margin)), constant_values=-1.0)
    table = lax.dynamic_slice_in_dim(table, chip_start, pairs * keys, 1)
    table = table.reshape(table.shape[0], pairs, 2, own_rows)
    table = jnp.where(core == 0, table, table[:, :, ::-1, :]).reshape(-1, pairs * keys)
    item_row = table[3]
    item_ids = jnp.arange(item_lengths.shape[0], dtype=F32)
    flags = jnp.where(item_lengths > 2 * MOL_MEAN, float(MOL_TYPES), 0.0)
    protein = jnp.sum(
        jnp.where(item_row[None, :] == item_ids[:, None], flags[:, None], 0.0), axis=0
    )
    table_row = table[6] + protein
    onehot = table_row[None, :] == jnp.arange(type_scale.shape[0], dtype=F32)[:, None]
    scale_row = jnp.sum(jnp.where(onehot, type_scale[:, None], 0.0), axis=0)
    shift_row = jnp.sum(jnp.where(onehot, type_shift[:, None], 0.0), axis=0)
    other = jnp.stack(
        [table[0], table[1], table[2], scale_row, shift_row, item_row, table[4], table[5]], axis=0
    )
    own = other[:, margin : margin + own_rows].T
    first_item = item_row[margin].astype(jnp.int32)
    last_item = item_row[margin + own_rows - 1].astype(jnp.int32)
    low_atom = jnp.sum((item_of_atom < first_item).astype(jnp.int32))
    high_atom = jnp.sum((item_of_atom <= last_item).astype(jnp.int32))
    first_pair = (low_atom - chip_start + margin) // keys
    last_pair = (high_atom - 1 - chip_start + margin) // keys
    span = jnp.stack([first_pair, last_pair]).astype(jnp.int32)

    lanes = (kernels, 128)
    tabs = jnp.stack(
        [
            jnp.broadcast_to(kernel_means[:, None], lanes),
            jnp.broadcast_to((KAPPA / kernel_widths)[:, None], lanes),
            jnp.broadcast_to((-LOG2E * jnp.log(ROOT_TWO_PI * kernel_widths))[:, None], lanes),
            jnp.broadcast_to((1.0 / (KAPPA * kernel_widths))[:, None], lanes),
        ]
    )
    column = jnp.arange(width)
    ones_row = ((column % PAD >= head_size) & (column % PAD < head_size + PIECES)).astype(F32)
    piece_of_column = column % PAD - head_size
    place_lane = jnp.arange(128)
    place_own = jnp.stack(
        [
            (
                (place_lane[:, None] == (column // PAD)[None, :]) & (piece_of_column == p)[None, :]
            ).astype(BF)
            for p in range(PIECES)
        ]
    )
    tail_width = 256
    tail_lane = jnp.arange(tail_width)
    column_lane = jnp.where(
        (piece_of_column >= 0) & (piece_of_column < PIECES),
        piece_of_column * heads + column // PAD,
        -1,
    )
    place_lse = (tail_lane[:, None] == column_lane[None, :]).astype(BF)
    place_delta = (
        (tail_lane[:, None] - PIECES * heads == column_lane[None, :])
        & (tail_lane[:, None] >= PIECES * heads)
    ).astype(BF)
    place_tail = jnp.stack([place_lse, place_delta])

    w_pad = jnp.concatenate(
        [
            pad_heads(w_qkv[:, model_width : 2 * model_width], heads, head_size),
            pad_heads(w_qkv[:, 2 * model_width :], heads, head_size),
            pad_heads(w_qkv[:, :model_width], heads, head_size),
        ],
        axis=1,
    )
    w_out_pad = jnp.pad(
        w_out.reshape(heads, head_size, model_width), ((0, 0), (0, PAD - head_size), (0, 0))
    ).reshape(width, model_width)

    mine, sib = window_of(tokens, chips)

    own_spec = fixed((own_rows, 8))
    other_spec = moving((8, keys), 1)
    bias_spec = moving((1, own_rows, heads, keys))
    bias = call(
        bias_kernel,
        pairs,
        [own_spec, other_spec, fixed((4, kernels, 128)), fixed((heads, kernels))],
        bias_spec,
        shape_of((pairs, own_rows, heads, keys)),
        [pltpu.VMEM((own_rows, keys), F32)],
        2 * own_rows * 4 * keys * kernels * 256,
        "pair_bias",
    )(span, own, other, tabs, kernel_weight.T)

    ln1 = jnp.stack([ln1_gain, ln1_bias])
    expanded = pltpu.VMEM((groups, own_rows * GROUP, SPAN), BF)
    summed = pltpu.VMEM((groups, own_rows * GROUP, SPAN), F32)
    mask_scratch = pltpu.VMEM((own_rows, GROUP, keys), F32)
    attended, q_aug, lse_pieces, normed_first_low, kvq = call(
        functools.partial(forward_kernel, scale2, groups),
        pairs,
        [
            own_spec,
            other_spec,
            moving((1, own_rows, model_width)),
            moving((1, own_rows, model_width)),
            fixed((own_rows, model_width)),
            fixed((2, model_width)),
            fixed((model_width, 3 * width)),
            fixed((1, width)),
            fixed((PIECES, 128, width)),
            bias_spec,
        ],
        [
            fixed((own_rows, width)),
            fixed((own_rows, width)),
            fixed((PIECES, own_rows, 128)),
            fixed((own_rows, model_width)),
            moving((1, keys, 3 * width)),
        ],
        [
            shape_of((own_rows, width)),
            shape_of((own_rows, width), BF),
            shape_of((PIECES, own_rows, 128), BF),
            shape_of((own_rows, model_width), BF),
            shape_of((pairs, keys, 3 * width), BF),
        ],
        [
            expanded,
            mask_scratch,
            pltpu.VMEM((groups, own_rows * GROUP, 128), F32),
            pltpu.VMEM((groups, own_rows * GROUP, 128), F32),
            summed,
            pltpu.VMEM((own_rows, 128), F32),
        ],
        2 * own_rows * GROUP * groups * 4 * keys * SPAN * 3,
        "attention_forward",
    )(span, own, other, mine, sib, tokens, ln1, w_pad, ones_row[None], place_own, bias)

    tokens_wide = tokens.astype(F32)
    attended_low_pad = attended.astype(BF)
    mixed = tokens_wide + dot_nn(attended_low_pad, w_out_pad)
    normed_second, second_back = jax.vjp(layer_norm, mixed, ln2_gain, ln2_bias)
    normed_second_low = normed_second.astype(BF)
    up_proj = dot_nn(normed_second_low, w_up)
    activated, gelu_back = jax.vjp(jax.nn.gelu, up_proj)
    hidden_low = activated.astype(BF)
    block_out = (mixed + dot_nn(hidden_low, w_down)).astype(BF)
    grad_hidden = dot_nt(out_cotangent, w_down)
    grad_up = gelu_back(grad_hidden)[0].astype(BF)
    grad_normed_second = dot_nt(grad_up, w_up)
    grad_mixed_norm, grad_gain_second, grad_shift_second = second_back(grad_normed_second)
    grad_mixed = out_cotangent.astype(F32) + grad_mixed_norm
    grad_mixed_low = grad_mixed.astype(BF)
    grad_attended = dot_nt(grad_mixed_low, w_out_pad).astype(BF)
    row_deltas = jnp.sum(
        (grad_attended.astype(F32) * attended).reshape(own_rows, heads, PAD), axis=2
    )
    delta_pieces = pieces_of(-row_deltas)
    do_aug = jnp.concatenate(
        [grad_attended.reshape(own_rows, heads, PAD)[:, :, :head_size]]
        + [piece[:, :, None] for piece in delta_pieces]
        + [jnp.zeros((own_rows, heads, PAD - head_size - PIECES), BF)],
        axis=2,
    ).reshape(own_rows, width)
    payload = jnp.concatenate(
        [grad_mixed_low]
        + [lse_pieces[p, :, :heads] for p in range(PIECES)]
        + delta_pieces
        + [jnp.zeros((own_rows, tail_width - 2 * PIECES * heads), BF)],
        axis=1,
    )
    payload_mine, payload_sib = window_of(payload, chips)

    dq_pad, grad_kernel, moments, own_atoms, key_atoms = call(
        functools.partial(query_grad_kernel, scale2, head_scale, groups),
        pairs,
        [
            own_spec,
            other_spec,
            fixed((own_rows, width)),
            fixed((own_rows, width)),
            moving((1, keys, 2 * width)),
            bias_spec,
            fixed((4, kernels, 128)),
            fixed((kernels, heads)),
        ],
        [
            fixed((own_rows, width)),
            fixed((kernels, heads)),
            fixed((2, kernels, 128)),
            fixed((own_rows, 128)),
            other_spec,
        ],
        [
            shape_of((own_rows, width), BF),
            shape_of((kernels, heads)),
            shape_of((2, kernels, 128)),
            shape_of((own_rows, 128)),
            shape_of((8, pairs * keys)),
        ],
        [
            expanded,
            expanded,
            mask_scratch,
            pltpu.VMEM((own_rows, keys), F32),
            pltpu.VMEM((own_rows, heads, keys), F32),
            summed,
            pltpu.VMEM((kernels, 8 * keys), F32),
            pltpu.VMEM((kernels, 8 * keys), BF),
            pltpu.VMEM((own_rows, keys), F32),
            pltpu.VMEM((5, own_rows, 128), F32),
        ],
        2 * own_rows * GROUP * groups * 4 * keys * SPAN * 8,
        "query_gradients",
    )(span, own, other, q_aug, do_aug, kvq, bias, tabs, kernel_weight)

    dkv_pad = call(
        functools.partial(key_grad_kernel, scale2, head_scale, groups, model_width),
        pairs,
        [
            own_spec,
            other_spec,
            fixed((1, own_rows, 2 * width), chips, 0, 0),
            moving((1, keys, width), 0, 2),
            moving((1, own_rows, model_width + tail_width)),
            moving((1, own_rows, model_width + tail_width)),
            fixed((width, model_width)),
            fixed((2, tail_width, width)),
            bias_spec,
        ],
        fixed((own_rows, 2 * width)),
        shape_of((own_rows, 2 * width), BF),
        [
            expanded,
            expanded,
            mask_scratch,
            pltpu.VMEM((keys, width), BF),
            pltpu.VMEM((keys, width), BF),
            summed,
            summed,
        ],
        2 * own_rows * GROUP * groups * 4 * keys * SPAN * 4,
        "key_gradients",
    )(
        span,
        own,
        other,
        kvq,
        kvq,
        payload_mine,
        payload_sib,
        w_out_pad,
        place_tail,
        bias,
    )

    grad_projected = jnp.concatenate(
        [
            drop_pad(dq_pad, heads, head_size),
            drop_pad(dkv_pad[:, :width], heads, head_size),
            drop_pad(dkv_pad[:, width:], heads, head_size),
        ],
        axis=1,
    )
    qkv_grad_weight = dot_nn(normed_first_low.T, grad_projected)
    grad_normed_first = dot_nt(grad_projected, w_qkv)
    unused, first_back = jax.vjp(layer_norm, tokens_wide, ln1_gain, ln1_bias)
    grad_tokens_norm, grad_gain_first, grad_shift_first = first_back(grad_normed_first)
    grad_tokens = grad_mixed + grad_tokens_norm

    pair_at = jnp.arange(pairs * keys) // keys
    visited = (pair_at >= first_pair) & (pair_at <= last_pair)
    key_atoms = jnp.where(visited[None, :], key_atoms[:5], 0.0)
    own_part = own_atoms[:, :5].T
    key_atoms = lax.dynamic_update_slice(
        key_atoms, key_atoms[:, margin : margin + own_rows] + own_part, (0, margin)
    )
    table_scale_grad = jnp.sum(jnp.where(onehot, key_atoms[3][None, :], 0.0), axis=1)
    table_shift_grad = jnp.sum(jnp.where(onehot, key_atoms[4][None, :], 0.0), axis=1)
    spots = key_atoms[:3].reshape(3, pairs, 2, own_rows)
    spots = jnp.where(core == 0, spots, spots[:, :, ::-1, :]).reshape(3, pairs * keys)
    everywhere = lax.dynamic_update_slice(
        jnp.zeros((3, atoms + 2 * margin), F32), spots, (0, chip_start)
    )[:, margin : margin + atoms]
    centre_sum = jnp.sum(moments[0], axis=1) / (KAPPA * kernel_widths)
    plain_sum = jnp.sum(grad_kernel * kernel_weight.astype(F32), axis=1)
    width_sum = (jnp.sum(moments[1], axis=1) / (KAPPA * KAPPA) - plain_sum) / kernel_widths

    small = lax.psum(
        (
            grad_gain_first,
            grad_shift_first,
            centre_sum,
            width_sum,
            grad_kernel,
            table_scale_grad,
            table_shift_grad,
            grad_gain_second,
            grad_shift_second,
            everywhere,
        ),
        MESH,
    )
    grad_positions = lax.dynamic_slice_in_dim(small[9], flat * own_rows, own_rows, 1)

    attended_low = drop_pad(attended_low_pad, heads, head_size)
    down_columns = dot_nn(out_cotangent.T, hidden_low)
    up_grad_weight = dot_nn(normed_second_low.T, grad_up)
    out_grad_weight = dot_nn(attended_low.T, grad_mixed_low)

    def over_ka(values):
        return lax.psum_scatter(values.astype(BF), "ka", scatter_dimension=1, tiled=True)

    pieces = tuple(
        over_ka(values)
        for values in (qkv_grad_weight, out_grad_weight, up_grad_weight, down_columns)
    )
    totals = tuple(lax.psum(piece, "pb").astype(F32) for piece in pieces)
    return (
        block_out,
        grad_tokens,
        grad_positions,
        small[0],
        small[1],
        totals[0],
        small[2],
        small[3],
        small[4],
        small[5],
        small[6],
        totals[1],
        small[7],
        small[8],
        totals[2],
        totals[3].T,
    )


def solution(mesh):
    rows = P(MESH, None)
    in_specs = (rows,) + (P(),) * 18 + (rows,)
    out_specs = (
        rows,
        rows,
        P(None, MESH),
        P(),
        P(),
        P(None, "ka"),
        P(),
        P(),
        P(),
        P(),
        P(),
        P(None, "ka"),
        P(),
        P(),
        P(None, "ka"),
        P("ka", None),
    )
    return jax.shard_map(
        on_device, mesh=mesh, in_specs=in_specs, out_specs=out_specs, check_vma=False
    )
```

```python
import functools
import math

import jax
import jax.numpy as jnp
import numpy as np
from jax import lax
from jax.experimental import pallas as pl
from jax.experimental.pallas import tpu as pltpu
from jax.sharding import PartitionSpec as P

MOL_TYPES = 128
PROT_LEN = 768
MOL_MEAN = 32

LN_EPS = 1e-05
GELU_SLOPE = math.sqrt(2.0 / math.pi)
GELU_CUBE = 0.044715
MASKED = -1e30
ROOT_TWO_PI = math.sqrt(2.0 * math.pi)
LOG2E = math.log2(math.e)
KAPPA = math.sqrt(0.5 * LOG2E)

PAD = 32
GROUP = 8
SPAN = PAD * GROUP
PIECES = 3
WEIGHT_PIECES = 2
CHUNK = 32
FEW = 8
MESH = ("pb", "ka")

BF = jnp.bfloat16
F32 = jnp.float32


def shifted(block, axis, distance):
    devices = range(lax.axis_size(axis))
    route = [(i - distance, i) for i in devices if i - distance in devices]
    return lax.ppermute(block, axis, route)


def core_flip(block):
    devices = range(lax.axis_size(MESH))
    return lax.ppermute(block, MESH, [(i, i ^ 1) for i in devices])


class Window:
    def __init__(self, block, sibling=None):
        devices = range(lax.axis_size(MESH))
        self.sibling = sibling
        far = [(i - 6 if (i >> 1) % 2 == 0 else i + 6, i) for i in devices]
        self.block = block
        self.before = shifted(block, MESH, 4)
        self.after = shifted(block, MESH, -4)
        self.far = lax.ppermute(block, MESH, [(i, j) for i, j in far if i in devices])
        self.beside = lax.ppermute(block, MESH, [(i, i ^ 2) for i in devices])

    def first(self):
        return [self.before, self.after, self.far, self.beside]

    def finish(self):
        devices = range(lax.axis_size(MESH))
        others = [lax.ppermute(x, MESH, [(i, i ^ 2) for i in devices]) for x in (self.before, self.after)]
        mine = [self.far, self.before, others[0], self.block, self.beside, self.after, others[1]]
        came = [core_flip(x) for x in mine if x is not self.block]
        own = core_flip(self.block) if self.sibling is None else self.sibling
        return mine + came[:3] + [own] + came[3:]


SLOTS = ((0, 1, 2, 3, 4, 5, 6), (2, 1, 4, 3, 6, 5, 0))
SPAN_FIRST, SPAN_LAST, SPAN_CORE, SPAN_CHIP, SPAN_SLOT = 0, 1, 2, 3, 4
SPAN_LOW = 16
SPAN_HIGH = 32
SPAN_ROWS = 48
LANES = 128
SIDE = 16


def flip_bit(block, axis, bit):
    devices = range(lax.axis_size(axis))
    return lax.ppermute(block, axis, [(i, i ^ (1 << bit)) for i in devices])


def bit_of(axis, bit):
    return (lax.axis_index(axis) >> bit) & 1


def bits_of(axis):
    return (lax.axis_size(axis) - 1).bit_length()


def halves_of(values, dim, at):
    return (
        lax.dynamic_index_in_dim(values, at, dim, keepdims=False),
        lax.dynamic_index_in_dim(values, 1 - at, dim, keepdims=False),
    )


def add_low(kept, came):
    return (kept.astype(F32) + came.astype(F32)).astype(BF)


class Slices:
    def __init__(self, kept, sent, order, skip=0):
        self.tail = kept.shape[-2:]
        count = 2 * kept.size // (self.tail[0] * self.tail[1])
        self.left = [bit for bit in range(count.bit_length() - 1) if bit != order[0]]
        self.todo = [("ka", bit) for bit in order]
        self.todo += [("pb", bit) for bit in range(skip, bits_of("pb"))]
        self.kept, self.sent = kept, sent

    def step(self):
        axis, bit = self.todo.pop(0)
        values = add_low(self.kept, flip_bit(self.sent, axis, bit + (axis == "ka")))
        if not self.todo:
            self.kept = values
        elif self.todo[0][0] == "pb":
            self.kept = self.sent = values.reshape(self.tail)
        else:
            bit = self.todo[0][1]
            above = sum(1 for b in self.left if b > bit)
            shape = (2**above, 2, 2 ** (len(self.left) - above - 1), *self.tail)
            self.kept, self.sent = halves_of(values.reshape(shape), 1, bit_of("ka", bit + 1))
            self.left.remove(bit)

    def result(self):
        while self.todo:
            self.step()
        return self.kept.reshape(self.tail)


class Columns:
    def __init__(self, kept, sent, order):
        self.order, self.kept, self.sent, self.inner = order, kept, sent, None

    def step(self):
        if self.inner is None:
            values = add_low(self.kept, flip_bit(self.sent, "pb", 0))
            bit = self.order[0]
            shape = (2 ** (values.shape[0].bit_length() - 2 - bit), 2, 2**bit, *values.shape[1:])
            halves = halves_of(values.reshape(shape), 1, bit_of("ka", bit + 1))
            self.inner = Slices(*halves, self.order, skip=1)
        else:
            self.inner.step()
        self.sent = self.inner.sent

    def result(self):
        if self.inner is None:
            self.step()
        mine = self.inner.result()
        other = flip_bit(mine, "pb", 0)
        return jnp.where(
            bit_of("pb", 0) == 0,
            jnp.concatenate([mine, other], axis=1),
            jnp.concatenate([other, mine], axis=1),
        )


def sum_everywhere(values):
    for axis in ("ka", "pb"):
        for bit in range(bits_of(axis)):
            values = values + flip_bit(values, axis, bit)
    return values


def layer_norm(values, ln_gain, ln_shift):
    centre = jnp.mean(values, axis=-1, keepdims=True)
    offsets = values - centre
    spread = jnp.mean(offsets * offsets, axis=-1, keepdims=True)
    return offsets * lax.rsqrt(spread + LN_EPS) * ln_gain + ln_shift


def dot_nn(left, right):
    return lax.dot_general(left, right, (((1,), (0,)), ((), ())), preferred_element_type=F32)


def dot_nt(left, right):
    return lax.dot_general(left, right, (((1,), (1,)), ((), ())), preferred_element_type=F32)


def dot_tn(left, right):
    return lax.dot_general(left, right, (((0,), (0,)), ((), ())), preferred_element_type=F32)


def select_table(head_size):
    column = np.arange(SPAN)
    source = (column // PAD) * head_size + column % PAD
    table = [
        (column[:, None] == (source + off)[None, :]) & (column % PAD < head_size)[None, :]
        for off in (0, 64)
    ]
    return np.stack(table).astype(BF)


def group_windows(groups, head_size):
    out = []
    for g in range(groups):
        start = g * GROUP * head_size
        out.append((start // LANES * LANES, (start % LANES) // 64))
    return out


def place_table(heads, head_size):
    column = np.arange(heads * PAD)
    lane = np.arange(LANES)
    return np.stack(
        [
            (lane[:, None] == (column // PAD)[None, :])
            & (column % PAD == head_size + p)[None, :]
            for p in range(PIECES)
        ]
    ).astype(BF)


def tail_tables(heads, head_size):
    lane, tail = np.arange(LANES), np.arange(2 * LANES)
    into = np.stack(
        [
            (lane[:, None] + p * heads == tail[None, :]) & (lane < heads)[:, None]
            for p in range(2 * PIECES)
        ]
    )
    column = np.arange(heads * PAD)
    piece = column % PAD - head_size
    free = (piece >= 0) & (piece < PIECES)
    lane_of = np.where(free, piece * heads + column // PAD, -1)
    out = np.stack(
        [
            (tail[:, None] == lane_of[None, :]) & free[None, :],
            (tail[:, None] - PIECES * heads == lane_of[None, :]) & free[None, :],
        ]
    )
    return into.astype(BF), out.astype(BF)


def ones_row(heads, head_size):
    column = np.arange(heads * PAD) % PAD
    return ((column >= head_size) & (column < head_size + PIECES)).astype(np.float32)[None]


def head_sum_table(heads):
    column = np.arange(heads * PAD)
    return (column[:, None] // PAD == np.arange(LANES)[None, :]).astype(BF)


def pad_columns(values, select_ref, windows):
    parts = [
        dot_nn(values[:, start : start + SPAN], select_ref[kind]).astype(BF)
        for start, kind in windows
    ]
    return jnp.concatenate(parts, axis=1)


def drop_columns(values, select_ref, windows):
    tiles = {}
    for g, (start, kind) in enumerate(windows):
        part = dot_nt(values[:, g * SPAN : (g + 1) * SPAN], select_ref[kind])
        for k in range(SPAN // LANES):
            tile = part[:, k * LANES : (k + 1) * LANES]
            at = start // LANES + k
            tiles[at] = tiles[at] + tile if at in tiles else tile
    return jnp.concatenate([tiles[at] for at in sorted(tiles)], axis=1).astype(BF)


def split(values, count):
    rest, out = values, []
    for _ in range(count):
        piece = rest.astype(BF)
        rest = rest - piece.astype(F32)
        out.append(piece)
    return out


def norm_parts(values):
    centre = jnp.mean(values, axis=-1, keepdims=True)
    offsets = values - centre
    spread = jnp.mean(offsets * offsets, axis=-1, keepdims=True)
    slope = lax.rsqrt(spread + LN_EPS)
    return offsets * slope, slope


def norm_back(grad, normal, slope, gain):
    inner = grad * gain
    mean = jnp.mean(inner, axis=-1, keepdims=True)
    tilt = jnp.mean(inner * normal, axis=-1, keepdims=True)
    by_gain = jnp.sum(grad * normal, axis=0, keepdims=True)
    by_shift = jnp.sum(grad, axis=0, keepdims=True)
    return slope * (inner - mean - normal * tilt), by_gain, by_shift


def stretched_of(own, other):
    delta = [own[:, i : i + 1] - other[i : i + 1, :] for i in range(3)]
    square = delta[0] * delta[0] + delta[1] * delta[1] + delta[2] * delta[2]
    dist = jnp.sqrt(square + 1.0)
    scales = own[:, 3:4] * other[3:4, :]
    stretched = scales * dist + own[:, 4:5] + other[4:5, :]
    return delta, dist, scales, stretched


def mask_of(own, other, key_is_own):
    same = own[:, 5:6] == other[5:6, :]
    itself = own[:, 7:8] == other[7:8, :]
    is_open = (own[:, 6:7] > 0.5) if key_is_own else (other[6:7, :] > 0.5)
    return jnp.where(same & (is_open | itself), 0.0, MASKED)


def line_atoms(lines):
    line = lax.broadcasted_iota(jnp.int32, (lines, lines // GROUP), 0)
    atom = lax.broadcasted_iota(jnp.int32, (lines, lines // GROUP), 1)
    return jnp.where(line // GROUP == atom, 1.0, 0.0).astype(BF)


def line_heads(lines):
    line = lax.broadcasted_iota(jnp.int32, (lines, SPAN), 0)
    column = lax.broadcasted_iota(jnp.int32, (lines, SPAN), 1)
    return jnp.where(column // PAD == line % GROUP, 1.0, 0.0)


def expand_into(out_ref, padded, groups):
    lines = CHUNK * GROUP
    keep = line_heads(lines).astype(BF)
    spread = line_atoms(lines)
    for g in range(groups):
        for i in range(padded.shape[0] // CHUNK):
            part = padded[i * CHUNK : (i + 1) * CHUNK, g * SPAN : (g + 1) * SPAN]
            out_ref[g, i * lines : (i + 1) * lines, :] = dot_nn(spread, part).astype(BF) * keep


def collapse(values):
    lines = values.shape[0]
    kept = values * line_heads(lines)
    high = kept.astype(BF)
    low = (kept - high.astype(F32)).astype(BF)
    line = lax.broadcasted_iota(jnp.int32, (lines // GROUP, lines), 1)
    atom = lax.broadcasted_iota(jnp.int32, (lines // GROUP, lines), 0)
    gather = jnp.where(line // GROUP == atom, 1.0, 0.0).astype(BF)
    return dot_nn(gather, high) + dot_nn(gather, low)


def fetch(span_ref, refs, out_ref):
    slot = span_ref[SPAN_SLOT + span_ref[SPAN_FIRST, 0] + pl.program_id(0), 0]
    count = len(refs) // 2
    rows = refs[0].shape[0]
    for k in range(count):

        @pl.when(slot == k)
        def _():
            out_ref[:rows] = refs[k][...]
            out_ref[rows:] = refs[count + k][...]


def spots_of(span_ref, rows):
    core = span_ref[SPAN_CORE, 0]
    return [pl.ds(pl.multiple_of(at * rows, rows), rows) for at in (core, 1 - core)]


def spread_mask(mask_ref, mask):
    mask_ref[...] = jnp.broadcast_to(mask[:, None, :], mask_ref.shape)


def reaches(span_ref, first, last, low, high):
    return (span_ref[SPAN_LOW + first, 0] <= high) & (span_ref[SPAN_HIGH + last, 0] >= low)


def head_steps(span_ref, rows, step):
    pair = span_ref[SPAN_FIRST, 0] + pl.program_id(0)
    few = CHUNK // FEW

    def one(i, carry):
        @pl.when(reaches(span_ref, i * few, i * few + few - 1, 2 * pair, 2 * pair + 1))
        def _():
            step(i)

        return carry

    lax.fori_loop(0, rows // CHUNK, one, 0)


def kernel_steps(span_ref, rows, step, skipped):
    pair = span_ref[SPAN_FIRST, 0] + pl.program_id(0)

    def one(i, carry):
        for half in range(2):
            block = 2 * pair + half
            needed = reaches(span_ref, i, i, block, block)

            @pl.when(needed)
            def _():
                step(i, half)

            @pl.when(jnp.logical_not(needed))
            def _():
                skipped(i, half)

        return carry

    lax.fori_loop(0, rows // FEW, one, 0)


def side_kernel(
    atoms_blocks,
    flat_ref,
    pos_ref,
    item_ref,
    open_ref,
    type_ref,
    length_ref,
    table_ref,
    means_ref,
    widths_ref,
    kw_ref,
    span_ref,
    other_ref,
    own_ref,
    line_ref,
    tab_ref,
    gw_ref,
    kwt_ref,
    par_ref,
):
    flat = flat_ref[0]
    chips = len(SLOTS[0]) // 2
    first_block = flat // 2 * 2 - 2 * chips
    ids = lax.broadcasted_iota(jnp.int32, (LANES, LANES), 0).astype(F32)
    lane = lax.broadcasted_iota(jnp.int32, (1, LANES), 1)
    tables = []
    for k in range(table_ref.shape[0] // 2):
        rows = split(table_ref[2 * k : 2 * k + 1, :], PIECES)
        rows += split(table_ref[2 * k + 1 : 2 * k + 2, :], PIECES)
        rows += [jnp.zeros((2, LANES), BF)]
        tables.append(jnp.concatenate([row.astype(F32) for row in rows], axis=0).astype(BF))
    flags = [
        jnp.broadcast_to(
            jnp.where(length_ref[k : k + 1, :] > 2 * MOL_MEAN, float(MOL_TYPES), 0.0), (8, LANES)
        ).astype(BF)
        for k in range(length_ref.shape[0])
    ]
    for b in range(other_ref.shape[1] // LANES):
        block = first_block + b
        inside = (block >= 0) & (block < atoms_blocks)
        source = jnp.clip(block, 0, atoms_blocks - 1)
        at = pl.ds(pl.multiple_of(source * LANES, LANES), LANES)
        item = jnp.where(inside, item_ref[pl.ds(source, 1), :].astype(F32), -1.0)
        kind = type_ref[pl.ds(source, 1), :].astype(F32)
        for k, flag in enumerate(flags):
            onehot = jnp.where(ids + float(k * LANES) == item, 1.0, 0.0).astype(BF)
            kind = kind + dot_nn(flag, onehot)[0:1, :]
        found = jnp.zeros((8, LANES), F32)
        for k, table in enumerate(tables):
            onehot = jnp.where(ids + float(k * LANES) == kind, 1.0, 0.0).astype(BF)
            found = found + dot_nn(table, onehot)
        rows = [pos_ref[k : k + 1, at] for k in range(3)]
        rows += [found[0:1] + found[1:2] + found[2:3], found[3:4] + found[4:5] + found[5:6]]
        rows += [item, open_ref[pl.ds(source, 1), :].astype(F32)]
        rows += [(block * LANES + lane).astype(F32), kind]
        rows += [jnp.zeros((SIDE - 9, LANES), F32)]
        side = jnp.concatenate(rows, axis=0)
        other_ref[:, b * LANES : (b + 1) * LANES] = side

        @pl.when(block == flat)
        def _():
            line_ref[...] = side

    line = line_ref[...]
    turned = jnp.transpose(
        jnp.concatenate([line, jnp.zeros((LANES - SIDE, LANES), F32)], axis=0)
    )
    own_ref[...] = turned
    chunks = LANES // FEW
    item_column = jnp.broadcast_to(own_ref[:, 5:6], (LANES, LANES))
    par_ref[...] = item_column
    first_item = par_ref[pl.ds(0, chunks, stride=FEW), :]
    last_item = par_ref[pl.ds(FEW - 1, chunks, stride=FEW), :]

    def count(k, carry):
        row = item_ref[pl.ds(k, 1), :].astype(F32)
        below, upto = carry
        return (
            below + jnp.where(row < first_item, 1.0, 0.0),
            upto + jnp.where(row <= last_item, 1.0, 0.0),
        )

    zero = jnp.zeros((chunks, LANES), F32)
    below, upto = lax.fori_loop(0, atoms_blocks, count, (zero, zero))
    below = jnp.sum(below, axis=1, keepdims=True).astype(jnp.int32)
    upto = jnp.sum(upto, axis=1, keepdims=True).astype(jnp.int32)
    low = jnp.right_shift(below - first_block * LANES, 7)
    high = jnp.right_shift(upto - 1 - first_block * LANES, 7)
    span_ref[SPAN_LOW : SPAN_LOW + chunks, :] = jnp.broadcast_to(low, (chunks, LANES))
    span_ref[SPAN_HIGH : SPAN_HIGH + chunks, :] = jnp.broadcast_to(high, (chunks, LANES))
    row = lax.broadcasted_iota(jnp.int32, (SPAN_LOW, LANES), 0)
    odd = (flat // 2) % 2
    head = jnp.where(row == SPAN_FIRST, jnp.right_shift(low[0:1, :], 1), 0)
    head = head + jnp.where(row == SPAN_LAST, jnp.right_shift(high[chunks - 1 :, :], 1), 0)
    head = head + jnp.where(row == SPAN_CORE, flat % 2, 0)
    head = head + jnp.where(row == SPAN_CHIP, flat // 2, 0)
    for k, (even_slot, odd_slot) in enumerate(zip(*SLOTS)):
        head = head + jnp.where(
            row == SPAN_SLOT + k, even_slot + odd * (odd_slot - even_slot), 0
        )
    span_ref[:SPAN_LOW, :] = head

    def column_of(ref):
        return jnp.transpose(jnp.broadcast_to(ref[...], (LANES, LANES)))

    means, widths = column_of(means_ref), column_of(widths_ref)
    peaks = 1.0 / (ROOT_TWO_PI * widths)
    bend = -(KAPPA * KAPPA) / (widths * widths)
    tab_ref[0] = means
    tab_ref[1] = KAPPA / widths
    tab_ref[2] = LOG2E * jnp.log(peaks)
    tab_ref[3] = bend
    weights = kw_ref[...].astype(F32)
    heads = weights.shape[1]
    scaled = weights * (peaks / (widths * widths))[:, :heads]
    gw_ref[...] = jnp.concatenate(split(scaled, WEIGHT_PIECES), axis=1)
    wide = jnp.concatenate([weights, jnp.zeros((LANES, LANES - heads), F32)], axis=1)
    kwt_ref[...] = jnp.transpose(wide)[:heads, :].astype(BF)
    lanes = lax.broadcasted_iota(jnp.int32, (LANES, LANES), 1)
    par = wide + jnp.where(lanes == heads, peaks, 0.0)
    par_ref[...] = par + jnp.where(lanes == heads + 1, 1.0 / widths, 0.0)


def bias_kernel(span_ref, own_ref, other_ref, tab_ref, kwt_ref, out_ref, str_ref):
    rows, keys = str_ref.shape
    kernels = tab_ref.shape[1]
    heads = kwt_ref.shape[0]
    half_keys = keys // 2
    str_ref[...] = stretched_of(own_ref[...], other_ref[...])[3]

    def step(i, half):
        columns = slice(half * half_keys, (half + 1) * half_keys)
        block = str_ref[pl.ds(pl.multiple_of(i * FEW, FEW), FEW), columns]
        parts = []
        for r in range(FEW):
            line = jnp.broadcast_to(block[r : r + 1], (kernels, half_keys))
            z = (line - tab_ref[0]) * tab_ref[1]
            parts.append(jnp.exp2(tab_ref[2] - z * z).astype(BF))
        for r in range(0, FEW, 2):
            phi = jnp.concatenate(parts[r : r + 2], axis=1)
            result = dot_nn(kwt_ref[...], phi) * LOG2E
            out_ref[0, i * FEW + r, :, columns] = result[:, :half_keys]
            out_ref[0, i * FEW + r + 1, :, columns] = result[:, half_keys:]

    def skipped(i, half):
        columns = slice(half * half_keys, (half + 1) * half_keys)
        out_ref[0, pl.ds(i * FEW, FEW), :, columns] = jnp.zeros((FEW, heads, half_keys), F32)

    kernel_steps(span_ref, rows, step, skipped)


def forward_kernel(
    scale2,
    groups,
    chips,
    span_ref,
    own_ref,
    other_ref,
    *refs,
):
    token_refs, refs = refs[:14], refs[14:]
    ln_ref, w_ref, select_ref, ones_ref, place_ref, bias_ref, *refs = refs
    att_ref, qaug_ref, lse_ref, now_ref, kvq_ref, *refs = refs
    qexp_ref, mask_ref, max_ref, sum_ref, acc_ref, lane_ref, both_ref = refs
    step = pl.program_id(0)
    width = groups * SPAN
    tok_ref = token_refs[3]
    rows, model_width = tok_ref.shape
    windows = group_windows(groups, model_width // (groups * GROUP))
    gain, shift = ln_ref[0:1, :], ln_ref[1:2, :]

    @pl.when(step == 0)
    def _():
        normed = layer_norm(tok_ref[...].astype(F32), gain, shift).astype(BF)
        query = dot_nn(normed, w_ref[:, :model_width]).astype(BF)
        query = pad_columns(query, select_ref, windows)
        qaug_ref[...] = query
        expand_into(qexp_ref, query, groups)
        max_ref[...] = jnp.full(max_ref.shape, 2.0 * MASKED, F32)
        sum_ref[...] = jnp.zeros(sum_ref.shape, F32)
        acc_ref[...] = jnp.zeros(acc_ref.shape, F32)

    fetch(span_ref, token_refs, both_ref)
    normed = layer_norm(both_ref[...].astype(F32), gain, shift).astype(BF)
    spots = spots_of(span_ref, rows)

    @pl.when(step + span_ref[SPAN_FIRST, 0] == chips)
    def _():
        now_ref[...] = normed

    for part in range(3):
        source = (part + 1) % 3 * model_width
        value = dot_nn(normed, w_ref[:, source : source + model_width]).astype(BF)
        value = pad_columns(value, select_ref, windows)
        if part < 2:
            value = value + ones_ref[...].astype(BF)
        for k in range(2):
            kvq_ref[0, spots[k], part * width : (part + 1) * width] = (
                value[k * rows : (k + 1) * rows]
            )
    spread_mask(mask_ref, mask_of(own_ref[...], other_ref[...], False))

    def chunk_step(i):
        at = pl.multiple_of(i * CHUNK, CHUNK)
        lines = pl.ds(pl.multiple_of(i * CHUNK * GROUP, CHUNK * GROUP), CHUNK * GROUP)
        mask = mask_ref[pl.ds(at, CHUNK)]
        for g in range(groups):
            columns = slice(g * SPAN, (g + 1) * SPAN)
            dots = dot_nt(qexp_ref[g, lines, :], kvq_ref[0, :, columns])
            bias = bias_ref[0, pl.ds(at, CHUNK), g * GROUP : (g + 1) * GROUP, :] + mask
            scores = dots * scale2 + bias.reshape(dots.shape)
            old = max_ref[g, lines, :]
            top = jnp.maximum(scores[:, :128], scores[:, 128:])
            new = jnp.maximum(old, jnp.max(top, axis=1, keepdims=True))
            alpha = jnp.exp2(old - new)
            low = jnp.exp2(scores[:, :128] - new)
            high = jnp.exp2(scores[:, 128:] - new)
            max_ref[g, lines, :] = new
            sum_ref[g, lines, :] = sum_ref[g, lines, :] * alpha + (low + high)
            probs = jnp.concatenate([low, high], axis=1).astype(BF)
            values = dot_nn(probs, kvq_ref[0, :, width + g * SPAN : width + (g + 1) * SPAN])
            wide = jnp.concatenate([alpha, alpha], axis=1)
            acc_ref[g, lines, :] = acc_ref[g, lines, :] * wide + values

    head_steps(span_ref, rows, chunk_step)

    @pl.when(step == span_ref[SPAN_LAST, 0] - span_ref[SPAN_FIRST, 0])
    def _():
        lane = lax.broadcasted_iota(jnp.int32, (GROUP, 128), 1)
        head = lax.broadcasted_iota(jnp.int32, (GROUP, 128), 0)

        def finish(i, carry):
            at = pl.multiple_of(i * CHUNK, CHUNK)
            lines = pl.ds(pl.multiple_of(i * CHUNK * GROUP, CHUNK * GROUP), CHUNK * GROUP)
            lanes = jnp.zeros((CHUNK, 128), F32)
            for g in range(groups):
                total = jnp.sum(sum_ref[g, lines, :], axis=1, keepdims=True)
                attended = collapse(acc_ref[g, lines, :] / total)
                att_ref[pl.ds(at, CHUNK), g * SPAN : (g + 1) * SPAN] = attended
                lse = max_ref[g, lines, :] + jnp.log(total) * LOG2E
                own_lane = jnp.where(lane == head + g * GROUP, 1.0, 0.0)
                lanes = lanes + jnp.sum(
                    lse.reshape(CHUNK, GROUP, 128) * own_lane[None], axis=1
                )
            lane_ref[pl.ds(at, CHUNK), :] = lanes
            return carry

        lax.fori_loop(0, rows // CHUNK, finish, 0)
        rest = lane_ref[...] * (-1.0 / scale2)
        query = qaug_ref[...].astype(F32)
        for p in range(PIECES):
            piece = rest.astype(BF)
            rest = rest - piece.astype(F32)
            lse_ref[p] = piece
            query = query + dot_nn(piece, place_ref[p])
        qaug_ref[...] = query.astype(BF)


def query_grad_kernel(
    scale2,
    head_scale,
    groups,
    span_ref,
    own_ref,
    other_ref,
    qaug_ref,
    doaug_ref,
    kv_ref,
    bias_ref,
    select_ref,
    dq_ref,
    ds_ref,
    qexp_ref,
    doexp_ref,
    mask_ref,
    dqacc_ref,
):
    step = pl.program_id(0)
    width = groups * SPAN
    rows, keys = own_ref.shape[0], other_ref.shape[1]
    windows = group_windows(groups, dq_ref.shape[1] // (groups * GROUP))

    @pl.when(step == 0)
    def _():
        expand_into(qexp_ref, qaug_ref[...], groups)
        expand_into(doexp_ref, doaug_ref[...], groups)
        dqacc_ref[...] = jnp.zeros(dqacc_ref.shape, F32)

    spread_mask(mask_ref, mask_of(own_ref[...], other_ref[...], False))

    def chunk_step(i):
        at = pl.multiple_of(i * CHUNK, CHUNK)
        lines = pl.ds(pl.multiple_of(i * CHUNK * GROUP, CHUNK * GROUP), CHUNK * GROUP)
        mask = mask_ref[pl.ds(at, CHUNK)]
        waiting = []
        for g in range(groups):
            key_block = kv_ref[0, :, g * SPAN : (g + 1) * SPAN]
            value_block = kv_ref[0, :, width + g * SPAN : width + (g + 1) * SPAN]
            dots = dot_nt(qexp_ref[g, lines, :], key_block)
            grads = dot_nt(doexp_ref[g, lines, :], value_block)
            bias = bias_ref[0, pl.ds(at, CHUNK), g * GROUP : (g + 1) * GROUP, :] + mask
            probs = jnp.exp2(dots * scale2 + bias.reshape(dots.shape))
            grad_scores = probs * grads
            dqacc_ref[g, lines, :] += dot_nn(grad_scores.astype(BF), key_block)
            waiting.append(grad_scores.reshape(CHUNK, GROUP, keys))
            if len(waiting) == 2:
                ds_ref[0, pl.ds(at, CHUNK), (g - 1) * GROUP : (g + 1) * GROUP, :] = (
                    jnp.concatenate(waiting, axis=1).astype(BF)
                )
                waiting = []

    head_steps(span_ref, rows, chunk_step)

    @pl.when(step == span_ref[SPAN_LAST, 0] - span_ref[SPAN_FIRST, 0])
    def _():
        def finish(i, carry):
            at = pl.multiple_of(i * CHUNK, CHUNK)
            lines = pl.ds(pl.multiple_of(i * CHUNK * GROUP, CHUNK * GROUP), CHUNK * GROUP)
            parts = [
                (collapse(dqacc_ref[g, lines, :]) * head_scale).astype(BF) for g in range(groups)
            ]
            dq_ref[pl.ds(at, CHUNK), :] = drop_columns(
                jnp.concatenate(parts, axis=1), select_ref, windows
            )
            return carry

        lax.fori_loop(0, rows // CHUNK, finish, 0)


def phi_grad_kernel(
    span_ref,
    own_ref,
    other_ref,
    line_ref,
    ds_ref,
    tab_ref,
    kw_ref,
    par_ref,
    small_ref,
    pos_ref,
    str_ref,
    dphi_ref,
    phi_ref,
    gs_ref,
    own_acc_ref,
    gkw_ref,
    moment_ref,
    type_ref,
):
    step = pl.program_id(0)
    rows, keys = str_ref.shape
    kernels = tab_ref.shape[1]
    heads = gkw_ref.shape[1]
    blocks = pos_ref.shape[0] // 3
    pair_block = 2 * (span_ref[SPAN_CHIP, 0] + span_ref[SPAN_FIRST, 0] + step)

    @pl.when(step == 0)
    def _():
        gkw_ref[...] = jnp.zeros(gkw_ref.shape, F32)
        moment_ref[...] = jnp.zeros(moment_ref.shape, F32)
        own_acc_ref[...] = jnp.zeros(own_acc_ref.shape, F32)
        pos_ref[...] = jnp.zeros(pos_ref.shape, F32)
        type_ref[...] = jnp.zeros(type_ref.shape, F32)

    def add_types(kind, by_scale, by_shift):
        count = type_ref.shape[1]
        onehot = lax.broadcasted_iota(jnp.int32, (count, LANES), 0).astype(F32) == kind
        type_ref[0] += jnp.where(onehot, by_scale, 0.0)
        type_ref[1] += jnp.where(onehot, by_shift, 0.0)

    own, other = own_ref[...], other_ref[...]
    str_ref[...] = stretched_of(own, other)[3]

    tile = 32
    half_keys = keys // 2

    def pair_step(i, half):
        columns = slice(half * half_keys, (half + 1) * half_keys)
        block = str_ref[pl.ds(pl.multiple_of(i * FEW, FEW), FEW), columns]

        def lows():
            return jnp.concatenate([ds_ref[0, i * FEW + r, :, columns] for r in range(FEW)], axis=1)

        low = lows()
        dphi_ref[...] = dot_nn(kw_ref[...], jnp.concatenate([low] * WEIGHT_PIECES, axis=0))
        partial = [None] * FEW
        for c in range(kernels // tile):
            cs = slice(c * tile, (c + 1) * tile)
            first = jnp.zeros((tile, half_keys), F32)
            second = jnp.zeros((tile, half_keys), F32)
            for r in range(FEW):
                spot = slice(r * half_keys, (r + 1) * half_keys)
                away = jnp.broadcast_to(block[r : r + 1], (tile, half_keys)) - tab_ref[0, cs, :]
                phi = jnp.exp2(away * away * tab_ref[3, cs, :])
                phi_ref[cs, spot] = phi.astype(BF)
                moved = dphi_ref[cs, spot] * phi * away
                first = first + moved
                second = second + moved * away
                term = jnp.sum(moved.reshape(tile // 8, 8, half_keys), axis=0)
                partial[r] = term if c == 0 else partial[r] + term
            moment_ref[0, cs, :] += first
            moment_ref[1, cs, :] += second
        lines = [jnp.sum(partial[r], axis=0, keepdims=True) for r in range(FEW)]
        gs_ref[pl.ds(pl.multiple_of(i * FEW, FEW), FEW), columns] = jnp.concatenate(lines, axis=0)
        gkw_ref[...] += dot_nt(phi_ref[...], lows())

    def skipped(i, half):
        columns = slice(half * half_keys, (half + 1) * half_keys)
        gs_ref[pl.ds(pl.multiple_of(i * FEW, FEW), FEW), columns] = jnp.zeros((FEW, half_keys), F32)

    kernel_steps(span_ref, rows, pair_step, skipped)

    delta, dist, scales, _ = stretched_of(own, other)
    grad = -gs_ref[...]
    by_scale = grad * dist
    pull = grad * scales / dist
    terms = [pull * delta[0], pull * delta[1], pull * delta[2], by_scale * other[3:4, :], grad]
    for k, term in enumerate(terms):
        own_acc_ref[k] += term[:, :128] + term[:, 128:]
    for half in range(2):
        part = slice(half * LANES, (half + 1) * LANES)
        for k in range(3):
            spot = pl.ds(k * blocks + pair_block + half, 1)
            pos_ref[spot, :] += -jnp.sum(terms[k][:, part], axis=0, keepdims=True)
        add_types(
            other[8:9, part],
            jnp.sum(by_scale[:, part] * own[:, 3:4], axis=0, keepdims=True),
            jnp.sum(grad[:, part], axis=0, keepdims=True),
        )

    @pl.when(step == span_ref[SPAN_LAST, 0] - span_ref[SPAN_FIRST, 0])
    def _():
        lane = lax.broadcasted_iota(jnp.int32, (rows, LANES), 1)
        total = jnp.zeros((rows, LANES), F32)
        for k in range(5):
            column = jnp.sum(own_acc_ref[k], axis=1, keepdims=True)
            total = total + jnp.where(lane == k, column, 0.0)
        turned = jnp.transpose(total)
        own_block = 2 * (span_ref[SPAN_CHIP, 0] + len(SLOTS[0]) // 2) + span_ref[SPAN_CORE, 0]
        for k in range(3):
            pos_ref[pl.ds(k * blocks + own_block, 1), :] += turned[k : k + 1, :]
        add_types(line_ref[8:9, :], turned[3:4, :], turned[4:5, :])

        par = par_ref[...]
        by_weight = gkw_ref[...] * par[:, heads : heads + 1]
        plain = jnp.sum(by_weight * par[:, :heads], axis=1, keepdims=True)
        by_mean = jnp.sum(moment_ref[0], axis=1, keepdims=True)
        by_width = jnp.sum(moment_ref[1], axis=1, keepdims=True) - plain
        columns = [by_mean, by_width * par[:, heads + 1 : heads + 2]]
        low, high = slice(0, LANES), slice(LANES, 2 * LANES)
        for part in (low, high):
            for k in range(2):
                columns.append(jnp.sum(type_ref[k, part, :], axis=1, keepdims=True))
        wide = jnp.concatenate([by_weight, jnp.zeros((LANES, LANES - heads), F32)], axis=1)
        for k, column in enumerate(columns):
            wide = wide + jnp.where(lane == heads + k, column, 0.0)
        small_ref[...] = wide


def middle_kernel(
    groups,
    tile,
    flat_ref,
    tok_ref,
    att_ref,
    lse_ref,
    ln_ref,
    cot_ref,
    wout_hbm,
    wup_hbm,
    wdown_hbm,
    select_ref,
    place_ref,
    sum_ref,
    into_ref,
    out_ref,
    gmix_ref,
    doaug_ref,
    payload_ref,
    attlow_ref,
    normed_ref,
    mine_ref,
    theirs_ref,
    lngrad_ref,
    wout_ref,
    wup_ref,
    wdown_ref,
    down_ref,
    back_ref,
    wout_sem,
    tile_sems,
):
    rows, model_width = tok_ref.shape
    width = groups * SPAN
    windows = group_windows(groups, model_width // (groups * GROUP))
    tiles = wup_ref.shape[1] // tile
    piece = mine_ref.shape[3]
    core = flat_ref[0] % 2

    def tile_copies(t):
        spot = pl.ds(pl.multiple_of(t * tile, LANES), tile)
        return (
            pltpu.make_async_copy(wup_hbm.at[:, spot], wup_ref.at[:, spot], tile_sems.at[0, t]),
            pltpu.make_async_copy(wdown_hbm.at[spot, :], wdown_ref.at[spot, :], tile_sems.at[1, t]),
        )

    first = pltpu.make_async_copy(wout_hbm, wout_ref, wout_sem)
    first.start()
    for t in range(tiles):
        for copy in tile_copies(t):
            copy.start()

    gain, shift = ln_ref[0:1, :], ln_ref[1:2, :]
    cotangent = cot_ref[...]
    attended = att_ref[...]
    attended_low = drop_columns(attended.astype(BF), select_ref, windows)
    attlow_ref[...] = attended_low
    first.wait()
    mixed = tok_ref[...].astype(F32) + dot_nn(attended_low, wout_ref[...])
    normal, slope = norm_parts(mixed)
    normed_ref[...] = (normal * gain + shift).astype(BF)
    down_ref[...] = mixed
    back_ref[...] = jnp.zeros(back_ref.shape, F32)

    def step(t, carry):
        for copy in tile_copies(t):
            copy.wait()
        spot = pl.ds(pl.multiple_of(t * tile, LANES), tile)
        up = dot_nn(normed_ref[...], wup_ref[:, spot])
        grad_hidden = dot_nt(cotangent, wdown_ref[spot, :])
        square = up * up
        bent = jnp.tanh(GELU_SLOPE * (up * (1.0 + GELU_CUBE * square)))
        gate = 0.5 * (1.0 + bent)
        inner = GELU_SLOPE * (1.0 + 3.0 * GELU_CUBE * square)
        hidden = (up * gate).astype(BF)
        grad_up = (grad_hidden * (gate + 0.5 * up * (1.0 - bent * bent) * inner)).astype(BF)
        for kind, value in enumerate((grad_up, hidden)):
            for q in range(tile // piece):
                part = value[:, q * piece : (q + 1) * piece]
                at = t * (tile // piece // 2) + q // 2

                @pl.when(core == q % 2)
                def _():
                    mine_ref[kind, at] = part

                @pl.when(core != q % 2)
                def _():
                    theirs_ref[kind, at] = part

        down_ref[...] += dot_nn(hidden, wdown_ref[spot, :])
        back_ref[...] += dot_nt(grad_up, wup_ref[:, spot])
        return carry

    lax.fori_loop(0, tiles, step, 0)
    out_ref[...] = down_ref[...].astype(BF)
    back, by_gain, by_shift = norm_back(back_ref[...], normal, slope, gain)
    lngrad_ref[...] = jnp.concatenate([by_gain, by_shift], axis=0)
    grad_mixed = cotangent.astype(F32) + back
    gmix_ref[...] = grad_mixed
    grad_low = grad_mixed.astype(BF)
    grad_attended = dot_nt(grad_low, wout_ref[...]).astype(BF)
    padded = pad_columns(grad_attended, select_ref, windows).astype(F32)
    high, low = split(padded * attended, 2)
    delta = dot_nn(high, sum_ref[...]) + dot_nn(low, sum_ref[...])
    pieces = split(-delta, PIECES)
    tail = jnp.zeros((rows, 2 * LANES), F32)
    for p in range(PIECES):
        padded = padded + dot_nn(pieces[p], place_ref[p])
        tail = tail + dot_nn(lse_ref[p], into_ref[p]) + dot_nn(pieces[p], into_ref[PIECES + p])
    doaug_ref[...] = padded.astype(BF)
    payload_ref[:, :model_width] = grad_low
    payload_ref[:, model_width:] = tail.astype(BF)


def weight_grads_kernel(
    ka_count,
    flat_ref,
    mine_ref,
    came_ref,
    normed_ref,
    normed_came_ref,
    cot_ref,
    cot_came_ref,
    attlow_ref,
    attlow_came_ref,
    payload_ref,
    payload_came_ref,
    up_kept_ref,
    up_sent_ref,
    rest_kept_ref,
    rest_sent_ref,
    payload_out_ref,
    product_ref,
):
    flat = flat_ref[0]
    core, bit, side = flat % 2, (flat // 2) % 2, (flat // ka_count) % 2
    model_width = normed_ref.shape[1]
    rows = up_kept_ref.shape[1]
    half = model_width // 2
    slices = up_kept_ref.shape[0] * 2
    out_rows = model_width // ka_count
    normed = jnp.concatenate([normed_ref[...], normed_came_ref[...]], axis=0)
    cotangent = jnp.concatenate([cot_ref[...], cot_came_ref[...]], axis=0)

    def columns(which):
        return pl.ds(pl.multiple_of(which * half, LANES), half)

    def step(m, carry):
        both = jnp.concatenate([mine_ref[0, m], came_ref[0, m]], axis=0)
        value = dot_tn(both, normed).astype(BF)

        @pl.when(m % 2 == bit)
        def _():
            up_kept_ref[m // 2] = value

        @pl.when(m % 2 != bit)
        def _():
            up_sent_ref[m // 2] = value

        both = jnp.concatenate([mine_ref[1, m], came_ref[1, m]], axis=0)
        product_ref[:rows, :] = dot_tn(both, cotangent)
        rest_kept_ref[m, :rows, :] = product_ref[:rows, columns(side)].astype(BF)
        rest_sent_ref[m, :rows, :] = product_ref[:rows, columns(1 - side)].astype(BF)
        return carry

    lax.fori_loop(0, slices, step, 0)
    grads = jnp.concatenate(
        [payload_ref[:, :model_width], payload_came_ref[:, :model_width]], axis=0
    )
    attended = jnp.concatenate([attlow_ref[...], attlow_came_ref[...]], axis=0)
    product_ref[...] = dot_tn(grads, attended)

    def out_step(m, carry):
        spot = pl.ds(pl.multiple_of((2 * m + core) * out_rows, 8), out_rows)
        rest_kept_ref[m, rows:, :] = product_ref[spot, columns(side)].astype(BF)
        rest_sent_ref[m, rows:, :] = product_ref[spot, columns(1 - side)].astype(BF)
        return carry

    lax.fori_loop(0, slices, out_step, 0)
    payload_out_ref[...] = payload_ref[...]


def qkv_grads_kernel(
    ka_count,
    split_at,
    flat_ref,
    dq_ref,
    dq_came_ref,
    dkv_ref,
    dkv_came_ref,
    normed_ref,
    a_kept_ref,
    a_sent_ref,
    b_kept_ref,
    b_sent_ref,
    product_ref,
):
    flat = flat_ref[0]
    core, bit, side = flat % 2, (flat // 2) % 2, (flat // ka_count) % 2
    model_width = normed_ref.shape[1]
    slices = a_kept_ref.shape[0] * 2
    rows = 3 * model_width // ka_count
    half = (model_width - split_at) // 2
    dq = jnp.concatenate([dq_ref[...], dq_came_ref[...]], axis=0)
    product_ref[:model_width, :] = dot_tn(dq, normed_ref[...])
    for part in range(2):
        spot = slice(part * model_width, (part + 1) * model_width)
        both = jnp.concatenate([dkv_ref[:, spot], dkv_came_ref[:, spot]], axis=0)
        product_ref[(part + 1) * model_width : (part + 2) * model_width, :] = dot_tn(
            both, normed_ref[...]
        )

    def step(m, carry):
        spot = pl.ds(pl.multiple_of((2 * m + core) * rows, 8), rows)
        value = product_ref[spot, :split_at].astype(BF)

        @pl.when(m % 2 == bit)
        def _():
            a_kept_ref[m // 2] = value

        @pl.when(m % 2 != bit)
        def _():
            a_sent_ref[m // 2] = value

        for which, ref in ((side, b_kept_ref), (1 - side, b_sent_ref)):
            at = pl.ds(pl.multiple_of(split_at + which * half, LANES), half)
            ref[m] = product_ref[spot, at].astype(BF)
        return carry

    lax.fori_loop(0, slices, step, 0)


def first_norm_kernel(
    tok_ref, ln_ref, dq_ref, dkv_ref, w_ref, gmix_ref, grad_ref, lngrad_ref
):
    model_width = tok_ref.shape[1]
    grad = dot_nt(dq_ref[...], w_ref[:, :model_width])
    for part in range(2):
        spot = slice(part * model_width, (part + 1) * model_width)
        after = slice((part + 1) * model_width, (part + 2) * model_width)
        grad = grad + dot_nt(dkv_ref[:, spot], w_ref[:, after])
    normal, slope = norm_parts(tok_ref[...].astype(F32))
    back, by_gain, by_shift = norm_back(grad, normal, slope, ln_ref[0:1, :])
    grad_ref[...] = gmix_ref[...] + back
    lngrad_ref[...] = jnp.concatenate([by_gain, by_shift], axis=0)


def key_grad_kernel(
    scale2,
    head_scale,
    groups,
    model_width,
    span_ref,
    own_ref,
    other_ref,
    kv_ref,
    q_ref,
    *refs,
):
    payload_refs, refs = refs[:14], refs[14:]
    wout_ref, select_ref, place_ref, bias_ref, dkv_ref, kexp_ref, vexp_ref, *refs = refs
    mask_ref, qb_ref, dob_ref, dk_ref, dv_ref, both_ref = refs
    step = pl.program_id(0)
    width = groups * SPAN
    rows = own_ref.shape[0]
    windows = group_windows(groups, model_width // (groups * GROUP))

    @pl.when(step == 0)
    def _():
        expand_into(kexp_ref, kv_ref[0, :, :width], groups)
        expand_into(vexp_ref, kv_ref[0, :, width:], groups)
        dk_ref[...] = jnp.zeros(dk_ref.shape, F32)
        dv_ref[...] = jnp.zeros(dv_ref.shape, F32)

    fetch(span_ref, payload_refs, both_ref)
    payload = both_ref[...]
    tail = payload[:, model_width:]
    grads = dot_nt(payload[:, :model_width], wout_ref[...]).astype(BF)
    grads = pad_columns(grads, select_ref, windows).astype(F32)
    grads = (grads + dot_nn(tail, place_ref[1])).astype(BF)
    shifts = dot_nn(tail, place_ref[0])
    for k, spot in enumerate(spots_of(span_ref, rows)):
        own_part = slice(k * rows, (k + 1) * rows)
        dob_ref[spot, :] = grads[own_part]
        qb_ref[spot, :] = (q_ref[0, spot, :].astype(F32) + shifts[own_part]).astype(BF)
    spread_mask(mask_ref, mask_of(own_ref[...], other_ref[...], True))

    def chunk_step(i):
        at = pl.multiple_of(i * CHUNK, CHUNK)
        lines = pl.ds(pl.multiple_of(i * CHUNK * GROUP, CHUNK * GROUP), CHUNK * GROUP)
        mask = mask_ref[pl.ds(at, CHUNK)]
        for g in range(groups):
            query_block = qb_ref[:, g * SPAN : (g + 1) * SPAN]
            grad_block = dob_ref[:, g * SPAN : (g + 1) * SPAN]
            dots = dot_nt(kexp_ref[g, lines, :], query_block)
            grads = dot_nt(vexp_ref[g, lines, :], grad_block)
            bias = bias_ref[0, pl.ds(at, CHUNK), g * GROUP : (g + 1) * GROUP, :] + mask
            probs = jnp.exp2(dots * scale2 + bias.reshape(dots.shape))
            grad_scores = (probs * grads).astype(BF)
            dk_ref[g, lines, :] += dot_nn(grad_scores, query_block)
            dv_ref[g, lines, :] += dot_nn(probs.astype(BF), grad_block)

    head_steps(span_ref, rows, chunk_step)

    @pl.when(step == span_ref[SPAN_LAST, 0] - span_ref[SPAN_FIRST, 0])
    def _():
        def finish(i, carry):
            at = pl.multiple_of(i * CHUNK, CHUNK)
            lines = pl.ds(pl.multiple_of(i * CHUNK * GROUP, CHUNK * GROUP), CHUNK * GROUP)
            for part, (ref, scale) in enumerate(((dk_ref, head_scale), (dv_ref, 1.0))):
                parts = [(collapse(ref[g, lines, :]) * scale).astype(BF) for g in range(groups)]
                dkv_ref[pl.ds(at, CHUNK), part * model_width : (part + 1) * model_width] = (
                    drop_columns(jnp.concatenate(parts, axis=1), select_ref, windows)
                )
            return carry

        lax.fori_loop(0, rows // CHUNK, finish, 0)


def fixed(shape):
    return pl.BlockSpec(shape, lambda j, span: (0,) * len(shape), pipeline_mode=pl.Buffered(1))


def pair_at(j, span):
    return jnp.minimum(span[SPAN_FIRST, 0] + j, span[SPAN_LAST, 0])


def moving(shape, rank_at=0, last=0):
    def index(j, span):
        at = [0] * len(shape)
        at[rank_at] = pair_at(j, span)
        if last:
            at[-1] = last
        return tuple(at)

    return pl.BlockSpec(shape, index)


def while_inside(kernel, extra):
    def body(span_ref, *refs):
        @pl.when(pl.program_id(0) <= span_ref[SPAN_LAST, 0] - span_ref[SPAN_FIRST, 0])
        def _():
            kernel(span_ref, *refs[extra:])

    return body


def call(kernel, steps, in_specs, out_specs, out_shapes, scratch, flops, name, after=()):
    inner = pl.pallas_call(
        while_inside(kernel, len(after)),
        grid_spec=pltpu.PrefetchScalarGridSpec(
            num_scalar_prefetch=1,
            grid=(steps,),
            in_specs=[pl.BlockSpec(memory_space=pl.ANY)] * len(after) + in_specs,
            out_specs=out_specs,
            scratch_shapes=scratch,
        ),
        out_shape=out_shapes,
        compiler_params=pltpu.CompilerParams(
            dimension_semantics=("arbitrary",), vmem_limit_bytes=56 * 1024 * 1024
        ),
        cost_estimate=pl.CostEstimate(flops=flops, bytes_accessed=20_000_000, transcendentals=0),
        name=name,
    )
    return lambda span, *operands: inner(span, *after, *operands)


def shape_of(shape, dtype=F32):
    return jax.ShapeDtypeStruct(shape, dtype)


def once(kernel, operands, out_shapes, scratch, flops, name, spaces=()):
    spaces = dict(spaces)

    def whole(shape):
        return pl.BlockSpec(shape, lambda j: (0,) * len(shape), pipeline_mode=pl.Buffered(1))

    return pl.pallas_call(
        kernel,
        grid=(1,),
        in_specs=[
            pl.BlockSpec(memory_space=spaces[k]) if k in spaces else whole(x.shape)
            for k, x in enumerate(operands)
        ],
        out_specs=[whole(x.shape) for x in out_shapes],
        out_shape=out_shapes,
        scratch_shapes=scratch,
        compiler_params=pltpu.CompilerParams(vmem_limit_bytes=56 * 1024 * 1024),
        cost_estimate=pl.CostEstimate(flops=flops, bytes_accessed=5_000_000, transcendentals=0),
        name=name,
    )(*operands)


def on_device(
    tokens,
    positions,
    item_of_atom,
    item_lengths,
    atom_types,
    key_mask,
    ln1_gain,
    ln1_bias,
    w_qkv,
    kernel_means,
    kernel_widths,
    kernel_weight,
    type_scale,
    type_shift,
    w_out,
    ln2_gain,
    ln2_bias,
    w_up,
    w_down,
    out_cotangent,
):
    own_rows, model_width = tokens.shape
    assert own_rows == LANES
    kernels, heads = kernel_weight.shape
    head_size = model_width // heads
    head_scale = head_size ** (-0.5)
    scale2 = head_scale * LOG2E
    groups = heads // GROUP
    width = groups * SPAN
    ff_width = w_up.shape[1]
    ka_count = lax.axis_size("ka")
    flat = lax.axis_index("pb") * ka_count + lax.axis_index("ka")
    flat_array = flat.astype(jnp.int32).reshape(1)
    reach = (PROT_LEN + own_rows - 2) // own_rows
    chips = (reach + 1) // 2
    pairs = 2 * chips + 1
    assert pairs == len(SLOTS[0])
    keys = 2 * own_rows
    atoms = positions.shape[1]
    atoms_blocks = atoms // LANES
    types = type_scale.shape[0]
    order = tuple(range(bits_of("ka") - 1))

    window = Window(tokens)
    cotangent_came = core_flip(out_cotangent)

    select = select_table(head_size)
    place = place_table(heads, head_size)
    into_tail, out_of_tail = tail_tables(heads, head_size)
    type_tiles = -(-types // LANES)
    tables = jnp.pad(
        jnp.stack([type_scale, type_shift]), ((0, 0), (0, type_tiles * LANES - types))
    )
    tables = tables.reshape(2, type_tiles, LANES).swapaxes(0, 1).reshape(2 * type_tiles, LANES)
    lengths = jnp.pad(item_lengths, (0, -item_lengths.shape[0] % LANES)).reshape(-1, LANES)
    span, other, own, own_line, tabs, grad_weights, weights_turned, par = once(
        functools.partial(side_kernel, atoms_blocks),
        (
            flat_array,
            positions,
            item_of_atom.reshape(-1, LANES),
            key_mask.reshape(-1, LANES),
            atom_types.reshape(-1, LANES),
            lengths,
            tables,
            kernel_means.reshape(1, LANES),
            kernel_widths.reshape(1, LANES),
            kernel_weight,
        ),
        [
            shape_of((SPAN_ROWS, LANES), jnp.int32),
            shape_of((SIDE, pairs * keys)),
            shape_of((own_rows, LANES)),
            shape_of((SIDE, LANES)),
            shape_of((4, kernels, LANES)),
            shape_of((kernels, WEIGHT_PIECES * heads), BF),
            shape_of((heads, kernels), BF),
            shape_of((LANES, LANES)),
        ],
        [],
        1_000_000_000,
        "sides",
        {0: pltpu.SMEM},
    )

    own_spec = fixed((own_rows, LANES))
    other_spec = moving((SIDE, keys), 1)
    bias_spec = moving((1, own_rows, heads, keys))
    bias = call(
        bias_kernel,
        pairs,
        [own_spec, other_spec, fixed((4, kernels, LANES)), fixed((heads, kernels))],
        bias_spec,
        shape_of((pairs, own_rows, heads, keys)),
        [pltpu.VMEM((own_rows, keys), F32)],
        30_000_000_000,
        "pair_bias",
        after=(window.before, window.after),
    )(span, own, other, tabs, weights_turned)
    token_blocks = window.finish()

    ln1 = jnp.stack([ln1_gain, ln1_bias])
    ln2 = jnp.stack([ln2_gain, ln2_bias])
    expanded = pltpu.VMEM((groups, own_rows * GROUP, SPAN), BF)
    summed = pltpu.VMEM((groups, own_rows * GROUP, SPAN), F32)
    mask_scratch = pltpu.VMEM((own_rows, GROUP, keys), F32)
    line_scratch = pltpu.VMEM((groups, own_rows * GROUP, LANES), F32)
    attended, q_aug, lse_pieces, normed_chip, kvq = call(
        functools.partial(forward_kernel, scale2, groups, chips),
        pairs,
        [own_spec, other_spec]
        + [fixed((own_rows, model_width))] * 14
        + [
            fixed((2, model_width)),
            fixed((model_width, 3 * model_width)),
            fixed(select.shape),
            fixed((1, width)),
            fixed(place.shape),
            bias_spec,
        ],
        [
            fixed((own_rows, width)),
            fixed((own_rows, width)),
            fixed((PIECES, own_rows, LANES)),
            fixed((keys, model_width)),
            moving((1, keys, 3 * width)),
        ],
        [
            shape_of((own_rows, width)),
            shape_of((own_rows, width), BF),
            shape_of((PIECES, own_rows, LANES), BF),
            shape_of((keys, model_width), BF),
            shape_of((pairs, keys, 3 * width), BF),
        ],
        [
            expanded,
            mask_scratch,
            line_scratch,
            line_scratch,
            summed,
            pltpu.VMEM((own_rows, LANES), F32),
            pltpu.VMEM((keys, model_width), BF),
        ],
        25_000_000_000,
        "attention_forward",
    )(
        span,
        own,
        other,
        *token_blocks,
        ln1,
        w_qkv,
        select,
        ones_row(heads, head_size),
        place,
        bias,
    )

    tile = 3 * LANES
    assert ff_width % tile == 0 and tile % (2 * ff_width // ka_count) == 0
    row_shape = shape_of((own_rows, model_width), BF)
    slices = ka_count // 2
    up_rows, out_rows = ff_width // ka_count, model_width // ka_count
    pieces = shape_of((2, slices, own_rows, up_rows), BF)
    block_out, grad_mixed, do_aug, payload, attended_low, normed_second, *parts, ln2_grads = once(
        functools.partial(middle_kernel, groups, tile),
        (
            flat_array,
            tokens,
            attended,
            lse_pieces,
            ln2,
            out_cotangent,
            w_out,
            w_up,
            w_down,
            select,
            place,
            head_sum_table(heads),
            into_tail,
        ),
        [
            row_shape,
            shape_of((own_rows, model_width)),
            shape_of((own_rows, width), BF),
            shape_of((own_rows, model_width + 2 * LANES), BF),
            row_shape,
            row_shape,
            pieces,
            pieces,
            shape_of((2, model_width)),
        ],
        [
            pltpu.VMEM((model_width, model_width), BF),
            pltpu.VMEM((model_width, ff_width), BF),
            pltpu.VMEM((ff_width, model_width), BF),
            pltpu.VMEM((own_rows, model_width), F32),
            pltpu.VMEM((own_rows, model_width), F32),
            pltpu.SemaphoreType.DMA,
            pltpu.SemaphoreType.DMA((2, ff_width // tile)),
        ],
        10_000_000_000,
        "feed_forward",
        {0: pltpu.SMEM, 6: pl.ANY, 7: pl.ANY, 8: pl.ANY},
    )
    came = [core_flip(x) for x in (parts[1], normed_second, attended_low, payload)]
    half = model_width // 2
    up_kept, up_sent, rest_kept, rest_sent, payload_now = once(
        functools.partial(weight_grads_kernel, ka_count),
        (
            flat_array,
            parts[0],
            came[0],
            normed_second,
            came[1],
            out_cotangent,
            cotangent_came,
            attended_low,
            came[2],
            payload,
            came[3],
        ),
        [shape_of((slices // 2, up_rows, model_width), BF)] * 2
        + [shape_of((slices, up_rows + out_rows, half), BF)] * 2
        + [shape_of(payload.shape, BF)],
        [pltpu.VMEM((model_width, model_width), F32)],
        5_000_000_000,
        "weight_gradients",
        {0: pltpu.SMEM},
    )
    window = Window(payload_now, came[3])
    up_sum, rest_sum = Slices(up_kept, up_sent, order), Columns(rest_kept, rest_sent, order)

    dq, grad_scores = call(
        functools.partial(query_grad_kernel, scale2, head_scale, groups),
        pairs,
        [
            own_spec,
            other_spec,
            fixed((own_rows, width)),
            fixed((own_rows, width)),
            moving((1, keys, 2 * width)),
            bias_spec,
            fixed(select.shape),
        ],
        [fixed((own_rows, model_width)), moving((1, own_rows, heads, keys))],
        [row_shape, shape_of((pairs, own_rows, heads, keys), BF)],
        [expanded, expanded, mask_scratch, summed],
        22_000_000_000,
        "query_gradients",
        after=(up_sum.sent, rest_sum.sent),
    )(span, own, other, q_aug, do_aug, kvq, bias, select)
    dq_came = core_flip(dq)
    up_sum.step()
    rest_sum.step()

    pos_blocks = atoms_blocks + 4 * chips
    small, pos_part = call(
        phi_grad_kernel,
        pairs,
        [
            own_spec,
            other_spec,
            fixed((SIDE, LANES)),
            moving((1, own_rows, heads, keys)),
            fixed((4, kernels, LANES)),
            fixed((kernels, WEIGHT_PIECES * heads)),
            fixed((LANES, LANES)),
        ],
        [fixed((LANES, LANES)), fixed((3 * pos_blocks, LANES))],
        [shape_of((LANES, LANES)), shape_of((3 * pos_blocks, LANES))],
        [
            pltpu.VMEM((own_rows, keys), F32),
            pltpu.VMEM((kernels, FEW * own_rows), F32),
            pltpu.VMEM((kernels, FEW * own_rows), BF),
            pltpu.VMEM((own_rows, keys), F32),
            pltpu.VMEM((5, own_rows, LANES), F32),
            pltpu.VMEM((kernels, heads), F32),
            pltpu.VMEM((2, kernels, LANES), F32),
            pltpu.VMEM((2, 2 * LANES, LANES), F32),
        ],
        45_000_000_000,
        "kernel_gradients",
        after=(*window.first(), up_sum.sent, rest_sum.sent),
    )(span, own, other, own_line, grad_scores, tabs, grad_weights, par)
    payload_blocks = window.finish()
    up_sum.step()
    rest_sum.step()

    dkv = call(
        functools.partial(key_grad_kernel, scale2, head_scale, groups, model_width),
        pairs,
        [
            own_spec,
            other_spec,
            pl.BlockSpec(
                (1, own_rows, 2 * width),
                lambda j, span: (chips, span[SPAN_CORE, 0], 0),
                pipeline_mode=pl.Buffered(1),
            ),
            moving((1, keys, width), 0, 2),
        ]
        + [fixed((own_rows, model_width + 2 * LANES))] * 14
        + [
            fixed((model_width, model_width)),
            fixed(select.shape),
            fixed(out_of_tail.shape),
            bias_spec,
        ],
        fixed((own_rows, 2 * model_width)),
        shape_of((own_rows, 2 * model_width), BF),
        [
            expanded,
            expanded,
            mask_scratch,
            pltpu.VMEM((keys, width), BF),
            pltpu.VMEM((keys, width), BF),
            summed,
            summed,
            pltpu.VMEM((keys, model_width + 2 * LANES), BF),
        ],
        28_000_000_000,
        "key_gradients",
        after=(up_sum.sent, rest_sum.sent),
    )(span, own, other, kvq, kvq, *payload_blocks, w_out, select, out_of_tail, bias)

    dkv_came = core_flip(dkv)
    split_at = model_width // 3
    qkv_rows = 3 * model_width // ka_count
    qkv_half = (model_width - split_at) // 2
    a_kept, a_sent, b_kept, b_sent = once(
        functools.partial(qkv_grads_kernel, ka_count, split_at),
        (flat_array, dq, dq_came, dkv, dkv_came, normed_chip),
        [shape_of((slices // 2, qkv_rows, split_at), BF)] * 2
        + [shape_of((slices, qkv_rows, qkv_half), BF)] * 2,
        [pltpu.VMEM((3 * model_width, model_width), F32)],
        3_000_000_000,
        "qkv_gradients",
        {0: pltpu.SMEM},
    )
    sums = [
        Slices(a_kept, a_sent, order),
        Columns(b_kept, b_sent, order),
        up_sum,
        rest_sum,
    ]
    grad_tokens, ln1_grads = once(
        first_norm_kernel,
        (tokens, ln1, dq, dkv, w_qkv, grad_mixed),
        [shape_of((own_rows, model_width)), shape_of((2, model_width))],
        [],
        2_000_000_000,
        "first_norm",
    )
    norm_rows = [x.reshape(-1, LANES) for x in (ln1_grads, ln2_grads)]
    joined = sum_everywhere(jnp.concatenate([small, *norm_rows, pos_part], axis=0))
    up_sum.step()
    rest_sum.step()
    a_total, b_total, up_total, rest_total = [part.result() for part in sums]

    small = joined[:LANES]
    count = norm_rows[0].shape[0]
    ln1_sum = joined[LANES : LANES + count].reshape(2, model_width)
    ln2_sum = joined[LANES + count : LANES + 2 * count].reshape(2, model_width)
    pos_rows = joined[LANES + 2 * count :].reshape(3, pos_blocks, LANES)
    grad_positions = lax.dynamic_index_in_dim(pos_rows, flat + 2 * chips, 1, keepdims=False)
    type_columns = small[:, heads + 2 : heads + 6]
    by_type = jnp.concatenate([type_columns[:, :2], type_columns[: types - LANES, 2:]], axis=0)
    qkv_total = jnp.concatenate([a_total, b_total], axis=1)
    return (
        block_out,
        grad_tokens,
        grad_positions,
        ln1_sum[0],
        ln1_sum[1],
        qkv_total.T.astype(F32),
        small[:, heads],
        small[:, heads + 1],
        small[:, :heads],
        by_type[:, 0],
        by_type[:, 1],
        rest_total[up_rows:].T.astype(F32),
        ln2_sum[0],
        ln2_sum[1],
        up_total.T.astype(F32),
        rest_total[:up_rows].astype(F32),
    )


def solution(mesh):
    rows = P(MESH, None)
    in_specs = (rows,) + (P(),) * 18 + (rows,)
    out_specs = (
        rows,
        rows,
        P(None, MESH),
        P(),
        P(),
        P(None, "ka"),
        P(),
        P(),
        P(),
        P(),
        P(),
        P(None, "ka"),
        P(),
        P(),
        P(None, "ka"),
        P("ka", None),
    )
    return jax.shard_map(
        on_device, mesh=mesh, in_specs=in_specs, out_specs=out_specs, check_vma=False
    )
```

```python
import functools
import math

import jax
import jax.numpy as jnp
import numpy as np
from jax import lax
from jax.experimental import pallas as pl
from jax.experimental.pallas import tpu as pltpu
from jax.sharding import PartitionSpec as P

MOL_TYPES = 128
PROT_LEN = 768
MOL_MEAN = 32

LN_EPS = 1e-05
GELU_SLOPE = math.sqrt(2.0 / math.pi)
GELU_CUBE = 0.044715
MASKED = -1e30
ROOT_TWO_PI = math.sqrt(2.0 * math.pi)
LOG2E = math.log2(math.e)
KAPPA = math.sqrt(0.5 * LOG2E)

PAD = 32
GROUP = 8
SPAN = PAD * GROUP
PIECES = 3
WEIGHT_PIECES = 2
CHUNK = 32
HEAD_ROWS = 32
BIAS_ROWS = 64
FEW = 8
MESH = ("pb", "ka")

BF = jnp.bfloat16
F32 = jnp.float32


def shifted(block, axis, distance):
    devices = range(lax.axis_size(axis))
    route = [(i - distance, i) for i in devices if i - distance in devices]
    return lax.ppermute(block, axis, route)


def core_flip(block):
    devices = range(lax.axis_size(MESH))
    return lax.ppermute(block, MESH, [(i, i ^ 1) for i in devices])


class Window:
    def __init__(self, block, sibling=None):
        devices = range(lax.axis_size(MESH))
        levels = len(devices) // 4

        def of(level, rest):
            return level % levels * 4 + rest

        one, two, far = [], [], []
        for i in devices:
            level, chip, core = i // 4, (i >> 1) & 1, i & 1
            odd = level & 1
            one.append((i, of(level + (-1 if odd else 1), i % 4)))
            two.append((i, of(level + (1 if odd else -1), i % 4)))
            far.append((i, of(level + (2 if chip else -2), (1 - chip) * 2 + core)))
        self.block, self.sibling = block, sibling
        self.one = lax.ppermute(block, MESH, one)
        self.two = lax.ppermute(block, MESH, two)
        self.far = lax.ppermute(block, MESH, far)

    def middle(self):
        self.other_chip = [flip_bit(x, "ka", 1) for x in (self.block, self.one, self.two)]
        return self.other_chip

    def finish(self):
        beside, one, two = self.other_chip
        mine = [self.far, self.one, one, self.block, beside, self.two, two]
        came = [core_flip(x) for x in mine if x is not self.block]
        own = core_flip(self.block) if self.sibling is None else self.sibling
        return mine + came[:3] + [own] + came[3:]


SLOTS = (
    (0, 5, 6, 3, 4, 1, 2),
    (6, 5, 4, 3, 2, 1, 0),
    (0, 1, 2, 3, 4, 5, 6),
    (2, 1, 4, 3, 6, 5, 0),
)
SPAN_FIRST, SPAN_LAST, SPAN_CORE, SPAN_CHIP, SPAN_SLOT = 0, 1, 2, 3, 4
SPAN_LOW = 16
SPAN_HIGH = 32
SPAN_ROWS = 48
LANES = 128
SIDE = 16


def flip_bit(block, axis, bit):
    devices = range(lax.axis_size(axis))
    return lax.ppermute(block, axis, [(i, i ^ (1 << bit)) for i in devices])


def bits_of(axis):
    return (lax.axis_size(axis) - 1).bit_length()


class Sum:
    def __init__(self, kept, sent, stages, left=()):
        self.kept, self.sent, self.stages, self.left = kept, sent, list(stages), list(left)
        self.total = None

    def came(self):
        return flip_bit(self.sent, *self.stages[0][:2])

    def plan(self):
        stage = self.stages.pop(0)
        if len(stage) == 3:
            return ("join",)
        if self.stages and self.stages[0][0] == "ka" and self.left:
            bit = self.stages[0][1] - 1
            self.left.remove(bit)
            below = sum(1 for b in self.left if b < bit)
            return ("halve", bit, 2 ** (len(self.left) - below), 2**below)
        return ("whole",)


def slices_sum(kept, sent, order):
    stages = [("ka", bit + 1) for bit in order]
    stages += [("pb", bit) for bit in range(bits_of("pb"))]
    return Sum(kept, sent, stages, [bit for bit in order if bit != order[0]])


def columns_sum(kept, sent, order):
    stages = [("pb", 0)] + [("ka", bit + 1) for bit in order]
    stages += [("pb", bit) for bit in range(1, bits_of("pb"))] + [("pb", 0, "join")]
    return Sum(kept, sent, stages, order)


def everywhere_sum(values):
    stages = [(axis, bit) for axis in ("ka", "pb") for bit in range(bits_of(axis))]
    return Sum(values, values, stages)


def stage_kernel(plans, side_bit, flat_ref, *refs):
    flat = flat_ref[0]
    count = len(plans)
    kept_refs, came_refs = refs[:count], refs[count : 2 * count]
    outs = list(refs[2 * count :])
    for plan, kept, came in zip(plans, kept_refs, came_refs):

        def total(*at):
            return kept[at].astype(F32) + came[at].astype(F32)

        out = outs.pop(0)
        if plan[0] == "whole":
            out[...] = total(Ellipsis).astype(out.dtype)
        elif plan[0] == "join":
            half = kept.shape[-1]
            side = jnp.right_shift(flat, side_bit) & 1
            out[:, pl.ds(pl.multiple_of(side * half, LANES), half)] = kept[...].astype(F32)
            out[:, pl.ds(pl.multiple_of((1 - side) * half, LANES), half)] = came[...].astype(F32)
        else:
            sent = outs.pop(0)
            _, bit, above, below = plan
            mine = jnp.right_shift(flat, bit + 1) & 1
            for i in range(above):
                for j in range(below):
                    for half, ref in ((mine, out), (1 - mine, sent)):
                        ref[i * below + j] = total((2 * i + half) * below + j).astype(BF)


def advance(sums, flat_array, name, after=()):
    sums = [one for one in sums if one.stages]
    came = [one.came() for one in sums]
    plans, shapes = [], []
    for one in sums:
        plan = one.plan()
        shape, dtype = one.kept.shape, one.kept.dtype
        if plan[0] == "join":
            shape, dtype = (shape[0], 2 * shape[1]), F32
        elif plan[0] == "halve":
            shape = (plan[2] * plan[3], *shape[1:])
            shapes.append(shape_of(shape, dtype))
        elif not one.stages:
            dtype = F32
        shapes.append(shape_of(shape, dtype))
        plans.append(plan)
    results = once(
        functools.partial(stage_kernel, plans, bits_of("ka")),
        (flat_array, *(one.kept for one in sums), *came),
        shapes,
        [],
        1_000_000_000,
        name,
        {0: pltpu.SMEM},
        after=after,
        room=24,
    )
    results = list(results)
    for one, plan in zip(sums, plans):
        one.kept = one.sent = results.pop(0)
        if plan[0] == "halve":
            one.sent = results.pop(0)
        elif not one.stages:
            one.total = one.kept
        if one.kept.ndim == 3 and one.kept.shape[0] == 1 and not (one.stages and one.stages[0][0] == "ka"):
            one.kept = one.kept.reshape(one.kept.shape[1:])
            one.sent = one.kept


def layer_norm(values, ln_gain, ln_shift):
    centre = jnp.mean(values, axis=-1, keepdims=True)
    offsets = values - centre
    spread = jnp.mean(offsets * offsets, axis=-1, keepdims=True)
    return offsets * lax.rsqrt(spread + LN_EPS) * ln_gain + ln_shift


def dot_nn(left, right):
    return lax.dot_general(left, right, (((1,), (0,)), ((), ())), preferred_element_type=F32)


def dot_nt(left, right):
    return lax.dot_general(left, right, (((1,), (1,)), ((), ())), preferred_element_type=F32)


def dot_tn(left, right):
    return lax.dot_general(left, right, (((0,), (0,)), ((), ())), preferred_element_type=F32)


def select_table(head_size):
    column = np.arange(SPAN)
    source = (column // PAD) * head_size + column % PAD
    table = [
        (column[:, None] == (source + off)[None, :]) & (column % PAD < head_size)[None, :]
        for off in (0, 64)
    ]
    return np.stack(table).astype(BF)


def group_windows(groups, head_size):
    out = []
    for g in range(groups):
        start = g * GROUP * head_size
        out.append((start // LANES * LANES, (start % LANES) // 64))
    return out


def place_table(heads, head_size):
    column = np.arange(heads * PAD)
    lane = np.arange(LANES)
    return np.stack(
        [
            (lane[:, None] == (column // PAD)[None, :])
            & (column % PAD == head_size + p)[None, :]
            for p in range(PIECES)
        ]
    ).astype(BF)


def tail_tables(heads, head_size):
    lane, tail = np.arange(LANES), np.arange(2 * LANES)
    into = np.stack(
        [
            (lane[:, None] + p * heads == tail[None, :]) & (lane < heads)[:, None]
            for p in range(2 * PIECES)
        ]
    )
    column = np.arange(heads * PAD)
    piece = column % PAD - head_size
    free = (piece >= 0) & (piece < PIECES)
    lane_of = np.where(free, piece * heads + column // PAD, -1)
    out = np.stack(
        [
            (tail[:, None] == lane_of[None, :]) & free[None, :],
            (tail[:, None] - PIECES * heads == lane_of[None, :]) & free[None, :],
        ]
    )
    return into.astype(BF), out.astype(BF)


def ones_row(heads, head_size):
    column = np.arange(heads * PAD) % PAD
    return ((column >= head_size) & (column < head_size + PIECES)).astype(np.float32)[None]


def head_sum_table(heads):
    column = np.arange(heads * PAD)
    return (column[:, None] // PAD == np.arange(LANES)[None, :]).astype(BF)


def pad_columns(values, select_ref, windows):
    parts = [
        dot_nn(values[:, start : start + SPAN], select_ref[kind]).astype(BF)
        for start, kind in windows
    ]
    return jnp.concatenate(parts, axis=1)


def drop_columns(values, select_ref, windows):
    tiles = {}
    for g, (start, kind) in enumerate(windows):
        part = dot_nt(values[:, g * SPAN : (g + 1) * SPAN], select_ref[kind])
        for k in range(SPAN // LANES):
            tile = part[:, k * LANES : (k + 1) * LANES]
            at = start // LANES + k
            tiles[at] = tiles[at] + tile if at in tiles else tile
    return jnp.concatenate([tiles[at] for at in sorted(tiles)], axis=1).astype(BF)


def drop_turned(values, select_ref, windows):
    tiles = {}
    for g, (start, kind) in enumerate(windows):
        part = dot_nt(select_ref[kind], values[:, g * SPAN : (g + 1) * SPAN])
        for k in range(SPAN // LANES):
            tile = part[k * LANES : (k + 1) * LANES]
            at = start // LANES + k
            tiles[at] = tiles[at] + tile if at in tiles else tile
    return jnp.concatenate([tiles[at] for at in sorted(tiles)], axis=0).astype(BF)


def split(values, count):
    rest, out = values, []
    for _ in range(count):
        piece = rest.astype(BF)
        rest = rest - piece.astype(F32)
        out.append(piece)
    return out


def norm_parts(values):
    centre = jnp.mean(values, axis=-1, keepdims=True)
    offsets = values - centre
    spread = jnp.mean(offsets * offsets, axis=-1, keepdims=True)
    slope = lax.rsqrt(spread + LN_EPS)
    return offsets * slope, slope


def norm_back(grad, normal, slope, gain):
    inner = grad * gain
    mean = jnp.mean(inner, axis=-1, keepdims=True)
    tilt = jnp.mean(inner * normal, axis=-1, keepdims=True)
    by_gain = jnp.sum(grad * normal, axis=0, keepdims=True)
    by_shift = jnp.sum(grad, axis=0, keepdims=True)
    return slope * (inner - mean - normal * tilt), by_gain, by_shift


def stretched_of(own, other):
    delta = [own[:, i : i + 1] - other[i : i + 1, :] for i in range(3)]
    square = delta[0] * delta[0] + delta[1] * delta[1] + delta[2] * delta[2]
    dist = jnp.sqrt(square + 1.0)
    scales = own[:, 3:4] * other[3:4, :]
    stretched = scales * dist + own[:, 4:5] + other[4:5, :]
    return delta, dist, scales, stretched


def mask_of(own, other, key_is_own):
    same = own[:, 5:6] == other[5:6, :]
    itself = own[:, 7:8] == other[7:8, :]
    is_open = (own[:, 6:7] > 0.5) if key_is_own else (other[6:7, :] > 0.5)
    return jnp.where(same & (is_open | itself), 0.0, MASKED)


def line_atoms(lines):
    line = lax.broadcasted_iota(jnp.int32, (lines, lines // GROUP), 0)
    atom = lax.broadcasted_iota(jnp.int32, (lines, lines // GROUP), 1)
    return jnp.where(line // GROUP == atom, 1.0, 0.0).astype(BF)


def line_heads(lines):
    line = lax.broadcasted_iota(jnp.int32, (lines, SPAN), 0)
    column = lax.broadcasted_iota(jnp.int32, (lines, SPAN), 1)
    return jnp.where(column // PAD == line % GROUP, 1.0, 0.0)


def expand_into(out_ref, padded, groups):
    lines = CHUNK * GROUP
    keep = line_heads(lines).astype(BF)
    spread = line_atoms(lines)
    for g in range(groups):
        for i in range(padded.shape[0] // CHUNK):
            part = padded[i * CHUNK : (i + 1) * CHUNK, g * SPAN : (g + 1) * SPAN]
            out_ref[g, i * lines : (i + 1) * lines, :] = dot_nn(spread, part).astype(BF) * keep


def collapse(values):
    lines = values.shape[0]
    kept = values * line_heads(lines)
    high = kept.astype(BF)
    low = (kept - high.astype(F32)).astype(BF)
    line = lax.broadcasted_iota(jnp.int32, (lines // GROUP, lines), 1)
    atom = lax.broadcasted_iota(jnp.int32, (lines // GROUP, lines), 0)
    gather = jnp.where(line // GROUP == atom, 1.0, 0.0).astype(BF)
    return dot_nn(gather, high) + dot_nn(gather, low)


def fetch(span_ref, refs, out_ref):
    slot = span_ref[SPAN_SLOT + span_ref[SPAN_FIRST, 0] + pl.program_id(0), 0]
    count = len(refs) // 2
    rows = refs[0].shape[0]
    for k in range(count):

        @pl.when(slot == k)
        def _():
            out_ref[:rows] = refs[k][...]
            out_ref[rows:] = refs[count + k][...]


def spots_of(span_ref, rows):
    core = span_ref[SPAN_CORE, 0]
    return [pl.ds(pl.multiple_of(at * rows, rows), rows) for at in (core, 1 - core)]


def spread_mask(mask_ref, mask):
    mask_ref[...] = jnp.broadcast_to(mask[:, None, :], mask_ref.shape)


def reaches(span_ref, first, last, low, high):
    return (span_ref[SPAN_LOW + first, 0] <= high) & (span_ref[SPAN_HIGH + last, 0] >= low)


def head_steps(span_ref, rows, step):
    pair = span_ref[SPAN_FIRST, 0] + pl.program_id(0)
    few = HEAD_ROWS // FEW
    last = rows // FEW - 1
    whole = reaches(span_ref, last, 0, 2 * pair, 2 * pair + 1)

    @pl.when(whole)
    def _():
        step(0, rows)

    @pl.when(jnp.logical_not(whole))
    def _():
        def one(i, carry):
            @pl.when(reaches(span_ref, i * few, i * few + few - 1, 2 * pair, 2 * pair + 1))
            def _():
                step(pl.multiple_of(i * HEAD_ROWS, HEAD_ROWS), HEAD_ROWS)

            return carry

        lax.fori_loop(0, rows // HEAD_ROWS, one, 0)


def kernel_steps(span_ref, first, rows, size, step, skipped):
    pair = span_ref[SPAN_FIRST, 0] + pl.program_id(0)
    few = size // FEW

    def one(i, carry):
        at = pl.multiple_of(i * size, size)
        chunk = first // FEW + i * few
        for half in range(2):
            block = 2 * pair + half
            needed = reaches(span_ref, chunk, chunk + few - 1, block, block)

            @pl.when(needed)
            def _():
                step(at, half)

            @pl.when(jnp.logical_not(needed))
            def _():
                skipped(at, half)

        return carry

    lax.fori_loop(0, rows // size, one, 0)


def side_kernel(
    atoms_blocks,
    flat_ref,
    pos_ref,
    item_ref,
    open_ref,
    type_ref,
    length_ref,
    table_ref,
    means_ref,
    widths_ref,
    kw_ref,
    span_ref,
    other_ref,
    own_ref,
    line_ref,
    tab_ref,
    gw_ref,
    kwt_ref,
    par_ref,
):
    flat = flat_ref[0]
    chips = len(SLOTS[0]) // 2
    first_block = flat // 2 * 2 - 2 * chips
    ids = lax.broadcasted_iota(jnp.int32, (LANES, LANES), 0).astype(F32)
    lane = lax.broadcasted_iota(jnp.int32, (1, LANES), 1)
    tables = []
    for k in range(table_ref.shape[0] // 2):
        rows = split(table_ref[2 * k : 2 * k + 1, :], PIECES)
        rows += split(table_ref[2 * k + 1 : 2 * k + 2, :], PIECES)
        rows += [jnp.zeros((2, LANES), BF)]
        tables.append(jnp.concatenate([row.astype(F32) for row in rows], axis=0).astype(BF))
    flags = [
        jnp.broadcast_to(
            jnp.where(length_ref[k : k + 1, :] > 2 * MOL_MEAN, float(MOL_TYPES), 0.0), (8, LANES)
        ).astype(BF)
        for k in range(length_ref.shape[0])
    ]
    for b in range(other_ref.shape[1] // LANES):
        block = first_block + b
        inside = (block >= 0) & (block < atoms_blocks)
        source = jnp.clip(block, 0, atoms_blocks - 1)
        at = pl.ds(pl.multiple_of(source * LANES, LANES), LANES)
        item = jnp.where(inside, item_ref[pl.ds(source, 1), :].astype(F32), -1.0)
        kind = type_ref[pl.ds(source, 1), :].astype(F32)
        for k, flag in enumerate(flags):
            onehot = jnp.where(ids + float(k * LANES) == item, 1.0, 0.0).astype(BF)
            kind = kind + dot_nn(flag, onehot)[0:1, :]
        found = jnp.zeros((8, LANES), F32)
        for k, table in enumerate(tables):
            onehot = jnp.where(ids + float(k * LANES) == kind, 1.0, 0.0).astype(BF)
            found = found + dot_nn(table, onehot)
        rows = [pos_ref[k : k + 1, at] for k in range(3)]
        rows += [found[0:1] + found[1:2] + found[2:3], found[3:4] + found[4:5] + found[5:6]]
        rows += [item, open_ref[pl.ds(source, 1), :].astype(F32)]
        rows += [(block * LANES + lane).astype(F32), kind]
        rows += [jnp.zeros((SIDE - 9, LANES), F32)]
        side = jnp.concatenate(rows, axis=0)
        other_ref[:, b * LANES : (b + 1) * LANES] = side

        @pl.when(block == flat)
        def _():
            line_ref[...] = side

    line = line_ref[...]
    turned = jnp.transpose(
        jnp.concatenate([line, jnp.zeros((LANES - SIDE, LANES), F32)], axis=0)
    )
    own_ref[...] = turned
    chunks = LANES // FEW
    item_column = jnp.broadcast_to(own_ref[:, 5:6], (LANES, LANES))
    par_ref[...] = item_column
    first_item = par_ref[pl.ds(0, chunks, stride=FEW), :]
    last_item = par_ref[pl.ds(FEW - 1, chunks, stride=FEW), :]

    def count(k, carry):
        row = item_ref[pl.ds(k, 1), :].astype(F32)
        below, upto = carry
        return (
            below + jnp.where(row < first_item, 1.0, 0.0),
            upto + jnp.where(row <= last_item, 1.0, 0.0),
        )

    zero = jnp.zeros((chunks, LANES), F32)
    below, upto = lax.fori_loop(0, atoms_blocks, count, (zero, zero))
    below = jnp.sum(below, axis=1, keepdims=True).astype(jnp.int32)
    upto = jnp.sum(upto, axis=1, keepdims=True).astype(jnp.int32)
    low = jnp.right_shift(below - first_block * LANES, 7)
    high = jnp.right_shift(upto - 1 - first_block * LANES, 7)
    span_ref[SPAN_LOW : SPAN_LOW + chunks, :] = jnp.broadcast_to(low, (chunks, LANES))
    span_ref[SPAN_HIGH : SPAN_HIGH + chunks, :] = jnp.broadcast_to(high, (chunks, LANES))
    row = lax.broadcasted_iota(jnp.int32, (SPAN_LOW, LANES), 0)
    kind = (flat // 2) % 4
    head = jnp.where(row == SPAN_FIRST, jnp.right_shift(low[0:1, :], 1), 0)
    head = head + jnp.where(row == SPAN_LAST, jnp.right_shift(high[chunks - 1 :, :], 1), 0)
    head = head + jnp.where(row == SPAN_CORE, flat % 2, 0)
    head = head + jnp.where(row == SPAN_CHIP, flat // 2, 0)
    for k, slots in enumerate(zip(*SLOTS)):
        slot = sum(jnp.where(kind == which, at, 0) for which, at in enumerate(slots))
        head = head + jnp.where(row == SPAN_SLOT + k, slot, 0)
    span_ref[:SPAN_LOW, :] = head

    def column_of(ref):
        return jnp.transpose(jnp.broadcast_to(ref[...], (LANES, LANES)))

    means, widths = column_of(means_ref), column_of(widths_ref)
    peaks = 1.0 / (ROOT_TWO_PI * widths)
    bend = -(KAPPA * KAPPA) / (widths * widths)
    tab_ref[0] = means
    tab_ref[1] = KAPPA / widths
    tab_ref[2] = LOG2E * jnp.log(peaks)
    tab_ref[3] = bend
    weights = kw_ref[...].astype(F32)
    heads = weights.shape[1]
    scaled = weights * (peaks / (widths * widths))[:, :heads]
    gw_ref[...] = jnp.concatenate(split(scaled, WEIGHT_PIECES), axis=1)
    wide = jnp.concatenate([weights, jnp.zeros((LANES, LANES - heads), F32)], axis=1)
    kwt_ref[...] = jnp.transpose(wide)[:heads, :].astype(BF)
    lanes = lax.broadcasted_iota(jnp.int32, (LANES, LANES), 1)
    par = wide + jnp.where(lanes == heads, peaks, 0.0)
    par_ref[...] = par + jnp.where(lanes == heads + 1, 1.0 / widths, 0.0)


def bias_kernel(span_ref, own_ref, other_ref, tab_ref, kwt_ref, out_ref, str_ref):
    rows, keys = str_ref.shape
    kernels = tab_ref.shape[1]
    heads = kwt_ref.shape[0]
    half_keys = keys // 2
    str_ref[...] = stretched_of(own_ref[...], other_ref[...])[3]

    def step(at, half):
        columns = slice(half * half_keys, (half + 1) * half_keys)
        block = str_ref[pl.ds(at, BIAS_ROWS), columns]
        for r in range(0, BIAS_ROWS, 2):
            parts = []
            for q in range(2):
                line = jnp.broadcast_to(block[r + q : r + q + 1], (kernels, half_keys))
                z = (line - tab_ref[0]) * tab_ref[1]
                parts.append(jnp.exp2(tab_ref[2] - z * z).astype(BF))
            result = dot_nn(kwt_ref[...], jnp.concatenate(parts, axis=1)) * LOG2E
            out_ref[0, at + r, :, columns] = result[:, :half_keys]
            out_ref[0, at + r + 1, :, columns] = result[:, half_keys:]

    def skipped(at, half):
        columns = slice(half * half_keys, (half + 1) * half_keys)
        out_ref[0, pl.ds(at, BIAS_ROWS), :, columns] = jnp.zeros((BIAS_ROWS, heads, half_keys), F32)

    kernel_steps(span_ref, 0, rows, BIAS_ROWS, step, skipped)


def forward_kernel(
    scale2,
    groups,
    span_ref,
    own_ref,
    other_ref,
    *refs,
):
    token_refs, refs = refs[:14], refs[14:]
    ln_ref, w_ref, select_ref, ones_ref, place_ref, bias_ref, *refs = refs
    att_ref, qaug_ref, lse_ref, kvq_ref, *refs = refs
    qexp_ref, mask_ref, max_ref, sum_ref, acc_ref, lane_ref, both_ref = refs
    step = pl.program_id(0)
    width = groups * SPAN
    tok_ref = token_refs[3]
    rows, model_width = tok_ref.shape
    windows = group_windows(groups, model_width // (groups * GROUP))
    gain, shift = ln_ref[0:1, :], ln_ref[1:2, :]

    @pl.when(step == 0)
    def _():
        normed = layer_norm(tok_ref[...].astype(F32), gain, shift).astype(BF)
        query = dot_nn(normed, w_ref[:, :model_width]).astype(BF)
        query = pad_columns(query, select_ref, windows)
        qaug_ref[...] = query
        expand_into(qexp_ref, query, groups)
        max_ref[...] = jnp.full(max_ref.shape, 2.0 * MASKED, F32)
        sum_ref[...] = jnp.zeros(sum_ref.shape, F32)
        acc_ref[...] = jnp.zeros(acc_ref.shape, F32)

    fetch(span_ref, token_refs, both_ref)
    normed = layer_norm(both_ref[...].astype(F32), gain, shift).astype(BF)
    spots = spots_of(span_ref, rows)

    for part in range(3):
        source = (part + 1) % 3 * model_width
        value = dot_nn(normed, w_ref[:, source : source + model_width]).astype(BF)
        value = pad_columns(value, select_ref, windows)
        if part < 2:
            value = value + ones_ref[...].astype(BF)
        for k in range(2):
            kvq_ref[0, spots[k], part * width : (part + 1) * width] = (
                value[k * rows : (k + 1) * rows]
            )
    spread_mask(mask_ref, mask_of(own_ref[...], other_ref[...], False))

    def chunk_step(at, count):
        lines = pl.ds(pl.multiple_of(at * GROUP, HEAD_ROWS * GROUP), count * GROUP)
        mask = mask_ref[pl.ds(at, count)]
        for g in range(groups):
            columns = slice(g * SPAN, (g + 1) * SPAN)
            dots = dot_nt(qexp_ref[g, lines, :], kvq_ref[0, :, columns])
            bias = bias_ref[0, pl.ds(at, count), g * GROUP : (g + 1) * GROUP, :] + mask
            scores = dots * scale2 + bias.reshape(dots.shape)
            old = max_ref[g, lines, :]
            top = jnp.maximum(scores[:, :128], scores[:, 128:])
            new = jnp.maximum(old, jnp.max(top, axis=1, keepdims=True))
            alpha = jnp.exp2(old - new)
            low = jnp.exp2(scores[:, :128] - new)
            high = jnp.exp2(scores[:, 128:] - new)
            max_ref[g, lines, :] = new
            sum_ref[g, lines, :] = sum_ref[g, lines, :] * alpha + (low + high)
            probs = jnp.concatenate([low, high], axis=1).astype(BF)
            values = dot_nn(probs, kvq_ref[0, :, width + g * SPAN : width + (g + 1) * SPAN])
            wide = jnp.concatenate([alpha, alpha], axis=1)
            acc_ref[g, lines, :] = acc_ref[g, lines, :] * wide + values

    head_steps(span_ref, rows, chunk_step)

    @pl.when(step == span_ref[SPAN_LAST, 0] - span_ref[SPAN_FIRST, 0])
    def _():
        lane = lax.broadcasted_iota(jnp.int32, (GROUP, 128), 1)
        head = lax.broadcasted_iota(jnp.int32, (GROUP, 128), 0)

        def finish(i, carry):
            at = pl.multiple_of(i * CHUNK, CHUNK)
            lines = pl.ds(pl.multiple_of(i * CHUNK * GROUP, CHUNK * GROUP), CHUNK * GROUP)
            lanes = jnp.zeros((CHUNK, 128), F32)
            for g in range(groups):
                total = jnp.sum(sum_ref[g, lines, :], axis=1, keepdims=True)
                attended = collapse(acc_ref[g, lines, :] / total)
                att_ref[pl.ds(at, CHUNK), g * SPAN : (g + 1) * SPAN] = attended
                lse = max_ref[g, lines, :] + jnp.log(total) * LOG2E
                own_lane = jnp.where(lane == head + g * GROUP, 1.0, 0.0)
                lanes = lanes + jnp.sum(
                    lse.reshape(CHUNK, GROUP, 128) * own_lane[None], axis=1
                )
            lane_ref[pl.ds(at, CHUNK), :] = lanes
            return carry

        lax.fori_loop(0, rows // CHUNK, finish, 0)
        rest = lane_ref[...] * (-1.0 / scale2)
        query = qaug_ref[...].astype(F32)
        for p in range(PIECES):
            piece = rest.astype(BF)
            rest = rest - piece.astype(F32)
            lse_ref[p] = piece
            query = query + dot_nn(piece, place_ref[p])
        qaug_ref[...] = query.astype(BF)


def query_grad_kernel(
    scale2,
    head_scale,
    groups,
    span_ref,
    own_ref,
    other_ref,
    qaug_ref,
    doaug_ref,
    kv_ref,
    bias_ref,
    select_ref,
    dq_ref,
    ds_ref,
    qexp_ref,
    doexp_ref,
    mask_ref,
    dqacc_ref,
    low_ref,
):
    step = pl.program_id(0)
    width = groups * SPAN
    rows, keys = own_ref.shape[0], other_ref.shape[1]
    windows = group_windows(groups, dq_ref.shape[0] // (groups * GROUP))

    @pl.when(step == 0)
    def _():
        expand_into(qexp_ref, qaug_ref[...], groups)
        expand_into(doexp_ref, doaug_ref[...], groups)
        dqacc_ref[...] = jnp.zeros(dqacc_ref.shape, F32)

    spread_mask(mask_ref, mask_of(own_ref[...], other_ref[...], False))

    def chunk_step(at, count):
        lines = pl.ds(pl.multiple_of(at * GROUP, HEAD_ROWS * GROUP), count * GROUP)
        mask = mask_ref[pl.ds(at, count)]
        waiting = []
        for g in range(groups):
            key_block = kv_ref[0, :, g * SPAN : (g + 1) * SPAN]
            value_block = kv_ref[0, :, width + g * SPAN : width + (g + 1) * SPAN]
            dots = dot_nt(qexp_ref[g, lines, :], key_block)
            grads = dot_nt(doexp_ref[g, lines, :], value_block)
            bias = bias_ref[0, pl.ds(at, count), g * GROUP : (g + 1) * GROUP, :] + mask
            probs = jnp.exp2(dots * scale2 + bias.reshape(dots.shape))
            grad_scores = probs * grads
            dqacc_ref[g, lines, :] += dot_nn(grad_scores.astype(BF), key_block)
            waiting.append(grad_scores.reshape(count, GROUP, keys))
            if len(waiting) == 2:
                ds_ref[0, pl.ds(at, count), (g - 1) * GROUP : (g + 1) * GROUP, :] = (
                    jnp.concatenate(waiting, axis=1).astype(BF)
                )
                waiting = []

    head_steps(span_ref, rows, chunk_step)

    @pl.when(step == span_ref[SPAN_LAST, 0] - span_ref[SPAN_FIRST, 0])
    def _():
        def finish(i, carry):
            at = pl.multiple_of(i * CHUNK, CHUNK)
            lines = pl.ds(pl.multiple_of(i * CHUNK * GROUP, CHUNK * GROUP), CHUNK * GROUP)
            for g in range(groups):
                value = collapse(dqacc_ref[g, lines, :]) * head_scale
                low_ref[pl.ds(at, CHUNK), g * SPAN : (g + 1) * SPAN] = value.astype(BF)
            return carry

        lax.fori_loop(0, rows // CHUNK, finish, 0)
        dq_ref[...] = drop_turned(low_ref[...], select_ref, windows)


def phi_grad_kernel(
    first_row,
    span_ref,
    own_ref,
    other_ref,
    line_ref,
    ds_ref,
    tab_ref,
    kw_ref,
    par_ref,
    small_ref,
    pos_ref,
    str_ref,
    gs_ref,
    own_acc_ref,
    gkw_ref,
    moment_ref,
    type_ref,
):
    step = pl.program_id(0)
    rows, keys = str_ref.shape
    kernels = tab_ref.shape[1]
    heads = gkw_ref.shape[1]
    blocks = pos_ref.shape[0] // 3
    pair_block = 2 * (span_ref[SPAN_CHIP, 0] + span_ref[SPAN_FIRST, 0] + step)

    @pl.when(step == 0)
    def _():
        gkw_ref[...] = jnp.zeros(gkw_ref.shape, F32)
        moment_ref[...] = jnp.zeros(moment_ref.shape, F32)
        own_acc_ref[...] = jnp.zeros(own_acc_ref.shape, F32)
        pos_ref[...] = jnp.zeros(pos_ref.shape, F32)
        type_ref[...] = jnp.zeros(type_ref.shape, F32)

    def add_types(kind, by_scale, by_shift):
        count = type_ref.shape[1]
        onehot = lax.broadcasted_iota(jnp.int32, (count, LANES), 0).astype(F32) == kind
        type_ref[0] += jnp.where(onehot, by_scale, 0.0)
        type_ref[1] += jnp.where(onehot, by_shift, 0.0)

    own, other = own_ref[first_row : first_row + rows, :], other_ref[...]
    str_ref[...] = stretched_of(own, other)[3]

    half_keys = keys // 2

    def pair_step(at, half):
        columns = slice(half * half_keys, (half + 1) * half_keys)
        block = str_ref[pl.ds(at, CHUNK), columns]
        first = second = weights = None
        lines = []
        for r in range(0, CHUNK, 2):
            low = jnp.concatenate([ds_ref[0, at + r + q, :, columns] for q in range(2)], axis=1)
            dphi = dot_nn(kw_ref[...], jnp.concatenate([low] * WEIGHT_PIECES, axis=0))
            phis = []
            for q in range(2):
                away = jnp.broadcast_to(block[r + q : r + q + 1], (kernels, half_keys)) - tab_ref[0]
                phi = jnp.exp2(away * away * tab_ref[3])
                phis.append(phi.astype(BF))
                moved = dphi[:, q * half_keys : (q + 1) * half_keys] * phi * away
                bent = moved * away
                first = moved if first is None else first + moved
                second = bent if second is None else second + bent
                lines.append(jnp.sum(moved, axis=0, keepdims=True))
            part = dot_nt(jnp.concatenate(phis, axis=1), low)
            weights = part if weights is None else weights + part
        moment_ref[0] += first
        moment_ref[1] += second
        gs_ref[pl.ds(at, CHUNK), columns] = jnp.concatenate(lines, axis=0)
        gkw_ref[...] += weights

    def skipped(at, half):
        columns = slice(half * half_keys, (half + 1) * half_keys)
        gs_ref[pl.ds(at, CHUNK), columns] = jnp.zeros((CHUNK, half_keys), F32)

    kernel_steps(span_ref, first_row, rows, CHUNK, pair_step, skipped)

    delta, dist, scales, _ = stretched_of(own, other)
    grad = -gs_ref[...]
    by_scale = grad * dist
    pull = grad * scales / dist
    terms = [pull * delta[0], pull * delta[1], pull * delta[2], by_scale * other[3:4, :], grad]
    for k, term in enumerate(terms):
        own_acc_ref[k] += term[:, :128] + term[:, 128:]
    for half in range(2):
        part = slice(half * LANES, (half + 1) * LANES)
        for k in range(3):
            spot = pl.ds(k * blocks + pair_block + half, 1)
            pos_ref[spot, :] += -jnp.sum(terms[k][:, part], axis=0, keepdims=True)
        add_types(
            other[8:9, part],
            jnp.sum(by_scale[:, part] * own[:, 3:4], axis=0, keepdims=True),
            jnp.sum(grad[:, part], axis=0, keepdims=True),
        )

    @pl.when(step == span_ref[SPAN_LAST, 0] - span_ref[SPAN_FIRST, 0])
    def _():
        lane = lax.broadcasted_iota(jnp.int32, (rows, LANES), 1)
        total = jnp.zeros((rows, LANES), F32)
        for k in range(5):
            column = jnp.sum(own_acc_ref[k], axis=1, keepdims=True)
            total = total + jnp.where(lane == k, column, 0.0)
        rest = [jnp.zeros((count, LANES), F32) for count in (first_row, LANES - first_row - rows)]
        total = jnp.concatenate([x for x in (rest[0], total, rest[1]) if x.shape[0]], axis=0)
        turned = jnp.transpose(total)
        own_block = 2 * (span_ref[SPAN_CHIP, 0] + len(SLOTS[0]) // 2) + span_ref[SPAN_CORE, 0]
        for k in range(3):
            pos_ref[pl.ds(k * blocks + own_block, 1), :] += turned[k : k + 1, :]
        add_types(line_ref[8:9, :], turned[3:4, :], turned[4:5, :])

        par = par_ref[...]
        by_weight = gkw_ref[...] * par[:, heads : heads + 1]
        plain = jnp.sum(by_weight * par[:, :heads], axis=1, keepdims=True)
        by_mean = jnp.sum(moment_ref[0], axis=1, keepdims=True)
        by_width = jnp.sum(moment_ref[1], axis=1, keepdims=True) - plain
        columns = [by_mean, by_width * par[:, heads + 1 : heads + 2]]
        low, high = slice(0, LANES), slice(LANES, 2 * LANES)
        for part in (low, high):
            for k in range(2):
                columns.append(jnp.sum(type_ref[k, part, :], axis=1, keepdims=True))
        lane = lax.broadcasted_iota(jnp.int32, (LANES, LANES), 1)
        wide = jnp.concatenate([by_weight, jnp.zeros((LANES, LANES - heads), F32)], axis=1)
        for k, column in enumerate(columns):
            wide = wide + jnp.where(lane == heads + k, column, 0.0)
        small_ref[...] = wide


def middle_kernel(
    groups,
    tile,
    flat_ref,
    tok_ref,
    att_ref,
    lse_ref,
    ln_ref,
    cot_ref,
    wout_hbm,
    wup_hbm,
    wdown_hbm,
    select_ref,
    place_ref,
    sum_ref,
    into_ref,
    out_ref,
    gmix_ref,
    doaug_ref,
    payload_ref,
    attlow_ref,
    normed_ref,
    mine_ref,
    theirs_ref,
    lngrad_ref,
    wout_ref,
    wup_ref,
    wdown_ref,
    down_ref,
    back_ref,
    wout_sem,
    tile_sems,
):
    rows, model_width = tok_ref.shape
    width = groups * SPAN
    windows = group_windows(groups, model_width // (groups * GROUP))
    tiles = wup_ref.shape[1] // tile
    piece = mine_ref.shape[3]
    core = flat_ref[0] % 2

    def tile_copies(t):
        spot = pl.ds(pl.multiple_of(t * tile, LANES), tile)
        return (
            pltpu.make_async_copy(wup_hbm.at[:, spot], wup_ref.at[:, spot], tile_sems.at[0, t]),
            pltpu.make_async_copy(wdown_hbm.at[spot, :], wdown_ref.at[spot, :], tile_sems.at[1, t]),
        )

    first = pltpu.make_async_copy(wout_hbm, wout_ref, wout_sem)
    first.start()
    for t in range(tiles):
        for copy in tile_copies(t):
            copy.start()

    gain, shift = ln_ref[0:1, :], ln_ref[1:2, :]
    cotangent = cot_ref[...]
    attended = att_ref[...]
    attended_low = drop_columns(attended.astype(BF), select_ref, windows)
    attlow_ref[...] = attended_low
    first.wait()
    mixed = tok_ref[...].astype(F32) + dot_nn(attended_low, wout_ref[...])
    normal, slope = norm_parts(mixed)
    normed_ref[...] = (normal * gain + shift).astype(BF)
    down_ref[...] = mixed
    back_ref[...] = jnp.zeros(back_ref.shape, F32)

    def step(t, carry):
        for copy in tile_copies(t):
            copy.wait()
        spot = pl.ds(pl.multiple_of(t * tile, LANES), tile)
        up = dot_nn(normed_ref[...], wup_ref[:, spot])
        grad_hidden = dot_nt(cotangent, wdown_ref[spot, :])
        square = up * up
        bent = jnp.tanh(GELU_SLOPE * (up * (1.0 + GELU_CUBE * square)))
        gate = 0.5 * (1.0 + bent)
        inner = GELU_SLOPE * (1.0 + 3.0 * GELU_CUBE * square)
        hidden = (up * gate).astype(BF)
        grad_up = (grad_hidden * (gate + 0.5 * up * (1.0 - bent * bent) * inner)).astype(BF)
        for kind, value in enumerate((grad_up, hidden)):
            for q in range(tile // piece):
                part = value[:, q * piece : (q + 1) * piece]
                at = t * (tile // piece // 2) + q // 2

                @pl.when(core == q % 2)
                def _():
                    mine_ref[kind, at] = part

                @pl.when(core != q % 2)
                def _():
                    theirs_ref[kind, at] = part

        down_ref[...] += dot_nn(hidden, wdown_ref[spot, :])
        back_ref[...] += dot_nt(grad_up, wup_ref[:, spot])
        return carry

    lax.fori_loop(0, tiles, step, 0)
    out_ref[...] = down_ref[...].astype(BF)
    back, by_gain, by_shift = norm_back(back_ref[...], normal, slope, gain)
    lngrad_ref[...] = jnp.concatenate([by_gain, by_shift], axis=0)
    grad_mixed = cotangent.astype(F32) + back
    gmix_ref[...] = grad_mixed
    grad_low = grad_mixed.astype(BF)
    grad_attended = dot_nt(grad_low, wout_ref[...]).astype(BF)
    padded = pad_columns(grad_attended, select_ref, windows).astype(F32)
    high, low = split(padded * attended, 2)
    delta = dot_nn(high, sum_ref[...]) + dot_nn(low, sum_ref[...])
    pieces = split(-delta, PIECES)
    tail = jnp.zeros((rows, 2 * LANES), F32)
    for p in range(PIECES):
        padded = padded + dot_nn(pieces[p], place_ref[p])
        tail = tail + dot_nn(lse_ref[p], into_ref[p]) + dot_nn(pieces[p], into_ref[PIECES + p])
    doaug_ref[...] = padded.astype(BF)
    payload_ref[:, :model_width] = grad_low
    payload_ref[:, model_width:] = tail.astype(BF)


def weight_grads_kernel(
    ka_count,
    flat_ref,
    mine_ref,
    came_ref,
    normed_ref,
    normed_came_ref,
    cot_ref,
    cot_came_ref,
    attlow_ref,
    attlow_came_ref,
    payload_ref,
    payload_came_ref,
    up_kept_ref,
    up_sent_ref,
    rest_kept_ref,
    rest_sent_ref,
    product_ref,
):
    flat = flat_ref[0]
    core, bit, side = flat % 2, (flat // 2) % 2, (flat // ka_count) % 2
    model_width = normed_ref.shape[1]
    rows = up_kept_ref.shape[1]
    half = model_width // 2
    slices = up_kept_ref.shape[0] * 2
    out_rows = model_width // ka_count
    normed = jnp.concatenate([normed_ref[...], normed_came_ref[...]], axis=0)
    cotangent = jnp.concatenate([cot_ref[...], cot_came_ref[...]], axis=0)

    def columns(which):
        return pl.ds(pl.multiple_of(which * half, LANES), half)

    def step(m, carry):
        both = jnp.concatenate([mine_ref[0, m], came_ref[0, m]], axis=0)
        value = dot_tn(both, normed).astype(BF)

        @pl.when(m % 2 == bit)
        def _():
            up_kept_ref[m // 2] = value

        @pl.when(m % 2 != bit)
        def _():
            up_sent_ref[m // 2] = value

        both = jnp.concatenate([mine_ref[1, m], came_ref[1, m]], axis=0)
        product_ref[:rows, :] = dot_tn(both, cotangent)
        rest_kept_ref[m, :rows, :] = product_ref[:rows, columns(side)].astype(BF)
        rest_sent_ref[m, :rows, :] = product_ref[:rows, columns(1 - side)].astype(BF)
        return carry

    lax.fori_loop(0, slices, step, 0)
    grads = jnp.concatenate(
        [payload_ref[:, :model_width], payload_came_ref[:, :model_width]], axis=0
    )
    attended = jnp.concatenate([attlow_ref[...], attlow_came_ref[...]], axis=0)
    product_ref[...] = dot_tn(grads, attended)

    def out_step(m, carry):
        spot = pl.ds(pl.multiple_of((2 * m + core) * out_rows, 8), out_rows)
        rest_kept_ref[m, rows:, :] = product_ref[spot, columns(side)].astype(BF)
        rest_sent_ref[m, rows:, :] = product_ref[spot, columns(1 - side)].astype(BF)
        return carry

    lax.fori_loop(0, slices, out_step, 0)


def normal_kernel(tok_ref, ln_ref, out_ref):
    normal, _ = norm_parts(tok_ref[...].astype(F32))
    out_ref[...] = (normal * ln_ref[0:1, :] + ln_ref[1:2, :]).astype(BF)


def qkv_grads_kernel(grads_ref, normed_ref, out_ref, norm_ref):
    devices, _, atoms = grads_ref.shape
    columns = out_ref.shape[0]
    total = parts = None
    for i in range(0, devices, 2):
        both = jnp.concatenate([grads_ref[i, :columns], grads_ref[i + 1, :columns]], axis=1)
        part = dot_nn(both, normed_ref[i * atoms : (i + 2) * atoms, :])
        total = part if total is None else total + part
        part = grads_ref[i, columns:].astype(F32) + grads_ref[i + 1, columns:].astype(F32)
        parts = part if parts is None else parts + part
    out_ref[...] = total.astype(BF)
    norm_ref[...] = parts


def results_kernel(
    heads,
    types,
    flat_ref,
    joined_ref,
    first_ref,
    norm_ref,
    weight_ref,
    mean_ref,
    width_ref,
    scale_ref,
    shift_ref,
    pos_ref,
):
    small = joined_ref[:LANES, :]
    weight_ref[...] = small[:, :heads]
    turned = jnp.transpose(small)
    rows = [turned[heads + k : heads + k + 1, :] for k in range(6)]
    mean_ref[...] = rows[0]
    width_ref[...] = rows[1]
    scale_ref[...] = jnp.concatenate([rows[2], rows[4]], axis=1)[:, :types]
    shift_ref[...] = jnp.concatenate([rows[3], rows[5]], axis=1)[:, :types]
    count = norm_ref.shape[1]
    for k in range(2):
        norm_ref[k] = first_ref[k * count : (k + 1) * count, :]
        norm_ref[2 + k] = joined_ref[LANES + k * count : LANES + (k + 1) * count, :]
    first = LANES + 2 * count
    blocks = (joined_ref.shape[0] - first) // 3
    for k in range(3):
        spot = first + k * blocks + len(SLOTS[0]) // 2 * 2 + flat_ref[0]
        pos_ref[k : k + 1, :] = joined_ref[pl.ds(spot, 1), :]


def first_norm_kernel(
    tok_ref, ln_ref, dq_ref, dkv_ref, w_ref, gmix_ref, grad_ref, all_ref, joined_ref
):
    model_width = tok_ref.shape[1]
    grad = dot_nn(w_ref[:, :model_width], dq_ref[...])
    grad = grad + dot_nn(w_ref[:, model_width:], dkv_ref[...])
    grad = jnp.transpose(grad)
    normal, slope = norm_parts(tok_ref[...].astype(F32))
    back, by_gain, by_shift = norm_back(grad, normal, slope, ln_ref[0:1, :])
    grad_ref[...] = gmix_ref[...] + back
    lines = [
        row[:, k : k + LANES] for row in (by_gain, by_shift) for k in range(0, model_width, LANES)
    ]
    joined_ref[:model_width, :] = dq_ref[...]
    joined_ref[model_width:, :] = dkv_ref[...]
    devices, rows = all_ref.shape[:2]
    columns = 3 * model_width // devices
    lines.append(jnp.zeros((rows - columns - len(lines), LANES), F32))
    lines = jnp.concatenate(lines, axis=0).astype(BF)
    for d in range(devices):
        all_ref[d, :columns, :] = joined_ref[d * columns : (d + 1) * columns, :]
        all_ref[d, columns:, :] = lines


def key_grad_kernel(
    scale2,
    head_scale,
    groups,
    model_width,
    span_ref,
    own_ref,
    other_ref,
    kv_ref,
    q_ref,
    *refs,
):
    payload_refs, refs = refs[:14], refs[14:]
    wout_ref, select_ref, place_ref, bias_ref, dkv_ref, kexp_ref, vexp_ref, *refs = refs
    mask_ref, qb_ref, dob_ref, dk_ref, dv_ref, both_ref, low_ref = refs
    step = pl.program_id(0)
    width = groups * SPAN
    rows = own_ref.shape[0]
    windows = group_windows(groups, model_width // (groups * GROUP))

    @pl.when(step == 0)
    def _():
        expand_into(kexp_ref, kv_ref[0, :, :width], groups)
        expand_into(vexp_ref, kv_ref[0, :, width:], groups)
        dk_ref[...] = jnp.zeros(dk_ref.shape, F32)
        dv_ref[...] = jnp.zeros(dv_ref.shape, F32)

    fetch(span_ref, payload_refs, both_ref)
    payload = both_ref[...]
    tail = payload[:, model_width:]
    grads = dot_nt(payload[:, :model_width], wout_ref[...]).astype(BF)
    grads = pad_columns(grads, select_ref, windows).astype(F32)
    grads = (grads + dot_nn(tail, place_ref[1])).astype(BF)
    shifts = dot_nn(tail, place_ref[0])
    for k, spot in enumerate(spots_of(span_ref, rows)):
        own_part = slice(k * rows, (k + 1) * rows)
        dob_ref[spot, :] = grads[own_part]
        qb_ref[spot, :] = (q_ref[0, spot, :].astype(F32) + shifts[own_part]).astype(BF)
    spread_mask(mask_ref, mask_of(own_ref[...], other_ref[...], True))

    def chunk_step(at, count):
        lines = pl.ds(pl.multiple_of(at * GROUP, HEAD_ROWS * GROUP), count * GROUP)
        mask = mask_ref[pl.ds(at, count)]
        for g in range(groups):
            query_block = qb_ref[:, g * SPAN : (g + 1) * SPAN]
            grad_block = dob_ref[:, g * SPAN : (g + 1) * SPAN]
            dots = dot_nt(kexp_ref[g, lines, :], query_block)
            grads = dot_nt(vexp_ref[g, lines, :], grad_block)
            bias = bias_ref[0, pl.ds(at, count), g * GROUP : (g + 1) * GROUP, :] + mask
            probs = jnp.exp2(dots * scale2 + bias.reshape(dots.shape))
            grad_scores = (probs * grads).astype(BF)
            dk_ref[g, lines, :] += dot_nn(grad_scores, query_block)
            dv_ref[g, lines, :] += dot_nn(probs.astype(BF), grad_block)

    head_steps(span_ref, rows, chunk_step)

    @pl.when(step == span_ref[SPAN_LAST, 0] - span_ref[SPAN_FIRST, 0])
    def _():
        def finish(i, carry):
            at = pl.multiple_of(i * CHUNK, CHUNK)
            lines = pl.ds(pl.multiple_of(i * CHUNK * GROUP, CHUNK * GROUP), CHUNK * GROUP)
            for part, (ref, scale) in enumerate(((dk_ref, head_scale), (dv_ref, 1.0))):
                for g in range(groups):
                    value = collapse(ref[g, lines, :]) * scale
                    low_ref[part, pl.ds(at, CHUNK), g * SPAN : (g + 1) * SPAN] = value.astype(BF)
            return carry

        lax.fori_loop(0, rows // CHUNK, finish, 0)
        for part in range(2):
            dkv_ref[part * model_width : (part + 1) * model_width, :] = drop_turned(
                low_ref[part], select_ref, windows
            )


def fixed(shape):
    return pl.BlockSpec(shape, lambda j, span: (0,) * len(shape), pipeline_mode=pl.Buffered(1))


def pair_at(j, span):
    return jnp.minimum(span[SPAN_FIRST, 0] + j, span[SPAN_LAST, 0])


def moving(shape, rank_at=0, last=0):
    def index(j, span):
        at = [0] * len(shape)
        at[rank_at] = pair_at(j, span)
        if last:
            at[-1] = last
        return tuple(at)

    return pl.BlockSpec(shape, index)


def while_inside(kernel, extra):
    def body(span_ref, *refs):
        @pl.when(pl.program_id(0) <= span_ref[SPAN_LAST, 0] - span_ref[SPAN_FIRST, 0])
        def _():
            kernel(span_ref, *refs[extra:])

    return body


def call(kernel, steps, in_specs, out_specs, out_shapes, scratch, flops, name, after=()):
    inner = pl.pallas_call(
        while_inside(kernel, len(after)),
        grid_spec=pltpu.PrefetchScalarGridSpec(
            num_scalar_prefetch=1,
            grid=(steps,),
            in_specs=[pl.BlockSpec(memory_space=pl.ANY)] * len(after) + in_specs,
            out_specs=out_specs,
            scratch_shapes=scratch,
        ),
        out_shape=out_shapes,
        compiler_params=pltpu.CompilerParams(
            dimension_semantics=("arbitrary",), vmem_limit_bytes=56 * 1024 * 1024
        ),
        cost_estimate=pl.CostEstimate(flops=flops, bytes_accessed=20_000_000, transcendentals=0),
        name=name,
    )
    return lambda span, *operands: inner(span, *after, *operands)


def shape_of(shape, dtype=F32):
    return jax.ShapeDtypeStruct(shape, dtype)


def once(
    kernel, operands, out_shapes, scratch, flops, name, spaces=(), after=(), carry=(), room=56
):
    spaces = dict(spaces)
    shapes = [*out_shapes, *(shape_of(x.shape, x.dtype) for x in carry)]
    count, extra = len(operands), len(after) + len(carry)
    anywhere = pl.BlockSpec(memory_space=pl.ANY)

    def whole(shape):
        return pl.BlockSpec(shape, lambda j: (0,) * len(shape), pipeline_mode=pl.Buffered(1))

    def body(*refs):
        outs = refs[count + extra : count + extra + len(out_shapes)]
        kernel(*refs[:count], *outs, *refs[count + extra + len(shapes) :])

    results = pl.pallas_call(
        body,
        grid=(1,),
        in_specs=[
            pl.BlockSpec(memory_space=spaces[k]) if k in spaces else whole(x.shape)
            for k, x in enumerate(operands)
        ]
        + [anywhere] * extra,
        out_specs=[whole(x.shape) for x in out_shapes] + [anywhere] * len(carry),
        out_shape=shapes,
        scratch_shapes=scratch,
        input_output_aliases={
            count + len(after) + k: len(out_shapes) + k for k in range(len(carry))
        },
        compiler_params=pltpu.CompilerParams(vmem_limit_bytes=room * 1024 * 1024),
        cost_estimate=pl.CostEstimate(flops=flops, bytes_accessed=5_000_000, transcendentals=0),
        name=name,
    )(*operands, *after, *carry)
    return results


def on_device(
    tokens,
    positions,
    item_of_atom,
    item_lengths,
    atom_types,
    key_mask,
    ln1_gain,
    ln1_bias,
    w_qkv,
    kernel_means,
    kernel_widths,
    kernel_weight,
    type_scale,
    type_shift,
    w_out,
    ln2_gain,
    ln2_bias,
    w_up,
    w_down,
    out_cotangent,
):
    own_rows, model_width = tokens.shape
    assert own_rows == LANES
    kernels, heads = kernel_weight.shape
    head_size = model_width // heads
    head_scale = head_size ** (-0.5)
    scale2 = head_scale * LOG2E
    groups = heads // GROUP
    width = groups * SPAN
    ff_width = w_up.shape[1]
    ka_count = lax.axis_size("ka")
    flat = lax.axis_index("pb") * ka_count + lax.axis_index("ka")
    flat_array = flat.astype(jnp.int32).reshape(1)
    reach = (PROT_LEN + own_rows - 2) // own_rows
    chips = (reach + 1) // 2
    pairs = 2 * chips + 1
    assert pairs == len(SLOTS[0])
    keys = 2 * own_rows
    atoms = positions.shape[1]
    atoms_blocks = atoms // LANES
    types = type_scale.shape[0]
    order = tuple(range(bits_of("ka") - 1))

    window = Window(tokens)
    cotangent_came = core_flip(out_cotangent)
    ln1 = jnp.stack([ln1_gain, ln1_bias])
    ln2 = jnp.stack([ln2_gain, ln2_bias])
    (normed_own,) = once(
        normal_kernel,
        (tokens, ln1),
        [shape_of(tokens.shape, BF)],
        [],
        1_000_000,
        "first_normal",
        room=16,
    )
    normed_all = lax.all_gather(normed_own, "ka", axis=0, tiled=True)

    select = select_table(head_size)
    place = place_table(heads, head_size)
    into_tail, out_of_tail = tail_tables(heads, head_size)
    type_tiles = -(-types // LANES)
    tables = jnp.pad(
        jnp.stack([type_scale, type_shift]), ((0, 0), (0, type_tiles * LANES - types))
    )
    tables = tables.reshape(2, type_tiles, LANES).swapaxes(0, 1).reshape(2 * type_tiles, LANES)
    lengths = jnp.pad(item_lengths, (0, -item_lengths.shape[0] % LANES)).reshape(-1, LANES)
    span, other, own, own_line, tabs, grad_weights, weights_turned, par = once(
        functools.partial(side_kernel, atoms_blocks),
        (
            flat_array,
            positions,
            item_of_atom.reshape(-1, LANES),
            key_mask.reshape(-1, LANES),
            atom_types.reshape(-1, LANES),
            lengths,
            tables,
            kernel_means.reshape(1, LANES),
            kernel_widths.reshape(1, LANES),
            kernel_weight,
        ),
        [
            shape_of((SPAN_ROWS, LANES), jnp.int32),
            shape_of((SIDE, pairs * keys)),
            shape_of((own_rows, LANES)),
            shape_of((SIDE, LANES)),
            shape_of((4, kernels, LANES)),
            shape_of((kernels, WEIGHT_PIECES * heads), BF),
            shape_of((heads, kernels), BF),
            shape_of((LANES, LANES)),
        ],
        [],
        1_000_000_000,
        "sides",
        {0: pltpu.SMEM},
    )

    own_spec = fixed((own_rows, LANES))
    other_spec = moving((SIDE, keys), 1)
    bias_spec = moving((1, own_rows, heads, keys))
    bias = call(
        bias_kernel,
        pairs,
        [own_spec, other_spec, fixed((4, kernels, LANES)), fixed((heads, kernels))],
        bias_spec,
        shape_of((pairs, own_rows, heads, keys)),
        [pltpu.VMEM((own_rows, keys), F32)],
        30_000_000_000,
        "pair_bias",
        after=(window.one, window.two, normed_own),
    )(span, own, other, tabs, weights_turned)
    window.middle()
    token_blocks = window.finish()

    expanded = pltpu.VMEM((groups, own_rows * GROUP, SPAN), BF)
    summed = pltpu.VMEM((groups, own_rows * GROUP, SPAN), F32)
    mask_scratch = pltpu.VMEM((own_rows, GROUP, keys), F32)
    line_scratch = pltpu.VMEM((groups, own_rows * GROUP, LANES), F32)
    attended, q_aug, lse_pieces, kvq = call(
        functools.partial(forward_kernel, scale2, groups),
        pairs,
        [own_spec, other_spec]
        + [fixed((own_rows, model_width))] * 14
        + [
            fixed((2, model_width)),
            fixed((model_width, 3 * model_width)),
            fixed(select.shape),
            fixed((1, width)),
            fixed(place.shape),
            bias_spec,
        ],
        [
            fixed((own_rows, width)),
            fixed((own_rows, width)),
            fixed((PIECES, own_rows, LANES)),
            moving((1, keys, 3 * width)),
        ],
        [
            shape_of((own_rows, width)),
            shape_of((own_rows, width), BF),
            shape_of((PIECES, own_rows, LANES), BF),
            shape_of((pairs, keys, 3 * width), BF),
        ],
        [
            expanded,
            mask_scratch,
            line_scratch,
            line_scratch,
            summed,
            pltpu.VMEM((own_rows, LANES), F32),
            pltpu.VMEM((keys, model_width), BF),
        ],
        25_000_000_000,
        "attention_forward",
    )(
        span,
        own,
        other,
        *token_blocks,
        ln1,
        w_qkv,
        select,
        ones_row(heads, head_size),
        place,
        bias,
    )

    tile = 3 * LANES
    assert ff_width % tile == 0 and tile % (2 * ff_width // ka_count) == 0
    row_shape = shape_of((own_rows, model_width), BF)
    slices = ka_count // 2
    up_rows, out_rows = ff_width // ka_count, model_width // ka_count
    pieces = shape_of((2, slices, own_rows, up_rows), BF)
    block_out, grad_mixed, do_aug, payload, attended_low, normed_second, *parts, ln2_grads = once(
        functools.partial(middle_kernel, groups, tile),
        (
            flat_array,
            tokens,
            attended,
            lse_pieces,
            ln2,
            out_cotangent,
            w_out,
            w_up,
            w_down,
            select,
            place,
            head_sum_table(heads),
            into_tail,
        ),
        [
            row_shape,
            shape_of((own_rows, model_width)),
            shape_of((own_rows, width), BF),
            shape_of((own_rows, model_width + 2 * LANES), BF),
            row_shape,
            row_shape,
            pieces,
            pieces,
            shape_of((2, model_width)),
        ],
        [
            pltpu.VMEM((model_width, model_width), BF),
            pltpu.VMEM((model_width, ff_width), BF),
            pltpu.VMEM((ff_width, model_width), BF),
            pltpu.VMEM((own_rows, model_width), F32),
            pltpu.VMEM((own_rows, model_width), F32),
            pltpu.SemaphoreType.DMA,
            pltpu.SemaphoreType.DMA((2, ff_width // tile)),
        ],
        10_000_000_000,
        "feed_forward",
        {0: pltpu.SMEM, 6: pl.ANY, 7: pl.ANY, 8: pl.ANY},
    )
    came = [core_flip(x) for x in (parts[1], normed_second, attended_low, payload)]
    window = Window(payload, came[3])
    half = model_width // 2
    up_kept, up_sent, rest_kept, rest_sent = once(
        functools.partial(weight_grads_kernel, ka_count),
        (
            flat_array,
            parts[0],
            came[0],
            normed_second,
            came[1],
            out_cotangent,
            cotangent_came,
            attended_low,
            came[2],
            payload,
            came[3],
        ),
        [shape_of((slices // 2, up_rows, model_width), BF)] * 2
        + [shape_of((slices, up_rows + out_rows, half), BF)] * 2,
        [pltpu.VMEM((model_width, model_width), F32)],
        5_000_000_000,
        "weight_gradients",
        {0: pltpu.SMEM},
    )
    up_sum, rest_sum = slices_sum(up_kept, up_sent, order), columns_sum(rest_kept, rest_sent, order)

    dq, grad_scores = call(
        functools.partial(query_grad_kernel, scale2, head_scale, groups),
        pairs,
        [
            own_spec,
            other_spec,
            fixed((own_rows, width)),
            fixed((own_rows, width)),
            moving((1, keys, 2 * width)),
            bias_spec,
            fixed(select.shape),
        ],
        [fixed((model_width, own_rows)), moving((1, own_rows, heads, keys))],
        [
            shape_of((model_width, own_rows), BF),
            shape_of((pairs, own_rows, heads, keys), BF),
        ],
        [expanded, expanded, mask_scratch, summed, pltpu.VMEM((own_rows, width), BF)],
        22_000_000_000,
        "query_gradients",
        after=(up_sum.sent, rest_sum.sent, window.one, window.two, window.far, normed_all),
    )(span, own, other, q_aug, do_aug, kvq, bias, select)

    pos_blocks = atoms_blocks + 4 * chips
    half_rows = own_rows // 2

    def kernel_gradients(part, after):
        return call(
            functools.partial(phi_grad_kernel, part * half_rows),
            pairs,
            [
                own_spec,
                other_spec,
                fixed((SIDE, LANES)),
                pl.BlockSpec(
                    (1, half_rows, heads, keys), lambda j, span: (pair_at(j, span), part, 0, 0)
                ),
                fixed((4, kernels, LANES)),
                fixed((kernels, WEIGHT_PIECES * heads)),
                fixed((LANES, LANES)),
            ],
            [fixed((LANES, LANES)), fixed((3 * pos_blocks, LANES))],
            [shape_of((LANES, LANES)), shape_of((3 * pos_blocks, LANES))],
            [
                pltpu.VMEM((half_rows, keys), F32),
                pltpu.VMEM((half_rows, keys), F32),
                pltpu.VMEM((5, half_rows, LANES), F32),
                pltpu.VMEM((kernels, heads), F32),
                pltpu.VMEM((2, kernels, LANES), F32),
                pltpu.VMEM((2, 2 * LANES, LANES), F32),
            ],
            20_000_000_000,
            "kernel_gradients",
            after=after,
        )(span, own, other, own_line, grad_scores, tabs, grad_weights, par)

    small_first, pos_first = kernel_gradients(0, ())
    advance([up_sum, rest_sum], flat_array, "sums_first", (small_first,))
    small_second, pos_second = kernel_gradients(
        1, (up_sum.sent, rest_sum.sent, *window.middle())
    )
    payload_blocks = window.finish()
    early_sum = everywhere_sum(
        jnp.concatenate(
            [
                small_first + small_second,
                ln2_grads.reshape(-1, LANES),
                pos_first + pos_second,
            ],
            axis=0,
        )
    )
    advance([up_sum, rest_sum, early_sum], flat_array, "sums_second", (small_second,))

    dkv = call(
        functools.partial(key_grad_kernel, scale2, head_scale, groups, model_width),
        pairs,
        [
            own_spec,
            other_spec,
            pl.BlockSpec(
                (1, own_rows, 2 * width),
                lambda j, span: (chips, span[SPAN_CORE, 0], 0),
                pipeline_mode=pl.Buffered(1),
            ),
            moving((1, keys, width), 0, 2),
        ]
        + [fixed((own_rows, model_width + 2 * LANES))] * 14
        + [
            fixed((model_width, model_width)),
            fixed(select.shape),
            fixed(out_of_tail.shape),
            bias_spec,
        ],
        fixed((2 * model_width, own_rows)),
        shape_of((2 * model_width, own_rows), BF),
        [
            expanded,
            expanded,
            mask_scratch,
            pltpu.VMEM((keys, width), BF),
            pltpu.VMEM((keys, width), BF),
            summed,
            summed,
            pltpu.VMEM((keys, model_width + 2 * LANES), BF),
            pltpu.VMEM((2, own_rows, width), BF),
        ],
        28_000_000_000,
        "key_gradients",
        after=(up_sum.sent, rest_sum.sent, early_sum.sent),
    )(span, own, other, kvq, kvq, *payload_blocks, w_out, select, out_of_tail, bias)

    advance([up_sum, rest_sum, early_sum], flat_array, "sums_third", (dkv,))
    qkv_rows = 3 * model_width // ka_count
    norm_count = model_width // LANES
    sent_rows = qkv_rows + -(-2 * norm_count // 16) * 16
    grad_tokens, projected_grads = once(
        first_norm_kernel,
        (tokens, ln1, dq, dkv, w_qkv, grad_mixed),
        [
            shape_of((own_rows, model_width)),
            shape_of((ka_count, sent_rows, own_rows), BF),
        ],
        [pltpu.VMEM((3 * model_width, own_rows), BF)],
        2_000_000_000,
        "first_norm",
        after=(early_sum.sent,),
        room=24,
    )
    grads_all = lax.all_to_all(projected_grads, "ka", split_axis=0, concat_axis=0, tiled=True)
    qkv_part, norm_part = once(
        qkv_grads_kernel,
        (grads_all, normed_all),
        [shape_of((qkv_rows, model_width), BF), shape_of((sent_rows - qkv_rows, LANES))],
        [],
        3_000_000_000,
        "qkv_gradients",
        room=24,
    )
    over_pb = [("pb", bit) for bit in range(bits_of("pb"))]
    qkv_sum, norm_sum = Sum(qkv_part, qkv_part, over_pb), Sum(norm_part, norm_part, over_pb)
    advance([up_sum, rest_sum, early_sum], flat_array, "sums_fourth", (grads_all,))
    sums = [qkv_sum, norm_sum, up_sum, rest_sum, early_sum]
    while any(one.stages for one in sums):
        advance(sums, flat_array, "sums_last")
    joined = early_sum.total
    up_total, rest_total = up_sum.total, rest_sum.total
    norms, by_weight, by_mean, by_width, by_scale, by_shift, grad_positions = once(
        functools.partial(results_kernel, heads, types),
        (flat_array, joined, norm_sum.total),
        [
            shape_of((4, norm_count, LANES)),
            shape_of((kernels, heads)),
            shape_of((1, kernels)),
            shape_of((1, kernels)),
            shape_of((1, types)),
            shape_of((1, types)),
            shape_of((3, LANES)),
        ],
        [],
        1_000_000,
        "results",
        {0: pltpu.SMEM},
        room=16,
    )
    qkv_total = qkv_sum.total
    return (
        block_out,
        grad_tokens,
        grad_positions,
        norms[0].reshape(-1),
        norms[1].reshape(-1),
        qkv_total.T,
        by_mean.reshape(-1),
        by_width.reshape(-1),
        by_weight,
        by_scale.reshape(-1),
        by_shift.reshape(-1),
        rest_total[up_rows:].T,
        norms[2].reshape(-1),
        norms[3].reshape(-1),
        up_total.T,
        rest_total[:up_rows],
    )


def solution(mesh):
    rows = P(MESH, None)
    in_specs = (rows,) + (P(),) * 18 + (rows,)
    out_specs = (
        rows,
        rows,
        P(None, MESH),
        P(),
        P(),
        P(None, "ka"),
        P(),
        P(),
        P(),
        P(),
        P(),
        P(None, "ka"),
        P(),
        P(),
        P(None, "ka"),
        P("ka", None),
    )
    return jax.shard_map(
        on_device, mesh=mesh, in_specs=in_specs, out_specs=out_specs, check_vma=False
    )
```

```python
import functools
import math

import jax
import jax.numpy as jnp
import numpy as np
from jax import lax
from jax.experimental import pallas as pl
from jax.experimental.pallas import tpu as pltpu
from jax.sharding import PartitionSpec as P

MOL_TYPES = 128
PROT_LEN = 768
MOL_MEAN = 32

LN_EPS = 1e-05
GELU_SLOPE = math.sqrt(2.0 / math.pi)
GELU_CUBE = 0.044715
MASKED = -1e30
ROOT_TWO_PI = math.sqrt(2.0 * math.pi)
LOG2E = math.log2(math.e)
KAPPA = math.sqrt(0.5 * LOG2E)

PAD = 32
GROUP = 8
SPAN = PAD * GROUP
PIECES = 3
WEIGHT_PIECES = 2
CHUNK = 32
HEAD_ROWS = 32
BIAS_ROWS = 64
FEW = 8
MESH = ("pb", "ka")

BF = jnp.bfloat16
F32 = jnp.float32


def shifted(block, axis, distance):
    devices = range(lax.axis_size(axis))
    route = [(i - distance, i) for i in devices if i - distance in devices]
    return lax.ppermute(block, axis, route)


def core_flip(block):
    devices = range(lax.axis_size(MESH))
    return lax.ppermute(block, MESH, [(i, i ^ 1) for i in devices])


class Window:
    def __init__(self, block, sibling=None):
        devices = range(lax.axis_size(MESH))
        levels = len(devices) // 4

        def of(level, rest):
            return level % levels * 4 + rest

        one, two, far = [], [], []
        for i in devices:
            level, chip, core = i // 4, (i >> 1) & 1, i & 1
            odd = level & 1
            one.append((i, of(level + (-1 if odd else 1), i % 4)))
            two.append((i, of(level + (1 if odd else -1), i % 4)))
            far.append((i, of(level + (2 if chip else -2), (1 - chip) * 2 + core)))
        self.block, self.sibling = block, sibling
        self.one = lax.ppermute(block, MESH, one)
        self.two = lax.ppermute(block, MESH, two)
        self.far = lax.ppermute(block, MESH, far)

    def middle(self):
        self.other_chip = [flip_bit(x, "ka", 1) for x in (self.block, self.one, self.two)]
        return self.other_chip

    def finish(self):
        beside, one, two = self.other_chip
        mine = [self.far, self.one, one, self.block, beside, self.two, two]
        came = [core_flip(x) for x in mine if x is not self.block]
        own = core_flip(self.block) if self.sibling is None else self.sibling
        return mine + came[:3] + [own] + came[3:]


class Gathered:
    def __init__(self, block):
        self.own, self.own_sibling = block, core_flip(block)
        self.beside = flip_bit(block, "ka", 1)

    def far(self):
        mine = jnp.stack([self.own, self.beside])
        self.groups = [
            flip_mask(mine, "ka", mask) for mask in range(4, lax.axis_size("ka"), 4)
        ]
        return self.groups

    def finish(self):
        self.beside_sibling = core_flip(self.beside)
        self.siblings = [core_flip(x) for x in self.groups]

    def arrays(self):
        return [
            *(x[None] for x in (self.own, self.own_sibling, self.beside, self.beside_sibling)),
            *self.groups,
            *self.siblings,
        ]

    def masks(self):
        far = range(4, lax.axis_size("ka"), 4)
        return [
            (0,), (1,), (2,), (3,),
            *((mask, mask + 2) for mask in far),
            *((mask + 1, mask + 3) for mask in far),
        ]


SLOTS = (
    (0, 5, 6, 3, 4, 1, 2),
    (6, 5, 4, 3, 2, 1, 0),
    (0, 1, 2, 3, 4, 5, 6),
    (2, 1, 4, 3, 6, 5, 0),
)
SPAN_FIRST, SPAN_LAST, SPAN_CORE, SPAN_CHIP, SPAN_SLOT = 0, 1, 2, 3, 4
SPAN_LOW = 16
SPAN_HIGH = 32
SPAN_ROWS = 48
LANES = 128
SIDE = 16


def flip_bit(block, axis, bit):
    devices = range(lax.axis_size(axis))
    return lax.ppermute(block, axis, [(i, i ^ (1 << bit)) for i in devices])


def bits_of(axis):
    return (lax.axis_size(axis) - 1).bit_length()


def flip_mask(block, axis, mask):
    devices = range(lax.axis_size(axis))
    return lax.ppermute(block, axis, [(i, i ^ mask) for i in devices])


class Sum:
    def __init__(self, kept, sent, stages, left=()):
        self.kept, self.sent, self.stages, self.left = kept, list(sent), list(stages), list(left)
        self.total = None

    def came(self):
        axis, bit, count = self.stages[0][:3]
        partners = range(1, 2**count)
        return [flip_mask(x, axis, p << bit) for x, p in zip(self.sent, partners, strict=True)]

    def plan(self):
        stage = self.stages.pop(0)
        if len(stage) == 4:
            return ("join",)
        if self.stages and self.stages[0][0] == "ka" and self.left:
            bit, count = self.stages[0][1] - 1, self.stages[0][2]
            self.left = [b for b in self.left if not bit <= b < bit + count]
            below = sum(1 for b in self.left if b < bit)
            return ("part", bit, count, 2 ** (len(self.left) - below), 2**below)
        return ("whole",)


def over(axis, first=0):
    return [(axis, bit, 1) for bit in range(first, bits_of(axis))]


def slices_sum(kept, sent, order):
    stages = [("ka", bit + 1, count) for bit, count in order] + over("pb")
    left = [b for bit, count in order[1:] for b in range(bit, bit + count)]
    return Sum(kept, [sent], stages, left)


def columns_sum(kept, sent, order):
    stages = [("pb", 0, 1)] + [("ka", bit + 1, count) for bit, count in order]
    left = [b for bit, count in order for b in range(bit, bit + count)]
    return Sum(kept, [sent], stages + over("pb", 1) + [("pb", 0, 1, "join")], left)


def everywhere_sum(values):
    return Sum(values, [values], over("ka") + over("pb"))


def stage_kernel(plans, counts, side_bit, flat_ref, *refs):
    flat = flat_ref[0]
    refs = list(refs)
    kept_refs = [refs.pop(0) for _ in plans]
    came_refs = [[refs.pop(0) for _ in range(count)] for count in counts]
    for plan, kept, came in zip(plans, kept_refs, came_refs):

        def total(*at):
            value = kept[at].astype(F32)
            for ref in came:
                value = value + ref[at].astype(F32)
            return value

        out = refs.pop(0)
        if plan[0] == "whole":
            out[...] = total(Ellipsis).astype(out.dtype)
        elif plan[0] == "join":
            half = kept.shape[-1]
            side = jnp.right_shift(flat, side_bit) & 1
            out[:, pl.ds(pl.multiple_of(side * half, LANES), half)] = kept[...].astype(F32)
            out[:, pl.ds(pl.multiple_of((1 - side) * half, LANES), half)] = came[0][...].astype(F32)
        else:
            _, bit, count, above, below = plan
            mine = jnp.right_shift(flat, bit + 1) & (2**count - 1)
            outs = [out] + [refs.pop(0) for _ in range(2**count - 1)]
            for i in range(above):
                for j in range(below):
                    for other, ref in enumerate(outs):
                        group = jnp.bitwise_xor(mine, other)
                        ref[i * below + j] = total((i * 2**count + group) * below + j).astype(BF)


def advance(sums, flat_array, name, after=()):
    sums = [one for one in sums if one.stages]
    came = [one.came() for one in sums]
    plans, shapes, sizes = [], [], []
    for one in sums:
        plan = one.plan()
        shape, dtype, size = one.kept.shape, one.kept.dtype, 1
        if plan[0] == "join":
            shape, dtype = (shape[0], 2 * shape[1]), F32
        elif plan[0] == "part":
            shape, size = (plan[3] * plan[4], *shape[1:]), 2 ** plan[2]
        elif not one.stages:
            dtype = F32
        shapes += [shape_of(shape, dtype)] * size
        plans.append(plan)
        sizes.append(size)
    results = once(
        functools.partial(stage_kernel, plans, [len(x) for x in came], bits_of("ka")),
        (flat_array, *(one.kept for one in sums), *(x for group in came for x in group)),
        shapes,
        [],
        1_000_000_000,
        name,
        {0: pltpu.SMEM},
        after=after,
        room=24,
    )
    results = list(results)
    for one, size in zip(sums, sizes):
        one.kept = results.pop(0)
        one.sent = [results.pop(0) for _ in range(size - 1)] or [one.kept]
        if not one.stages:
            one.total = one.kept
        elif one.kept.ndim == 3 and one.kept.shape[0] == 1 and one.stages[0][0] == "pb":
            one.kept = one.kept.reshape(one.kept.shape[1:])
            one.sent = [one.kept]


def layer_norm(values, ln_gain, ln_shift):
    centre = jnp.mean(values, axis=-1, keepdims=True)
    offsets = values - centre
    spread = jnp.mean(offsets * offsets, axis=-1, keepdims=True)
    return offsets * lax.rsqrt(spread + LN_EPS) * ln_gain + ln_shift


def dot_nn(left, right):
    return lax.dot_general(left, right, (((1,), (0,)), ((), ())), preferred_element_type=F32)


def dot_nt(left, right):
    return lax.dot_general(left, right, (((1,), (1,)), ((), ())), preferred_element_type=F32)


def dot_tn(left, right):
    return lax.dot_general(left, right, (((0,), (0,)), ((), ())), preferred_element_type=F32)


def select_table(head_size):
    column = np.arange(SPAN)
    source = (column // PAD) * head_size + column % PAD
    table = [
        (column[:, None] == (source + off)[None, :]) & (column % PAD < head_size)[None, :]
        for off in (0, 64)
    ]
    return np.stack(table).astype(BF)


def group_windows(groups, head_size):
    out = []
    for g in range(groups):
        start = g * GROUP * head_size
        out.append((start // LANES * LANES, (start % LANES) // 64))
    return out


def place_table(heads, head_size):
    column = np.arange(heads * PAD)
    lane = np.arange(LANES)
    return np.stack(
        [
            (lane[:, None] == (column // PAD)[None, :])
            & (column % PAD == head_size + p)[None, :]
            for p in range(PIECES)
        ]
    ).astype(BF)


def tail_tables(heads, head_size):
    lane, tail = np.arange(LANES), np.arange(2 * LANES)
    into = np.stack(
        [
            (lane[:, None] + p * heads == tail[None, :]) & (lane < heads)[:, None]
            for p in range(2 * PIECES)
        ]
    )
    column = np.arange(heads * PAD)
    piece = column % PAD - head_size
    free = (piece >= 0) & (piece < PIECES)
    lane_of = np.where(free, piece * heads + column // PAD, -1)
    out = np.stack(
        [
            (tail[:, None] == lane_of[None, :]) & free[None, :],
            (tail[:, None] - PIECES * heads == lane_of[None, :]) & free[None, :],
        ]
    )
    return into.astype(BF), out.astype(BF)


def ones_row(heads, head_size):
    column = np.arange(heads * PAD) % PAD
    return ((column >= head_size) & (column < head_size + PIECES)).astype(np.float32)[None]


def head_sum_table(heads):
    column = np.arange(heads * PAD)
    return (column[:, None] // PAD == np.arange(LANES)[None, :]).astype(BF)


def pad_columns(values, select_ref, windows):
    parts = [
        dot_nn(values[:, start : start + SPAN], select_ref[kind]).astype(BF)
        for start, kind in windows
    ]
    return jnp.concatenate(parts, axis=1)


def drop_columns(values, select_ref, windows):
    tiles = {}
    for g, (start, kind) in enumerate(windows):
        part = dot_nt(values[:, g * SPAN : (g + 1) * SPAN], select_ref[kind])
        for k in range(SPAN // LANES):
            tile = part[:, k * LANES : (k + 1) * LANES]
            at = start // LANES + k
            tiles[at] = tiles[at] + tile if at in tiles else tile
    return jnp.concatenate([tiles[at] for at in sorted(tiles)], axis=1).astype(BF)


def drop_turned(values, select_ref, windows):
    tiles = {}
    for g, (start, kind) in enumerate(windows):
        part = dot_nt(select_ref[kind], values[:, g * SPAN : (g + 1) * SPAN])
        for k in range(SPAN // LANES):
            tile = part[k * LANES : (k + 1) * LANES]
            at = start // LANES + k
            tiles[at] = tiles[at] + tile if at in tiles else tile
    return jnp.concatenate([tiles[at] for at in sorted(tiles)], axis=0).astype(BF)


def row_of(ref):
    return jnp.concatenate([ref[k : k + 1, :] for k in range(ref.shape[0])], axis=1)


def split(values, count):
    rest, out = values, []
    for _ in range(count):
        piece = rest.astype(BF)
        rest = rest - piece.astype(F32)
        out.append(piece)
    return out


def norm_parts(values):
    centre = jnp.mean(values, axis=-1, keepdims=True)
    offsets = values - centre
    spread = jnp.mean(offsets * offsets, axis=-1, keepdims=True)
    slope = lax.rsqrt(spread + LN_EPS)
    return offsets * slope, slope


def norm_back(grad, normal, slope, gain):
    inner = grad * gain
    mean = jnp.mean(inner, axis=-1, keepdims=True)
    tilt = jnp.mean(inner * normal, axis=-1, keepdims=True)
    by_gain = jnp.sum(grad * normal, axis=0, keepdims=True)
    by_shift = jnp.sum(grad, axis=0, keepdims=True)
    return slope * (inner - mean - normal * tilt), by_gain, by_shift


def stretched_of(own, other):
    delta = [own[:, i : i + 1] - other[i : i + 1, :] for i in range(3)]
    square = delta[0] * delta[0] + delta[1] * delta[1] + delta[2] * delta[2]
    dist = jnp.sqrt(square + 1.0)
    scales = own[:, 3:4] * other[3:4, :]
    stretched = scales * dist + own[:, 4:5] + other[4:5, :]
    return delta, dist, scales, stretched


def mask_of(own, other, key_is_own):
    same = own[:, 5:6] == other[5:6, :]
    itself = own[:, 7:8] == other[7:8, :]
    is_open = (own[:, 6:7] > 0.5) if key_is_own else (other[6:7, :] > 0.5)
    return jnp.where(same & (is_open | itself), 0.0, MASKED)


def line_atoms(lines):
    line = lax.broadcasted_iota(jnp.int32, (lines, lines // GROUP), 0)
    atom = lax.broadcasted_iota(jnp.int32, (lines, lines // GROUP), 1)
    return jnp.where(line // GROUP == atom, 1.0, 0.0).astype(BF)


def line_heads(lines):
    line = lax.broadcasted_iota(jnp.int32, (lines, SPAN), 0)
    column = lax.broadcasted_iota(jnp.int32, (lines, SPAN), 1)
    return jnp.where(column // PAD == line % GROUP, 1.0, 0.0)


def expand_into(out_ref, padded, groups):
    lines = CHUNK * GROUP
    keep = line_heads(lines).astype(BF)
    spread = line_atoms(lines)
    for g in range(groups):
        for i in range(padded.shape[0] // CHUNK):
            part = padded[i * CHUNK : (i + 1) * CHUNK, g * SPAN : (g + 1) * SPAN]
            out_ref[g, i * lines : (i + 1) * lines, :] = dot_nn(spread, part).astype(BF) * keep


def collapse(values):
    lines = values.shape[0]
    kept = values * line_heads(lines)
    high = kept.astype(BF)
    low = (kept - high.astype(F32)).astype(BF)
    line = lax.broadcasted_iota(jnp.int32, (lines // GROUP, lines), 1)
    atom = lax.broadcasted_iota(jnp.int32, (lines // GROUP, lines), 0)
    gather = jnp.where(line // GROUP == atom, 1.0, 0.0).astype(BF)
    return dot_nn(gather, high) + dot_nn(gather, low)


def fetch(span_ref, refs, out_ref):
    slot = span_ref[SPAN_SLOT + span_ref[SPAN_FIRST, 0] + pl.program_id(0), 0]
    count = len(refs) // 2
    rows = refs[0].shape[0]
    for k in range(count):

        @pl.when(slot == k)
        def _():
            out_ref[:rows] = refs[k][...]
            out_ref[rows:] = refs[count + k][...]


def spots_of(span_ref, rows):
    core = span_ref[SPAN_CORE, 0]
    return [pl.ds(pl.multiple_of(at * rows, rows), rows) for at in (core, 1 - core)]


def spread_mask(mask_ref, mask):
    mask_ref[...] = jnp.broadcast_to(mask[:, None, :], mask_ref.shape)


def reaches(span_ref, first, last, low, high):
    return (span_ref[SPAN_LOW + first, 0] <= high) & (span_ref[SPAN_HIGH + last, 0] >= low)


def head_steps(span_ref, rows, step):
    pair = span_ref[SPAN_FIRST, 0] + pl.program_id(0)
    few = HEAD_ROWS // FEW
    last = rows // FEW - 1
    whole = reaches(span_ref, last, 0, 2 * pair, 2 * pair + 1)

    @pl.when(whole)
    def _():
        step(0, rows)

    @pl.when(jnp.logical_not(whole))
    def _():
        def one(i, carry):
            @pl.when(reaches(span_ref, i * few, i * few + few - 1, 2 * pair, 2 * pair + 1))
            def _():
                step(pl.multiple_of(i * HEAD_ROWS, HEAD_ROWS), HEAD_ROWS)

            return carry

        lax.fori_loop(0, rows // HEAD_ROWS, one, 0)


def kernel_steps(span_ref, first, rows, size, step, skipped):
    pair = span_ref[SPAN_FIRST, 0] + pl.program_id(0)
    few = size // FEW

    def one(i, carry):
        at = pl.multiple_of(i * size, size)
        chunk = first // FEW + i * few
        for half in range(2):
            block = 2 * pair + half
            needed = reaches(span_ref, chunk, chunk + few - 1, block, block)

            @pl.when(needed)
            def _():
                step(at, half)

            @pl.when(jnp.logical_not(needed))
            def _():
                skipped(at, half)

        return carry

    lax.fori_loop(0, rows // size, one, 0)


def side_kernel(
    atoms_blocks,
    flat_ref,
    pos_ref,
    item_ref,
    open_ref,
    type_ref,
    length_ref,
    table_ref,
    means_ref,
    widths_ref,
    kw_ref,
    span_ref,
    other_ref,
    own_ref,
    line_ref,
    tab_ref,
    gw_ref,
    kwt_ref,
    par_ref,
):
    flat = flat_ref[0]
    chips = len(SLOTS[0]) // 2
    first_block = flat // 2 * 2 - 2 * chips
    ids = lax.broadcasted_iota(jnp.int32, (LANES, LANES), 0).astype(F32)
    lane = lax.broadcasted_iota(jnp.int32, (1, LANES), 1)
    tables = []
    for k in range(table_ref.shape[0] // 2):
        rows = split(table_ref[2 * k : 2 * k + 1, :], PIECES)
        rows += split(table_ref[2 * k + 1 : 2 * k + 2, :], PIECES)
        rows += [jnp.zeros((2, LANES), BF)]
        tables.append(jnp.concatenate([row.astype(F32) for row in rows], axis=0).astype(BF))
    flags = [
        jnp.broadcast_to(
            jnp.where(length_ref[k : k + 1, :] > 2 * MOL_MEAN, float(MOL_TYPES), 0.0), (8, LANES)
        ).astype(BF)
        for k in range(length_ref.shape[0])
    ]
    for b in range(other_ref.shape[1] // LANES):
        block = first_block + b
        inside = (block >= 0) & (block < atoms_blocks)
        source = jnp.clip(block, 0, atoms_blocks - 1)
        at = pl.ds(pl.multiple_of(source * LANES, LANES), LANES)
        item = jnp.where(inside, item_ref[pl.ds(source, 1), :].astype(F32), -1.0)
        kind = type_ref[pl.ds(source, 1), :].astype(F32)
        for k, flag in enumerate(flags):
            onehot = jnp.where(ids + float(k * LANES) == item, 1.0, 0.0).astype(BF)
            kind = kind + dot_nn(flag, onehot)[0:1, :]
        found = jnp.zeros((8, LANES), F32)
        for k, table in enumerate(tables):
            onehot = jnp.where(ids + float(k * LANES) == kind, 1.0, 0.0).astype(BF)
            found = found + dot_nn(table, onehot)
        rows = [pos_ref[k : k + 1, at] for k in range(3)]
        rows += [found[0:1] + found[1:2] + found[2:3], found[3:4] + found[4:5] + found[5:6]]
        rows += [item, open_ref[pl.ds(source, 1), :].astype(F32)]
        rows += [(block * LANES + lane).astype(F32), kind]
        rows += [jnp.zeros((SIDE - 9, LANES), F32)]
        side = jnp.concatenate(rows, axis=0)
        other_ref[:, b * LANES : (b + 1) * LANES] = side

        @pl.when(block == flat)
        def _():
            line_ref[...] = side

    line = line_ref[...]
    turned = jnp.transpose(
        jnp.concatenate([line, jnp.zeros((LANES - SIDE, LANES), F32)], axis=0)
    )
    own_ref[...] = turned
    chunks = LANES // FEW
    item_column = jnp.broadcast_to(own_ref[:, 5:6], (LANES, LANES))
    par_ref[...] = item_column
    first_item = par_ref[pl.ds(0, chunks, stride=FEW), :]
    last_item = par_ref[pl.ds(FEW - 1, chunks, stride=FEW), :]

    def count(k, carry):
        row = item_ref[pl.ds(k, 1), :].astype(F32)
        below, upto = carry
        return (
            below + jnp.where(row < first_item, 1.0, 0.0),
            upto + jnp.where(row <= last_item, 1.0, 0.0),
        )

    zero = jnp.zeros((chunks, LANES), F32)
    below, upto = lax.fori_loop(0, atoms_blocks, count, (zero, zero))
    below = jnp.sum(below, axis=1, keepdims=True).astype(jnp.int32)
    upto = jnp.sum(upto, axis=1, keepdims=True).astype(jnp.int32)
    low = jnp.right_shift(below - first_block * LANES, 7)
    high = jnp.right_shift(upto - 1 - first_block * LANES, 7)
    span_ref[SPAN_LOW : SPAN_LOW + chunks, :] = jnp.broadcast_to(low, (chunks, LANES))
    span_ref[SPAN_HIGH : SPAN_HIGH + chunks, :] = jnp.broadcast_to(high, (chunks, LANES))
    row = lax.broadcasted_iota(jnp.int32, (SPAN_LOW, LANES), 0)
    kind = (flat // 2) % 4
    head = jnp.where(row == SPAN_FIRST, jnp.right_shift(low[0:1, :], 1), 0)
    head = head + jnp.where(row == SPAN_LAST, jnp.right_shift(high[chunks - 1 :, :], 1), 0)
    head = head + jnp.where(row == SPAN_CORE, flat % 2, 0)
    head = head + jnp.where(row == SPAN_CHIP, flat // 2, 0)
    for k, slots in enumerate(zip(*SLOTS)):
        slot = sum(jnp.where(kind == which, at, 0) for which, at in enumerate(slots))
        head = head + jnp.where(row == SPAN_SLOT + k, slot, 0)
    span_ref[:SPAN_LOW, :] = head

    def column_of(ref):
        return jnp.transpose(jnp.broadcast_to(ref[...], (LANES, LANES)))

    means, widths = column_of(means_ref), column_of(widths_ref)
    peaks = 1.0 / (ROOT_TWO_PI * widths)
    bend = -(KAPPA * KAPPA) / (widths * widths)
    tab_ref[0] = means
    tab_ref[1] = KAPPA / widths
    tab_ref[2] = LOG2E * jnp.log(peaks)
    tab_ref[3] = bend
    turned_weights = kw_ref[...].astype(F32)
    heads = turned_weights.shape[0]
    filler = jnp.zeros((LANES - heads, LANES), F32)
    wide = jnp.transpose(jnp.concatenate([turned_weights, filler], axis=0))
    weights = wide[:, :heads]
    scaled = weights * (peaks / (widths * widths))[:, :heads]
    gw_ref[...] = jnp.concatenate(split(scaled, WEIGHT_PIECES), axis=1)
    kwt_ref[...] = kw_ref[...]
    lanes = lax.broadcasted_iota(jnp.int32, (LANES, LANES), 1)
    par = wide + jnp.where(lanes == heads, peaks, 0.0)
    par_ref[...] = par + jnp.where(lanes == heads + 1, 1.0 / widths, 0.0)


def bias_kernel(span_ref, own_ref, other_ref, tab_ref, kwt_ref, out_ref, str_ref):
    rows, keys = str_ref.shape
    kernels = tab_ref.shape[1]
    heads = kwt_ref.shape[0]
    half_keys = keys // 2
    str_ref[...] = stretched_of(own_ref[...], other_ref[...])[3]

    def step(at, half):
        columns = slice(half * half_keys, (half + 1) * half_keys)
        block = str_ref[pl.ds(at, BIAS_ROWS), columns]
        for r in range(0, BIAS_ROWS, 2):
            parts = []
            for q in range(2):
                line = jnp.broadcast_to(block[r + q : r + q + 1], (kernels, half_keys))
                z = (line - tab_ref[0]) * tab_ref[1]
                parts.append(jnp.exp2(tab_ref[2] - z * z).astype(BF))
            result = dot_nn(kwt_ref[...], jnp.concatenate(parts, axis=1)) * LOG2E
            out_ref[0, at + r, :, columns] = result[:, :half_keys]
            out_ref[0, at + r + 1, :, columns] = result[:, half_keys:]

    def skipped(at, half):
        columns = slice(half * half_keys, (half + 1) * half_keys)
        out_ref[0, pl.ds(at, BIAS_ROWS), :, columns] = jnp.zeros((BIAS_ROWS, heads, half_keys), F32)

    kernel_steps(span_ref, 0, rows, BIAS_ROWS, step, skipped)


def forward_kernel(
    scale2,
    groups,
    span_ref,
    own_ref,
    other_ref,
    *refs,
):
    token_refs, refs = refs[:14], refs[14:]
    gain_ref, shift_ref, w_ref, select_ref, ones_ref, place_ref, bias_ref, *refs = refs
    att_ref, qaug_ref, lse_ref, kvq_ref, *refs = refs
    qexp_ref, mask_ref, max_ref, sum_ref, acc_ref, lane_ref, both_ref = refs
    step = pl.program_id(0)
    width = groups * SPAN
    tok_ref = token_refs[3]
    rows, model_width = tok_ref.shape
    windows = group_windows(groups, model_width // (groups * GROUP))
    gain, shift = row_of(gain_ref), row_of(shift_ref)

    @pl.when(step == 0)
    def _():
        normed = layer_norm(tok_ref[...].astype(F32), gain, shift).astype(BF)
        query = dot_nn(normed, w_ref[:, :model_width]).astype(BF)
        query = pad_columns(query, select_ref, windows)
        qaug_ref[...] = query
        expand_into(qexp_ref, query, groups)
        max_ref[...] = jnp.full(max_ref.shape, 2.0 * MASKED, F32)
        sum_ref[...] = jnp.zeros(sum_ref.shape, F32)
        acc_ref[...] = jnp.zeros(acc_ref.shape, F32)

    fetch(span_ref, token_refs, both_ref)
    normed = layer_norm(both_ref[...].astype(F32), gain, shift).astype(BF)
    spots = spots_of(span_ref, rows)

    for part in range(3):
        source = (part + 1) % 3 * model_width
        value = dot_nn(normed, w_ref[:, source : source + model_width]).astype(BF)
        value = pad_columns(value, select_ref, windows)
        if part < 2:
            value = value + ones_ref[...].astype(BF)
        for k in range(2):
            kvq_ref[0, spots[k], part * width : (part + 1) * width] = (
                value[k * rows : (k + 1) * rows]
            )
    spread_mask(mask_ref, mask_of(own_ref[...], other_ref[...], False))

    def chunk_step(at, count):
        lines = pl.ds(pl.multiple_of(at * GROUP, HEAD_ROWS * GROUP), count * GROUP)
        mask = mask_ref[pl.ds(at, count)]
        for g in range(groups):
            columns = slice(g * SPAN, (g + 1) * SPAN)
            dots = dot_nt(qexp_ref[g, lines, :], kvq_ref[0, :, columns])
            bias = bias_ref[0, pl.ds(at, count), g * GROUP : (g + 1) * GROUP, :] + mask
            scores = dots * scale2 + bias.reshape(dots.shape)
            old = max_ref[g, lines, :]
            top = jnp.maximum(scores[:, :128], scores[:, 128:])
            new = jnp.maximum(old, jnp.max(top, axis=1, keepdims=True))
            alpha = jnp.exp2(old - new)
            low = jnp.exp2(scores[:, :128] - new)
            high = jnp.exp2(scores[:, 128:] - new)
            max_ref[g, lines, :] = new
            sum_ref[g, lines, :] = sum_ref[g, lines, :] * alpha + (low + high)
            probs = jnp.concatenate([low, high], axis=1).astype(BF)
            values = dot_nn(probs, kvq_ref[0, :, width + g * SPAN : width + (g + 1) * SPAN])
            wide = jnp.concatenate([alpha, alpha], axis=1)
            acc_ref[g, lines, :] = acc_ref[g, lines, :] * wide + values

    head_steps(span_ref, rows, chunk_step)

    @pl.when(step == span_ref[SPAN_LAST, 0] - span_ref[SPAN_FIRST, 0])
    def _():
        lane = lax.broadcasted_iota(jnp.int32, (GROUP, 128), 1)
        head = lax.broadcasted_iota(jnp.int32, (GROUP, 128), 0)

        def finish(i, carry):
            at = pl.multiple_of(i * CHUNK, CHUNK)
            lines = pl.ds(pl.multiple_of(i * CHUNK * GROUP, CHUNK * GROUP), CHUNK * GROUP)
            lanes = jnp.zeros((CHUNK, 128), F32)
            for g in range(groups):
                total = jnp.sum(sum_ref[g, lines, :], axis=1, keepdims=True)
                attended = collapse(acc_ref[g, lines, :] / total)
                att_ref[pl.ds(at, CHUNK), g * SPAN : (g + 1) * SPAN] = attended
                lse = max_ref[g, lines, :] + jnp.log(total) * LOG2E
                own_lane = jnp.where(lane == head + g * GROUP, 1.0, 0.0)
                lanes = lanes + jnp.sum(
                    lse.reshape(CHUNK, GROUP, 128) * own_lane[None], axis=1
                )
            lane_ref[pl.ds(at, CHUNK), :] = lanes
            return carry

        lax.fori_loop(0, rows // CHUNK, finish, 0)
        rest = lane_ref[...] * (-1.0 / scale2)
        query = qaug_ref[...].astype(F32)
        for p in range(PIECES):
            piece = rest.astype(BF)
            rest = rest - piece.astype(F32)
            lse_ref[p] = piece
            query = query + dot_nn(piece, place_ref[p])
        qaug_ref[...] = query.astype(BF)


def query_grad_kernel(
    scale2,
    head_scale,
    groups,
    span_ref,
    own_ref,
    other_ref,
    qaug_ref,
    doaug_ref,
    kv_ref,
    bias_ref,
    select_ref,
    dq_ref,
    ds_ref,
    qexp_ref,
    doexp_ref,
    mask_ref,
    dqacc_ref,
    low_ref,
):
    step = pl.program_id(0)
    width = groups * SPAN
    rows, keys = own_ref.shape[0], other_ref.shape[1]
    windows = group_windows(groups, dq_ref.shape[0] // (groups * GROUP))

    @pl.when(step == 0)
    def _():
        expand_into(qexp_ref, qaug_ref[...], groups)
        expand_into(doexp_ref, doaug_ref[...], groups)
        dqacc_ref[...] = jnp.zeros(dqacc_ref.shape, F32)

    spread_mask(mask_ref, mask_of(own_ref[...], other_ref[...], False))

    def chunk_step(at, count):
        lines = pl.ds(pl.multiple_of(at * GROUP, HEAD_ROWS * GROUP), count * GROUP)
        mask = mask_ref[pl.ds(at, count)]
        waiting = []
        for g in range(groups):
            key_block = kv_ref[0, :, g * SPAN : (g + 1) * SPAN]
            value_block = kv_ref[0, :, width + g * SPAN : width + (g + 1) * SPAN]
            dots = dot_nt(qexp_ref[g, lines, :], key_block)
            grads = dot_nt(doexp_ref[g, lines, :], value_block)
            bias = bias_ref[0, pl.ds(at, count), g * GROUP : (g + 1) * GROUP, :] + mask
            probs = jnp.exp2(dots * scale2 + bias.reshape(dots.shape))
            grad_scores = probs * grads
            dqacc_ref[g, lines, :] += dot_nn(grad_scores.astype(BF), key_block)
            waiting.append(grad_scores.reshape(count, GROUP, keys))
            if len(waiting) == 2:
                ds_ref[0, pl.ds(at, count), (g - 1) * GROUP : (g + 1) * GROUP, :] = (
                    jnp.concatenate(waiting, axis=1).astype(BF)
                )
                waiting = []

    head_steps(span_ref, rows, chunk_step)

    @pl.when(step == span_ref[SPAN_LAST, 0] - span_ref[SPAN_FIRST, 0])
    def _():
        def finish(i, carry):
            at = pl.multiple_of(i * CHUNK, CHUNK)
            lines = pl.ds(pl.multiple_of(i * CHUNK * GROUP, CHUNK * GROUP), CHUNK * GROUP)
            for g in range(groups):
                value = collapse(dqacc_ref[g, lines, :]) * head_scale
                low_ref[pl.ds(at, CHUNK), g * SPAN : (g + 1) * SPAN] = value.astype(BF)
            return carry

        lax.fori_loop(0, rows // CHUNK, finish, 0)
        dq_ref[...] = drop_turned(low_ref[...], select_ref, windows)


def phi_grad_kernel(
    first_row,
    span_ref,
    own_ref,
    other_ref,
    line_ref,
    ds_ref,
    tab_ref,
    kw_ref,
    par_ref,
    small_ref,
    pos_ref,
    str_ref,
    gs_ref,
    own_acc_ref,
    gkw_ref,
    moment_ref,
    type_ref,
):
    step = pl.program_id(0)
    rows, keys = str_ref.shape
    kernels = tab_ref.shape[1]
    heads = gkw_ref.shape[1]
    blocks = pos_ref.shape[0] // 3
    pair_block = 2 * (span_ref[SPAN_CHIP, 0] + span_ref[SPAN_FIRST, 0] + step)

    @pl.when(step == 0)
    def _():
        gkw_ref[...] = jnp.zeros(gkw_ref.shape, F32)
        moment_ref[...] = jnp.zeros(moment_ref.shape, F32)
        own_acc_ref[...] = jnp.zeros(own_acc_ref.shape, F32)
        pos_ref[...] = jnp.zeros(pos_ref.shape, F32)
        type_ref[...] = jnp.zeros(type_ref.shape, F32)

    def add_types(kind, by_scale, by_shift):
        count = type_ref.shape[1]
        onehot = lax.broadcasted_iota(jnp.int32, (count, LANES), 0).astype(F32) == kind
        type_ref[0] += jnp.where(onehot, by_scale, 0.0)
        type_ref[1] += jnp.where(onehot, by_shift, 0.0)

    own, other = own_ref[first_row : first_row + rows, :], other_ref[...]
    str_ref[...] = stretched_of(own, other)[3]

    half_keys = keys // 2

    def pair_step(at, half):
        columns = slice(half * half_keys, (half + 1) * half_keys)
        block = str_ref[pl.ds(at, CHUNK), columns]
        first = second = weights = None
        lines = []
        for r in range(0, CHUNK, 2):
            low = jnp.concatenate([ds_ref[0, at + r + q, :, columns] for q in range(2)], axis=1)
            dphi = dot_nn(kw_ref[...], jnp.concatenate([low] * WEIGHT_PIECES, axis=0))
            phis = []
            for q in range(2):
                away = jnp.broadcast_to(block[r + q : r + q + 1], (kernels, half_keys)) - tab_ref[0]
                phi = jnp.exp2(away * away * tab_ref[3])
                phis.append(phi.astype(BF))
                moved = dphi[:, q * half_keys : (q + 1) * half_keys] * phi * away
                bent = moved * away
                first = moved if first is None else first + moved
                second = bent if second is None else second + bent
                lines.append(jnp.sum(moved, axis=0, keepdims=True))
            part = dot_nt(jnp.concatenate(phis, axis=1), low)
            weights = part if weights is None else weights + part
        moment_ref[0] += first
        moment_ref[1] += second
        gs_ref[pl.ds(at, CHUNK), columns] = jnp.concatenate(lines, axis=0)
        gkw_ref[...] += weights

    def skipped(at, half):
        columns = slice(half * half_keys, (half + 1) * half_keys)
        gs_ref[pl.ds(at, CHUNK), columns] = jnp.zeros((CHUNK, half_keys), F32)

    kernel_steps(span_ref, first_row, rows, CHUNK, pair_step, skipped)

    delta, dist, scales, _ = stretched_of(own, other)
    grad = -gs_ref[...]
    by_scale = grad * dist
    pull = grad * scales / dist
    terms = [pull * delta[0], pull * delta[1], pull * delta[2], by_scale * other[3:4, :], grad]
    for k, term in enumerate(terms):
        own_acc_ref[k] += term[:, :128] + term[:, 128:]
    for half in range(2):
        part = slice(half * LANES, (half + 1) * LANES)
        for k in range(3):
            spot = pl.ds(k * blocks + pair_block + half, 1)
            pos_ref[spot, :] += -jnp.sum(terms[k][:, part], axis=0, keepdims=True)
        add_types(
            other[8:9, part],
            jnp.sum(by_scale[:, part] * own[:, 3:4], axis=0, keepdims=True),
            jnp.sum(grad[:, part], axis=0, keepdims=True),
        )

    @pl.when(step == span_ref[SPAN_LAST, 0] - span_ref[SPAN_FIRST, 0])
    def _():
        lane = lax.broadcasted_iota(jnp.int32, (rows, LANES), 1)
        total = jnp.zeros((rows, LANES), F32)
        for k in range(5):
            column = jnp.sum(own_acc_ref[k], axis=1, keepdims=True)
            total = total + jnp.where(lane == k, column, 0.0)
        rest = [jnp.zeros((count, LANES), F32) for count in (first_row, LANES - first_row - rows)]
        total = jnp.concatenate([x for x in (rest[0], total, rest[1]) if x.shape[0]], axis=0)
        turned = jnp.transpose(total)
        own_block = 2 * (span_ref[SPAN_CHIP, 0] + len(SLOTS[0]) // 2) + span_ref[SPAN_CORE, 0]
        for k in range(3):
            pos_ref[pl.ds(k * blocks + own_block, 1), :] += turned[k : k + 1, :]
        add_types(line_ref[8:9, :], turned[3:4, :], turned[4:5, :])

        par = par_ref[...]
        by_weight = gkw_ref[...] * par[:, heads : heads + 1]
        plain = jnp.sum(by_weight * par[:, :heads], axis=1, keepdims=True)
        by_mean = jnp.sum(moment_ref[0], axis=1, keepdims=True)
        by_width = jnp.sum(moment_ref[1], axis=1, keepdims=True) - plain
        columns = [by_mean, by_width * par[:, heads + 1 : heads + 2]]
        low, high = slice(0, LANES), slice(LANES, 2 * LANES)
        for part in (low, high):
            for k in range(2):
                columns.append(jnp.sum(type_ref[k, part, :], axis=1, keepdims=True))
        lane = lax.broadcasted_iota(jnp.int32, (LANES, LANES), 1)
        wide = jnp.concatenate([by_weight, jnp.zeros((LANES, LANES - heads), F32)], axis=1)
        for k, column in enumerate(columns):
            wide = wide + jnp.where(lane == heads + k, column, 0.0)
        small_ref[...] = wide


def middle_kernel(
    groups,
    tile,
    flat_ref,
    tok_ref,
    att_ref,
    lse_ref,
    gain_ref,
    shift_ref,
    cot_ref,
    wout_hbm,
    wup_hbm,
    wdown_hbm,
    select_ref,
    place_ref,
    sum_ref,
    into_ref,
    out_ref,
    gmix_ref,
    doaug_ref,
    payload_ref,
    attlow_ref,
    normed_ref,
    mine_ref,
    theirs_ref,
    lngrad_ref,
    wout_ref,
    wup_ref,
    wdown_ref,
    down_ref,
    back_ref,
    wout_sem,
    tile_sems,
):
    rows, model_width = tok_ref.shape
    width = groups * SPAN
    windows = group_windows(groups, model_width // (groups * GROUP))
    tiles = wup_ref.shape[1] // tile
    piece = mine_ref.shape[2]
    core = flat_ref[0] % 2

    def tile_copies(t):
        spot = pl.ds(pl.multiple_of(t * tile, LANES), tile)
        return (
            pltpu.make_async_copy(wup_hbm.at[:, spot], wup_ref.at[:, spot], tile_sems.at[0, t]),
            pltpu.make_async_copy(wdown_hbm.at[spot, :], wdown_ref.at[spot, :], tile_sems.at[1, t]),
        )

    first = pltpu.make_async_copy(wout_hbm, wout_ref, wout_sem)
    first.start()
    for t in range(tiles):
        for copy in tile_copies(t):
            copy.start()

    gain, shift = row_of(gain_ref), row_of(shift_ref)
    cotangent = cot_ref[...]
    attended = att_ref[...]
    attended_low = drop_columns(attended.astype(BF), select_ref, windows)
    attlow_ref[...] = attended_low
    first.wait()
    mixed = tok_ref[...].astype(F32) + dot_nn(attended_low, wout_ref[...])
    normal, slope = norm_parts(mixed)
    normed_ref[...] = (normal * gain + shift).astype(BF)
    down_ref[...] = mixed
    back_ref[...] = jnp.zeros(back_ref.shape, F32)

    def step(t, carry):
        for copy in tile_copies(t):
            copy.wait()
        spot = pl.ds(pl.multiple_of(t * tile, LANES), tile)
        up = dot_nn(normed_ref[...], wup_ref[:, spot])
        grad_hidden = dot_nt(cotangent, wdown_ref[spot, :])
        square = up * up
        bent = jnp.tanh(GELU_SLOPE * (up * (1.0 + GELU_CUBE * square)))
        gate = 0.5 * (1.0 + bent)
        inner = GELU_SLOPE * (1.0 + 3.0 * GELU_CUBE * square)
        hidden = (up * gate).astype(BF)
        grad_up = (grad_hidden * (gate + 0.5 * up * (1.0 - bent * bent) * inner)).astype(BF)
        for kind, value in enumerate((grad_up, hidden)):
            value = jnp.transpose(value.astype(F32)).astype(BF)
            for q in range(tile // piece):
                part = value[q * piece : (q + 1) * piece]
                at = t * (tile // piece // 2) + q // 2

                @pl.when(core == q % 2)
                def _():
                    mine_ref[kind, at] = part

                @pl.when(core != q % 2)
                def _():
                    theirs_ref[kind, at] = part

        down_ref[...] += dot_nn(hidden, wdown_ref[spot, :])
        back_ref[...] += dot_nt(grad_up, wup_ref[:, spot])
        return carry

    lax.fori_loop(0, tiles, step, 0)
    out_ref[...] = down_ref[...].astype(BF)
    back, by_gain, by_shift = norm_back(back_ref[...], normal, slope, gain)
    lngrad_ref[...] = jnp.concatenate([by_gain, by_shift], axis=0)
    grad_mixed = cotangent.astype(F32) + back
    gmix_ref[...] = grad_mixed
    grad_low = grad_mixed.astype(BF)
    grad_attended = dot_nt(grad_low, wout_ref[...]).astype(BF)
    padded = pad_columns(grad_attended, select_ref, windows).astype(F32)
    high, low = split(padded * attended, 2)
    delta = dot_nn(high, sum_ref[...]) + dot_nn(low, sum_ref[...])
    pieces = split(-delta, PIECES)
    tail = jnp.zeros((rows, 2 * LANES), F32)
    for p in range(PIECES):
        padded = padded + dot_nn(pieces[p], place_ref[p])
        tail = tail + dot_nn(lse_ref[p], into_ref[p]) + dot_nn(pieces[p], into_ref[PIECES + p])
    doaug_ref[...] = padded.astype(BF)
    payload_ref[:, :model_width] = grad_low
    payload_ref[:, model_width:] = tail.astype(BF)


def weight_grads_kernel(
    ka_count,
    flat_ref,
    mine_ref,
    came_ref,
    normed_ref,
    normed_came_ref,
    cot_ref,
    cot_came_ref,
    attlow_ref,
    attlow_came_ref,
    payload_ref,
    payload_came_ref,
    up_kept_ref,
    up_sent_ref,
    rest_kept_ref,
    rest_sent_ref,
    product_ref,
):
    flat = flat_ref[0]
    core, bit, side = flat % 2, (flat // 2) % 2, (flat // ka_count) % 2
    model_width = normed_ref.shape[1]
    rows = up_kept_ref.shape[1]
    half = model_width // 2
    slices = up_kept_ref.shape[0] * 2
    out_rows = model_width // ka_count
    normed = jnp.concatenate([normed_ref[...], normed_came_ref[...]], axis=0)
    cotangent = jnp.concatenate([cot_ref[...], cot_came_ref[...]], axis=0)

    def columns(which):
        return pl.ds(pl.multiple_of(which * half, LANES), half)

    def step(m, carry):
        both = jnp.concatenate([mine_ref[0, m], came_ref[0, m]], axis=1)
        value = dot_nn(both, normed).astype(BF)

        @pl.when(m % 2 == bit)
        def _():
            up_kept_ref[m // 2] = value

        @pl.when(m % 2 != bit)
        def _():
            up_sent_ref[m // 2] = value

        both = jnp.concatenate([mine_ref[1, m], came_ref[1, m]], axis=1)
        product_ref[:rows, :] = dot_nn(both, cotangent)
        rest_kept_ref[m, :rows, :] = product_ref[:rows, columns(side)].astype(BF)
        rest_sent_ref[m, :rows, :] = product_ref[:rows, columns(1 - side)].astype(BF)
        return carry

    lax.fori_loop(0, slices, step, 0)
    grads = jnp.concatenate(
        [payload_ref[:, :model_width], payload_came_ref[:, :model_width]], axis=0
    )
    attended = jnp.concatenate([attlow_ref[...], attlow_came_ref[...]], axis=0)
    product_ref[...] = dot_tn(grads, attended)

    def out_step(m, carry):
        spot = pl.ds(pl.multiple_of((2 * m + core) * out_rows, 8), out_rows)
        rest_kept_ref[m, rows:, :] = product_ref[spot, columns(side)].astype(BF)
        rest_sent_ref[m, rows:, :] = product_ref[spot, columns(1 - side)].astype(BF)
        return carry

    lax.fori_loop(0, slices, out_step, 0)


def normal_kernel(tok_ref, gain_ref, shift_ref, out_ref):
    normal, _ = norm_parts(tok_ref[...].astype(F32))
    out_ref[...] = (normal * row_of(gain_ref) + row_of(shift_ref)).astype(BF)


def qkv_grads_kernel(ka_count, masks, flat_ref, grads_ref, *refs):
    normed_refs, out_ref, norm_ref = refs[:-2], refs[-2], refs[-1]
    here = flat_ref[0] % ka_count
    columns = out_ref.shape[0]
    lefts, rights, parts = [], [], None
    for ref, group in zip(normed_refs, masks):
        for i, mask in enumerate(group):
            grads = grads_ref[jnp.bitwise_xor(here, mask)]
            lefts.append(grads[:columns])
            rights.append(ref[i])
            part = grads[columns:].astype(F32)
            parts = part if parts is None else parts + part
    total = None
    for i in range(0, len(lefts), 2):
        part = dot_nn(
            jnp.concatenate(lefts[i : i + 2], axis=1), jnp.concatenate(rights[i : i + 2], axis=0)
        )
        total = part if total is None else total + part
    out_ref[...] = total.astype(BF)
    norm_ref[...] = parts


def results_kernel(
    heads,
    types,
    flat_ref,
    joined_ref,
    first_ref,
    norm_ref,
    weight_ref,
    mean_ref,
    width_ref,
    scale_ref,
    shift_ref,
    pos_ref,
):
    small = joined_ref[:LANES, :]
    weight_ref[...] = small[:, :heads]
    turned = jnp.transpose(small)
    rows = [turned[heads + k : heads + k + 1, :] for k in range(6)]
    mean_ref[...] = rows[0]
    width_ref[...] = rows[1]
    scale_ref[...] = jnp.concatenate([rows[2], rows[4]], axis=1)[:, :types]
    shift_ref[...] = jnp.concatenate([rows[3], rows[5]], axis=1)[:, :types]
    count = norm_ref.shape[1]
    for k in range(2):
        norm_ref[k] = first_ref[k * count : (k + 1) * count, :]
        norm_ref[2 + k] = joined_ref[LANES + k * count : LANES + (k + 1) * count, :]
    first = LANES + 2 * count
    blocks = (joined_ref.shape[0] - first) // 3
    for k in range(3):
        spot = first + k * blocks + len(SLOTS[0]) // 2 * 2 + flat_ref[0]
        pos_ref[k : k + 1, :] = joined_ref[pl.ds(spot, 1), :]


def first_norm_kernel(
    tok_ref, gain_ref, dq_ref, dkv_ref, w_ref, gmix_ref, grad_ref, all_ref, joined_ref
):
    model_width = tok_ref.shape[1]
    grad = dot_nn(w_ref[:, :model_width], dq_ref[...])
    grad = grad + dot_nn(w_ref[:, model_width:], dkv_ref[...])
    grad = jnp.transpose(grad)
    normal, slope = norm_parts(tok_ref[...].astype(F32))
    back, by_gain, by_shift = norm_back(grad, normal, slope, row_of(gain_ref))
    grad_ref[...] = gmix_ref[...] + back
    lines = [
        row[:, k : k + LANES] for row in (by_gain, by_shift) for k in range(0, model_width, LANES)
    ]
    joined_ref[:model_width, :] = dq_ref[...]
    joined_ref[model_width:, :] = dkv_ref[...]
    devices, rows = all_ref.shape[:2]
    columns = 3 * model_width // devices
    lines.append(jnp.zeros((rows - columns - len(lines), LANES), F32))
    lines = jnp.concatenate(lines, axis=0).astype(BF)
    for d in range(devices):
        all_ref[d, :columns, :] = joined_ref[d * columns : (d + 1) * columns, :]
        all_ref[d, columns:, :] = lines


def key_grad_kernel(
    scale2,
    head_scale,
    groups,
    model_width,
    span_ref,
    own_ref,
    other_ref,
    kv_ref,
    q_ref,
    *refs,
):
    payload_refs, refs = refs[:14], refs[14:]
    wout_ref, select_ref, place_ref, bias_ref, dkv_ref, kexp_ref, vexp_ref, *refs = refs
    mask_ref, qb_ref, dob_ref, dk_ref, dv_ref, both_ref, low_ref = refs
    step = pl.program_id(0)
    width = groups * SPAN
    rows = own_ref.shape[0]
    windows = group_windows(groups, model_width // (groups * GROUP))

    @pl.when(step == 0)
    def _():
        expand_into(kexp_ref, kv_ref[0, :, :width], groups)
        expand_into(vexp_ref, kv_ref[0, :, width:], groups)
        dk_ref[...] = jnp.zeros(dk_ref.shape, F32)
        dv_ref[...] = jnp.zeros(dv_ref.shape, F32)

    fetch(span_ref, payload_refs, both_ref)
    payload = both_ref[...]
    tail = payload[:, model_width:]
    grads = dot_nt(payload[:, :model_width], wout_ref[...]).astype(BF)
    grads = pad_columns(grads, select_ref, windows).astype(F32)
    grads = (grads + dot_nn(tail, place_ref[1])).astype(BF)
    shifts = dot_nn(tail, place_ref[0])
    for k, spot in enumerate(spots_of(span_ref, rows)):
        own_part = slice(k * rows, (k + 1) * rows)
        dob_ref[spot, :] = grads[own_part]
        qb_ref[spot, :] = (q_ref[0, spot, :].astype(F32) + shifts[own_part]).astype(BF)
    spread_mask(mask_ref, mask_of(own_ref[...], other_ref[...], True))

    def chunk_step(at, count):
        lines = pl.ds(pl.multiple_of(at * GROUP, HEAD_ROWS * GROUP), count * GROUP)
        mask = mask_ref[pl.ds(at, count)]
        for g in range(groups):
            query_block = qb_ref[:, g * SPAN : (g + 1) * SPAN]
            grad_block = dob_ref[:, g * SPAN : (g + 1) * SPAN]
            dots = dot_nt(kexp_ref[g, lines, :], query_block)
            grads = dot_nt(vexp_ref[g, lines, :], grad_block)
            bias = bias_ref[0, pl.ds(at, count), g * GROUP : (g + 1) * GROUP, :] + mask
            probs = jnp.exp2(dots * scale2 + bias.reshape(dots.shape))
            grad_scores = (probs * grads).astype(BF)
            dk_ref[g, lines, :] += dot_nn(grad_scores, query_block)
            dv_ref[g, lines, :] += dot_nn(probs.astype(BF), grad_block)

    head_steps(span_ref, rows, chunk_step)

    @pl.when(step == span_ref[SPAN_LAST, 0] - span_ref[SPAN_FIRST, 0])
    def _():
        def finish(i, carry):
            at = pl.multiple_of(i * CHUNK, CHUNK)
            lines = pl.ds(pl.multiple_of(i * CHUNK * GROUP, CHUNK * GROUP), CHUNK * GROUP)
            for part, (ref, scale) in enumerate(((dk_ref, head_scale), (dv_ref, 1.0))):
                for g in range(groups):
                    value = collapse(ref[g, lines, :]) * scale
                    low_ref[part, pl.ds(at, CHUNK), g * SPAN : (g + 1) * SPAN] = value.astype(BF)
            return carry

        lax.fori_loop(0, rows // CHUNK, finish, 0)
        for part in range(2):
            dkv_ref[part * model_width : (part + 1) * model_width, :] = drop_turned(
                low_ref[part], select_ref, windows
            )


def fixed(shape):
    return pl.BlockSpec(shape, lambda j, span: (0,) * len(shape), pipeline_mode=pl.Buffered(1))


def pair_at(j, span):
    return jnp.minimum(span[SPAN_FIRST, 0] + j, span[SPAN_LAST, 0])


def moving(shape, rank_at=0, last=0):
    def index(j, span):
        at = [0] * len(shape)
        at[rank_at] = pair_at(j, span)
        if last:
            at[-1] = last
        return tuple(at)

    return pl.BlockSpec(shape, index)


def call(
    kernel, steps, in_specs, out_specs, out_shapes, scratch, flops, name, after=(), carry=(), room=56
):
    extra, given = len(after) + len(carry), len(in_specs)
    single = not isinstance(out_shapes, list)
    if single:
        out_specs, out_shapes = [out_specs], [out_shapes]
    made = len(out_shapes)
    anywhere = pl.BlockSpec(memory_space=pl.ANY)

    def body(span_ref, *refs):
        @pl.when(pl.program_id(0) <= span_ref[SPAN_LAST, 0] - span_ref[SPAN_FIRST, 0])
        def _():
            outs = refs[extra + given : extra + given + made]
            kernel(
                span_ref, *refs[extra : extra + given], *outs, *refs[extra + given + made + len(carry) :]
            )

    inner = pl.pallas_call(
        body,
        grid_spec=pltpu.PrefetchScalarGridSpec(
            num_scalar_prefetch=1,
            grid=(steps,),
            in_specs=[anywhere] * extra + in_specs,
            out_specs=out_specs + [anywhere] * len(carry),
            scratch_shapes=scratch,
        ),
        out_shape=out_shapes + [shape_of(x.shape, x.dtype) for x in carry],
        input_output_aliases={1 + len(after) + k: made + k for k in range(len(carry))},
        compiler_params=pltpu.CompilerParams(
            dimension_semantics=("arbitrary",), vmem_limit_bytes=room * 1024 * 1024
        ),
        cost_estimate=pl.CostEstimate(flops=flops, bytes_accessed=20_000_000, transcendentals=0),
        name=name,
    )

    def run(span, *operands):
        results = inner(span, *after, *carry, *operands)
        return results[0] if single else results

    return run


def shape_of(shape, dtype=F32):
    return jax.ShapeDtypeStruct(shape, dtype)


def once(
    kernel, operands, out_shapes, scratch, flops, name, spaces=(), after=(), carry=(), room=56
):
    spaces = dict(spaces)
    shapes = [*out_shapes, *(shape_of(x.shape, x.dtype) for x in carry)]
    count, extra = len(operands), len(after) + len(carry)
    anywhere = pl.BlockSpec(memory_space=pl.ANY)

    def whole(shape):
        return pl.BlockSpec(shape, lambda j: (0,) * len(shape), pipeline_mode=pl.Buffered(1))

    def body(*refs):
        outs = refs[count + extra : count + extra + len(out_shapes)]
        kernel(*refs[:count], *outs, *refs[count + extra + len(shapes) :])

    results = pl.pallas_call(
        body,
        grid=(1,),
        in_specs=[
            pl.BlockSpec(memory_space=spaces[k]) if k in spaces else whole(x.shape)
            for k, x in enumerate(operands)
        ]
        + [anywhere] * extra,
        out_specs=[whole(x.shape) for x in out_shapes] + [anywhere] * len(carry),
        out_shape=shapes,
        scratch_shapes=scratch,
        input_output_aliases={
            count + len(after) + k: len(out_shapes) + k for k in range(len(carry))
        },
        compiler_params=pltpu.CompilerParams(vmem_limit_bytes=room * 1024 * 1024),
        cost_estimate=pl.CostEstimate(flops=flops, bytes_accessed=5_000_000, transcendentals=0),
        name=name,
    )(*operands, *after, *carry)
    return results


def on_device(
    tokens,
    positions,
    item_of_atom,
    item_lengths,
    atom_types,
    key_mask,
    ln1_gain,
    ln1_bias,
    w_qkv,
    kernel_means,
    kernel_widths,
    kernel_weight,
    type_scale,
    type_shift,
    w_out,
    ln2_gain,
    ln2_bias,
    w_up,
    w_down,
    out_cotangent,
):
    own_rows, model_width = tokens.shape
    assert own_rows == LANES
    kernels, heads = kernel_weight.shape
    head_size = model_width // heads
    head_scale = head_size ** (-0.5)
    scale2 = head_scale * LOG2E
    groups = heads // GROUP
    width = groups * SPAN
    ff_width = w_up.shape[1]
    ka_count = lax.axis_size("ka")
    flat = lax.axis_index("pb") * ka_count + lax.axis_index("ka")
    flat_array = flat.astype(jnp.int32).reshape(1)
    reach = (PROT_LEN + own_rows - 2) // own_rows
    chips = (reach + 1) // 2
    pairs = 2 * chips + 1
    assert pairs == len(SLOTS[0])
    keys = 2 * own_rows
    atoms = positions.shape[1]
    atoms_blocks = atoms // LANES
    types = type_scale.shape[0]
    bits = bits_of("ka") - 1
    up_order = [(0, 1), (1, 2)] + [(bit, 1) for bit in range(3, bits)]
    rest_order = [(bit, 1) for bit in range(bits)]

    window = Window(tokens)
    cotangent_came = core_flip(out_cotangent)
    ln1 = [x.reshape(-1, LANES) for x in (ln1_gain, ln1_bias)]
    ln2 = [x.reshape(-1, LANES) for x in (ln2_gain, ln2_bias)]
    (normed_own,) = once(
        normal_kernel,
        (tokens, *ln1),
        [shape_of(tokens.shape, BF)],
        [],
        1_000_000,
        "first_normal",
        room=16,
    )
    gathered = Gathered(normed_own)

    select = select_table(head_size)
    place = place_table(heads, head_size)
    into_tail, out_of_tail = tail_tables(heads, head_size)
    type_tiles = -(-types // LANES)
    tables = jnp.pad(
        jnp.stack([type_scale, type_shift]), ((0, 0), (0, type_tiles * LANES - types))
    )
    tables = tables.reshape(2, type_tiles, LANES).swapaxes(0, 1).reshape(2 * type_tiles, LANES)
    lengths = jnp.pad(item_lengths, (0, -item_lengths.shape[0] % LANES)).reshape(-1, LANES)
    span, other, own, own_line, tabs, grad_weights, weights_turned, par = once(
        functools.partial(side_kernel, atoms_blocks),
        (
            flat_array,
            positions,
            item_of_atom.reshape(-1, LANES),
            key_mask.reshape(-1, LANES),
            atom_types.reshape(-1, LANES),
            lengths,
            tables,
            kernel_means.reshape(1, LANES),
            kernel_widths.reshape(1, LANES),
            kernel_weight.T,
        ),
        [
            shape_of((SPAN_ROWS, LANES), jnp.int32),
            shape_of((SIDE, pairs * keys)),
            shape_of((own_rows, LANES)),
            shape_of((SIDE, LANES)),
            shape_of((4, kernels, LANES)),
            shape_of((kernels, WEIGHT_PIECES * heads), BF),
            shape_of((heads, kernels), BF),
            shape_of((LANES, LANES)),
        ],
        [],
        1_000_000_000,
        "sides",
        {0: pltpu.SMEM},
    )

    own_spec = fixed((own_rows, LANES))
    other_spec = moving((SIDE, keys), 1)
    bias_spec = moving((1, own_rows, heads, keys))
    bias = call(
        bias_kernel,
        pairs,
        [own_spec, other_spec, fixed((4, kernels, LANES)), fixed((heads, kernels))],
        bias_spec,
        shape_of((pairs, own_rows, heads, keys)),
        [pltpu.VMEM((own_rows, keys), F32)],
        30_000_000_000,
        "pair_bias",
        after=(window.one, window.two, normed_own),
    )(span, own, other, tabs, weights_turned)
    window.middle()
    token_blocks = window.finish()

    expanded = pltpu.VMEM((groups, own_rows * GROUP, SPAN), BF)
    summed = pltpu.VMEM((groups, own_rows * GROUP, SPAN), F32)
    mask_scratch = pltpu.VMEM((own_rows, GROUP, keys), F32)
    line_scratch = pltpu.VMEM((groups, own_rows * GROUP, LANES), F32)
    attended, q_aug, lse_pieces, kvq = call(
        functools.partial(forward_kernel, scale2, groups),
        pairs,
        [own_spec, other_spec]
        + [fixed((own_rows, model_width))] * 14
        + [
            fixed((model_width // LANES, LANES)),
            fixed((model_width // LANES, LANES)),
            fixed((model_width, 3 * model_width)),
            fixed(select.shape),
            fixed((1, width)),
            fixed(place.shape),
            bias_spec,
        ],
        [
            fixed((own_rows, width)),
            fixed((own_rows, width)),
            fixed((PIECES, own_rows, LANES)),
            moving((1, keys, 3 * width)),
        ],
        [
            shape_of((own_rows, width)),
            shape_of((own_rows, width), BF),
            shape_of((PIECES, own_rows, LANES), BF),
            shape_of((pairs, keys, 3 * width), BF),
        ],
        [
            expanded,
            mask_scratch,
            line_scratch,
            line_scratch,
            summed,
            pltpu.VMEM((own_rows, LANES), F32),
            pltpu.VMEM((keys, model_width), BF),
        ],
        25_000_000_000,
        "attention_forward",
        after=(gathered.beside,),
    )(
        span,
        own,
        other,
        *token_blocks,
        *ln1,
        w_qkv,
        select,
        ones_row(heads, head_size),
        place,
        bias,
    )

    far_rows = gathered.far()
    tile = 3 * LANES
    assert ff_width % tile == 0 and tile % (2 * ff_width // ka_count) == 0
    row_shape = shape_of((own_rows, model_width), BF)
    slices = ka_count // 2
    up_rows, out_rows = ff_width // ka_count, model_width // ka_count
    pieces = shape_of((2, slices, up_rows, own_rows), BF)
    block_out, grad_mixed, do_aug, payload, attended_low, normed_second, *parts, ln2_grads = once(
        functools.partial(middle_kernel, groups, tile),
        (
            flat_array,
            tokens,
            attended,
            lse_pieces,
            *ln2,
            out_cotangent,
            w_out,
            w_up,
            w_down,
            select,
            place,
            head_sum_table(heads),
            into_tail,
        ),
        [
            row_shape,
            shape_of((own_rows, model_width)),
            shape_of((own_rows, width), BF),
            shape_of((own_rows, model_width + 2 * LANES), BF),
            row_shape,
            row_shape,
            pieces,
            pieces,
            shape_of((2, model_width)),
        ],
        [
            pltpu.VMEM((model_width, model_width), BF),
            pltpu.VMEM((model_width, ff_width), BF),
            pltpu.VMEM((ff_width, model_width), BF),
            pltpu.VMEM((own_rows, model_width), F32),
            pltpu.VMEM((own_rows, model_width), F32),
            pltpu.SemaphoreType.DMA,
            pltpu.SemaphoreType.DMA((2, ff_width // tile)),
        ],
        10_000_000_000,
        "feed_forward",
        {0: pltpu.SMEM, 7: pl.ANY, 8: pl.ANY, 9: pl.ANY},
        after=tuple(far_rows),
    )
    came = [core_flip(x) for x in (parts[1], normed_second, attended_low, payload)]
    window = Window(payload, came[3])
    gathered.finish()
    half = model_width // 2
    up_kept, up_sent, rest_kept, rest_sent = once(
        functools.partial(weight_grads_kernel, ka_count),
        (
            flat_array,
            parts[0],
            came[0],
            normed_second,
            came[1],
            out_cotangent,
            cotangent_came,
            attended_low,
            came[2],
            payload,
            came[3],
        ),
        [shape_of((slices // 2, up_rows, model_width), BF)] * 2
        + [shape_of((slices, up_rows + out_rows, half), BF)] * 2,
        [pltpu.VMEM((model_width, model_width), F32)],
        5_000_000_000,
        "weight_gradients",
        {0: pltpu.SMEM},
    )
    up_sum = slices_sum(up_kept, up_sent, up_order)
    rest_sum = columns_sum(rest_kept, rest_sent, rest_order)

    dq, grad_scores, window.one, window.two = call(
        functools.partial(query_grad_kernel, scale2, head_scale, groups),
        pairs,
        [
            own_spec,
            other_spec,
            fixed((own_rows, width)),
            fixed((own_rows, width)),
            moving((1, keys, 2 * width)),
            bias_spec,
            fixed(select.shape),
        ],
        [fixed((model_width, own_rows)), moving((1, own_rows, heads, keys))],
        [
            shape_of((model_width, own_rows), BF),
            shape_of((pairs, own_rows, heads, keys), BF),
        ],
        [expanded, expanded, mask_scratch, summed, pltpu.VMEM((own_rows, width), BF)],
        22_000_000_000,
        "query_gradients",
        after=(*up_sum.sent, *rest_sum.sent, window.far),
        carry=(window.one, window.two),
    )(span, own, other, q_aug, do_aug, kvq, bias, select)

    pos_blocks = atoms_blocks + 4 * chips
    small, pos_part = call(
        functools.partial(phi_grad_kernel, 0),
        pairs,
        [
            own_spec,
            other_spec,
            fixed((SIDE, LANES)),
            moving((1, own_rows, heads, keys)),
            fixed((4, kernels, LANES)),
            fixed((kernels, WEIGHT_PIECES * heads)),
            fixed((LANES, LANES)),
        ],
        [fixed((LANES, LANES)), fixed((3 * pos_blocks, LANES))],
        [shape_of((LANES, LANES)), shape_of((3 * pos_blocks, LANES))],
        [
            pltpu.VMEM((own_rows, keys), F32),
            pltpu.VMEM((own_rows, keys), F32),
            pltpu.VMEM((5, own_rows, LANES), F32),
            pltpu.VMEM((kernels, heads), F32),
            pltpu.VMEM((2, kernels, LANES), F32),
            pltpu.VMEM((2, 2 * LANES, LANES), F32),
        ],
        40_000_000_000,
        "kernel_gradients",
    )(span, own, other, own_line, grad_scores, tabs, grad_weights, par)
    window.middle()
    payload_blocks = window.finish()
    early_sum = everywhere_sum(
        jnp.concatenate([small, ln2_grads.reshape(-1, LANES), pos_part], axis=0)
    )
    advance([up_sum, rest_sum, early_sum], flat_array, "sums_first", (small,))

    dkv = call(
        functools.partial(key_grad_kernel, scale2, head_scale, groups, model_width),
        pairs,
        [
            own_spec,
            other_spec,
            pl.BlockSpec(
                (1, own_rows, 2 * width),
                lambda j, span: (chips, span[SPAN_CORE, 0], 0),
                pipeline_mode=pl.Buffered(1),
            ),
            moving((1, keys, width), 0, 2),
        ]
        + [fixed((own_rows, model_width + 2 * LANES))] * 14
        + [
            fixed((model_width, model_width)),
            fixed(select.shape),
            fixed(out_of_tail.shape),
            bias_spec,
        ],
        fixed((2 * model_width, own_rows)),
        shape_of((2 * model_width, own_rows), BF),
        [
            expanded,
            expanded,
            mask_scratch,
            pltpu.VMEM((keys, width), BF),
            pltpu.VMEM((keys, width), BF),
            summed,
            summed,
            pltpu.VMEM((keys, model_width + 2 * LANES), BF),
            pltpu.VMEM((2, own_rows, width), BF),
        ],
        28_000_000_000,
        "key_gradients",
        after=(*up_sum.sent, *rest_sum.sent, *early_sum.sent),
    )(span, own, other, kvq, kvq, *payload_blocks, w_out, select, out_of_tail, bias)

    advance([up_sum, rest_sum, early_sum], flat_array, "sums_second", (dkv,))
    qkv_rows = 3 * model_width // ka_count
    norm_count = model_width // LANES
    sent_rows = qkv_rows + -(-2 * norm_count // 16) * 16
    grad_tokens, projected_grads = once(
        first_norm_kernel,
        (tokens, ln1[0], dq, dkv, w_qkv, grad_mixed),
        [
            shape_of((own_rows, model_width)),
            shape_of((ka_count, sent_rows, own_rows), BF),
        ],
        [pltpu.VMEM((3 * model_width, own_rows), BF)],
        2_000_000_000,
        "first_norm",
        after=tuple(early_sum.sent),
        room=24,
    )
    grads_all = lax.all_to_all(projected_grads, "ka", split_axis=0, concat_axis=0, tiled=True)
    qkv_part, norm_part = once(
        functools.partial(qkv_grads_kernel, ka_count, gathered.masks()),
        (flat_array, grads_all, *gathered.arrays()),
        [shape_of((qkv_rows, model_width), BF), shape_of((sent_rows - qkv_rows, LANES))],
        [],
        3_000_000_000,
        "qkv_gradients",
        {0: pltpu.SMEM},
        room=24,
    )
    qkv_sum = Sum(qkv_part, [qkv_part], over("pb"))
    norm_sum = Sum(norm_part, [norm_part], over("pb"))
    advance([up_sum, rest_sum, early_sum], flat_array, "sums_third", (grads_all,))
    sums = [qkv_sum, norm_sum, up_sum, rest_sum, early_sum]
    while any(one.stages for one in sums):
        advance(sums, flat_array, "sums_last")
    joined = early_sum.total
    up_total, rest_total = up_sum.total, rest_sum.total
    norms, by_weight, by_mean, by_width, by_scale, by_shift, grad_positions = once(
        functools.partial(results_kernel, heads, types),
        (flat_array, joined, norm_sum.total),
        [
            shape_of((4, norm_count, LANES)),
            shape_of((kernels, heads)),
            shape_of((1, kernels)),
            shape_of((1, kernels)),
            shape_of((1, types)),
            shape_of((1, types)),
            shape_of((3, LANES)),
        ],
        [],
        1_000_000,
        "results",
        {0: pltpu.SMEM},
        room=16,
    )
    qkv_total = qkv_sum.total
    return (
        block_out,
        grad_tokens,
        grad_positions,
        norms[0].reshape(-1),
        norms[1].reshape(-1),
        qkv_total.T,
        by_mean.reshape(-1),
        by_width.reshape(-1),
        by_weight,
        by_scale.reshape(-1),
        by_shift.reshape(-1),
        rest_total[up_rows:].T,
        norms[2].reshape(-1),
        norms[3].reshape(-1),
        up_total.T,
        rest_total[:up_rows],
    )


def solution(mesh):
    rows = P(MESH, None)
    in_specs = (rows,) + (P(),) * 18 + (rows,)
    out_specs = (
        rows,
        rows,
        P(None, MESH),
        P(),
        P(),
        P(None, "ka"),
        P(),
        P(),
        P(),
        P(),
        P(),
        P(None, "ka"),
        P(),
        P(),
        P(None, "ka"),
        P("ka", None),
    )
    return jax.shard_map(
        on_device, mesh=mesh, in_specs=in_specs, out_specs=out_specs, check_vma=False
    )
```

```python
import functools
import math

import jax
import jax.numpy as jnp
import numpy as np
from jax import lax
from jax.experimental import pallas as pl
from jax.experimental.pallas import tpu as pltpu
from jax.sharding import PartitionSpec as P

MOL_TYPES = 128
PROT_LEN = 768
MOL_MEAN = 32

LN_EPS = 1e-05
GELU_SLOPE = math.sqrt(2.0 / math.pi)
GELU_CUBE = 0.044715
MASKED = -1e30
ROOT_TWO_PI = math.sqrt(2.0 * math.pi)
LOG2E = math.log2(math.e)
KAPPA = math.sqrt(0.5 * LOG2E)

PAD = 32
GROUP = 8
SPAN = PAD * GROUP
PIECES = 3
WEIGHT_PIECES = 2
CHUNK = 32
HEAD_ROWS = 32
BIAS_ROWS = 64
FEW = 8
MESH = ("pb", "ka")

BF = jnp.bfloat16
F32 = jnp.float32


def shifted(block, axis, distance):
    devices = range(lax.axis_size(axis))
    route = [(i - distance, i) for i in devices if i - distance in devices]
    return lax.ppermute(block, axis, route)


def core_flip(block):
    devices = range(lax.axis_size(MESH))
    return lax.ppermute(block, MESH, [(i, i ^ 1) for i in devices])


class Window:
    def __init__(self, block, sibling=None):
        devices = range(lax.axis_size(MESH))
        levels = len(devices) // 4

        def of(level, rest):
            return level % levels * 4 + rest

        one, two, far = [], [], []
        for i in devices:
            level, chip, core = i // 4, (i >> 1) & 1, i & 1
            odd = level & 1
            one.append((i, of(level + (-1 if odd else 1), i % 4)))
            two.append((i, of(level + (1 if odd else -1), i % 4)))
            far.append((i, of(level + (2 if chip else -2), (1 - chip) * 2 + core)))
        self.block, self.sibling = block, sibling
        self.one = lax.ppermute(block, MESH, one)
        self.two = lax.ppermute(block, MESH, two)
        self.far = lax.ppermute(block, MESH, far)

    def middle(self):
        self.other_chip = [flip_bit(x, "ka", 1) for x in (self.block, self.one, self.two)]
        return self.other_chip

    def finish(self):
        beside, one, two = self.other_chip
        mine = [self.far, self.one, one, self.block, beside, self.two, two]
        came = [core_flip(x) for x in mine if x is not self.block]
        own = core_flip(self.block) if self.sibling is None else self.sibling
        return mine + came[:3] + [own] + came[3:]


class Gathered:
    def __init__(self, block):
        self.own, self.own_sibling = block, core_flip(block)
        self.beside = flip_bit(block, "ka", 1)

    def far(self):
        mine = jnp.stack([self.own, self.beside])
        self.groups = [
            flip_mask(mine, "ka", mask) for mask in range(4, lax.axis_size("ka"), 4)
        ]
        return self.groups

    def finish(self):
        self.beside_sibling = core_flip(self.beside)
        self.siblings = [core_flip(x) for x in self.groups]

    def arrays(self):
        return [
            *(x[None] for x in (self.own, self.own_sibling, self.beside, self.beside_sibling)),
            *self.groups,
            *self.siblings,
        ]

    def masks(self):
        far = range(4, lax.axis_size("ka"), 4)
        return [
            (0,), (1,), (2,), (3,),
            *((mask, mask + 2) for mask in far),
            *((mask + 1, mask + 3) for mask in far),
        ]


SLOTS = (
    (0, 5, 6, 3, 4, 1, 2),
    (6, 5, 4, 3, 2, 1, 0),
    (0, 1, 2, 3, 4, 5, 6),
    (2, 1, 4, 3, 6, 5, 0),
)
SPAN_FIRST, SPAN_LAST, SPAN_CORE, SPAN_CHIP, SPAN_SLOT = 0, 1, 2, 3, 4
SPAN_LOW = 16
SPAN_HIGH = 32
SPAN_ROWS = 48
LANES = 128
SIDE = 16


def flip_bit(block, axis, bit):
    devices = range(lax.axis_size(axis))
    return lax.ppermute(block, axis, [(i, i ^ (1 << bit)) for i in devices])


def bits_of(axis):
    return (lax.axis_size(axis) - 1).bit_length()


def flip_mask(block, axis, mask):
    devices = range(lax.axis_size(axis))
    return lax.ppermute(block, axis, [(i, i ^ mask) for i in devices])


class Sum:
    def __init__(self, kept, sent, stages, left=()):
        self.kept, self.sent, self.stages, self.left = kept, list(sent), list(stages), list(left)
        self.total = None

    def came(self):
        axis, bit, count = self.stages[0][:3]
        partners = range(1, 2**count)
        return [flip_mask(x, axis, p << bit) for x, p in zip(self.sent, partners, strict=True)]

    def plan(self):
        stage = self.stages.pop(0)
        if len(stage) == 4:
            return ("join",)
        if self.stages and self.stages[0][0] == "ka" and self.left:
            bit, count = self.stages[0][1] - 1, self.stages[0][2]
            self.left = [b for b in self.left if not bit <= b < bit + count]
            below = sum(1 for b in self.left if b < bit)
            return ("part", bit, count, 2 ** (len(self.left) - below), 2**below)
        return ("whole",)


def over(axis, first=0):
    return [(axis, bit, 1) for bit in range(first, bits_of(axis))]


def slices_sum(kept, sent, order):
    stages = [("ka", bit + 1, count) for bit, count in order] + over("pb")
    left = [b for bit, count in order[1:] for b in range(bit, bit + count)]
    return Sum(kept, [sent], stages, left)


def columns_sum(kept, sent, order):
    stages = [("pb", 0, 1)] + [("ka", bit + 1, count) for bit, count in order]
    left = [b for bit, count in order for b in range(bit, bit + count)]
    return Sum(kept, [sent], stages + over("pb", 1) + [("pb", 0, 1, "join")], left)


def everywhere_sum(values):
    return Sum(values, [values], over("ka") + over("pb"))


def stage_kernel(plans, counts, side_bit, flat_ref, *refs):
    flat = flat_ref[0]
    refs = list(refs)
    kept_refs = [refs.pop(0) for _ in plans]
    came_refs = [[refs.pop(0) for _ in range(count)] for count in counts]
    for plan, kept, came in zip(plans, kept_refs, came_refs):

        def total(*at):
            value = kept[at].astype(F32)
            for ref in came:
                value = value + ref[at].astype(F32)
            return value

        out = refs.pop(0)
        if plan[0] == "whole":
            out[...] = total(Ellipsis).astype(out.dtype)
        elif plan[0] == "join":
            half = kept.shape[-1]
            side = jnp.right_shift(flat, side_bit) & 1
            out[:, pl.ds(pl.multiple_of(side * half, LANES), half)] = kept[...].astype(F32)
            out[:, pl.ds(pl.multiple_of((1 - side) * half, LANES), half)] = came[0][...].astype(F32)
        else:
            _, bit, count, above, below = plan
            mine = jnp.right_shift(flat, bit + 1) & (2**count - 1)
            outs = [out] + [refs.pop(0) for _ in range(2**count - 1)]
            for i in range(above):
                for j in range(below):
                    for other, ref in enumerate(outs):
                        group = jnp.bitwise_xor(mine, other)
                        ref[i * below + j] = total((i * 2**count + group) * below + j).astype(BF)


def advance(sums, flat_array, name, after=()):
    sums = [one for one in sums if one.stages]
    if not sums:
        return
    came = [one.came() for one in sums]
    plans, shapes, sizes = [], [], []
    for one in sums:
        plan = one.plan()
        shape, dtype, size = one.kept.shape, one.kept.dtype, 1
        if plan[0] == "join":
            shape, dtype = (shape[0], 2 * shape[1]), F32
        elif plan[0] == "part":
            shape, size = (plan[3] * plan[4], *shape[1:]), 2 ** plan[2]
        elif not one.stages:
            dtype = F32
        shapes += [shape_of(shape, dtype)] * size
        plans.append(plan)
        sizes.append(size)
    results = once(
        functools.partial(stage_kernel, plans, [len(x) for x in came], bits_of("ka")),
        (flat_array, *(one.kept for one in sums), *(x for group in came for x in group)),
        shapes,
        [],
        1_000_000_000,
        name,
        {0: pltpu.SMEM},
        after=after,
        room=24,
    )
    results = list(results)
    for one, size in zip(sums, sizes):
        one.kept = results.pop(0)
        one.sent = [results.pop(0) for _ in range(size - 1)] or [one.kept]
        if not one.stages:
            one.total = one.kept
        elif one.kept.ndim == 3 and one.kept.shape[0] == 1 and one.stages[0][0] == "pb":
            one.kept = one.kept.reshape(one.kept.shape[1:])
            one.sent = [one.kept]


def layer_norm(values, ln_gain, ln_shift):
    centre = jnp.mean(values, axis=-1, keepdims=True)
    offsets = values - centre
    spread = jnp.mean(offsets * offsets, axis=-1, keepdims=True)
    return offsets * lax.rsqrt(spread + LN_EPS) * ln_gain + ln_shift


def dot_nn(left, right):
    return lax.dot_general(left, right, (((1,), (0,)), ((), ())), preferred_element_type=F32)


def dot_nt(left, right):
    return lax.dot_general(left, right, (((1,), (1,)), ((), ())), preferred_element_type=F32)


def dot_tn(left, right):
    return lax.dot_general(left, right, (((0,), (0,)), ((), ())), preferred_element_type=F32)


def select_table(head_size):
    column = np.arange(SPAN)
    source = (column // PAD) * head_size + column % PAD
    table = [
        (column[:, None] == (source + off)[None, :]) & (column % PAD < head_size)[None, :]
        for off in (0, 64)
    ]
    return np.stack(table).astype(BF)


def group_windows(groups, head_size):
    out = []
    for g in range(groups):
        start = g * GROUP * head_size
        out.append((start // LANES * LANES, (start % LANES) // 64))
    return out


def place_table(heads, head_size):
    column = np.arange(heads * PAD)
    lane = np.arange(LANES)
    return np.stack(
        [
            (lane[:, None] == (column // PAD)[None, :])
            & (column % PAD == head_size + p)[None, :]
            for p in range(PIECES)
        ]
    ).astype(BF)


def tail_tables(heads, head_size):
    lane, tail = np.arange(LANES), np.arange(2 * LANES)
    into = np.stack(
        [
            (lane[:, None] + p * heads == tail[None, :]) & (lane < heads)[:, None]
            for p in range(2 * PIECES)
        ]
    )
    column = np.arange(heads * PAD)
    piece = column % PAD - head_size
    free = (piece >= 0) & (piece < PIECES)
    lane_of = np.where(free, piece * heads + column // PAD, -1)
    out = np.stack(
        [
            (tail[:, None] == lane_of[None, :]) & free[None, :],
            (tail[:, None] - PIECES * heads == lane_of[None, :]) & free[None, :],
        ]
    )
    return into.astype(BF), out.astype(BF)


def ones_row(heads, head_size):
    column = np.arange(heads * PAD) % PAD
    return ((column >= head_size) & (column < head_size + PIECES)).astype(np.float32)[None]


def head_sum_table(heads):
    column = np.arange(heads * PAD)
    return (column[:, None] // PAD == np.arange(LANES)[None, :]).astype(BF)


def pad_columns(values, select_ref, windows):
    parts = [
        dot_nn(values[:, start : start + SPAN], select_ref[kind]).astype(BF)
        for start, kind in windows
    ]
    return jnp.concatenate(parts, axis=1)


def drop_columns(values, select_ref, windows):
    tiles = {}
    for g, (start, kind) in enumerate(windows):
        part = dot_nt(values[:, g * SPAN : (g + 1) * SPAN], select_ref[kind])
        for k in range(SPAN // LANES):
            tile = part[:, k * LANES : (k + 1) * LANES]
            at = start // LANES + k
            tiles[at] = tiles[at] + tile if at in tiles else tile
    return jnp.concatenate([tiles[at] for at in sorted(tiles)], axis=1).astype(BF)


def drop_turned(values, select_ref, windows):
    tiles = {}
    for g, (start, kind) in enumerate(windows):
        part = dot_nt(select_ref[kind], values[:, g * SPAN : (g + 1) * SPAN])
        for k in range(SPAN // LANES):
            tile = part[k * LANES : (k + 1) * LANES]
            at = start // LANES + k
            tiles[at] = tiles[at] + tile if at in tiles else tile
    return jnp.concatenate([tiles[at] for at in sorted(tiles)], axis=0).astype(BF)


def row_of(ref):
    return jnp.concatenate([ref[k : k + 1, :] for k in range(ref.shape[0])], axis=1)


def split(values, count):
    rest, out = values, []
    for _ in range(count):
        piece = rest.astype(BF)
        rest = rest - piece.astype(F32)
        out.append(piece)
    return out


def norm_parts(values):
    centre = jnp.mean(values, axis=-1, keepdims=True)
    offsets = values - centre
    spread = jnp.mean(offsets * offsets, axis=-1, keepdims=True)
    slope = lax.rsqrt(spread + LN_EPS)
    return offsets * slope, slope


def norm_back(grad, normal, slope, gain):
    inner = grad * gain
    mean = jnp.mean(inner, axis=-1, keepdims=True)
    tilt = jnp.mean(inner * normal, axis=-1, keepdims=True)
    by_gain = jnp.sum(grad * normal, axis=0, keepdims=True)
    by_shift = jnp.sum(grad, axis=0, keepdims=True)
    return slope * (inner - mean - normal * tilt), by_gain, by_shift


def stretched_of(own, other):
    delta = [own[:, i : i + 1] - other[i : i + 1, :] for i in range(3)]
    square = delta[0] * delta[0] + delta[1] * delta[1] + delta[2] * delta[2]
    dist = jnp.sqrt(square + 1.0)
    scales = own[:, 3:4] * other[3:4, :]
    stretched = scales * dist + own[:, 4:5] + other[4:5, :]
    return delta, dist, scales, stretched


def mask_of(own, other, key_is_own):
    same = own[:, 5:6] == other[5:6, :]
    itself = own[:, 7:8] == other[7:8, :]
    is_open = (own[:, 6:7] > 0.5) if key_is_own else (other[6:7, :] > 0.5)
    return jnp.where(same & (is_open | itself), 0.0, MASKED)


def line_atoms(lines):
    line = lax.broadcasted_iota(jnp.int32, (lines, lines // GROUP), 0)
    atom = lax.broadcasted_iota(jnp.int32, (lines, lines // GROUP), 1)
    return jnp.where(line // GROUP == atom, 1.0, 0.0).astype(BF)


def line_heads(lines):
    line = lax.broadcasted_iota(jnp.int32, (lines, SPAN), 0)
    column = lax.broadcasted_iota(jnp.int32, (lines, SPAN), 1)
    return jnp.where(column // PAD == line % GROUP, 1.0, 0.0)


def expand_into(out_ref, padded, groups):
    lines = CHUNK * GROUP
    keep = line_heads(lines).astype(BF)
    spread = line_atoms(lines)
    for g in range(groups):
        for i in range(padded.shape[0] // CHUNK):
            part = padded[i * CHUNK : (i + 1) * CHUNK, g * SPAN : (g + 1) * SPAN]
            out_ref[g, i * lines : (i + 1) * lines, :] = dot_nn(spread, part).astype(BF) * keep


def collapse(values):
    lines = values.shape[0]
    kept = values * line_heads(lines)
    high = kept.astype(BF)
    low = (kept - high.astype(F32)).astype(BF)
    line = lax.broadcasted_iota(jnp.int32, (lines // GROUP, lines), 1)
    atom = lax.broadcasted_iota(jnp.int32, (lines // GROUP, lines), 0)
    gather = jnp.where(line // GROUP == atom, 1.0, 0.0).astype(BF)
    return dot_nn(gather, high) + dot_nn(gather, low)


def fetch(span_ref, refs, out_ref):
    slot = span_ref[SPAN_SLOT + span_ref[SPAN_FIRST, 0] + pl.program_id(0), 0]
    count = len(refs) // 2
    rows = refs[0].shape[0]
    for k in range(count):

        @pl.when(slot == k)
        def _():
            out_ref[:rows] = refs[k][...]
            out_ref[rows:] = refs[count + k][...]


def spots_of(span_ref, rows):
    core = span_ref[SPAN_CORE, 0]
    return [pl.ds(pl.multiple_of(at * rows, rows), rows) for at in (core, 1 - core)]


def spread_mask(mask_ref, mask):
    mask_ref[...] = jnp.broadcast_to(mask[:, None, :], mask_ref.shape)


def reaches(span_ref, first, last, low, high):
    return (span_ref[SPAN_LOW + first, 0] <= high) & (span_ref[SPAN_HIGH + last, 0] >= low)


def head_steps(span_ref, rows, step):
    pair = span_ref[SPAN_FIRST, 0] + pl.program_id(0)
    few = HEAD_ROWS // FEW
    last = rows // FEW - 1
    whole = reaches(span_ref, last, 0, 2 * pair, 2 * pair + 1)

    @pl.when(whole)
    def _():
        step(0, rows)

    @pl.when(jnp.logical_not(whole))
    def _():
        def one(i, carry):
            @pl.when(reaches(span_ref, i * few, i * few + few - 1, 2 * pair, 2 * pair + 1))
            def _():
                step(pl.multiple_of(i * HEAD_ROWS, HEAD_ROWS), HEAD_ROWS)

            return carry

        lax.fori_loop(0, rows // HEAD_ROWS, one, 0)


def kernel_steps(span_ref, first, rows, size, step, skipped):
    pair = span_ref[SPAN_FIRST, 0] + pl.program_id(0)
    few = size // FEW

    def one(i, carry):
        at = pl.multiple_of(i * size, size)
        chunk = first // FEW + i * few
        for half in range(2):
            block = 2 * pair + half
            needed = reaches(span_ref, chunk, chunk + few - 1, block, block)

            @pl.when(needed)
            def _():
                step(at, half)

            @pl.when(jnp.logical_not(needed))
            def _():
                skipped(at, half)

        return carry

    lax.fori_loop(0, rows // size, one, 0)


def side_kernel(
    atoms_blocks,
    flat_ref,
    pos_ref,
    item_ref,
    open_ref,
    type_ref,
    length_ref,
    table_ref,
    means_ref,
    widths_ref,
    kw_ref,
    span_ref,
    other_ref,
    own_ref,
    line_ref,
    tab_ref,
    gw_ref,
    kwt_ref,
    par_ref,
):
    flat = flat_ref[0]
    chips = len(SLOTS[0]) // 2
    first_block = flat // 2 * 2 - 2 * chips
    ids = lax.broadcasted_iota(jnp.int32, (LANES, LANES), 0).astype(F32)
    lane = lax.broadcasted_iota(jnp.int32, (1, LANES), 1)
    tables = []
    for k in range(table_ref.shape[0] // 2):
        rows = split(table_ref[2 * k : 2 * k + 1, :], PIECES)
        rows += split(table_ref[2 * k + 1 : 2 * k + 2, :], PIECES)
        rows += [jnp.zeros((2, LANES), BF)]
        tables.append(jnp.concatenate([row.astype(F32) for row in rows], axis=0).astype(BF))
    flags = [
        jnp.broadcast_to(
            jnp.where(length_ref[k : k + 1, :] > 2 * MOL_MEAN, float(MOL_TYPES), 0.0), (8, LANES)
        ).astype(BF)
        for k in range(length_ref.shape[0])
    ]
    for b in range(other_ref.shape[1] // LANES):
        block = first_block + b
        inside = (block >= 0) & (block < atoms_blocks)
        source = jnp.clip(block, 0, atoms_blocks - 1)
        at = pl.ds(pl.multiple_of(source * LANES, LANES), LANES)
        item = jnp.where(inside, item_ref[pl.ds(source, 1), :].astype(F32), -1.0)
        kind = type_ref[pl.ds(source, 1), :].astype(F32)
        for k, flag in enumerate(flags):
            onehot = jnp.where(ids + float(k * LANES) == item, 1.0, 0.0).astype(BF)
            kind = kind + dot_nn(flag, onehot)[0:1, :]
        found = jnp.zeros((8, LANES), F32)
        for k, table in enumerate(tables):
            onehot = jnp.where(ids + float(k * LANES) == kind, 1.0, 0.0).astype(BF)
            found = found + dot_nn(table, onehot)
        rows = [pos_ref[k : k + 1, at] for k in range(3)]
        rows += [found[0:1] + found[1:2] + found[2:3], found[3:4] + found[4:5] + found[5:6]]
        rows += [item, open_ref[pl.ds(source, 1), :].astype(F32)]
        rows += [(block * LANES + lane).astype(F32), kind]
        rows += [jnp.zeros((SIDE - 9, LANES), F32)]
        side = jnp.concatenate(rows, axis=0)
        other_ref[:, b * LANES : (b + 1) * LANES] = side

        @pl.when(block == flat)
        def _():
            line_ref[...] = side

    line = line_ref[...]
    turned = jnp.transpose(
        jnp.concatenate([line, jnp.zeros((LANES - SIDE, LANES), F32)], axis=0)
    )
    own_ref[...] = turned
    chunks = LANES // FEW
    item_column = jnp.broadcast_to(own_ref[:, 5:6], (LANES, LANES))
    par_ref[...] = item_column
    first_item = par_ref[pl.ds(0, chunks, stride=FEW), :]
    last_item = par_ref[pl.ds(FEW - 1, chunks, stride=FEW), :]

    def count(k, carry):
        row = item_ref[pl.ds(k, 1), :].astype(F32)
        below, upto = carry
        return (
            below + jnp.where(row < first_item, 1.0, 0.0),
            upto + jnp.where(row <= last_item, 1.0, 0.0),
        )

    zero = jnp.zeros((chunks, LANES), F32)
    below, upto = lax.fori_loop(0, atoms_blocks, count, (zero, zero))
    below = jnp.sum(below, axis=1, keepdims=True).astype(jnp.int32)
    upto = jnp.sum(upto, axis=1, keepdims=True).astype(jnp.int32)
    low = jnp.right_shift(below - first_block * LANES, 7)
    high = jnp.right_shift(upto - 1 - first_block * LANES, 7)
    span_ref[SPAN_LOW : SPAN_LOW + chunks, :] = jnp.broadcast_to(low, (chunks, LANES))
    span_ref[SPAN_HIGH : SPAN_HIGH + chunks, :] = jnp.broadcast_to(high, (chunks, LANES))
    row = lax.broadcasted_iota(jnp.int32, (SPAN_LOW, LANES), 0)
    kind = (flat // 2) % 4
    head = jnp.where(row == SPAN_FIRST, jnp.right_shift(low[0:1, :], 1), 0)
    head = head + jnp.where(row == SPAN_LAST, jnp.right_shift(high[chunks - 1 :, :], 1), 0)
    head = head + jnp.where(row == SPAN_CORE, flat % 2, 0)
    head = head + jnp.where(row == SPAN_CHIP, flat // 2, 0)
    for k, slots in enumerate(zip(*SLOTS)):
        slot = sum(jnp.where(kind == which, at, 0) for which, at in enumerate(slots))
        head = head + jnp.where(row == SPAN_SLOT + k, slot, 0)
    span_ref[:SPAN_LOW, :] = head

    def column_of(ref):
        return jnp.transpose(jnp.broadcast_to(ref[...], (LANES, LANES)))

    means, widths = column_of(means_ref), column_of(widths_ref)
    peaks = 1.0 / (ROOT_TWO_PI * widths)
    bend = -(KAPPA * KAPPA) / (widths * widths)
    tab_ref[0] = means
    tab_ref[1] = KAPPA / widths
    tab_ref[2] = LOG2E * jnp.log(peaks)
    tab_ref[3] = bend
    turned_weights = kw_ref[...].astype(F32)
    heads = turned_weights.shape[0]
    filler = jnp.zeros((LANES - heads, LANES), F32)
    wide = jnp.transpose(jnp.concatenate([turned_weights, filler], axis=0))
    weights = wide[:, :heads]
    scaled = weights * (peaks / (widths * widths))[:, :heads]
    gw_ref[...] = jnp.concatenate(split(scaled, WEIGHT_PIECES), axis=1)
    kwt_ref[...] = kw_ref[...]
    lanes = lax.broadcasted_iota(jnp.int32, (LANES, LANES), 1)
    par = wide + jnp.where(lanes == heads, peaks, 0.0)
    par_ref[...] = par + jnp.where(lanes == heads + 1, 1.0 / widths, 0.0)


def bias_kernel(span_ref, own_ref, other_ref, tab_ref, kwt_ref, out_ref, str_ref):
    rows, keys = str_ref.shape
    kernels = tab_ref.shape[1]
    heads = kwt_ref.shape[0]
    half_keys = keys // 2
    str_ref[...] = stretched_of(own_ref[...], other_ref[...])[3]

    def step(at, half):
        columns = slice(half * half_keys, (half + 1) * half_keys)
        block = str_ref[pl.ds(at, BIAS_ROWS), columns]
        for r in range(0, BIAS_ROWS, 2):
            parts = []
            for q in range(2):
                line = jnp.broadcast_to(block[r + q : r + q + 1], (kernels, half_keys))
                z = (line - tab_ref[0]) * tab_ref[1]
                parts.append(jnp.exp2(tab_ref[2] - z * z).astype(BF))
            result = dot_nn(kwt_ref[...], jnp.concatenate(parts, axis=1)) * LOG2E
            out_ref[0, at + r, :, columns] = result[:, :half_keys]
            out_ref[0, at + r + 1, :, columns] = result[:, half_keys:]

    def skipped(at, half):
        columns = slice(half * half_keys, (half + 1) * half_keys)
        out_ref[0, pl.ds(at, BIAS_ROWS), :, columns] = jnp.zeros((BIAS_ROWS, heads, half_keys), F32)

    kernel_steps(span_ref, 0, rows, BIAS_ROWS, step, skipped)


def forward_kernel(
    scale2,
    groups,
    span_ref,
    own_ref,
    other_ref,
    *refs,
):
    token_refs, refs = refs[:14], refs[14:]
    gain_ref, shift_ref, w_ref, select_ref, ones_ref, place_ref, bias_ref, *refs = refs
    att_ref, qaug_ref, lse_ref, kvq_ref, *refs = refs
    qexp_ref, mask_ref, max_ref, sum_ref, acc_ref, lane_ref, both_ref = refs
    step = pl.program_id(0)
    width = groups * SPAN
    tok_ref = token_refs[3]
    rows, model_width = tok_ref.shape
    windows = group_windows(groups, model_width // (groups * GROUP))
    gain, shift = row_of(gain_ref), row_of(shift_ref)

    @pl.when(step == 0)
    def _():
        normed = layer_norm(tok_ref[...].astype(F32), gain, shift).astype(BF)
        query = dot_nn(normed, w_ref[:, :model_width]).astype(BF)
        query = pad_columns(query, select_ref, windows)
        qaug_ref[...] = query
        expand_into(qexp_ref, query, groups)
        max_ref[...] = jnp.full(max_ref.shape, 2.0 * MASKED, F32)
        sum_ref[...] = jnp.zeros(sum_ref.shape, F32)
        acc_ref[...] = jnp.zeros(acc_ref.shape, F32)

    fetch(span_ref, token_refs, both_ref)
    normed = layer_norm(both_ref[...].astype(F32), gain, shift).astype(BF)
    spots = spots_of(span_ref, rows)

    for part in range(3):
        source = (part + 1) % 3 * model_width
        value = dot_nn(normed, w_ref[:, source : source + model_width]).astype(BF)
        value = pad_columns(value, select_ref, windows)
        if part < 2:
            value = value + ones_ref[...].astype(BF)
        for k in range(2):
            kvq_ref[0, spots[k], part * width : (part + 1) * width] = (
                value[k * rows : (k + 1) * rows]
            )
    spread_mask(mask_ref, mask_of(own_ref[...], other_ref[...], False))

    def chunk_step(at, count):
        lines = pl.ds(pl.multiple_of(at * GROUP, HEAD_ROWS * GROUP), count * GROUP)
        mask = mask_ref[pl.ds(at, count)]
        for g in range(groups):
            columns = slice(g * SPAN, (g + 1) * SPAN)
            dots = dot_nt(qexp_ref[g, lines, :], kvq_ref[0, :, columns])
            bias = bias_ref[0, pl.ds(at, count), g * GROUP : (g + 1) * GROUP, :] + mask
            scores = dots * scale2 + bias.reshape(dots.shape)
            old = max_ref[g, lines, :]
            top = jnp.maximum(scores[:, :128], scores[:, 128:])
            new = jnp.maximum(old, jnp.max(top, axis=1, keepdims=True))
            alpha = jnp.exp2(old - new)
            low = jnp.exp2(scores[:, :128] - new)
            high = jnp.exp2(scores[:, 128:] - new)
            max_ref[g, lines, :] = new
            sum_ref[g, lines, :] = sum_ref[g, lines, :] * alpha + (low + high)
            probs = jnp.concatenate([low, high], axis=1).astype(BF)
            values = dot_nn(probs, kvq_ref[0, :, width + g * SPAN : width + (g + 1) * SPAN])
            wide = jnp.concatenate([alpha, alpha], axis=1)
            acc_ref[g, lines, :] = acc_ref[g, lines, :] * wide + values

    head_steps(span_ref, rows, chunk_step)

    @pl.when(step == span_ref[SPAN_LAST, 0] - span_ref[SPAN_FIRST, 0])
    def _():
        lane = lax.broadcasted_iota(jnp.int32, (GROUP, 128), 1)
        head = lax.broadcasted_iota(jnp.int32, (GROUP, 128), 0)

        def finish(i, carry):
            at = pl.multiple_of(i * CHUNK, CHUNK)
            lines = pl.ds(pl.multiple_of(i * CHUNK * GROUP, CHUNK * GROUP), CHUNK * GROUP)
            lanes = jnp.zeros((CHUNK, 128), F32)
            for g in range(groups):
                total = jnp.sum(sum_ref[g, lines, :], axis=1, keepdims=True)
                attended = collapse(acc_ref[g, lines, :] / total)
                att_ref[pl.ds(at, CHUNK), g * SPAN : (g + 1) * SPAN] = attended
                lse = max_ref[g, lines, :] + jnp.log(total) * LOG2E
                own_lane = jnp.where(lane == head + g * GROUP, 1.0, 0.0)
                lanes = lanes + jnp.sum(
                    lse.reshape(CHUNK, GROUP, 128) * own_lane[None], axis=1
                )
            lane_ref[pl.ds(at, CHUNK), :] = lanes
            return carry

        lax.fori_loop(0, rows // CHUNK, finish, 0)
        rest = lane_ref[...] * (-1.0 / scale2)
        query = qaug_ref[...].astype(F32)
        for p in range(PIECES):
            piece = rest.astype(BF)
            rest = rest - piece.astype(F32)
            lse_ref[p] = piece
            query = query + dot_nn(piece, place_ref[p])
        qaug_ref[...] = query.astype(BF)


def query_grad_kernel(
    scale2,
    head_scale,
    groups,
    span_ref,
    own_ref,
    other_ref,
    qaug_ref,
    doaug_ref,
    kv_ref,
    bias_ref,
    select_ref,
    dq_ref,
    ds_ref,
    qexp_ref,
    doexp_ref,
    mask_ref,
    dqacc_ref,
    low_ref,
):
    step = pl.program_id(0)
    width = groups * SPAN
    rows, keys = own_ref.shape[0], other_ref.shape[1]
    windows = group_windows(groups, dq_ref.shape[0] // (groups * GROUP))

    @pl.when(step == 0)
    def _():
        expand_into(qexp_ref, qaug_ref[...], groups)
        expand_into(doexp_ref, doaug_ref[...], groups)
        dqacc_ref[...] = jnp.zeros(dqacc_ref.shape, F32)

    spread_mask(mask_ref, mask_of(own_ref[...], other_ref[...], False))

    def chunk_step(at, count):
        lines = pl.ds(pl.multiple_of(at * GROUP, HEAD_ROWS * GROUP), count * GROUP)
        mask = mask_ref[pl.ds(at, count)]
        waiting = []
        for g in range(groups):
            key_block = kv_ref[0, :, g * SPAN : (g + 1) * SPAN]
            value_block = kv_ref[0, :, width + g * SPAN : width + (g + 1) * SPAN]
            dots = dot_nt(qexp_ref[g, lines, :], key_block)
            grads = dot_nt(doexp_ref[g, lines, :], value_block)
            bias = bias_ref[0, pl.ds(at, count), g * GROUP : (g + 1) * GROUP, :] + mask
            probs = jnp.exp2(dots * scale2 + bias.reshape(dots.shape))
            grad_scores = probs * grads
            dqacc_ref[g, lines, :] += dot_nn(grad_scores.astype(BF), key_block)
            waiting.append(grad_scores.reshape(count, GROUP, keys))
            if len(waiting) == 2:
                ds_ref[0, pl.ds(at, count), (g - 1) * GROUP : (g + 1) * GROUP, :] = (
                    jnp.concatenate(waiting, axis=1).astype(BF)
                )
                waiting = []

    head_steps(span_ref, rows, chunk_step)

    @pl.when(step == span_ref[SPAN_LAST, 0] - span_ref[SPAN_FIRST, 0])
    def _():
        def finish(i, carry):
            at = pl.multiple_of(i * CHUNK, CHUNK)
            lines = pl.ds(pl.multiple_of(i * CHUNK * GROUP, CHUNK * GROUP), CHUNK * GROUP)
            for g in range(groups):
                value = collapse(dqacc_ref[g, lines, :]) * head_scale
                low_ref[pl.ds(at, CHUNK), g * SPAN : (g + 1) * SPAN] = value.astype(BF)
            return carry

        lax.fori_loop(0, rows // CHUNK, finish, 0)
        dq_ref[...] = drop_turned(low_ref[...], select_ref, windows)


def phi_grad_kernel(
    first_row,
    span_ref,
    own_ref,
    other_ref,
    line_ref,
    ds_ref,
    tab_ref,
    kw_ref,
    par_ref,
    small_ref,
    pos_ref,
    str_ref,
    gs_ref,
    own_acc_ref,
    gkw_ref,
    moment_ref,
    type_ref,
):
    step = pl.program_id(0)
    rows, keys = str_ref.shape
    kernels = tab_ref.shape[1]
    heads = gkw_ref.shape[1]
    blocks = pos_ref.shape[0] // 3
    pair_block = 2 * (span_ref[SPAN_CHIP, 0] + span_ref[SPAN_FIRST, 0] + step)

    @pl.when(step == 0)
    def _():
        gkw_ref[...] = jnp.zeros(gkw_ref.shape, F32)
        moment_ref[...] = jnp.zeros(moment_ref.shape, F32)
        own_acc_ref[...] = jnp.zeros(own_acc_ref.shape, F32)
        pos_ref[...] = jnp.zeros(pos_ref.shape, F32)
        type_ref[...] = jnp.zeros(type_ref.shape, F32)

    def add_types(kind, by_scale, by_shift):
        count = type_ref.shape[1]
        onehot = lax.broadcasted_iota(jnp.int32, (count, LANES), 0).astype(F32) == kind
        type_ref[0] += jnp.where(onehot, by_scale, 0.0)
        type_ref[1] += jnp.where(onehot, by_shift, 0.0)

    own, other = own_ref[first_row : first_row + rows, :], other_ref[...]
    str_ref[...] = stretched_of(own, other)[3]

    half_keys = keys // 2

    def pair_step(at, half):
        columns = slice(half * half_keys, (half + 1) * half_keys)
        block = str_ref[pl.ds(at, CHUNK), columns]
        first = second = weights = None
        lines = []
        for r in range(0, CHUNK, 2):
            low = jnp.concatenate([ds_ref[0, at + r + q, :, columns] for q in range(2)], axis=1)
            dphi = dot_nn(kw_ref[...], jnp.concatenate([low] * WEIGHT_PIECES, axis=0))
            phis = []
            for q in range(2):
                away = jnp.broadcast_to(block[r + q : r + q + 1], (kernels, half_keys)) - tab_ref[0]
                phi = jnp.exp2(away * away * tab_ref[3])
                phis.append(phi.astype(BF))
                moved = dphi[:, q * half_keys : (q + 1) * half_keys] * phi * away
                bent = moved * away
                first = moved if first is None else first + moved
                second = bent if second is None else second + bent
                lines.append(jnp.sum(moved, axis=0, keepdims=True))
            part = dot_nt(jnp.concatenate(phis, axis=1), low)
            weights = part if weights is None else weights + part
        moment_ref[0] += first
        moment_ref[1] += second
        gs_ref[pl.ds(at, CHUNK), columns] = jnp.concatenate(lines, axis=0)
        gkw_ref[...] += weights

    def skipped(at, half):
        columns = slice(half * half_keys, (half + 1) * half_keys)
        gs_ref[pl.ds(at, CHUNK), columns] = jnp.zeros((CHUNK, half_keys), F32)

    kernel_steps(span_ref, first_row, rows, CHUNK, pair_step, skipped)

    delta, dist, scales, _ = stretched_of(own, other)
    grad = -gs_ref[...]
    by_scale = grad * dist
    pull = grad * scales / dist
    terms = [pull * delta[0], pull * delta[1], pull * delta[2], by_scale * other[3:4, :], grad]
    for k, term in enumerate(terms):
        own_acc_ref[k] += term[:, :128] + term[:, 128:]
    for half in range(2):
        part = slice(half * LANES, (half + 1) * LANES)
        for k in range(3):
            spot = pl.ds(k * blocks + pair_block + half, 1)
            pos_ref[spot, :] += -jnp.sum(terms[k][:, part], axis=0, keepdims=True)
        add_types(
            other[8:9, part],
            jnp.sum(by_scale[:, part] * own[:, 3:4], axis=0, keepdims=True),
            jnp.sum(grad[:, part], axis=0, keepdims=True),
        )

    @pl.when(step == span_ref[SPAN_LAST, 0] - span_ref[SPAN_FIRST, 0])
    def _():
        lane = lax.broadcasted_iota(jnp.int32, (rows, LANES), 1)
        total = jnp.zeros((rows, LANES), F32)
        for k in range(5):
            column = jnp.sum(own_acc_ref[k], axis=1, keepdims=True)
            total = total + jnp.where(lane == k, column, 0.0)
        rest = [jnp.zeros((count, LANES), F32) for count in (first_row, LANES - first_row - rows)]
        total = jnp.concatenate([x for x in (rest[0], total, rest[1]) if x.shape[0]], axis=0)
        turned = jnp.transpose(total)
        own_block = 2 * (span_ref[SPAN_CHIP, 0] + len(SLOTS[0]) // 2) + span_ref[SPAN_CORE, 0]
        for k in range(3):
            pos_ref[pl.ds(k * blocks + own_block, 1), :] += turned[k : k + 1, :]
        add_types(line_ref[8:9, :], turned[3:4, :], turned[4:5, :])

        par = par_ref[...]
        by_weight = gkw_ref[...] * par[:, heads : heads + 1]
        plain = jnp.sum(by_weight * par[:, :heads], axis=1, keepdims=True)
        by_mean = jnp.sum(moment_ref[0], axis=1, keepdims=True)
        by_width = jnp.sum(moment_ref[1], axis=1, keepdims=True) - plain
        columns = [by_mean, by_width * par[:, heads + 1 : heads + 2]]
        low, high = slice(0, LANES), slice(LANES, 2 * LANES)
        for part in (low, high):
            for k in range(2):
                columns.append(jnp.sum(type_ref[k, part, :], axis=1, keepdims=True))
        lane = lax.broadcasted_iota(jnp.int32, (LANES, LANES), 1)
        wide = jnp.concatenate([by_weight, jnp.zeros((LANES, LANES - heads), F32)], axis=1)
        for k, column in enumerate(columns):
            wide = wide + jnp.where(lane == heads + k, column, 0.0)
        small_ref[...] = wide


def middle_kernel(
    groups,
    tile,
    flat_ref,
    tok_ref,
    att_ref,
    lse_ref,
    gain_ref,
    shift_ref,
    cot_ref,
    wout_hbm,
    wup_hbm,
    wdown_hbm,
    select_ref,
    place_ref,
    sum_ref,
    into_ref,
    out_ref,
    gmix_ref,
    doaug_ref,
    payload_ref,
    attlow_ref,
    normed_ref,
    mine_ref,
    theirs_ref,
    lngrad_ref,
    wout_ref,
    wup_ref,
    wdown_ref,
    down_ref,
    back_ref,
    wout_sem,
    tile_sems,
):
    rows, model_width = tok_ref.shape
    width = groups * SPAN
    windows = group_windows(groups, model_width // (groups * GROUP))
    tiles = wup_ref.shape[1] // tile
    piece = mine_ref.shape[2]
    core = flat_ref[0] % 2

    def tile_copies(t):
        spot = pl.ds(pl.multiple_of(t * tile, LANES), tile)
        return (
            pltpu.make_async_copy(wup_hbm.at[:, spot], wup_ref.at[:, spot], tile_sems.at[0, t]),
            pltpu.make_async_copy(wdown_hbm.at[spot, :], wdown_ref.at[spot, :], tile_sems.at[1, t]),
        )

    first = pltpu.make_async_copy(wout_hbm, wout_ref, wout_sem)
    first.start()
    for t in range(tiles):
        for copy in tile_copies(t):
            copy.start()

    gain, shift = row_of(gain_ref), row_of(shift_ref)
    cotangent = cot_ref[...]
    attended = att_ref[...]
    attended_low = drop_columns(attended.astype(BF), select_ref, windows)
    attlow_ref[...] = attended_low
    first.wait()
    mixed = tok_ref[...].astype(F32) + dot_nn(attended_low, wout_ref[...])
    normal, slope = norm_parts(mixed)
    normed_ref[...] = (normal * gain + shift).astype(BF)
    down_ref[...] = mixed
    back_ref[...] = jnp.zeros(back_ref.shape, F32)

    def step(t, carry):
        for copy in tile_copies(t):
            copy.wait()
        spot = pl.ds(pl.multiple_of(t * tile, LANES), tile)
        up = dot_nn(normed_ref[...], wup_ref[:, spot])
        grad_hidden = dot_nt(cotangent, wdown_ref[spot, :])
        square = up * up
        bent = jnp.tanh(GELU_SLOPE * (up * (1.0 + GELU_CUBE * square)))
        gate = 0.5 * (1.0 + bent)
        inner = GELU_SLOPE * (1.0 + 3.0 * GELU_CUBE * square)
        hidden = (up * gate).astype(BF)
        grad_up = (grad_hidden * (gate + 0.5 * up * (1.0 - bent * bent) * inner)).astype(BF)
        for kind, value in enumerate((grad_up, hidden)):
            value = jnp.transpose(value.astype(F32)).astype(BF)
            for q in range(tile // piece):
                part = value[q * piece : (q + 1) * piece]
                at = t * (tile // piece // 2) + q // 2

                @pl.when(core == q % 2)
                def _():
                    mine_ref[kind, at] = part

                @pl.when(core != q % 2)
                def _():
                    theirs_ref[kind, at] = part

        down_ref[...] += dot_nn(hidden, wdown_ref[spot, :])
        back_ref[...] += dot_nt(grad_up, wup_ref[:, spot])
        return carry

    lax.fori_loop(0, tiles, step, 0)
    out_ref[...] = down_ref[...].astype(BF)
    back, by_gain, by_shift = norm_back(back_ref[...], normal, slope, gain)
    lngrad_ref[...] = jnp.concatenate([by_gain, by_shift], axis=0)
    grad_mixed = cotangent.astype(F32) + back
    gmix_ref[...] = grad_mixed
    grad_low = grad_mixed.astype(BF)
    grad_attended = dot_nt(grad_low, wout_ref[...]).astype(BF)
    padded = pad_columns(grad_attended, select_ref, windows).astype(F32)
    high, low = split(padded * attended, 2)
    delta = dot_nn(high, sum_ref[...]) + dot_nn(low, sum_ref[...])
    pieces = split(-delta, PIECES)
    tail = jnp.zeros((rows, 2 * LANES), F32)
    for p in range(PIECES):
        padded = padded + dot_nn(pieces[p], place_ref[p])
        tail = tail + dot_nn(lse_ref[p], into_ref[p]) + dot_nn(pieces[p], into_ref[PIECES + p])
    doaug_ref[...] = padded.astype(BF)
    payload_ref[:, :model_width] = grad_low
    payload_ref[:, model_width:] = tail.astype(BF)


def weight_grads_kernel(
    ka_count,
    flat_ref,
    mine_ref,
    came_ref,
    normed_ref,
    normed_came_ref,
    cot_ref,
    cot_came_ref,
    attlow_ref,
    attlow_came_ref,
    payload_ref,
    payload_came_ref,
    up_kept_ref,
    up_sent_ref,
    rest_kept_ref,
    rest_sent_ref,
    product_ref,
):
    flat = flat_ref[0]
    core, bit, side = flat % 2, (flat // 2) % 2, (flat // ka_count) % 2
    model_width = normed_ref.shape[1]
    rows = up_kept_ref.shape[1]
    half = model_width // 2
    slices = up_kept_ref.shape[0] * 2
    out_rows = model_width // ka_count
    normed = jnp.concatenate([normed_ref[...], normed_came_ref[...]], axis=0)
    cotangent = jnp.concatenate([cot_ref[...], cot_came_ref[...]], axis=0)

    def columns(which):
        return pl.ds(pl.multiple_of(which * half, LANES), half)

    def step(m, carry):
        both = jnp.concatenate([mine_ref[0, m], came_ref[0, m]], axis=1)
        value = dot_nn(both, normed).astype(BF)

        @pl.when(m % 2 == bit)
        def _():
            up_kept_ref[m // 2] = value

        @pl.when(m % 2 != bit)
        def _():
            up_sent_ref[m // 2] = value

        both = jnp.concatenate([mine_ref[1, m], came_ref[1, m]], axis=1)
        product_ref[:rows, :] = dot_nn(both, cotangent)
        rest_kept_ref[m, :rows, :] = product_ref[:rows, columns(side)].astype(BF)
        rest_sent_ref[m, :rows, :] = product_ref[:rows, columns(1 - side)].astype(BF)
        return carry

    lax.fori_loop(0, slices, step, 0)
    grads = jnp.concatenate(
        [payload_ref[:, :model_width], payload_came_ref[:, :model_width]], axis=0
    )
    attended = jnp.concatenate([attlow_ref[...], attlow_came_ref[...]], axis=0)
    product_ref[...] = dot_tn(grads, attended)

    def out_step(m, carry):
        spot = pl.ds(pl.multiple_of((2 * m + core) * out_rows, 8), out_rows)
        rest_kept_ref[m, rows:, :] = product_ref[spot, columns(side)].astype(BF)
        rest_sent_ref[m, rows:, :] = product_ref[spot, columns(1 - side)].astype(BF)
        return carry

    lax.fori_loop(0, slices, out_step, 0)


def normal_kernel(tok_ref, gain_ref, shift_ref, out_ref):
    normal, _ = norm_parts(tok_ref[...].astype(F32))
    out_ref[...] = (normal * row_of(gain_ref) + row_of(shift_ref)).astype(BF)


def qkv_grads_kernel(masks, groups, *refs):
    grads_refs, normed_refs, out_ref, norm_ref = refs[:groups], refs[groups:-2], refs[-2], refs[-1]
    columns = out_ref.shape[0]
    lefts, rights, parts = [], [], None
    for ref, group in zip(normed_refs, masks):
        for i, mask in enumerate(group):
            grads = grads_refs[mask // 4][mask % 4]
            lefts.append(grads[:columns])
            rights.append(ref[i])
            part = grads[columns:].astype(F32)
            parts = part if parts is None else parts + part
    total = None
    for i in range(0, len(lefts), 2):
        part = dot_nn(
            jnp.concatenate(lefts[i : i + 2], axis=1), jnp.concatenate(rights[i : i + 2], axis=0)
        )
        total = part if total is None else total + part
    out_ref[...] = total.astype(BF)
    norm_ref[...] = parts


def results_kernel(
    heads,
    types,
    flat_ref,
    joined_ref,
    first_ref,
    norm_ref,
    weight_ref,
    mean_ref,
    width_ref,
    scale_ref,
    shift_ref,
    pos_ref,
):
    small = joined_ref[:LANES, :]
    weight_ref[...] = small[:, :heads]
    turned = jnp.transpose(small)
    rows = [turned[heads + k : heads + k + 1, :] for k in range(6)]
    mean_ref[...] = rows[0]
    width_ref[...] = rows[1]
    scale_ref[...] = jnp.concatenate([rows[2], rows[4]], axis=1)[:, :types]
    shift_ref[...] = jnp.concatenate([rows[3], rows[5]], axis=1)[:, :types]
    count = norm_ref.shape[1]
    for k in range(2):
        norm_ref[k] = first_ref[k * count : (k + 1) * count, :]
        norm_ref[2 + k] = joined_ref[LANES + k * count : LANES + (k + 1) * count, :]
    first = LANES + 2 * count
    blocks = (joined_ref.shape[0] - first) // 3
    for k in range(3):
        spot = first + k * blocks + len(SLOTS[0]) // 2 * 2 + flat_ref[0]
        pos_ref[k : k + 1, :] = joined_ref[pl.ds(spot, 1), :]


def first_norm_kernel(
    ka_count,
    flat_ref,
    tok_ref,
    gain_ref,
    dq_ref,
    dkv_ref,
    w_ref,
    gmix_ref,
    grad_ref,
    *refs,
):
    *part_refs, joined_ref = refs
    model_width = tok_ref.shape[1]
    grad = dot_nn(w_ref[:, :model_width], dq_ref[...])
    grad = grad + dot_nn(w_ref[:, model_width:], dkv_ref[...])
    grad = jnp.transpose(grad)
    normal, slope = norm_parts(tok_ref[...].astype(F32))
    back, by_gain, by_shift = norm_back(grad, normal, slope, row_of(gain_ref))
    grad_ref[...] = gmix_ref[...] + back
    lines = [
        row[:, k : k + LANES] for row in (by_gain, by_shift) for k in range(0, model_width, LANES)
    ]
    joined_ref[:model_width, :] = dq_ref[...]
    joined_ref[model_width:, :] = dkv_ref[...]
    here = flat_ref[0] % ka_count
    rows = part_refs[0].shape[1]
    columns = 3 * model_width // ka_count
    lines.append(jnp.zeros((rows - columns - len(lines), LANES), F32))
    lines = jnp.concatenate(lines, axis=0).astype(BF)
    for ref in part_refs:
        for i in range(ka_count // 4):
            ref[i, columns:, :] = lines
    for d in range(ka_count):
        value = joined_ref[d * columns : (d + 1) * columns, :]
        differs = jnp.bitwise_xor(here, d)
        for k, ref in enumerate(part_refs):

            @pl.when(differs % 4 == k)
            def _():
                ref[differs // 4, :columns, :] = value


def regroup_kernel(*refs):
    ins, outs = refs[:4], refs[4:]
    for i, out in enumerate(outs):
        for k, ref in enumerate(ins):
            out[k] = ref[i]


def key_grad_kernel(
    scale2,
    head_scale,
    groups,
    model_width,
    span_ref,
    own_ref,
    other_ref,
    kv_ref,
    q_ref,
    *refs,
):
    payload_refs, refs = refs[:14], refs[14:]
    wout_ref, select_ref, place_ref, bias_ref, dkv_ref, kexp_ref, vexp_ref, *refs = refs
    mask_ref, qb_ref, dob_ref, dk_ref, dv_ref, both_ref, low_ref = refs
    step = pl.program_id(0)
    width = groups * SPAN
    rows = own_ref.shape[0]
    windows = group_windows(groups, model_width // (groups * GROUP))

    @pl.when(step == 0)
    def _():
        expand_into(kexp_ref, kv_ref[0, :, :width], groups)
        expand_into(vexp_ref, kv_ref[0, :, width:], groups)
        dk_ref[...] = jnp.zeros(dk_ref.shape, F32)
        dv_ref[...] = jnp.zeros(dv_ref.shape, F32)

    fetch(span_ref, payload_refs, both_ref)
    payload = both_ref[...]
    tail = payload[:, model_width:]
    grads = dot_nt(payload[:, :model_width], wout_ref[...]).astype(BF)
    grads = pad_columns(grads, select_ref, windows).astype(F32)
    grads = (grads + dot_nn(tail, place_ref[1])).astype(BF)
    shifts = dot_nn(tail, place_ref[0])
    for k, spot in enumerate(spots_of(span_ref, rows)):
        own_part = slice(k * rows, (k + 1) * rows)
        dob_ref[spot, :] = grads[own_part]
        qb_ref[spot, :] = (q_ref[0, spot, :].astype(F32) + shifts[own_part]).astype(BF)
    spread_mask(mask_ref, mask_of(own_ref[...], other_ref[...], True))

    def chunk_step(at, count):
        lines = pl.ds(pl.multiple_of(at * GROUP, HEAD_ROWS * GROUP), count * GROUP)
        mask = mask_ref[pl.ds(at, count)]
        for g in range(groups):
            query_block = qb_ref[:, g * SPAN : (g + 1) * SPAN]
            grad_block = dob_ref[:, g * SPAN : (g + 1) * SPAN]
            dots = dot_nt(kexp_ref[g, lines, :], query_block)
            grads = dot_nt(vexp_ref[g, lines, :], grad_block)
            bias = bias_ref[0, pl.ds(at, count), g * GROUP : (g + 1) * GROUP, :] + mask
            probs = jnp.exp2(dots * scale2 + bias.reshape(dots.shape))
            grad_scores = (probs * grads).astype(BF)
            dk_ref[g, lines, :] += dot_nn(grad_scores, query_block)
            dv_ref[g, lines, :] += dot_nn(probs.astype(BF), grad_block)

    head_steps(span_ref, rows, chunk_step)

    @pl.when(step == span_ref[SPAN_LAST, 0] - span_ref[SPAN_FIRST, 0])
    def _():
        def finish(i, carry):
            at = pl.multiple_of(i * CHUNK, CHUNK)
            lines = pl.ds(pl.multiple_of(i * CHUNK * GROUP, CHUNK * GROUP), CHUNK * GROUP)
            for part, (ref, scale) in enumerate(((dk_ref, head_scale), (dv_ref, 1.0))):
                for g in range(groups):
                    value = collapse(ref[g, lines, :]) * scale
                    low_ref[part, pl.ds(at, CHUNK), g * SPAN : (g + 1) * SPAN] = value.astype(BF)
            return carry

        lax.fori_loop(0, rows // CHUNK, finish, 0)
        for part in range(2):
            dkv_ref[part * model_width : (part + 1) * model_width, :] = drop_turned(
                low_ref[part], select_ref, windows
            )


def fixed(shape):
    return pl.BlockSpec(shape, lambda j, span: (0,) * len(shape), pipeline_mode=pl.Buffered(1))


def pair_at(j, span):
    return jnp.minimum(span[SPAN_FIRST, 0] + j, span[SPAN_LAST, 0])


def moving(shape, rank_at=0, last=0):
    def index(j, span):
        at = [0] * len(shape)
        at[rank_at] = pair_at(j, span)
        if last:
            at[-1] = last
        return tuple(at)

    return pl.BlockSpec(shape, index)


def call(
    kernel, steps, in_specs, out_specs, out_shapes, scratch, flops, name, after=(), carry=(), room=56
):
    extra, given = len(after) + len(carry), len(in_specs)
    single = not isinstance(out_shapes, list)
    if single:
        out_specs, out_shapes = [out_specs], [out_shapes]
    made = len(out_shapes)
    anywhere = pl.BlockSpec(memory_space=pl.ANY)

    def body(span_ref, *refs):
        @pl.when(pl.program_id(0) <= span_ref[SPAN_LAST, 0] - span_ref[SPAN_FIRST, 0])
        def _():
            outs = refs[extra + given : extra + given + made]
            kernel(
                span_ref, *refs[extra : extra + given], *outs, *refs[extra + given + made + len(carry) :]
            )

    inner = pl.pallas_call(
        body,
        grid_spec=pltpu.PrefetchScalarGridSpec(
            num_scalar_prefetch=1,
            grid=(steps,),
            in_specs=[anywhere] * extra + in_specs,
            out_specs=out_specs + [anywhere] * len(carry),
            scratch_shapes=scratch,
        ),
        out_shape=out_shapes + [shape_of(x.shape, x.dtype) for x in carry],
        input_output_aliases={1 + len(after) + k: made + k for k in range(len(carry))},
        compiler_params=pltpu.CompilerParams(
            dimension_semantics=("arbitrary",), vmem_limit_bytes=room * 1024 * 1024
        ),
        cost_estimate=pl.CostEstimate(flops=flops, bytes_accessed=20_000_000, transcendentals=0),
        name=name,
    )

    def run(span, *operands):
        results = inner(span, *after, *carry, *operands)
        return results[0] if single else results

    return run


def shape_of(shape, dtype=F32):
    return jax.ShapeDtypeStruct(shape, dtype)


def once(
    kernel, operands, out_shapes, scratch, flops, name, spaces=(), after=(), carry=(), room=56
):
    spaces = dict(spaces)
    shapes = [*out_shapes, *(shape_of(x.shape, x.dtype) for x in carry)]
    count, extra = len(operands), len(after) + len(carry)
    anywhere = pl.BlockSpec(memory_space=pl.ANY)

    def whole(shape):
        return pl.BlockSpec(shape, lambda j: (0,) * len(shape), pipeline_mode=pl.Buffered(1))

    def body(*refs):
        outs = refs[count + extra : count + extra + len(out_shapes)]
        kernel(*refs[:count], *outs, *refs[count + extra + len(shapes) :])

    results = pl.pallas_call(
        body,
        grid=(1,),
        in_specs=[
            pl.BlockSpec(memory_space=spaces[k]) if k in spaces else whole(x.shape)
            for k, x in enumerate(operands)
        ]
        + [anywhere] * extra,
        out_specs=[whole(x.shape) for x in out_shapes] + [anywhere] * len(carry),
        out_shape=shapes,
        scratch_shapes=scratch,
        input_output_aliases={
            count + len(after) + k: len(out_shapes) + k for k in range(len(carry))
        },
        compiler_params=pltpu.CompilerParams(vmem_limit_bytes=room * 1024 * 1024),
        cost_estimate=pl.CostEstimate(flops=flops, bytes_accessed=5_000_000, transcendentals=0),
        name=name,
    )(*operands, *after, *carry)
    return results


def on_device(
    tokens,
    positions,
    item_of_atom,
    item_lengths,
    atom_types,
    key_mask,
    ln1_gain,
    ln1_bias,
    w_qkv,
    kernel_means,
    kernel_widths,
    kernel_weight,
    type_scale,
    type_shift,
    w_out,
    ln2_gain,
    ln2_bias,
    w_up,
    w_down,
    out_cotangent,
):
    own_rows, model_width = tokens.shape
    assert own_rows == LANES
    kernels, heads = kernel_weight.shape
    head_size = model_width // heads
    head_scale = head_size ** (-0.5)
    scale2 = head_scale * LOG2E
    groups = heads // GROUP
    width = groups * SPAN
    ff_width = w_up.shape[1]
    ka_count = lax.axis_size("ka")
    flat = lax.axis_index("pb") * ka_count + lax.axis_index("ka")
    flat_array = flat.astype(jnp.int32).reshape(1)
    reach = (PROT_LEN + own_rows - 2) // own_rows
    chips = (reach + 1) // 2
    pairs = 2 * chips + 1
    assert pairs == len(SLOTS[0])
    keys = 2 * own_rows
    atoms = positions.shape[1]
    atoms_blocks = atoms // LANES
    types = type_scale.shape[0]
    bits = bits_of("ka") - 1
    up_order = [(0, 1), (1, 2)] + [(bit, 1) for bit in range(3, bits)]
    rest_order = [(bit, 1) for bit in range(bits)]

    window = Window(tokens)
    cotangent_came = core_flip(out_cotangent)
    ln1 = [x.reshape(-1, LANES) for x in (ln1_gain, ln1_bias)]
    ln2 = [x.reshape(-1, LANES) for x in (ln2_gain, ln2_bias)]
    (normed_own,) = once(
        normal_kernel,
        (tokens, *ln1),
        [shape_of(tokens.shape, BF)],
        [],
        1_000_000,
        "first_normal",
        room=16,
    )
    gathered = Gathered(normed_own)

    select = select_table(head_size)
    place = place_table(heads, head_size)
    into_tail, out_of_tail = tail_tables(heads, head_size)
    type_tiles = -(-types // LANES)
    tables = jnp.pad(
        jnp.stack([type_scale, type_shift]), ((0, 0), (0, type_tiles * LANES - types))
    )
    tables = tables.reshape(2, type_tiles, LANES).swapaxes(0, 1).reshape(2 * type_tiles, LANES)
    lengths = jnp.pad(item_lengths, (0, -item_lengths.shape[0] % LANES)).reshape(-1, LANES)
    span, other, own, own_line, tabs, grad_weights, weights_turned, par = once(
        functools.partial(side_kernel, atoms_blocks),
        (
            flat_array,
            positions,
            item_of_atom.reshape(-1, LANES),
            key_mask.reshape(-1, LANES),
            atom_types.reshape(-1, LANES),
            lengths,
            tables,
            kernel_means.reshape(1, LANES),
            kernel_widths.reshape(1, LANES),
            kernel_weight.T,
        ),
        [
            shape_of((SPAN_ROWS, LANES), jnp.int32),
            shape_of((SIDE, pairs * keys)),
            shape_of((own_rows, LANES)),
            shape_of((SIDE, LANES)),
            shape_of((4, kernels, LANES)),
            shape_of((kernels, WEIGHT_PIECES * heads), BF),
            shape_of((heads, kernels), BF),
            shape_of((LANES, LANES)),
        ],
        [],
        1_000_000_000,
        "sides",
        {0: pltpu.SMEM},
    )

    own_spec = fixed((own_rows, LANES))
    other_spec = moving((SIDE, keys), 1)
    bias_spec = moving((1, own_rows, heads, keys))
    bias = call(
        bias_kernel,
        pairs,
        [own_spec, other_spec, fixed((4, kernels, LANES)), fixed((heads, kernels))],
        bias_spec,
        shape_of((pairs, own_rows, heads, keys)),
        [pltpu.VMEM((own_rows, keys), F32)],
        30_000_000_000,
        "pair_bias",
        after=(window.one, window.two, normed_own),
    )(span, own, other, tabs, weights_turned)
    window.middle()
    token_blocks = window.finish()

    expanded = pltpu.VMEM((groups, own_rows * GROUP, SPAN), BF)
    summed = pltpu.VMEM((groups, own_rows * GROUP, SPAN), F32)
    mask_scratch = pltpu.VMEM((own_rows, GROUP, keys), F32)
    line_scratch = pltpu.VMEM((groups, own_rows * GROUP, LANES), F32)
    attended, q_aug, lse_pieces, kvq = call(
        functools.partial(forward_kernel, scale2, groups),
        pairs,
        [own_spec, other_spec]
        + [fixed((own_rows, model_width))] * 14
        + [
            fixed((model_width // LANES, LANES)),
            fixed((model_width // LANES, LANES)),
            fixed((model_width, 3 * model_width)),
            fixed(select.shape),
            fixed((1, width)),
            fixed(place.shape),
            bias_spec,
        ],
        [
            fixed((own_rows, width)),
            fixed((own_rows, width)),
            fixed((PIECES, own_rows, LANES)),
            moving((1, keys, 3 * width)),
        ],
        [
            shape_of((own_rows, width)),
            shape_of((own_rows, width), BF),
            shape_of((PIECES, own_rows, LANES), BF),
            shape_of((pairs, keys, 3 * width), BF),
        ],
        [
            expanded,
            mask_scratch,
            line_scratch,
            line_scratch,
            summed,
            pltpu.VMEM((own_rows, LANES), F32),
            pltpu.VMEM((keys, model_width), BF),
        ],
        25_000_000_000,
        "attention_forward",
        after=(gathered.beside,),
    )(
        span,
        own,
        other,
        *token_blocks,
        *ln1,
        w_qkv,
        select,
        ones_row(heads, head_size),
        place,
        bias,
    )

    far_rows = gathered.far()
    tile = 3 * LANES
    assert ff_width % tile == 0 and tile % (2 * ff_width // ka_count) == 0
    row_shape = shape_of((own_rows, model_width), BF)
    slices = ka_count // 2
    up_rows, out_rows = ff_width // ka_count, model_width // ka_count
    pieces = shape_of((2, slices, up_rows, own_rows), BF)
    block_out, grad_mixed, do_aug, payload, attended_low, normed_second, *parts, ln2_grads = once(
        functools.partial(middle_kernel, groups, tile),
        (
            flat_array,
            tokens,
            attended,
            lse_pieces,
            *ln2,
            out_cotangent,
            w_out,
            w_up,
            w_down,
            select,
            place,
            head_sum_table(heads),
            into_tail,
        ),
        [
            row_shape,
            shape_of((own_rows, model_width)),
            shape_of((own_rows, width), BF),
            shape_of((own_rows, model_width + 2 * LANES), BF),
            row_shape,
            row_shape,
            pieces,
            pieces,
            shape_of((2, model_width)),
        ],
        [
            pltpu.VMEM((model_width, model_width), BF),
            pltpu.VMEM((model_width, ff_width), BF),
            pltpu.VMEM((ff_width, model_width), BF),
            pltpu.VMEM((own_rows, model_width), F32),
            pltpu.VMEM((own_rows, model_width), F32),
            pltpu.SemaphoreType.DMA,
            pltpu.SemaphoreType.DMA((2, ff_width // tile)),
        ],
        10_000_000_000,
        "feed_forward",
        {0: pltpu.SMEM, 7: pl.ANY, 8: pl.ANY, 9: pl.ANY},
        after=tuple(far_rows),
    )
    came = [core_flip(x) for x in (parts[1], normed_second, attended_low, payload)]
    window = Window(payload, came[3])
    gathered.finish()
    half = model_width // 2
    up_kept, up_sent, rest_kept, rest_sent = once(
        functools.partial(weight_grads_kernel, ka_count),
        (
            flat_array,
            parts[0],
            came[0],
            normed_second,
            came[1],
            out_cotangent,
            cotangent_came,
            attended_low,
            came[2],
            payload,
            came[3],
        ),
        [shape_of((slices // 2, up_rows, model_width), BF)] * 2
        + [shape_of((slices, up_rows + out_rows, half), BF)] * 2,
        [pltpu.VMEM((model_width, model_width), F32)],
        5_000_000_000,
        "weight_gradients",
        {0: pltpu.SMEM},
    )
    up_sum = slices_sum(up_kept, up_sent, up_order)
    rest_sum = columns_sum(rest_kept, rest_sent, rest_order)

    dq, grad_scores, window.one, window.two = call(
        functools.partial(query_grad_kernel, scale2, head_scale, groups),
        pairs,
        [
            own_spec,
            other_spec,
            fixed((own_rows, width)),
            fixed((own_rows, width)),
            moving((1, keys, 2 * width)),
            bias_spec,
            fixed(select.shape),
        ],
        [fixed((model_width, own_rows)), moving((1, own_rows, heads, keys))],
        [
            shape_of((model_width, own_rows), BF),
            shape_of((pairs, own_rows, heads, keys), BF),
        ],
        [expanded, expanded, mask_scratch, summed, pltpu.VMEM((own_rows, width), BF)],
        22_000_000_000,
        "query_gradients",
        after=(*up_sum.sent, *rest_sum.sent, window.far),
        carry=(window.one, window.two),
    )(span, own, other, q_aug, do_aug, kvq, bias, select)

    pos_blocks = atoms_blocks + 4 * chips
    small, pos_part = call(
        functools.partial(phi_grad_kernel, 0),
        pairs,
        [
            own_spec,
            other_spec,
            fixed((SIDE, LANES)),
            moving((1, own_rows, heads, keys)),
            fixed((4, kernels, LANES)),
            fixed((kernels, WEIGHT_PIECES * heads)),
            fixed((LANES, LANES)),
        ],
        [fixed((LANES, LANES)), fixed((3 * pos_blocks, LANES))],
        [shape_of((LANES, LANES)), shape_of((3 * pos_blocks, LANES))],
        [
            pltpu.VMEM((own_rows, keys), F32),
            pltpu.VMEM((own_rows, keys), F32),
            pltpu.VMEM((5, own_rows, LANES), F32),
            pltpu.VMEM((kernels, heads), F32),
            pltpu.VMEM((2, kernels, LANES), F32),
            pltpu.VMEM((2, 2 * LANES, LANES), F32),
        ],
        40_000_000_000,
        "kernel_gradients",
    )(span, own, other, own_line, grad_scores, tabs, grad_weights, par)
    window.middle()
    payload_blocks = window.finish()
    early_sum = everywhere_sum(
        jnp.concatenate([small, ln2_grads.reshape(-1, LANES), pos_part], axis=0)
    )
    advance([up_sum, rest_sum, early_sum], flat_array, "sums_first", (small,))

    dkv = call(
        functools.partial(key_grad_kernel, scale2, head_scale, groups, model_width),
        pairs,
        [
            own_spec,
            other_spec,
            pl.BlockSpec(
                (1, own_rows, 2 * width),
                lambda j, span: (chips, span[SPAN_CORE, 0], 0),
                pipeline_mode=pl.Buffered(1),
            ),
            moving((1, keys, width), 0, 2),
        ]
        + [fixed((own_rows, model_width + 2 * LANES))] * 14
        + [
            fixed((model_width, model_width)),
            fixed(select.shape),
            fixed(out_of_tail.shape),
            bias_spec,
        ],
        fixed((2 * model_width, own_rows)),
        shape_of((2 * model_width, own_rows), BF),
        [
            expanded,
            expanded,
            mask_scratch,
            pltpu.VMEM((keys, width), BF),
            pltpu.VMEM((keys, width), BF),
            summed,
            summed,
            pltpu.VMEM((keys, model_width + 2 * LANES), BF),
            pltpu.VMEM((2, own_rows, width), BF),
        ],
        28_000_000_000,
        "key_gradients",
        after=(*up_sum.sent, *rest_sum.sent, *early_sum.sent),
    )(span, own, other, kvq, kvq, *payload_blocks, w_out, select, out_of_tail, bias)

    advance([up_sum, rest_sum, early_sum], flat_array, "sums_second", (dkv,))
    qkv_rows = 3 * model_width // ka_count
    norm_count = model_width // LANES
    sent_rows = qkv_rows + -(-2 * norm_count // 16) * 16
    part_shape = shape_of((ka_count // 4, sent_rows, own_rows), BF)
    grad_tokens, stay, to_core, to_chip, to_both = once(
        functools.partial(first_norm_kernel, ka_count),
        (flat_array, tokens, ln1[0], dq, dkv, w_qkv, grad_mixed),
        [shape_of((own_rows, model_width))] + [part_shape] * 4,
        [pltpu.VMEM((3 * model_width, own_rows), BF)],
        2_000_000_000,
        "first_norm",
        {0: pltpu.SMEM},
        after=tuple(early_sum.sent),
        room=24,
    )
    core_stay, core_go = core_flip(to_core), core_flip(to_both)
    chip_own, chip_core = flip_bit(to_chip, "ka", 1), flip_bit(core_go, "ka", 1)
    groups_out = once(
        regroup_kernel,
        (stay, core_stay, chip_own, chip_core),
        [shape_of((4, sent_rows, own_rows), BF)] * (ka_count // 4),
        [],
        1_000_000,
        "regroup",
        room=24,
    )
    advance([up_sum, rest_sum, early_sum], flat_array, "sums_third", (groups_out[0],))
    groups_in = [groups_out[0]] + [
        flip_mask(groups_out[i], "ka", 4 * i) for i in range(1, ka_count // 4)
    ]
    qkv_part, norm_part = once(
        functools.partial(qkv_grads_kernel, gathered.masks(), ka_count // 4),
        (*groups_in, *gathered.arrays()),
        [shape_of((qkv_rows, model_width), BF), shape_of((sent_rows - qkv_rows, LANES))],
        [],
        3_000_000_000,
        "qkv_gradients",
    )
    qkv_sum = Sum(qkv_part, [qkv_part], over("pb"))
    norm_sum = Sum(norm_part, [norm_part], over("pb"))
    advance([up_sum, rest_sum, early_sum], flat_array, "sums_fourth", (qkv_part,))
    sums = [qkv_sum, norm_sum, up_sum, rest_sum, early_sum]
    while any(one.stages for one in sums):
        advance(sums, flat_array, "sums_last")
    joined = early_sum.total
    up_total, rest_total = up_sum.total, rest_sum.total
    norms, by_weight, by_mean, by_width, by_scale, by_shift, grad_positions = once(
        functools.partial(results_kernel, heads, types),
        (flat_array, joined, norm_sum.total),
        [
            shape_of((4, norm_count, LANES)),
            shape_of((kernels, heads)),
            shape_of((1, kernels)),
            shape_of((1, kernels)),
            shape_of((1, types)),
            shape_of((1, types)),
            shape_of((3, LANES)),
        ],
        [],
        1_000_000,
        "results",
        {0: pltpu.SMEM},
        room=16,
    )
    qkv_total = qkv_sum.total
    return (
        block_out,
        grad_tokens,
        grad_positions,
        norms[0].reshape(-1),
        norms[1].reshape(-1),
        qkv_total.T,
        by_mean.reshape(-1),
        by_width.reshape(-1),
        by_weight,
        by_scale.reshape(-1),
        by_shift.reshape(-1),
        rest_total[up_rows:].T,
        norms[2].reshape(-1),
        norms[3].reshape(-1),
        up_total.T,
        rest_total[:up_rows],
    )


def solution(mesh):
    rows = P(MESH, None)
    in_specs = (rows,) + (P(),) * 18 + (rows,)
    out_specs = (
        rows,
        rows,
        P(None, MESH),
        P(),
        P(),
        P(None, "ka"),
        P(),
        P(),
        P(),
        P(),
        P(),
        P(None, "ka"),
        P(),
        P(),
        P(None, "ka"),
        P("ka", None),
    )
    return jax.shard_map(
        on_device, mesh=mesh, in_specs=in_specs, out_specs=out_specs, check_vma=False
    )
```

```python
import functools
import math

import jax
import jax.numpy as jnp
import numpy as np
from jax import lax
from jax.experimental import pallas as pl
from jax.experimental.pallas import tpu as pltpu
from jax.sharding import PartitionSpec as P

MOL_TYPES = 128
PROT_LEN = 768
MOL_MEAN = 32

LN_EPS = 1e-05
GELU_SLOPE = math.sqrt(2.0 / math.pi)
GELU_CUBE = 0.044715
MASKED = -1e30
ROOT_TWO_PI = math.sqrt(2.0 * math.pi)
LOG2E = math.log2(math.e)
KAPPA = math.sqrt(0.5 * LOG2E)

PAD = 32
GROUP = 8
SPAN = PAD * GROUP
PIECES = 3
WEIGHT_PIECES = 2
CHUNK = 32
HEAD_ROWS = 64
BIAS_ROWS = 64
FEW = 8
MESH = ("pb", "ka")

BF = jnp.bfloat16
F32 = jnp.float32


def shifted(block, axis, distance):
    devices = range(lax.axis_size(axis))
    route = [(i - distance, i) for i in devices if i - distance in devices]
    return lax.ppermute(block, axis, route)


def core_flip(block):
    devices = range(lax.axis_size(MESH))
    return lax.ppermute(block, MESH, [(i, i ^ 1) for i in devices])


class Window:
    def __init__(self, block, sibling=None):
        devices = range(lax.axis_size(MESH))
        levels = len(devices) // 4

        def of(level, rest):
            return level % levels * 4 + rest

        one, two, far = [], [], []
        for i in devices:
            level, chip, core = i // 4, (i >> 1) & 1, i & 1
            odd = level & 1
            one.append((i, of(level + (-1 if odd else 1), i % 4)))
            two.append((i, of(level + (1 if odd else -1), i % 4)))
            far.append((i, of(level + (2 if chip else -2), (1 - chip) * 2 + core)))
        self.block, self.sibling = block, sibling
        self.one = lax.ppermute(block, MESH, one)
        self.two = lax.ppermute(block, MESH, two)
        self.far = lax.ppermute(block, MESH, far)

    def middle(self):
        self.other_chip = [flip_bit(x, "ka", 1) for x in (self.block, self.one, self.two)]
        return self.other_chip

    def finish(self):
        beside, one, two = self.other_chip
        mine = [self.far, self.one, one, self.block, beside, self.two, two]
        came = [core_flip(x) for x in mine if x is not self.block]
        own = core_flip(self.block) if self.sibling is None else self.sibling
        return mine + came[:3] + [own] + came[3:]


class Gathered:
    def __init__(self, block):
        self.own, self.own_sibling = block, core_flip(block)
        self.beside = flip_bit(block, "ka", 1)

    def far(self):
        mine = jnp.stack([self.own, self.beside])
        self.groups = [
            flip_mask(mine, "ka", mask) for mask in range(4, lax.axis_size("ka"), 4)
        ]
        return self.groups

    def finish(self):
        self.beside_sibling = core_flip(self.beside)
        self.siblings = [core_flip(x) for x in self.groups]

    def arrays(self):
        return [
            *(x[None] for x in (self.own, self.own_sibling, self.beside, self.beside_sibling)),
            *self.groups,
            *self.siblings,
        ]

    def masks(self):
        far = range(4, lax.axis_size("ka"), 4)
        return [
            (0,), (1,), (2,), (3,),
            *((mask, mask + 2) for mask in far),
            *((mask + 1, mask + 3) for mask in far),
        ]


SLOTS = (
    (0, 5, 6, 3, 4, 1, 2),
    (6, 5, 4, 3, 2, 1, 0),
    (0, 1, 2, 3, 4, 5, 6),
    (2, 1, 4, 3, 6, 5, 0),
)
SPAN_FIRST, SPAN_LAST, SPAN_CORE, SPAN_CHIP, SPAN_SLOT = 0, 1, 2, 3, 4
SPAN_LOW = 16
SPAN_HIGH = 32
SPAN_ROWS = 48
LANES = 128
SIDE = 16


def flip_bit(block, axis, bit):
    devices = range(lax.axis_size(axis))
    return lax.ppermute(block, axis, [(i, i ^ (1 << bit)) for i in devices])


def bits_of(axis):
    return (lax.axis_size(axis) - 1).bit_length()


def flip_mask(block, axis, mask):
    devices = range(lax.axis_size(axis))
    return lax.ppermute(block, axis, [(i, i ^ mask) for i in devices])


class Sum:
    def __init__(self, kept, sent, stages, left=()):
        self.kept, self.sent, self.stages, self.left = kept, list(sent), list(stages), list(left)
        self.total = None

    def came(self):
        axis, bit, count = self.stages[0][:3]
        partners = range(1, 2**count)
        return [flip_mask(x, axis, p << bit) for x, p in zip(self.sent, partners, strict=True)]

    def plan(self):
        stage = self.stages.pop(0)
        if len(stage) == 4:
            return ("join",)
        if self.stages and self.stages[0][0] == "ka" and self.left:
            bit, count = self.stages[0][1] - 1, self.stages[0][2]
            self.left = [b for b in self.left if not bit <= b < bit + count]
            below = sum(1 for b in self.left if b < bit)
            return ("part", bit, count, 2 ** (len(self.left) - below), 2**below)
        return ("whole",)


def over(axis, first=0):
    return [(axis, bit, 1) for bit in range(first, bits_of(axis))]


def slices_sum(kept, sent, order):
    stages = [("ka", bit + 1, count) for bit, count in order] + over("pb")
    left = [b for bit, count in order[1:] for b in range(bit, bit + count)]
    return Sum(kept, [sent], stages, left)


def columns_sum(kept, sent, order):
    stages = [("pb", 0, 1)] + [("ka", bit + 1, count) for bit, count in order]
    left = [b for bit, count in order for b in range(bit, bit + count)]
    return Sum(kept, [sent], stages + over("pb", 1) + [("pb", 0, 1, "join")], left)


def everywhere_sum(values):
    return Sum(values, [values], over("ka") + over("pb"))


def stage_kernel(plans, counts, side_bit, flat_ref, *refs):
    flat = flat_ref[0]
    refs = list(refs)
    kept_refs = [refs.pop(0) for _ in plans]
    came_refs = [[refs.pop(0) for _ in range(count)] for count in counts]
    for plan, kept, came in zip(plans, kept_refs, came_refs):

        def total(*at):
            value = kept[at].astype(F32)
            for ref in came:
                value = value + ref[at].astype(F32)
            return value

        out = refs.pop(0)
        if plan[0] == "whole":
            out[...] = total(Ellipsis).astype(out.dtype)
        elif plan[0] == "join":
            half = kept.shape[-1]
            side = jnp.right_shift(flat, side_bit) & 1
            out[:, pl.ds(pl.multiple_of(side * half, LANES), half)] = kept[...].astype(F32)
            out[:, pl.ds(pl.multiple_of((1 - side) * half, LANES), half)] = came[0][...].astype(F32)
        else:
            _, bit, count, above, below = plan
            mine = jnp.right_shift(flat, bit + 1) & (2**count - 1)
            outs = [out] + [refs.pop(0) for _ in range(2**count - 1)]
            for i in range(above):
                for j in range(below):
                    for other, ref in enumerate(outs):
                        group = jnp.bitwise_xor(mine, other)
                        ref[i * below + j] = total((i * 2**count + group) * below + j).astype(BF)


def advance(sums, flat_array, name, after=()):
    sums = [one for one in sums if one.stages]
    if not sums:
        return
    came = [one.came() for one in sums]
    plans, shapes, sizes = [], [], []
    for one in sums:
        plan = one.plan()
        shape, dtype, size = one.kept.shape, one.kept.dtype, 1
        if plan[0] == "join":
            shape, dtype = (shape[0], 2 * shape[1]), F32
        elif plan[0] == "part":
            shape, size = (plan[3] * plan[4], *shape[1:]), 2 ** plan[2]
        elif not one.stages:
            dtype = F32
        shapes += [shape_of(shape, dtype)] * size
        plans.append(plan)
        sizes.append(size)
    results = once(
        functools.partial(stage_kernel, plans, [len(x) for x in came], bits_of("ka")),
        (flat_array, *(one.kept for one in sums), *(x for group in came for x in group)),
        shapes,
        [],
        1_000_000_000,
        name,
        {0: pltpu.SMEM},
        after=after,
        room=24,
    )
    results = list(results)
    for one, size in zip(sums, sizes):
        one.kept = results.pop(0)
        one.sent = [results.pop(0) for _ in range(size - 1)] or [one.kept]
        if not one.stages:
            one.total = one.kept
        elif one.kept.ndim == 3 and one.kept.shape[0] == 1 and one.stages[0][0] == "pb":
            one.kept = one.kept.reshape(one.kept.shape[1:])
            one.sent = [one.kept]


def layer_norm(values, ln_gain, ln_shift):
    centre = jnp.mean(values, axis=-1, keepdims=True)
    offsets = values - centre
    spread = jnp.mean(offsets * offsets, axis=-1, keepdims=True)
    return offsets * lax.rsqrt(spread + LN_EPS) * ln_gain + ln_shift


def dot_nn(left, right):
    return lax.dot_general(left, right, (((1,), (0,)), ((), ())), preferred_element_type=F32)


def dot_nt(left, right):
    return lax.dot_general(left, right, (((1,), (1,)), ((), ())), preferred_element_type=F32)


def dot_tn(left, right):
    return lax.dot_general(left, right, (((0,), (0,)), ((), ())), preferred_element_type=F32)


def select_table(head_size):
    column = np.arange(SPAN)
    source = (column // PAD) * head_size + column % PAD
    table = [
        (column[:, None] == (source + off)[None, :]) & (column % PAD < head_size)[None, :]
        for off in (0, 64)
    ]
    return np.stack(table).astype(BF)


def group_windows(groups, head_size):
    out = []
    for g in range(groups):
        start = g * GROUP * head_size
        out.append((start // LANES * LANES, (start % LANES) // 64))
    return out


def place_table(heads, head_size):
    column = np.arange(heads * PAD)
    lane = np.arange(LANES)
    return np.stack(
        [
            (lane[:, None] == (column // PAD)[None, :])
            & (column % PAD == head_size + p)[None, :]
            for p in range(PIECES)
        ]
    ).astype(BF)


def tail_tables(heads, head_size):
    lane, tail = np.arange(LANES), np.arange(2 * LANES)
    into = np.stack(
        [
            (lane[:, None] + p * heads == tail[None, :]) & (lane < heads)[:, None]
            for p in range(2 * PIECES)
        ]
    )
    column = np.arange(heads * PAD)
    piece = column % PAD - head_size
    free = (piece >= 0) & (piece < PIECES)
    lane_of = np.where(free, piece * heads + column // PAD, -1)
    out = np.stack(
        [
            (tail[:, None] == lane_of[None, :]) & free[None, :],
            (tail[:, None] - PIECES * heads == lane_of[None, :]) & free[None, :],
        ]
    )
    return into.astype(BF), out.astype(BF)


def ones_row(heads, head_size):
    column = np.arange(heads * PAD) % PAD
    return ((column >= head_size) & (column < head_size + PIECES)).astype(np.float32)[None]


def head_sum_table(heads):
    column = np.arange(heads * PAD)
    return (column[:, None] // PAD == np.arange(LANES)[None, :]).astype(BF)


def pad_columns(values, select_ref, windows):
    parts = [
        dot_nn(values[:, start : start + SPAN], select_ref[kind]).astype(BF)
        for start, kind in windows
    ]
    return jnp.concatenate(parts, axis=1)


def drop_columns(values, select_ref, windows):
    tiles = {}
    for g, (start, kind) in enumerate(windows):
        part = dot_nt(values[:, g * SPAN : (g + 1) * SPAN], select_ref[kind])
        for k in range(SPAN // LANES):
            tile = part[:, k * LANES : (k + 1) * LANES]
            at = start // LANES + k
            tiles[at] = tiles[at] + tile if at in tiles else tile
    return jnp.concatenate([tiles[at] for at in sorted(tiles)], axis=1).astype(BF)


def drop_turned(values, select_ref, windows):
    tiles = {}
    for g, (start, kind) in enumerate(windows):
        part = dot_nt(select_ref[kind], values[:, g * SPAN : (g + 1) * SPAN])
        for k in range(SPAN // LANES):
            tile = part[k * LANES : (k + 1) * LANES]
            at = start // LANES + k
            tiles[at] = tiles[at] + tile if at in tiles else tile
    return jnp.concatenate([tiles[at] for at in sorted(tiles)], axis=0).astype(BF)


def row_of(ref):
    return jnp.concatenate([ref[k : k + 1, :] for k in range(ref.shape[0])], axis=1)


def split(values, count):
    rest, out = values, []
    for _ in range(count):
        piece = rest.astype(BF)
        rest = rest - piece.astype(F32)
        out.append(piece)
    return out


def norm_parts(values):
    centre = jnp.mean(values, axis=-1, keepdims=True)
    offsets = values - centre
    spread = jnp.mean(offsets * offsets, axis=-1, keepdims=True)
    slope = lax.rsqrt(spread + LN_EPS)
    return offsets * slope, slope


def norm_back(grad, normal, slope, gain):
    inner = grad * gain
    mean = jnp.mean(inner, axis=-1, keepdims=True)
    tilt = jnp.mean(inner * normal, axis=-1, keepdims=True)
    by_gain = jnp.sum(grad * normal, axis=0, keepdims=True)
    by_shift = jnp.sum(grad, axis=0, keepdims=True)
    return slope * (inner - mean - normal * tilt), by_gain, by_shift


def stretched_of(own, other):
    delta = [own[:, i : i + 1] - other[i : i + 1, :] for i in range(3)]
    square = delta[0] * delta[0] + delta[1] * delta[1] + delta[2] * delta[2]
    dist = jnp.sqrt(square + 1.0)
    scales = own[:, 3:4] * other[3:4, :]
    stretched = scales * dist + own[:, 4:5] + other[4:5, :]
    return delta, dist, scales, stretched


def mask_of(own, other, key_is_own):
    same = own[:, 5:6] == other[5:6, :]
    itself = own[:, 7:8] == other[7:8, :]
    is_open = (own[:, 6:7] > 0.5) if key_is_own else (other[6:7, :] > 0.5)
    return jnp.where(same & (is_open | itself), 0.0, MASKED)


def line_atoms(lines):
    line = lax.broadcasted_iota(jnp.int32, (lines, lines // GROUP), 0)
    atom = lax.broadcasted_iota(jnp.int32, (lines, lines // GROUP), 1)
    return jnp.where(line // GROUP == atom, 1.0, 0.0).astype(BF)


def line_heads(lines):
    line = lax.broadcasted_iota(jnp.int32, (lines, SPAN), 0)
    column = lax.broadcasted_iota(jnp.int32, (lines, SPAN), 1)
    return jnp.where(column // PAD == line % GROUP, 1.0, 0.0)


def expand_into(out_ref, padded, groups):
    lines = CHUNK * GROUP
    keep = line_heads(lines).astype(BF)
    spread = line_atoms(lines)
    for g in range(groups):
        for i in range(padded.shape[0] // CHUNK):
            part = padded[i * CHUNK : (i + 1) * CHUNK, g * SPAN : (g + 1) * SPAN]
            out_ref[g, i * lines : (i + 1) * lines, :] = dot_nn(spread, part).astype(BF) * keep


def collapse(values):
    lines = values.shape[0]
    kept = values * line_heads(lines)
    high = kept.astype(BF)
    low = (kept - high.astype(F32)).astype(BF)
    line = lax.broadcasted_iota(jnp.int32, (lines // GROUP, lines), 1)
    atom = lax.broadcasted_iota(jnp.int32, (lines // GROUP, lines), 0)
    gather = jnp.where(line // GROUP == atom, 1.0, 0.0).astype(BF)
    return dot_nn(gather, high) + dot_nn(gather, low)


def fetch(span_ref, refs, out_ref):
    slot = span_ref[SPAN_SLOT + span_ref[SPAN_FIRST, 0] + pl.program_id(0), 0]
    count = len(refs) // 2
    rows = refs[0].shape[0]
    for k in range(count):

        @pl.when(slot == k)
        def _():
            out_ref[:rows] = refs[k][...]
            out_ref[rows:] = refs[count + k][...]


def spots_of(span_ref, rows):
    core = span_ref[SPAN_CORE, 0]
    return [pl.ds(pl.multiple_of(at * rows, rows), rows) for at in (core, 1 - core)]


def spread_mask(mask_ref, mask):
    mask_ref[...] = jnp.broadcast_to(mask[:, None, :], mask_ref.shape)


def reaches(span_ref, first, last, low, high):
    return (span_ref[SPAN_LOW + first, 0] <= high) & (span_ref[SPAN_HIGH + last, 0] >= low)


def head_steps(span_ref, rows, step):
    pair = span_ref[SPAN_FIRST, 0] + pl.program_id(0)
    few = HEAD_ROWS // FEW

    def one(i, carry):
        @pl.when(reaches(span_ref, i * few, i * few + few - 1, 2 * pair, 2 * pair + 1))
        def _():
            step(pl.multiple_of(i * HEAD_ROWS, HEAD_ROWS), HEAD_ROWS)

        return carry

    lax.fori_loop(0, rows // HEAD_ROWS, one, 0)


def kernel_steps(span_ref, first, rows, size, step, skipped):
    pair = span_ref[SPAN_FIRST, 0] + pl.program_id(0)
    few = size // FEW

    def one(i, carry):
        at = pl.multiple_of(i * size, size)
        chunk = first // FEW + i * few
        for half in range(2):
            block = 2 * pair + half
            needed = reaches(span_ref, chunk, chunk + few - 1, block, block)

            @pl.when(needed)
            def _():
                step(at, half)

            @pl.when(jnp.logical_not(needed))
            def _():
                skipped(at, half)

        return carry

    lax.fori_loop(0, rows // size, one, 0)


def side_kernel(
    atoms_blocks,
    flat_ref,
    pos_ref,
    item_ref,
    open_ref,
    type_ref,
    length_ref,
    table_ref,
    means_ref,
    widths_ref,
    kw_ref,
    span_ref,
    other_ref,
    own_ref,
    line_ref,
    tab_ref,
    gw_ref,
    kwt_ref,
    par_ref,
):
    flat = flat_ref[0]
    chips = len(SLOTS[0]) // 2
    first_block = flat // 2 * 2 - 2 * chips
    ids = lax.broadcasted_iota(jnp.int32, (LANES, LANES), 0).astype(F32)
    lane = lax.broadcasted_iota(jnp.int32, (1, LANES), 1)
    tables = []
    for k in range(table_ref.shape[0] // 2):
        rows = split(table_ref[2 * k : 2 * k + 1, :], PIECES)
        rows += split(table_ref[2 * k + 1 : 2 * k + 2, :], PIECES)
        rows += [jnp.zeros((2, LANES), BF)]
        tables.append(jnp.concatenate([row.astype(F32) for row in rows], axis=0).astype(BF))
    flags = [
        jnp.broadcast_to(
            jnp.where(length_ref[k : k + 1, :] > 2 * MOL_MEAN, float(MOL_TYPES), 0.0), (8, LANES)
        ).astype(BF)
        for k in range(length_ref.shape[0])
    ]
    for b in range(other_ref.shape[1] // LANES):
        block = first_block + b
        inside = (block >= 0) & (block < atoms_blocks)
        source = jnp.clip(block, 0, atoms_blocks - 1)
        at = pl.ds(pl.multiple_of(source * LANES, LANES), LANES)
        item = jnp.where(inside, item_ref[pl.ds(source, 1), :].astype(F32), -1.0)
        kind = type_ref[pl.ds(source, 1), :].astype(F32)
        for k, flag in enumerate(flags):
            onehot = jnp.where(ids + float(k * LANES) == item, 1.0, 0.0).astype(BF)
            kind = kind + dot_nn(flag, onehot)[0:1, :]
        found = jnp.zeros((8, LANES), F32)
        for k, table in enumerate(tables):
            onehot = jnp.where(ids + float(k * LANES) == kind, 1.0, 0.0).astype(BF)
            found = found + dot_nn(table, onehot)
        rows = [pos_ref[k : k + 1, at] for k in range(3)]
        rows += [found[0:1] + found[1:2] + found[2:3], found[3:4] + found[4:5] + found[5:6]]
        rows += [item, open_ref[pl.ds(source, 1), :].astype(F32)]
        rows += [(block * LANES + lane).astype(F32), kind]
        rows += [jnp.zeros((SIDE - 9, LANES), F32)]
        side = jnp.concatenate(rows, axis=0)
        other_ref[:, b * LANES : (b + 1) * LANES] = side

        @pl.when(block == flat)
        def _():
            line_ref[...] = side

    line = line_ref[...]
    turned = jnp.transpose(
        jnp.concatenate([line, jnp.zeros((LANES - SIDE, LANES), F32)], axis=0)
    )
    own_ref[...] = turned
    chunks = LANES // FEW
    item_column = jnp.broadcast_to(own_ref[:, 5:6], (LANES, LANES))
    par_ref[...] = item_column
    first_item = par_ref[pl.ds(0, chunks, stride=FEW), :]
    last_item = par_ref[pl.ds(FEW - 1, chunks, stride=FEW), :]

    def count(k, carry):
        row = item_ref[pl.ds(k, 1), :].astype(F32)
        below, upto = carry
        return (
            below + jnp.where(row < first_item, 1.0, 0.0),
            upto + jnp.where(row <= last_item, 1.0, 0.0),
        )

    zero = jnp.zeros((chunks, LANES), F32)
    below, upto = lax.fori_loop(0, atoms_blocks, count, (zero, zero))
    below = jnp.sum(below, axis=1, keepdims=True).astype(jnp.int32)
    upto = jnp.sum(upto, axis=1, keepdims=True).astype(jnp.int32)
    low = jnp.right_shift(below - first_block * LANES, 7)
    high = jnp.right_shift(upto - 1 - first_block * LANES, 7)
    span_ref[SPAN_LOW : SPAN_LOW + chunks, :] = jnp.broadcast_to(low, (chunks, LANES))
    span_ref[SPAN_HIGH : SPAN_HIGH + chunks, :] = jnp.broadcast_to(high, (chunks, LANES))
    row = lax.broadcasted_iota(jnp.int32, (SPAN_LOW, LANES), 0)
    kind = (flat // 2) % 4
    head = jnp.where(row == SPAN_FIRST, jnp.right_shift(low[0:1, :], 1), 0)
    head = head + jnp.where(row == SPAN_LAST, jnp.right_shift(high[chunks - 1 :, :], 1), 0)
    head = head + jnp.where(row == SPAN_CORE, flat % 2, 0)
    head = head + jnp.where(row == SPAN_CHIP, flat // 2, 0)
    for k, slots in enumerate(zip(*SLOTS)):
        slot = sum(jnp.where(kind == which, at, 0) for which, at in enumerate(slots))
        head = head + jnp.where(row == SPAN_SLOT + k, slot, 0)
    span_ref[:SPAN_LOW, :] = head

    def column_of(ref):
        return jnp.transpose(jnp.broadcast_to(ref[...], (LANES, LANES)))

    means, widths = column_of(means_ref), column_of(widths_ref)
    peaks = 1.0 / (ROOT_TWO_PI * widths)
    bend = -(KAPPA * KAPPA) / (widths * widths)
    tab_ref[0] = means
    tab_ref[1] = KAPPA / widths
    tab_ref[2] = LOG2E * jnp.log(peaks)
    tab_ref[3] = bend
    turned_weights = kw_ref[...].astype(F32)
    heads = turned_weights.shape[0]
    filler = jnp.zeros((LANES - heads, LANES), F32)
    wide = jnp.transpose(jnp.concatenate([turned_weights, filler], axis=0))
    weights = wide[:, :heads]
    scaled = weights * (peaks / (widths * widths))[:, :heads]
    gw_ref[...] = jnp.concatenate(split(scaled, WEIGHT_PIECES), axis=1)
    kwt_ref[...] = kw_ref[...]
    lanes = lax.broadcasted_iota(jnp.int32, (LANES, LANES), 1)
    par = wide + jnp.where(lanes == heads, peaks, 0.0)
    par_ref[...] = par + jnp.where(lanes == heads + 1, 1.0 / widths, 0.0)


def bias_kernel(span_ref, own_ref, other_ref, tab_ref, kwt_ref, out_ref, str_ref):
    rows, keys = str_ref.shape
    kernels = tab_ref.shape[1]
    heads = kwt_ref.shape[0]
    half_keys = keys // 2
    str_ref[...] = stretched_of(own_ref[...], other_ref[...])[3]

    def step(at, half):
        columns = slice(half * half_keys, (half + 1) * half_keys)
        block = str_ref[pl.ds(at, BIAS_ROWS), columns]
        for r in range(0, BIAS_ROWS, 2):
            parts = []
            for q in range(2):
                line = jnp.broadcast_to(block[r + q : r + q + 1], (kernels, half_keys))
                z = (line - tab_ref[0]) * tab_ref[1]
                parts.append(jnp.exp2(tab_ref[2] - z * z).astype(BF))
            result = dot_nn(kwt_ref[...], jnp.concatenate(parts, axis=1)) * LOG2E
            out_ref[0, at + r, :, columns] = result[:, :half_keys]
            out_ref[0, at + r + 1, :, columns] = result[:, half_keys:]

    def skipped(at, half):
        columns = slice(half * half_keys, (half + 1) * half_keys)
        out_ref[0, pl.ds(at, BIAS_ROWS), :, columns] = jnp.zeros((BIAS_ROWS, heads, half_keys), F32)

    kernel_steps(span_ref, 0, rows, BIAS_ROWS, step, skipped)


def forward_kernel(
    scale2,
    groups,
    span_ref,
    own_ref,
    other_ref,
    *refs,
):
    token_refs, refs = refs[:14], refs[14:]
    gain_ref, shift_ref, w_ref, select_ref, ones_ref, place_ref, bias_ref, *refs = refs
    att_ref, qaug_ref, lse_ref, kvq_ref, *refs = refs
    qexp_ref, mask_ref, max_ref, sum_ref, acc_ref, lane_ref, both_ref = refs
    step = pl.program_id(0)
    width = groups * SPAN
    tok_ref = token_refs[3]
    rows, model_width = tok_ref.shape
    windows = group_windows(groups, model_width // (groups * GROUP))
    gain, shift = row_of(gain_ref), row_of(shift_ref)

    @pl.when(step == 0)
    def _():
        normed = layer_norm(tok_ref[...].astype(F32), gain, shift).astype(BF)
        query = dot_nn(normed, w_ref[:, :model_width]).astype(BF)
        query = pad_columns(query, select_ref, windows)
        qaug_ref[...] = query
        expand_into(qexp_ref, query, groups)
        max_ref[...] = jnp.full(max_ref.shape, 2.0 * MASKED, F32)
        sum_ref[...] = jnp.zeros(sum_ref.shape, F32)
        acc_ref[...] = jnp.zeros(acc_ref.shape, F32)

    fetch(span_ref, token_refs, both_ref)
    normed = layer_norm(both_ref[...].astype(F32), gain, shift).astype(BF)
    spots = spots_of(span_ref, rows)

    for part in range(3):
        source = (part + 1) % 3 * model_width
        value = dot_nn(normed, w_ref[:, source : source + model_width]).astype(BF)
        value = pad_columns(value, select_ref, windows)
        if part < 2:
            value = value + ones_ref[...].astype(BF)
        for k in range(2):
            kvq_ref[0, spots[k], part * width : (part + 1) * width] = (
                value[k * rows : (k + 1) * rows]
            )
    spread_mask(mask_ref, mask_of(own_ref[...], other_ref[...], False))

    def chunk_step(at, count):
        lines = pl.ds(pl.multiple_of(at * GROUP, HEAD_ROWS * GROUP), count * GROUP)
        mask = mask_ref[pl.ds(at, count)]
        for g in range(groups):
            columns = slice(g * SPAN, (g + 1) * SPAN)
            dots = dot_nt(qexp_ref[g, lines, :], kvq_ref[0, :, columns])
            bias = bias_ref[0, pl.ds(at, count), g * GROUP : (g + 1) * GROUP, :] + mask
            scores = dots * scale2 + bias.reshape(dots.shape)
            old = max_ref[g, lines, :]
            top = jnp.maximum(scores[:, :128], scores[:, 128:])
            new = jnp.maximum(old, jnp.max(top, axis=1, keepdims=True))
            alpha = jnp.exp2(old - new)
            low = jnp.exp2(scores[:, :128] - new)
            high = jnp.exp2(scores[:, 128:] - new)
            max_ref[g, lines, :] = new
            sum_ref[g, lines, :] = sum_ref[g, lines, :] * alpha + (low + high)
            probs = jnp.concatenate([low, high], axis=1).astype(BF)
            values = dot_nn(probs, kvq_ref[0, :, width + g * SPAN : width + (g + 1) * SPAN])
            wide = jnp.concatenate([alpha, alpha], axis=1)
            acc_ref[g, lines, :] = acc_ref[g, lines, :] * wide + values

    head_steps(span_ref, rows, chunk_step)

    @pl.when(step == span_ref[SPAN_LAST, 0] - span_ref[SPAN_FIRST, 0])
    def _():
        lane = lax.broadcasted_iota(jnp.int32, (GROUP, 128), 1)
        head = lax.broadcasted_iota(jnp.int32, (GROUP, 128), 0)

        def finish(i, carry):
            at = pl.multiple_of(i * CHUNK, CHUNK)
            lines = pl.ds(pl.multiple_of(i * CHUNK * GROUP, CHUNK * GROUP), CHUNK * GROUP)
            lanes = jnp.zeros((CHUNK, 128), F32)
            for g in range(groups):
                total = jnp.sum(sum_ref[g, lines, :], axis=1, keepdims=True)
                attended = collapse(acc_ref[g, lines, :] / total)
                att_ref[pl.ds(at, CHUNK), g * SPAN : (g + 1) * SPAN] = attended
                lse = max_ref[g, lines, :] + jnp.log(total) * LOG2E
                own_lane = jnp.where(lane == head + g * GROUP, 1.0, 0.0)
                lanes = lanes + jnp.sum(
                    lse.reshape(CHUNK, GROUP, 128) * own_lane[None], axis=1
                )
            lane_ref[pl.ds(at, CHUNK), :] = lanes
            return carry

        lax.fori_loop(0, rows // CHUNK, finish, 0)
        rest = lane_ref[...] * (-1.0 / scale2)
        query = qaug_ref[...].astype(F32)
        for p in range(PIECES):
            piece = rest.astype(BF)
            rest = rest - piece.astype(F32)
            lse_ref[p] = piece
            query = query + dot_nn(piece, place_ref[p])
        qaug_ref[...] = query.astype(BF)


def query_grad_kernel(
    scale2,
    head_scale,
    groups,
    span_ref,
    own_ref,
    other_ref,
    qaug_ref,
    doaug_ref,
    kv_ref,
    bias_ref,
    select_ref,
    dq_ref,
    ds_ref,
    qexp_ref,
    doexp_ref,
    mask_ref,
    dqacc_ref,
    low_ref,
):
    step = pl.program_id(0)
    width = groups * SPAN
    rows, keys = own_ref.shape[0], other_ref.shape[1]
    windows = group_windows(groups, dq_ref.shape[0] // (groups * GROUP))

    @pl.when(step == 0)
    def _():
        expand_into(qexp_ref, qaug_ref[...], groups)
        expand_into(doexp_ref, doaug_ref[...], groups)
        dqacc_ref[...] = jnp.zeros(dqacc_ref.shape, F32)

    spread_mask(mask_ref, mask_of(own_ref[...], other_ref[...], False))

    def chunk_step(at, count):
        lines = pl.ds(pl.multiple_of(at * GROUP, HEAD_ROWS * GROUP), count * GROUP)
        mask = mask_ref[pl.ds(at, count)]
        waiting = []
        for g in range(groups):
            key_block = kv_ref[0, :, g * SPAN : (g + 1) * SPAN]
            value_block = kv_ref[0, :, width + g * SPAN : width + (g + 1) * SPAN]
            dots = dot_nt(qexp_ref[g, lines, :], key_block)
            grads = dot_nt(doexp_ref[g, lines, :], value_block)
            bias = bias_ref[0, pl.ds(at, count), g * GROUP : (g + 1) * GROUP, :] + mask
            probs = jnp.exp2(dots * scale2 + bias.reshape(dots.shape))
            grad_scores = probs * grads
            dqacc_ref[g, lines, :] += dot_nn(grad_scores.astype(BF), key_block)
            waiting.append(grad_scores.reshape(count, GROUP, keys))
            if len(waiting) == 2:
                ds_ref[0, pl.ds(at, count), (g - 1) * GROUP : (g + 1) * GROUP, :] = (
                    jnp.concatenate(waiting, axis=1).astype(BF)
                )
                waiting = []

    head_steps(span_ref, rows, chunk_step)

    @pl.when(step == span_ref[SPAN_LAST, 0] - span_ref[SPAN_FIRST, 0])
    def _():
        def finish(i, carry):
            at = pl.multiple_of(i * CHUNK, CHUNK)
            lines = pl.ds(pl.multiple_of(i * CHUNK * GROUP, CHUNK * GROUP), CHUNK * GROUP)
            for g in range(groups):
                value = collapse(dqacc_ref[g, lines, :]) * head_scale
                low_ref[pl.ds(at, CHUNK), g * SPAN : (g + 1) * SPAN] = value.astype(BF)
            return carry

        lax.fori_loop(0, rows // CHUNK, finish, 0)
        dq_ref[...] = drop_turned(low_ref[...], select_ref, windows)


def phi_grad_kernel(
    first_row,
    span_ref,
    own_ref,
    other_ref,
    line_ref,
    ds_ref,
    tab_ref,
    kw_ref,
    par_ref,
    small_ref,
    pos_ref,
    str_ref,
    gs_ref,
    own_acc_ref,
    gkw_ref,
    moment_ref,
    type_ref,
):
    step = pl.program_id(0)
    rows, keys = str_ref.shape
    kernels = tab_ref.shape[1]
    heads = gkw_ref.shape[1]
    blocks = pos_ref.shape[0] // 3
    pair_block = 2 * (span_ref[SPAN_CHIP, 0] + span_ref[SPAN_FIRST, 0] + step)

    @pl.when(step == 0)
    def _():
        gkw_ref[...] = jnp.zeros(gkw_ref.shape, F32)
        moment_ref[...] = jnp.zeros(moment_ref.shape, F32)
        own_acc_ref[...] = jnp.zeros(own_acc_ref.shape, F32)
        pos_ref[...] = jnp.zeros(pos_ref.shape, F32)
        type_ref[...] = jnp.zeros(type_ref.shape, F32)

    def add_types(kind, by_scale, by_shift):
        count = type_ref.shape[1]
        onehot = lax.broadcasted_iota(jnp.int32, (count, LANES), 0).astype(F32) == kind
        type_ref[0] += jnp.where(onehot, by_scale, 0.0)
        type_ref[1] += jnp.where(onehot, by_shift, 0.0)

    own, other = own_ref[first_row : first_row + rows, :], other_ref[...]
    str_ref[...] = stretched_of(own, other)[3]

    half_keys = keys // 2

    def pair_step(at, half):
        columns = slice(half * half_keys, (half + 1) * half_keys)
        block = str_ref[pl.ds(at, CHUNK), columns]
        first = second = weights = None
        lines = []
        for r in range(0, CHUNK, 2):
            low = jnp.concatenate([ds_ref[0, at + r + q, :, columns] for q in range(2)], axis=1)
            dphi = dot_nn(kw_ref[...], jnp.concatenate([low] * WEIGHT_PIECES, axis=0))
            phis = []
            for q in range(2):
                away = jnp.broadcast_to(block[r + q : r + q + 1], (kernels, half_keys)) - tab_ref[0]
                phi = jnp.exp2(away * away * tab_ref[3])
                phis.append(phi.astype(BF))
                moved = dphi[:, q * half_keys : (q + 1) * half_keys] * phi * away
                bent = moved * away
                first = moved if first is None else first + moved
                second = bent if second is None else second + bent
                lines.append(jnp.sum(moved, axis=0, keepdims=True))
            part = dot_nt(jnp.concatenate(phis, axis=1), low)
            weights = part if weights is None else weights + part
        moment_ref[0] += first
        moment_ref[1] += second
        gs_ref[pl.ds(at, CHUNK), columns] = jnp.concatenate(lines, axis=0)
        gkw_ref[...] += weights

    def skipped(at, half):
        columns = slice(half * half_keys, (half + 1) * half_keys)
        gs_ref[pl.ds(at, CHUNK), columns] = jnp.zeros((CHUNK, half_keys), F32)

    kernel_steps(span_ref, first_row, rows, CHUNK, pair_step, skipped)

    delta, dist, scales, _ = stretched_of(own, other)
    grad = -gs_ref[...]
    by_scale = grad * dist
    pull = grad * scales / dist
    terms = [pull * delta[0], pull * delta[1], pull * delta[2], by_scale * other[3:4, :], grad]
    for k, term in enumerate(terms):
        own_acc_ref[k] += term[:, :128] + term[:, 128:]
    for half in range(2):
        part = slice(half * LANES, (half + 1) * LANES)
        for k in range(3):
            spot = pl.ds(k * blocks + pair_block + half, 1)
            pos_ref[spot, :] += -jnp.sum(terms[k][:, part], axis=0, keepdims=True)
        add_types(
            other[8:9, part],
            jnp.sum(by_scale[:, part] * own[:, 3:4], axis=0, keepdims=True),
            jnp.sum(grad[:, part], axis=0, keepdims=True),
        )

    @pl.when(step == span_ref[SPAN_LAST, 0] - span_ref[SPAN_FIRST, 0])
    def _():
        lane = lax.broadcasted_iota(jnp.int32, (rows, LANES), 1)
        total = jnp.zeros((rows, LANES), F32)
        for k in range(5):
            column = jnp.sum(own_acc_ref[k], axis=1, keepdims=True)
            total = total + jnp.where(lane == k, column, 0.0)
        rest = [jnp.zeros((count, LANES), F32) for count in (first_row, LANES - first_row - rows)]
        total = jnp.concatenate([x for x in (rest[0], total, rest[1]) if x.shape[0]], axis=0)
        turned = jnp.transpose(total)
        own_block = 2 * (span_ref[SPAN_CHIP, 0] + len(SLOTS[0]) // 2) + span_ref[SPAN_CORE, 0]
        for k in range(3):
            pos_ref[pl.ds(k * blocks + own_block, 1), :] += turned[k : k + 1, :]
        add_types(line_ref[8:9, :], turned[3:4, :], turned[4:5, :])

        par = par_ref[...]
        by_weight = gkw_ref[...] * par[:, heads : heads + 1]
        plain = jnp.sum(by_weight * par[:, :heads], axis=1, keepdims=True)
        by_mean = jnp.sum(moment_ref[0], axis=1, keepdims=True)
        by_width = jnp.sum(moment_ref[1], axis=1, keepdims=True) - plain
        columns = [by_mean, by_width * par[:, heads + 1 : heads + 2]]
        low, high = slice(0, LANES), slice(LANES, 2 * LANES)
        for part in (low, high):
            for k in range(2):
                columns.append(jnp.sum(type_ref[k, part, :], axis=1, keepdims=True))
        lane = lax.broadcasted_iota(jnp.int32, (LANES, LANES), 1)
        wide = jnp.concatenate([by_weight, jnp.zeros((LANES, LANES - heads), F32)], axis=1)
        for k, column in enumerate(columns):
            wide = wide + jnp.where(lane == heads + k, column, 0.0)
        small_ref[...] = wide


def middle_kernel(
    groups,
    tile,
    flat_ref,
    tok_ref,
    att_ref,
    lse_ref,
    gain_ref,
    shift_ref,
    cot_ref,
    wout_hbm,
    wup_hbm,
    wdown_hbm,
    select_ref,
    place_ref,
    sum_ref,
    into_ref,
    out_ref,
    gmix_ref,
    doaug_ref,
    payload_ref,
    attlow_ref,
    normed_ref,
    mine_ref,
    theirs_ref,
    lngrad_ref,
    wout_ref,
    wup_ref,
    wdown_ref,
    down_ref,
    back_ref,
    wout_sem,
    tile_sems,
):
    rows, model_width = tok_ref.shape
    width = groups * SPAN
    windows = group_windows(groups, model_width // (groups * GROUP))
    tiles = wup_ref.shape[1] // tile
    piece = mine_ref.shape[2]
    core = flat_ref[0] % 2

    def tile_copies(t):
        spot = pl.ds(pl.multiple_of(t * tile, LANES), tile)
        return (
            pltpu.make_async_copy(wup_hbm.at[:, spot], wup_ref.at[:, spot], tile_sems.at[0, t]),
            pltpu.make_async_copy(wdown_hbm.at[spot, :], wdown_ref.at[spot, :], tile_sems.at[1, t]),
        )

    first = pltpu.make_async_copy(wout_hbm, wout_ref, wout_sem)
    first.start()
    for t in range(tiles):
        for copy in tile_copies(t):
            copy.start()

    gain, shift = row_of(gain_ref), row_of(shift_ref)
    cotangent = cot_ref[...]
    attended = att_ref[...]
    attended_low = drop_columns(attended.astype(BF), select_ref, windows)
    attlow_ref[...] = attended_low
    first.wait()
    mixed = tok_ref[...].astype(F32) + dot_nn(attended_low, wout_ref[...])
    normal, slope = norm_parts(mixed)
    normed_ref[...] = (normal * gain + shift).astype(BF)
    down_ref[...] = mixed
    back_ref[...] = jnp.zeros(back_ref.shape, F32)

    def step(t, carry):
        for copy in tile_copies(t):
            copy.wait()
        spot = pl.ds(pl.multiple_of(t * tile, LANES), tile)
        up = dot_nn(normed_ref[...], wup_ref[:, spot])
        grad_hidden = dot_nt(cotangent, wdown_ref[spot, :])
        square = up * up
        bent = jnp.tanh(GELU_SLOPE * (up * (1.0 + GELU_CUBE * square)))
        gate = 0.5 * (1.0 + bent)
        inner = GELU_SLOPE * (1.0 + 3.0 * GELU_CUBE * square)
        hidden = (up * gate).astype(BF)
        grad_up = (grad_hidden * (gate + 0.5 * up * (1.0 - bent * bent) * inner)).astype(BF)
        for kind, value in enumerate((grad_up, hidden)):
            value = jnp.transpose(value.astype(F32)).astype(BF)
            for q in range(tile // piece):
                part = value[q * piece : (q + 1) * piece]
                at = t * (tile // piece // 2) + q // 2

                @pl.when(core == q % 2)
                def _():
                    mine_ref[kind, at] = part

                @pl.when(core != q % 2)
                def _():
                    theirs_ref[kind, at] = part

        down_ref[...] += dot_nn(hidden, wdown_ref[spot, :])
        back_ref[...] += dot_nt(grad_up, wup_ref[:, spot])
        return carry

    lax.fori_loop(0, tiles, step, 0)
    out_ref[...] = down_ref[...].astype(BF)
    back, by_gain, by_shift = norm_back(back_ref[...], normal, slope, gain)
    lngrad_ref[...] = jnp.concatenate([by_gain, by_shift], axis=0)
    grad_mixed = cotangent.astype(F32) + back
    gmix_ref[...] = grad_mixed
    grad_low = grad_mixed.astype(BF)
    grad_attended = dot_nt(grad_low, wout_ref[...]).astype(BF)
    padded = pad_columns(grad_attended, select_ref, windows).astype(F32)
    high, low = split(padded * attended, 2)
    delta = dot_nn(high, sum_ref[...]) + dot_nn(low, sum_ref[...])
    pieces = split(-delta, PIECES)
    tail = jnp.zeros((rows, 2 * LANES), F32)
    for p in range(PIECES):
        padded = padded + dot_nn(pieces[p], place_ref[p])
        tail = tail + dot_nn(lse_ref[p], into_ref[p]) + dot_nn(pieces[p], into_ref[PIECES + p])
    doaug_ref[...] = padded.astype(BF)
    payload_ref[:, :model_width] = grad_low
    payload_ref[:, model_width:] = tail.astype(BF)


def weight_grads_kernel(
    ka_count,
    flat_ref,
    mine_ref,
    came_ref,
    normed_ref,
    normed_came_ref,
    cot_ref,
    cot_came_ref,
    attlow_ref,
    attlow_came_ref,
    payload_ref,
    payload_came_ref,
    up_kept_ref,
    up_sent_ref,
    rest_kept_ref,
    rest_sent_ref,
    product_ref,
):
    flat = flat_ref[0]
    core, bit, side = flat % 2, (flat // 2) % 2, (flat // ka_count) % 2
    model_width = normed_ref.shape[1]
    rows = up_kept_ref.shape[1]
    half = model_width // 2
    slices = up_kept_ref.shape[0] * 2
    out_rows = model_width // ka_count
    normed = jnp.concatenate([normed_ref[...], normed_came_ref[...]], axis=0)
    cotangent = jnp.concatenate([cot_ref[...], cot_came_ref[...]], axis=0)

    def columns(which):
        return pl.ds(pl.multiple_of(which * half, LANES), half)

    def step(m, carry):
        both = jnp.concatenate([mine_ref[0, m], came_ref[0, m]], axis=1)
        value = dot_nn(both, normed).astype(BF)

        @pl.when(m % 2 == bit)
        def _():
            up_kept_ref[m // 2] = value

        @pl.when(m % 2 != bit)
        def _():
            up_sent_ref[m // 2] = value

        both = jnp.concatenate([mine_ref[1, m], came_ref[1, m]], axis=1)
        product_ref[:rows, :] = dot_nn(both, cotangent)
        rest_kept_ref[m, :rows, :] = product_ref[:rows, columns(side)].astype(BF)
        rest_sent_ref[m, :rows, :] = product_ref[:rows, columns(1 - side)].astype(BF)
        return carry

    lax.fori_loop(0, slices, step, 0)
    grads = jnp.concatenate(
        [payload_ref[:, :model_width], payload_came_ref[:, :model_width]], axis=0
    )
    attended = jnp.concatenate([attlow_ref[...], attlow_came_ref[...]], axis=0)
    product_ref[...] = dot_tn(grads, attended)

    def out_step(m, carry):
        spot = pl.ds(pl.multiple_of((2 * m + core) * out_rows, 8), out_rows)
        rest_kept_ref[m, rows:, :] = product_ref[spot, columns(side)].astype(BF)
        rest_sent_ref[m, rows:, :] = product_ref[spot, columns(1 - side)].astype(BF)
        return carry

    lax.fori_loop(0, slices, out_step, 0)


def normal_kernel(tok_ref, gain_ref, shift_ref, out_ref):
    normal, _ = norm_parts(tok_ref[...].astype(F32))
    out_ref[...] = (normal * row_of(gain_ref) + row_of(shift_ref)).astype(BF)


def qkv_grads_kernel(masks, groups, *refs):
    grads_refs, normed_refs, out_ref, norm_ref = refs[:groups], refs[groups:-2], refs[-2], refs[-1]
    columns = out_ref.shape[0]
    lefts, rights, parts = [], [], None
    for ref, group in zip(normed_refs, masks):
        for i, mask in enumerate(group):
            grads = grads_refs[mask // 4][mask % 4]
            lefts.append(grads[:columns])
            rights.append(ref[i])
            part = grads[columns:].astype(F32)
            parts = part if parts is None else parts + part
    total = None
    for i in range(0, len(lefts), 2):
        part = dot_nn(
            jnp.concatenate(lefts[i : i + 2], axis=1), jnp.concatenate(rights[i : i + 2], axis=0)
        )
        total = part if total is None else total + part
    out_ref[...] = total.astype(BF)
    norm_ref[...] = parts


def results_kernel(
    heads,
    types,
    flat_ref,
    joined_ref,
    first_ref,
    norm_ref,
    weight_ref,
    mean_ref,
    width_ref,
    scale_ref,
    shift_ref,
    pos_ref,
):
    small = joined_ref[:LANES, :]
    weight_ref[...] = small[:, :heads]
    turned = jnp.transpose(small)
    rows = [turned[heads + k : heads + k + 1, :] for k in range(6)]
    mean_ref[...] = rows[0]
    width_ref[...] = rows[1]
    scale_ref[...] = jnp.concatenate([rows[2], rows[4]], axis=1)[:, :types]
    shift_ref[...] = jnp.concatenate([rows[3], rows[5]], axis=1)[:, :types]
    count = norm_ref.shape[1]
    for k in range(2):
        norm_ref[k] = first_ref[k * count : (k + 1) * count, :]
        norm_ref[2 + k] = joined_ref[LANES + k * count : LANES + (k + 1) * count, :]
    first = LANES + 2 * count
    blocks = (joined_ref.shape[0] - first) // 3
    for k in range(3):
        spot = first + k * blocks + len(SLOTS[0]) // 2 * 2 + flat_ref[0]
        pos_ref[k : k + 1, :] = joined_ref[pl.ds(spot, 1), :]


def first_norm_kernel(
    ka_count,
    flat_ref,
    tok_ref,
    gain_ref,
    dq_ref,
    dkv_ref,
    w_ref,
    gmix_ref,
    grad_ref,
    *refs,
):
    *part_refs, joined_ref = refs
    model_width = tok_ref.shape[1]
    grad = dot_nn(w_ref[:, :model_width], dq_ref[...])
    grad = grad + dot_nn(w_ref[:, model_width:], dkv_ref[...])
    grad = jnp.transpose(grad)
    normal, slope = norm_parts(tok_ref[...].astype(F32))
    back, by_gain, by_shift = norm_back(grad, normal, slope, row_of(gain_ref))
    grad_ref[...] = gmix_ref[...] + back
    lines = [
        row[:, k : k + LANES] for row in (by_gain, by_shift) for k in range(0, model_width, LANES)
    ]
    joined_ref[:model_width, :] = dq_ref[...]
    joined_ref[model_width:, :] = dkv_ref[...]
    here = flat_ref[0] % ka_count
    rows = part_refs[0].shape[1]
    columns = 3 * model_width // ka_count
    lines.append(jnp.zeros((rows - columns - len(lines), LANES), F32))
    lines = jnp.concatenate(lines, axis=0).astype(BF)
    for ref in part_refs:
        for i in range(ka_count // 4):
            ref[i, columns:, :] = lines
    for d in range(ka_count):
        value = joined_ref[d * columns : (d + 1) * columns, :]
        differs = jnp.bitwise_xor(here, d)
        for k, ref in enumerate(part_refs):

            @pl.when(differs % 4 == k)
            def _():
                ref[differs // 4, :columns, :] = value


def regroup_kernel(*refs):
    ins, outs = refs[:4], refs[4:]
    for i, out in enumerate(outs):
        for k, ref in enumerate(ins):
            out[k] = ref[i]


def key_grad_kernel(
    scale2,
    head_scale,
    groups,
    model_width,
    span_ref,
    own_ref,
    other_ref,
    kv_ref,
    q_ref,
    *refs,
):
    payload_refs, refs = refs[:14], refs[14:]
    wout_ref, select_ref, place_ref, bias_ref, dkv_ref, kexp_ref, vexp_ref, *refs = refs
    mask_ref, qb_ref, dob_ref, dk_ref, dv_ref, both_ref, low_ref = refs
    step = pl.program_id(0)
    width = groups * SPAN
    rows = own_ref.shape[0]
    windows = group_windows(groups, model_width // (groups * GROUP))

    @pl.when(step == 0)
    def _():
        expand_into(kexp_ref, kv_ref[0, :, :width], groups)
        expand_into(vexp_ref, kv_ref[0, :, width:], groups)
        dk_ref[...] = jnp.zeros(dk_ref.shape, F32)
        dv_ref[...] = jnp.zeros(dv_ref.shape, F32)

    fetch(span_ref, payload_refs, both_ref)
    payload = both_ref[...]
    tail = payload[:, model_width:]
    grads = dot_nt(payload[:, :model_width], wout_ref[...]).astype(BF)
    grads = pad_columns(grads, select_ref, windows).astype(F32)
    grads = (grads + dot_nn(tail, place_ref[1])).astype(BF)
    shifts = dot_nn(tail, place_ref[0])
    for k, spot in enumerate(spots_of(span_ref, rows)):
        own_part = slice(k * rows, (k + 1) * rows)
        dob_ref[spot, :] = grads[own_part]
        qb_ref[spot, :] = (q_ref[0, spot, :].astype(F32) + shifts[own_part]).astype(BF)
    spread_mask(mask_ref, mask_of(own_ref[...], other_ref[...], True))

    def chunk_step(at, count):
        lines = pl.ds(pl.multiple_of(at * GROUP, HEAD_ROWS * GROUP), count * GROUP)
        mask = mask_ref[pl.ds(at, count)]
        for g in range(groups):
            query_block = qb_ref[:, g * SPAN : (g + 1) * SPAN]
            grad_block = dob_ref[:, g * SPAN : (g + 1) * SPAN]
            dots = dot_nt(kexp_ref[g, lines, :], query_block)
            grads = dot_nt(vexp_ref[g, lines, :], grad_block)
            bias = bias_ref[0, pl.ds(at, count), g * GROUP : (g + 1) * GROUP, :] + mask
            probs = jnp.exp2(dots * scale2 + bias.reshape(dots.shape))
            grad_scores = (probs * grads).astype(BF)
            dk_ref[g, lines, :] += dot_nn(grad_scores, query_block)
            dv_ref[g, lines, :] += dot_nn(probs.astype(BF), grad_block)

    head_steps(span_ref, rows, chunk_step)

    @pl.when(step == span_ref[SPAN_LAST, 0] - span_ref[SPAN_FIRST, 0])
    def _():
        def finish(i, carry):
            at = pl.multiple_of(i * CHUNK, CHUNK)
            lines = pl.ds(pl.multiple_of(i * CHUNK * GROUP, CHUNK * GROUP), CHUNK * GROUP)
            for part, (ref, scale) in enumerate(((dk_ref, head_scale), (dv_ref, 1.0))):
                for g in range(groups):
                    value = collapse(ref[g, lines, :]) * scale
                    low_ref[part, pl.ds(at, CHUNK), g * SPAN : (g + 1) * SPAN] = value.astype(BF)
            return carry

        lax.fori_loop(0, rows // CHUNK, finish, 0)
        for part in range(2):
            dkv_ref[part * model_width : (part + 1) * model_width, :] = drop_turned(
                low_ref[part], select_ref, windows
            )


def fixed(shape):
    return pl.BlockSpec(shape, lambda j, span: (0,) * len(shape), pipeline_mode=pl.Buffered(1))


def pair_at(j, span):
    return jnp.minimum(span[SPAN_FIRST, 0] + j, span[SPAN_LAST, 0])


def moving(shape, rank_at=0, last=0):
    def index(j, span):
        at = [0] * len(shape)
        at[rank_at] = pair_at(j, span)
        if last:
            at[-1] = last
        return tuple(at)

    return pl.BlockSpec(shape, index)


def call(
    kernel, steps, in_specs, out_specs, out_shapes, scratch, flops, name, after=(), carry=(), room=56
):
    extra, given = len(after) + len(carry), len(in_specs)
    single = not isinstance(out_shapes, list)
    if single:
        out_specs, out_shapes = [out_specs], [out_shapes]
    made = len(out_shapes)
    anywhere = pl.BlockSpec(memory_space=pl.ANY)

    def body(span_ref, *refs):
        @pl.when(pl.program_id(0) <= span_ref[SPAN_LAST, 0] - span_ref[SPAN_FIRST, 0])
        def _():
            outs = refs[extra + given : extra + given + made]
            kernel(
                span_ref, *refs[extra : extra + given], *outs, *refs[extra + given + made + len(carry) :]
            )

    inner = pl.pallas_call(
        body,
        grid_spec=pltpu.PrefetchScalarGridSpec(
            num_scalar_prefetch=1,
            grid=(steps,),
            in_specs=[anywhere] * extra + in_specs,
            out_specs=out_specs + [anywhere] * len(carry),
            scratch_shapes=scratch,
        ),
        out_shape=out_shapes + [shape_of(x.shape, x.dtype) for x in carry],
        input_output_aliases={1 + len(after) + k: made + k for k in range(len(carry))},
        compiler_params=pltpu.CompilerParams(
            dimension_semantics=("arbitrary",), vmem_limit_bytes=room * 1024 * 1024
        ),
        cost_estimate=pl.CostEstimate(flops=flops, bytes_accessed=20_000_000, transcendentals=0),
        name=name,
    )

    def run(span, *operands):
        results = inner(span, *after, *carry, *operands)
        return results[0] if single else results

    return run


def shape_of(shape, dtype=F32):
    return jax.ShapeDtypeStruct(shape, dtype)


def once(
    kernel, operands, out_shapes, scratch, flops, name, spaces=(), after=(), carry=(), room=56
):
    spaces = dict(spaces)
    shapes = [*out_shapes, *(shape_of(x.shape, x.dtype) for x in carry)]
    count, extra = len(operands), len(after) + len(carry)
    anywhere = pl.BlockSpec(memory_space=pl.ANY)

    def whole(shape):
        return pl.BlockSpec(shape, lambda j: (0,) * len(shape), pipeline_mode=pl.Buffered(1))

    def body(*refs):
        outs = refs[count + extra : count + extra + len(out_shapes)]
        kernel(*refs[:count], *outs, *refs[count + extra + len(shapes) :])

    results = pl.pallas_call(
        body,
        grid=(1,),
        in_specs=[
            pl.BlockSpec(memory_space=spaces[k]) if k in spaces else whole(x.shape)
            for k, x in enumerate(operands)
        ]
        + [anywhere] * extra,
        out_specs=[whole(x.shape) for x in out_shapes] + [anywhere] * len(carry),
        out_shape=shapes,
        scratch_shapes=scratch,
        input_output_aliases={
            count + len(after) + k: len(out_shapes) + k for k in range(len(carry))
        },
        compiler_params=pltpu.CompilerParams(vmem_limit_bytes=room * 1024 * 1024),
        cost_estimate=pl.CostEstimate(flops=flops, bytes_accessed=5_000_000, transcendentals=0),
        name=name,
    )(*operands, *after, *carry)
    return results


def on_device(
    tokens,
    positions,
    item_of_atom,
    item_lengths,
    atom_types,
    key_mask,
    ln1_gain,
    ln1_bias,
    w_qkv,
    kernel_means,
    kernel_widths,
    kernel_weight,
    type_scale,
    type_shift,
    w_out,
    ln2_gain,
    ln2_bias,
    w_up,
    w_down,
    out_cotangent,
):
    own_rows, model_width = tokens.shape
    assert own_rows == LANES
    kernels, heads = kernel_weight.shape
    head_size = model_width // heads
    head_scale = head_size ** (-0.5)
    scale2 = head_scale * LOG2E
    groups = heads // GROUP
    width = groups * SPAN
    ff_width = w_up.shape[1]
    ka_count = lax.axis_size("ka")
    flat = lax.axis_index("pb") * ka_count + lax.axis_index("ka")
    flat_array = flat.astype(jnp.int32).reshape(1)
    reach = (PROT_LEN + own_rows - 2) // own_rows
    chips = (reach + 1) // 2
    pairs = 2 * chips + 1
    assert pairs == len(SLOTS[0])
    keys = 2 * own_rows
    atoms = positions.shape[1]
    atoms_blocks = atoms // LANES
    types = type_scale.shape[0]
    bits = bits_of("ka") - 1
    up_order = [(0, 1), (1, 2)] + [(bit, 1) for bit in range(3, bits)]
    rest_order = [(bit, 1) for bit in range(bits)]

    window = Window(tokens)
    cotangent_came = core_flip(out_cotangent)
    ln1 = [x.reshape(-1, LANES) for x in (ln1_gain, ln1_bias)]
    ln2 = [x.reshape(-1, LANES) for x in (ln2_gain, ln2_bias)]
    (normed_own,) = once(
        normal_kernel,
        (tokens, *ln1),
        [shape_of(tokens.shape, BF)],
        [],
        1_000_000,
        "first_normal",
        room=16,
    )
    gathered = Gathered(normed_own)

    select = select_table(head_size)
    place = place_table(heads, head_size)
    into_tail, out_of_tail = tail_tables(heads, head_size)
    type_tiles = -(-types // LANES)
    tables = jnp.pad(
        jnp.stack([type_scale, type_shift]), ((0, 0), (0, type_tiles * LANES - types))
    )
    tables = tables.reshape(2, type_tiles, LANES).swapaxes(0, 1).reshape(2 * type_tiles, LANES)
    lengths = jnp.pad(item_lengths, (0, -item_lengths.shape[0] % LANES)).reshape(-1, LANES)
    span, other, own, own_line, tabs, grad_weights, weights_turned, par = once(
        functools.partial(side_kernel, atoms_blocks),
        (
            flat_array,
            positions,
            item_of_atom.reshape(-1, LANES),
            key_mask.reshape(-1, LANES),
            atom_types.reshape(-1, LANES),
            lengths,
            tables,
            kernel_means.reshape(1, LANES),
            kernel_widths.reshape(1, LANES),
            kernel_weight.T,
        ),
        [
            shape_of((SPAN_ROWS, LANES), jnp.int32),
            shape_of((SIDE, pairs * keys)),
            shape_of((own_rows, LANES)),
            shape_of((SIDE, LANES)),
            shape_of((4, kernels, LANES)),
            shape_of((kernels, WEIGHT_PIECES * heads), BF),
            shape_of((heads, kernels), BF),
            shape_of((LANES, LANES)),
        ],
        [],
        1_000_000_000,
        "sides",
        {0: pltpu.SMEM},
    )

    own_spec = fixed((own_rows, LANES))
    other_spec = moving((SIDE, keys), 1)
    bias_spec = moving((1, own_rows, heads, keys))
    bias = call(
        bias_kernel,
        pairs,
        [own_spec, other_spec, fixed((4, kernels, LANES)), fixed((heads, kernels))],
        bias_spec,
        shape_of((pairs, own_rows, heads, keys)),
        [pltpu.VMEM((own_rows, keys), F32)],
        30_000_000_000,
        "pair_bias",
        after=(window.one, window.two, normed_own),
    )(span, own, other, tabs, weights_turned)
    window.middle()
    token_blocks = window.finish()

    expanded = pltpu.VMEM((groups, own_rows * GROUP, SPAN), BF)
    summed = pltpu.VMEM((groups, own_rows * GROUP, SPAN), F32)
    mask_scratch = pltpu.VMEM((own_rows, GROUP, keys), F32)
    line_scratch = pltpu.VMEM((groups, own_rows * GROUP, LANES), F32)
    attended, q_aug, lse_pieces, kvq = call(
        functools.partial(forward_kernel, scale2, groups),
        pairs,
        [own_spec, other_spec]
        + [fixed((own_rows, model_width))] * 14
        + [
            fixed((model_width // LANES, LANES)),
            fixed((model_width // LANES, LANES)),
            fixed((model_width, 3 * model_width)),
            fixed(select.shape),
            fixed((1, width)),
            fixed(place.shape),
            bias_spec,
        ],
        [
            fixed((own_rows, width)),
            fixed((own_rows, width)),
            fixed((PIECES, own_rows, LANES)),
            moving((1, keys, 3 * width)),
        ],
        [
            shape_of((own_rows, width)),
            shape_of((own_rows, width), BF),
            shape_of((PIECES, own_rows, LANES), BF),
            shape_of((pairs, keys, 3 * width), BF),
        ],
        [
            expanded,
            mask_scratch,
            line_scratch,
            line_scratch,
            summed,
            pltpu.VMEM((own_rows, LANES), F32),
            pltpu.VMEM((keys, model_width), BF),
        ],
        25_000_000_000,
        "attention_forward",
        after=(gathered.beside,),
    )(
        span,
        own,
        other,
        *token_blocks,
        *ln1,
        w_qkv,
        select,
        ones_row(heads, head_size),
        place,
        bias,
    )

    far_rows = gathered.far()
    tile = 3 * LANES
    assert ff_width % tile == 0 and tile % (2 * ff_width // ka_count) == 0
    row_shape = shape_of((own_rows, model_width), BF)
    slices = ka_count // 2
    up_rows, out_rows = ff_width // ka_count, model_width // ka_count
    pieces = shape_of((2, slices, up_rows, own_rows), BF)
    block_out, grad_mixed, do_aug, payload, attended_low, normed_second, *parts, ln2_grads = once(
        functools.partial(middle_kernel, groups, tile),
        (
            flat_array,
            tokens,
            attended,
            lse_pieces,
            *ln2,
            out_cotangent,
            w_out,
            w_up,
            w_down,
            select,
            place,
            head_sum_table(heads),
            into_tail,
        ),
        [
            row_shape,
            shape_of((own_rows, model_width)),
            shape_of((own_rows, width), BF),
            shape_of((own_rows, model_width + 2 * LANES), BF),
            row_shape,
            row_shape,
            pieces,
            pieces,
            shape_of((2, model_width)),
        ],
        [
            pltpu.VMEM((model_width, model_width), BF),
            pltpu.VMEM((model_width, ff_width), BF),
            pltpu.VMEM((ff_width, model_width), BF),
            pltpu.VMEM((own_rows, model_width), F32),
            pltpu.VMEM((own_rows, model_width), F32),
            pltpu.SemaphoreType.DMA,
            pltpu.SemaphoreType.DMA((2, ff_width // tile)),
        ],
        10_000_000_000,
        "feed_forward",
        {0: pltpu.SMEM, 7: pl.ANY, 8: pl.ANY, 9: pl.ANY},
        after=tuple(far_rows),
    )
    came = [core_flip(x) for x in (parts[1], normed_second, attended_low, payload)]
    window = Window(payload, came[3])
    gathered.finish()
    half = model_width // 2
    up_kept, up_sent, rest_kept, rest_sent = once(
        functools.partial(weight_grads_kernel, ka_count),
        (
            flat_array,
            parts[0],
            came[0],
            normed_second,
            came[1],
            out_cotangent,
            cotangent_came,
            attended_low,
            came[2],
            payload,
            came[3],
        ),
        [shape_of((slices // 2, up_rows, model_width), BF)] * 2
        + [shape_of((slices, up_rows + out_rows, half), BF)] * 2,
        [pltpu.VMEM((model_width, model_width), F32)],
        5_000_000_000,
        "weight_gradients",
        {0: pltpu.SMEM},
    )
    up_sum = slices_sum(up_kept, up_sent, up_order)
    rest_sum = columns_sum(rest_kept, rest_sent, rest_order)

    dq, grad_scores, window.one, window.two = call(
        functools.partial(query_grad_kernel, scale2, head_scale, groups),
        pairs,
        [
            own_spec,
            other_spec,
            fixed((own_rows, width)),
            fixed((own_rows, width)),
            moving((1, keys, 2 * width)),
            bias_spec,
            fixed(select.shape),
        ],
        [fixed((model_width, own_rows)), moving((1, own_rows, heads, keys))],
        [
            shape_of((model_width, own_rows), BF),
            shape_of((pairs, own_rows, heads, keys), BF),
        ],
        [expanded, expanded, mask_scratch, summed, pltpu.VMEM((own_rows, width), BF)],
        22_000_000_000,
        "query_gradients",
        after=(*up_sum.sent, *rest_sum.sent, window.far),
        carry=(window.one, window.two),
    )(span, own, other, q_aug, do_aug, kvq, bias, select)

    pos_blocks = atoms_blocks + 4 * chips
    small, pos_part = call(
        functools.partial(phi_grad_kernel, 0),
        pairs,
        [
            own_spec,
            other_spec,
            fixed((SIDE, LANES)),
            moving((1, own_rows, heads, keys)),
            fixed((4, kernels, LANES)),
            fixed((kernels, WEIGHT_PIECES * heads)),
            fixed((LANES, LANES)),
        ],
        [fixed((LANES, LANES)), fixed((3 * pos_blocks, LANES))],
        [shape_of((LANES, LANES)), shape_of((3 * pos_blocks, LANES))],
        [
            pltpu.VMEM((own_rows, keys), F32),
            pltpu.VMEM((own_rows, keys), F32),
            pltpu.VMEM((5, own_rows, LANES), F32),
            pltpu.VMEM((kernels, heads), F32),
            pltpu.VMEM((2, kernels, LANES), F32),
            pltpu.VMEM((2, 2 * LANES, LANES), F32),
        ],
        40_000_000_000,
        "kernel_gradients",
    )(span, own, other, own_line, grad_scores, tabs, grad_weights, par)
    window.middle()
    payload_blocks = window.finish()
    early_sum = everywhere_sum(
        jnp.concatenate([small, ln2_grads.reshape(-1, LANES), pos_part], axis=0)
    )
    advance([up_sum, rest_sum, early_sum], flat_array, "sums_first", (small,))

    dkv = call(
        functools.partial(key_grad_kernel, scale2, head_scale, groups, model_width),
        pairs,
        [
            own_spec,
            other_spec,
            pl.BlockSpec(
                (1, own_rows, 2 * width),
                lambda j, span: (chips, span[SPAN_CORE, 0], 0),
                pipeline_mode=pl.Buffered(1),
            ),
            moving((1, keys, width), 0, 2),
        ]
        + [fixed((own_rows, model_width + 2 * LANES))] * 14
        + [
            fixed((model_width, model_width)),
            fixed(select.shape),
            fixed(out_of_tail.shape),
            bias_spec,
        ],
        fixed((2 * model_width, own_rows)),
        shape_of((2 * model_width, own_rows), BF),
        [
            expanded,
            expanded,
            mask_scratch,
            pltpu.VMEM((keys, width), BF),
            pltpu.VMEM((keys, width), BF),
            summed,
            summed,
            pltpu.VMEM((keys, model_width + 2 * LANES), BF),
            pltpu.VMEM((2, own_rows, width), BF),
        ],
        28_000_000_000,
        "key_gradients",
        after=(*up_sum.sent, *rest_sum.sent, *early_sum.sent),
    )(span, own, other, kvq, kvq, *payload_blocks, w_out, select, out_of_tail, bias)

    advance([up_sum, rest_sum, early_sum], flat_array, "sums_second", (dkv,))
    qkv_rows = 3 * model_width // ka_count
    norm_count = model_width // LANES
    sent_rows = qkv_rows + -(-2 * norm_count // 16) * 16
    part_shape = shape_of((ka_count // 4, sent_rows, own_rows), BF)
    grad_tokens, stay, to_core, to_chip, to_both = once(
        functools.partial(first_norm_kernel, ka_count),
        (flat_array, tokens, ln1[0], dq, dkv, w_qkv, grad_mixed),
        [shape_of((own_rows, model_width))] + [part_shape] * 4,
        [pltpu.VMEM((3 * model_width, own_rows), BF)],
        2_000_000_000,
        "first_norm",
        {0: pltpu.SMEM},
        after=tuple(early_sum.sent),
        room=24,
    )
    core_stay, core_go = core_flip(to_core), core_flip(to_both)
    chip_own, chip_core = flip_bit(to_chip, "ka", 1), flip_bit(core_go, "ka", 1)
    groups_out = once(
        regroup_kernel,
        (stay, core_stay, chip_own, chip_core),
        [shape_of((4, sent_rows, own_rows), BF)] * (ka_count // 4),
        [],
        1_000_000,
        "regroup",
        room=24,
    )
    advance([up_sum, rest_sum, early_sum], flat_array, "sums_third", (groups_out[0],))
    groups_in = [groups_out[0]] + [
        flip_mask(groups_out[i], "ka", 4 * i) for i in range(1, ka_count // 4)
    ]
    qkv_part, norm_part = once(
        functools.partial(qkv_grads_kernel, gathered.masks(), ka_count // 4),
        (*groups_in, *gathered.arrays()),
        [shape_of((qkv_rows, model_width), BF), shape_of((sent_rows - qkv_rows, LANES))],
        [],
        3_000_000_000,
        "qkv_gradients",
    )
    qkv_sum = Sum(qkv_part, [qkv_part], over("pb"))
    norm_sum = Sum(norm_part, [norm_part], over("pb"))
    advance([up_sum, rest_sum, early_sum], flat_array, "sums_fourth", (qkv_part,))
    sums = [qkv_sum, norm_sum, up_sum, rest_sum, early_sum]
    while any(one.stages for one in sums):
        advance(sums, flat_array, "sums_last")
    joined = early_sum.total
    up_total, rest_total = up_sum.total, rest_sum.total
    norms, by_weight, by_mean, by_width, by_scale, by_shift, grad_positions = once(
        functools.partial(results_kernel, heads, types),
        (flat_array, joined, norm_sum.total),
        [
            shape_of((4, norm_count, LANES)),
            shape_of((kernels, heads)),
            shape_of((1, kernels)),
            shape_of((1, kernels)),
            shape_of((1, types)),
            shape_of((1, types)),
            shape_of((3, LANES)),
        ],
        [],
        1_000_000,
        "results",
        {0: pltpu.SMEM},
        room=16,
    )
    qkv_total = qkv_sum.total
    return (
        block_out,
        grad_tokens,
        grad_positions,
        norms[0].reshape(-1),
        norms[1].reshape(-1),
        qkv_total.T,
        by_mean.reshape(-1),
        by_width.reshape(-1),
        by_weight,
        by_scale.reshape(-1),
        by_shift.reshape(-1),
        rest_total[up_rows:].T,
        norms[2].reshape(-1),
        norms[3].reshape(-1),
        up_total.T,
        rest_total[:up_rows],
    )


def solution(mesh):
    rows = P(MESH, None)
    in_specs = (rows,) + (P(),) * 18 + (rows,)
    out_specs = (
        rows,
        rows,
        P(None, MESH),
        P(),
        P(),
        P(None, "ka"),
        P(),
        P(),
        P(),
        P(),
        P(),
        P(None, "ka"),
        P(),
        P(),
        P(None, "ka"),
        P("ka", None),
    )
    return jax.shard_map(
        on_device, mesh=mesh, in_specs=in_specs, out_specs=out_specs, check_vma=False
    )
```

```python
import functools
import math

import jax
import jax.numpy as jnp
import numpy as np
from jax import lax
from jax.experimental import pallas as pl
from jax.experimental.pallas import tpu as pltpu
from jax.sharding import PartitionSpec as P

MOL_TYPES = 128
PROT_LEN = 768
MOL_MEAN = 32

LN_EPS = 1e-05
GELU_SLOPE = math.sqrt(2.0 / math.pi)
GELU_CUBE = 0.044715
MASKED = -1e30
ROOT_TWO_PI = math.sqrt(2.0 * math.pi)
LOG2E = math.log2(math.e)
KAPPA = math.sqrt(0.5 * LOG2E)

PAD = 32
GROUP = 8
SPAN = PAD * GROUP
PIECES = 3
WEIGHT_PIECES = 2
CHUNK = 32
HEAD_ROWS = 64
BIAS_ROWS = 64
FEW = 8
MESH = ("pb", "ka")

BF = jnp.bfloat16
F32 = jnp.float32


def shifted(block, axis, distance):
    devices = range(lax.axis_size(axis))
    route = [(i - distance, i) for i in devices if i - distance in devices]
    return lax.ppermute(block, axis, route)


def core_flip(block):
    devices = range(lax.axis_size(MESH))
    return lax.ppermute(block, MESH, [(i, i ^ 1) for i in devices])


class Window:
    def __init__(self, block, sibling=None):
        devices = range(lax.axis_size(MESH))
        levels = len(devices) // 4

        def of(level, rest):
            return level % levels * 4 + rest

        one, two, far = [], [], []
        for i in devices:
            level, chip, core = i // 4, (i >> 1) & 1, i & 1
            odd = level & 1
            one.append((i, of(level + (-1 if odd else 1), i % 4)))
            two.append((i, of(level + (1 if odd else -1), i % 4)))
            far.append((i, of(level + (2 if chip else -2), (1 - chip) * 2 + core)))
        self.block, self.sibling = block, sibling
        self.one = lax.ppermute(block, MESH, one)
        self.two = lax.ppermute(block, MESH, two)
        self.far = lax.ppermute(block, MESH, far)

    def middle(self):
        self.other_chip = [flip_bit(x, "ka", 1) for x in (self.block, self.one, self.two)]
        return self.other_chip

    def finish(self):
        beside, one, two = self.other_chip
        mine = [self.far, self.one, one, self.block, beside, self.two, two]
        came = [core_flip(x) for x in mine if x is not self.block]
        own = core_flip(self.block) if self.sibling is None else self.sibling
        return mine + came[:3] + [own] + came[3:]


class Gathered:
    def __init__(self, block):
        self.own, self.own_sibling = block, core_flip(block)
        self.beside = flip_bit(block, "ka", 1)

    def far(self):
        mine = jnp.stack([self.own, self.beside])
        self.groups = [
            flip_mask(mine, "ka", mask) for mask in range(4, lax.axis_size("ka"), 4)
        ]
        return self.groups

    def finish(self):
        self.beside_sibling = core_flip(self.beside)
        self.siblings = [core_flip(x) for x in self.groups]

    def arrays(self):
        return [
            *(x[None] for x in (self.own, self.own_sibling, self.beside, self.beside_sibling)),
            *self.groups,
            *self.siblings,
        ]

    def masks(self):
        far = range(4, lax.axis_size("ka"), 4)
        return [
            (0,), (1,), (2,), (3,),
            *((mask, mask + 2) for mask in far),
            *((mask + 1, mask + 3) for mask in far),
        ]


SLOTS = (
    (0, 5, 6, 3, 4, 1, 2),
    (6, 5, 4, 3, 2, 1, 0),
    (0, 1, 2, 3, 4, 5, 6),
    (2, 1, 4, 3, 6, 5, 0),
)
SPAN_FIRST, SPAN_LAST, SPAN_CORE, SPAN_CHIP, SPAN_SLOT = 0, 1, 2, 3, 4
SPAN_LOW = 16
SPAN_HIGH = 32
SPAN_ROWS = 48
LANES = 128
SIDE = 16


def flip_bit(block, axis, bit):
    devices = range(lax.axis_size(axis))
    return lax.ppermute(block, axis, [(i, i ^ (1 << bit)) for i in devices])


def bits_of(axis):
    return (lax.axis_size(axis) - 1).bit_length()


def flip_mask(block, axis, mask):
    devices = range(lax.axis_size(axis))
    return lax.ppermute(block, axis, [(i, i ^ mask) for i in devices])


class Sum:
    def __init__(self, kept, sent, stages, left=()):
        self.kept, self.sent, self.stages, self.left = kept, list(sent), list(stages), list(left)
        self.total, self.cut = None, 0

    def came(self):
        axis, bit, count = self.stages[0][:3]
        partners = range(1, 2**count)
        return [flip_mask(x, axis, p << bit) for x, p in zip(self.sent, partners, strict=True)]

    def plan(self):
        stage = self.stages.pop(0)
        if len(stage) == 4:
            return ("join", self.cut)
        if self.stages and self.stages[0][0] == "ka" and self.left:
            bit, count = self.stages[0][1] - 1, self.stages[0][2]
            self.left = [b for b in self.left if not bit <= b < bit + count]
            below = sum(1 for b in self.left if b < bit)
            return ("part", bit, count, 2 ** (len(self.left) - below), 2**below)
        return ("whole",)


def over(axis, first=0):
    return [(axis, bit, 1) for bit in range(first, bits_of(axis))]


def slices_sum(kept, sent, order):
    stages = [("ka", bit + 1, count) for bit, count in order] + over("pb")
    left = [b for bit, count in order[1:] for b in range(bit, bit + count)]
    return Sum(kept, [sent], stages, left)


def columns_sum(kept, sent, order):
    stages = [("pb", 0, 1)] + [("ka", bit + 1, count) for bit, count in order]
    left = [b for bit, count in order for b in range(bit, bit + count)]
    return Sum(kept, [sent], stages + over("pb", 1) + [("pb", 0, 1, "join")], left)


def everywhere_sum(values):
    return Sum(values, [values], over("ka") + over("pb"))


def stage_kernel(plans, counts, side_bit, flat_ref, *refs):
    flat = flat_ref[0]
    refs = list(refs)
    kept_refs = [refs.pop(0) for _ in plans]
    came_refs = [[refs.pop(0) for _ in range(count)] for count in counts]
    for plan, kept, came in zip(plans, kept_refs, came_refs):

        def total(*at):
            value = kept[at].astype(F32)
            for ref in came:
                value = value + ref[at].astype(F32)
            return value

        out = refs.pop(0)
        if plan[0] == "whole":
            out[...] = total(Ellipsis).astype(out.dtype)
        elif plan[0] == "join":
            half, cut = kept.shape[-1], plan[1]
            side = jnp.right_shift(flat, side_bit) & 1
            for ref, rows in ((out, slice(0, cut)), (refs.pop(0), slice(cut, None))):
                for which, given in ((side, kept), (1 - side, came[0])):
                    spot = pl.ds(pl.multiple_of(which * half, LANES), half)
                    ref[:, spot] = given[rows, :].astype(F32)
        else:
            _, bit, count, above, below = plan
            mine = jnp.right_shift(flat, bit + 1) & (2**count - 1)
            outs = [out] + [refs.pop(0) for _ in range(2**count - 1)]
            for i in range(above):
                for j in range(below):
                    for other, ref in enumerate(outs):
                        group = jnp.bitwise_xor(mine, other)
                        ref[i * below + j] = total((i * 2**count + group) * below + j).astype(BF)


def advance(sums, flat_array, name, after=()):
    sums = [one for one in sums if one.stages]
    if not sums:
        return
    came = [one.came() for one in sums]
    plans, shapes, sizes = [], [], []
    for one in sums:
        plan = one.plan()
        shape, dtype, size = one.kept.shape, one.kept.dtype, 1
        if plan[0] == "join":
            shapes.append(shape_of((plan[1], 2 * shape[1]), F32))
            shape, dtype = (shape[0] - plan[1], 2 * shape[1]), F32
        elif plan[0] == "part":
            shape, size = (plan[3] * plan[4], *shape[1:]), 2 ** plan[2]
        elif not one.stages:
            dtype = F32
        shapes += [shape_of(shape, dtype)] * size
        plans.append(plan)
        sizes.append(2 if plan[0] == "join" else size)
    results = once(
        functools.partial(stage_kernel, plans, [len(x) for x in came], bits_of("ka")),
        (flat_array, *(one.kept for one in sums), *(x for group in came for x in group)),
        shapes,
        [],
        1_000_000_000,
        name,
        {0: pltpu.SMEM},
        after=after,
        room=24,
    )
    results = list(results)
    for one, size, plan in zip(sums, sizes, plans):
        if plan[0] == "join":
            one.total = [results.pop(0) for _ in range(size)]
            continue
        one.kept = results.pop(0)
        one.sent = [results.pop(0) for _ in range(size - 1)] or [one.kept]
        if not one.stages:
            one.total = one.kept
        elif one.kept.ndim == 3 and one.kept.shape[0] == 1 and one.stages[0][0] == "pb":
            one.kept = one.kept.reshape(one.kept.shape[1:])
            one.sent = [one.kept]


def layer_norm(values, ln_gain, ln_shift):
    centre = jnp.mean(values, axis=-1, keepdims=True)
    offsets = values - centre
    spread = jnp.mean(offsets * offsets, axis=-1, keepdims=True)
    return offsets * lax.rsqrt(spread + LN_EPS) * ln_gain + ln_shift


def dot_nn(left, right):
    return lax.dot_general(left, right, (((1,), (0,)), ((), ())), preferred_element_type=F32)


def dot_nt(left, right):
    return lax.dot_general(left, right, (((1,), (1,)), ((), ())), preferred_element_type=F32)


def dot_tn(left, right):
    return lax.dot_general(left, right, (((0,), (0,)), ((), ())), preferred_element_type=F32)


def select_table(head_size):
    column = np.arange(SPAN)
    source = (column // PAD) * head_size + column % PAD
    table = [
        (column[:, None] == (source + off)[None, :]) & (column % PAD < head_size)[None, :]
        for off in (0, 64)
    ]
    return np.stack(table).astype(BF)


def group_windows(groups, head_size):
    out = []
    for g in range(groups):
        start = g * GROUP * head_size
        out.append((start // LANES * LANES, (start % LANES) // 64))
    return out


def place_table(heads, head_size):
    column = np.arange(heads * PAD)
    lane = np.arange(LANES)
    return np.stack(
        [
            (lane[:, None] == (column // PAD)[None, :])
            & (column % PAD == head_size + p)[None, :]
            for p in range(PIECES)
        ]
    ).astype(BF)


def tail_tables(heads, head_size):
    lane, tail = np.arange(LANES), np.arange(2 * LANES)
    into = np.stack(
        [
            (lane[:, None] + p * heads == tail[None, :]) & (lane < heads)[:, None]
            for p in range(2 * PIECES)
        ]
    )
    column = np.arange(heads * PAD)
    piece = column % PAD - head_size
    free = (piece >= 0) & (piece < PIECES)
    lane_of = np.where(free, piece * heads + column // PAD, -1)
    out = np.stack(
        [
            (tail[:, None] == lane_of[None, :]) & free[None, :],
            (tail[:, None] - PIECES * heads == lane_of[None, :]) & free[None, :],
        ]
    )
    return into.astype(BF), out.astype(BF)


def ones_row(heads, head_size):
    column = np.arange(heads * PAD) % PAD
    return ((column >= head_size) & (column < head_size + PIECES)).astype(np.float32)[None]


def head_sum_table(heads):
    column = np.arange(heads * PAD)
    return (column[:, None] // PAD == np.arange(LANES)[None, :]).astype(BF)


def pad_columns(values, select_ref, windows):
    parts = [
        dot_nn(values[:, start : start + SPAN], select_ref[kind]).astype(BF)
        for start, kind in windows
    ]
    return jnp.concatenate(parts, axis=1)


def drop_columns(values, select_ref, windows):
    tiles = {}
    for g, (start, kind) in enumerate(windows):
        part = dot_nt(values[:, g * SPAN : (g + 1) * SPAN], select_ref[kind])
        for k in range(SPAN // LANES):
            tile = part[:, k * LANES : (k + 1) * LANES]
            at = start // LANES + k
            tiles[at] = tiles[at] + tile if at in tiles else tile
    return jnp.concatenate([tiles[at] for at in sorted(tiles)], axis=1).astype(BF)


def drop_turned(values, select_ref, windows):
    tiles = {}
    for g, (start, kind) in enumerate(windows):
        part = dot_nt(select_ref[kind], values[:, g * SPAN : (g + 1) * SPAN])
        for k in range(SPAN // LANES):
            tile = part[k * LANES : (k + 1) * LANES]
            at = start // LANES + k
            tiles[at] = tiles[at] + tile if at in tiles else tile
    return jnp.concatenate([tiles[at] for at in sorted(tiles)], axis=0).astype(BF)


def row_of(ref):
    return jnp.concatenate([ref[k : k + 1, :] for k in range(ref.shape[0])], axis=1)


def split(values, count):
    rest, out = values, []
    for _ in range(count):
        piece = rest.astype(BF)
        rest = rest - piece.astype(F32)
        out.append(piece)
    return out


def norm_parts(values):
    centre = jnp.mean(values, axis=-1, keepdims=True)
    offsets = values - centre
    spread = jnp.mean(offsets * offsets, axis=-1, keepdims=True)
    slope = lax.rsqrt(spread + LN_EPS)
    return offsets * slope, slope


def norm_back(grad, normal, slope, gain):
    inner = grad * gain
    mean = jnp.mean(inner, axis=-1, keepdims=True)
    tilt = jnp.mean(inner * normal, axis=-1, keepdims=True)
    by_gain = jnp.sum(grad * normal, axis=0, keepdims=True)
    by_shift = jnp.sum(grad, axis=0, keepdims=True)
    return slope * (inner - mean - normal * tilt), by_gain, by_shift


def stretched_of(own, other):
    delta = [own[:, i : i + 1] - other[i : i + 1, :] for i in range(3)]
    square = delta[0] * delta[0] + delta[1] * delta[1] + delta[2] * delta[2]
    dist = jnp.sqrt(square + 1.0)
    scales = own[:, 3:4] * other[3:4, :]
    stretched = scales * dist + own[:, 4:5] + other[4:5, :]
    return delta, dist, scales, stretched


def mask_of(own, other, key_is_own):
    same = own[:, 5:6] == other[5:6, :]
    itself = own[:, 7:8] == other[7:8, :]
    is_open = (own[:, 6:7] > 0.5) if key_is_own else (other[6:7, :] > 0.5)
    return jnp.where(same & (is_open | itself), 0.0, MASKED)


def line_atoms(lines):
    line = lax.broadcasted_iota(jnp.int32, (lines, lines // GROUP), 0)
    atom = lax.broadcasted_iota(jnp.int32, (lines, lines // GROUP), 1)
    return jnp.where(line // GROUP == atom, 1.0, 0.0).astype(BF)


def line_heads(lines):
    line = lax.broadcasted_iota(jnp.int32, (lines, SPAN), 0)
    column = lax.broadcasted_iota(jnp.int32, (lines, SPAN), 1)
    return jnp.where(column // PAD == line % GROUP, 1.0, 0.0)


def expand_into(out_ref, padded, groups):
    lines = CHUNK * GROUP
    keep = line_heads(lines).astype(BF)
    spread = line_atoms(lines)
    for g in range(groups):
        for i in range(padded.shape[0] // CHUNK):
            part = padded[i * CHUNK : (i + 1) * CHUNK, g * SPAN : (g + 1) * SPAN]
            out_ref[g, i * lines : (i + 1) * lines, :] = dot_nn(spread, part).astype(BF) * keep


def collapse(values):
    lines = values.shape[0]
    kept = values * line_heads(lines)
    high = kept.astype(BF)
    low = (kept - high.astype(F32)).astype(BF)
    line = lax.broadcasted_iota(jnp.int32, (lines // GROUP, lines), 1)
    atom = lax.broadcasted_iota(jnp.int32, (lines // GROUP, lines), 0)
    gather = jnp.where(line // GROUP == atom, 1.0, 0.0).astype(BF)
    return dot_nn(gather, high) + dot_nn(gather, low)


def fetch(span_ref, refs, out_ref):
    slot = span_ref[SPAN_SLOT + span_ref[SPAN_FIRST, 0] + pl.program_id(0), 0]
    count = len(refs) // 2
    rows = refs[0].shape[0]
    for k in range(count):

        @pl.when(slot == k)
        def _():
            out_ref[:rows] = refs[k][...]
            out_ref[rows:] = refs[count + k][...]


def spots_of(span_ref, rows):
    core = span_ref[SPAN_CORE, 0]
    return [pl.ds(pl.multiple_of(at * rows, rows), rows) for at in (core, 1 - core)]


def spread_mask(mask_ref, mask):
    mask_ref[...] = jnp.broadcast_to(mask[:, None, :], mask_ref.shape)


def reaches(span_ref, first, last, low, high):
    return (span_ref[SPAN_LOW + first, 0] <= high) & (span_ref[SPAN_HIGH + last, 0] >= low)


def head_steps(span_ref, rows, step):
    pair = span_ref[SPAN_FIRST, 0] + pl.program_id(0)
    few = HEAD_ROWS // FEW

    def one(i, carry):
        @pl.when(reaches(span_ref, i * few, i * few + few - 1, 2 * pair, 2 * pair + 1))
        def _():
            step(pl.multiple_of(i * HEAD_ROWS, HEAD_ROWS), HEAD_ROWS)

        return carry

    lax.fori_loop(0, rows // HEAD_ROWS, one, 0)


def kernel_steps(span_ref, first, rows, size, step, skipped):
    pair = span_ref[SPAN_FIRST, 0] + pl.program_id(0)
    few = size // FEW

    def one(i, carry):
        at = pl.multiple_of(i * size, size)
        chunk = first // FEW + i * few
        for half in range(2):
            block = 2 * pair + half
            needed = reaches(span_ref, chunk, chunk + few - 1, block, block)

            @pl.when(needed)
            def _():
                step(at, half)

            @pl.when(jnp.logical_not(needed))
            def _():
                skipped(at, half)

        return carry

    lax.fori_loop(0, rows // size, one, 0)


def side_kernel(
    atoms_blocks,
    flat_ref,
    pos_ref,
    item_ref,
    open_ref,
    type_ref,
    length_ref,
    table_ref,
    means_ref,
    widths_ref,
    kw_ref,
    span_ref,
    other_ref,
    own_ref,
    line_ref,
    tab_ref,
    gw_ref,
    kwt_ref,
    par_ref,
):
    flat = flat_ref[0]
    chips = len(SLOTS[0]) // 2
    first_block = flat // 2 * 2 - 2 * chips
    lane = lax.broadcasted_iota(jnp.int32, (1, LANES), 1)
    tables = []
    for k in range(table_ref.shape[0] // 2):
        rows = split(table_ref[2 * k : 2 * k + 1, :], PIECES)
        rows += split(table_ref[2 * k + 1 : 2 * k + 2, :], PIECES)
        rows += [jnp.zeros((2, LANES), BF)]
        tables.append(jnp.concatenate([row.astype(F32) for row in rows], axis=0).astype(BF))
    flags = [
        jnp.broadcast_to(
            jnp.where(length_ref[k : k + 1, :] > 2 * MOL_MEAN, float(MOL_TYPES), 0.0), (8, LANES)
        ).astype(BF)
        for k in range(length_ref.shape[0])
    ]
    gathered = [[] for _ in range(7)]
    for b in range(other_ref.shape[1] // LANES):
        block = first_block + b
        inside = (block >= 0) & (block < atoms_blocks)
        source = jnp.clip(block, 0, atoms_blocks - 1)
        at = pl.ds(pl.multiple_of(source * LANES, LANES), LANES)
        for k in range(3):
            gathered[k].append(pos_ref[k : k + 1, at])
        gathered[3].append(jnp.where(inside, item_ref[pl.ds(source, 1), :].astype(F32), -1.0))
        gathered[4].append(open_ref[pl.ds(source, 1), :].astype(F32))
        gathered[5].append((block * LANES + lane).astype(F32))
        gathered[6].append(type_ref[pl.ds(source, 1), :].astype(F32))
    rows = [jnp.concatenate(row, axis=1) for row in gathered]
    item, kind = rows[3], rows[6]
    ids = lax.broadcasted_iota(jnp.int32, (LANES, item.shape[1]), 0).astype(F32)
    protein = jnp.zeros_like(kind)
    for k, flag in enumerate(flags):
        onehot = jnp.where(ids + float(k * LANES) == item, 1.0, 0.0).astype(BF)
        protein = protein + dot_nn(flag, onehot)[0:1, :]
    kind = kind + protein
    found = jnp.zeros((8, item.shape[1]), F32)
    for k, table in enumerate(tables):
        onehot = jnp.where(ids + float(k * LANES) == kind, 1.0, 0.0).astype(BF)
        found = found + dot_nn(table, onehot)
    scale = found[0:1] + found[1:2] + found[2:3]
    shift = found[3:4] + found[4:5] + found[5:6]
    rows = [*rows[:3], scale, shift, item, rows[4], rows[5], kind]
    rows.append(jnp.zeros((SIDE - len(rows), item.shape[1]), F32))
    other_ref[...] = jnp.concatenate(rows, axis=0)
    own_at = pl.ds(pl.multiple_of((flat - first_block) * LANES, LANES), LANES)
    line_ref[...] = other_ref[:, own_at]

    line = line_ref[...]
    turned = jnp.transpose(
        jnp.concatenate([line, jnp.zeros((LANES - SIDE, LANES), F32)], axis=0)
    )
    own_ref[...] = turned
    chunks = LANES // FEW
    item_column = jnp.broadcast_to(own_ref[:, 5:6], (LANES, LANES))
    par_ref[...] = item_column
    first_item = par_ref[pl.ds(0, chunks, stride=FEW), :]
    last_item = par_ref[pl.ds(FEW - 1, chunks, stride=FEW), :]

    def count(k, carry):
        row = item_ref[pl.ds(k, 1), :].astype(F32)
        below, upto = carry
        return (
            below + jnp.where(row < first_item, 1.0, 0.0),
            upto + jnp.where(row <= last_item, 1.0, 0.0),
        )

    zero = jnp.zeros((chunks, LANES), F32)
    below, upto = lax.fori_loop(0, atoms_blocks, count, (zero, zero))
    below = jnp.sum(below, axis=1, keepdims=True).astype(jnp.int32)
    upto = jnp.sum(upto, axis=1, keepdims=True).astype(jnp.int32)
    low = jnp.right_shift(below - first_block * LANES, 7)
    high = jnp.right_shift(upto - 1 - first_block * LANES, 7)
    span_ref[SPAN_LOW : SPAN_LOW + chunks, :] = jnp.broadcast_to(low, (chunks, LANES))
    span_ref[SPAN_HIGH : SPAN_HIGH + chunks, :] = jnp.broadcast_to(high, (chunks, LANES))
    row = lax.broadcasted_iota(jnp.int32, (SPAN_LOW, LANES), 0)
    kind = (flat // 2) % 4
    head = jnp.where(row == SPAN_FIRST, jnp.right_shift(low[0:1, :], 1), 0)
    head = head + jnp.where(row == SPAN_LAST, jnp.right_shift(high[chunks - 1 :, :], 1), 0)
    head = head + jnp.where(row == SPAN_CORE, flat % 2, 0)
    head = head + jnp.where(row == SPAN_CHIP, flat // 2, 0)
    for k, slots in enumerate(zip(*SLOTS)):
        slot = sum(jnp.where(kind == which, at, 0) for which, at in enumerate(slots))
        head = head + jnp.where(row == SPAN_SLOT + k, slot, 0)
    span_ref[:SPAN_LOW, :] = head

    def column_of(ref):
        return jnp.transpose(jnp.broadcast_to(ref[...], (LANES, LANES)))

    means, widths = column_of(means_ref), column_of(widths_ref)
    peaks = 1.0 / (ROOT_TWO_PI * widths)
    bend = -(KAPPA * KAPPA) / (widths * widths)
    tab_ref[0] = means
    tab_ref[1] = KAPPA / widths
    tab_ref[2] = LOG2E * jnp.log(peaks)
    tab_ref[3] = bend
    turned_weights = kw_ref[...].astype(F32)
    heads = turned_weights.shape[0]
    filler = jnp.zeros((LANES - heads, LANES), F32)
    wide = jnp.transpose(jnp.concatenate([turned_weights, filler], axis=0))
    weights = wide[:, :heads]
    scaled = weights * (peaks / (widths * widths))[:, :heads]
    gw_ref[...] = jnp.concatenate(split(scaled, WEIGHT_PIECES), axis=1)
    kwt_ref[...] = kw_ref[...]
    lanes = lax.broadcasted_iota(jnp.int32, (LANES, LANES), 1)
    par = wide + jnp.where(lanes == heads, peaks, 0.0)
    par_ref[...] = par + jnp.where(lanes == heads + 1, 1.0 / widths, 0.0)


def bias_kernel(span_ref, own_ref, other_ref, tab_ref, kwt_ref, out_ref, str_ref):
    rows, keys = str_ref.shape
    kernels = tab_ref.shape[1]
    heads = kwt_ref.shape[0]
    half_keys = keys // 2
    str_ref[...] = stretched_of(own_ref[...], other_ref[...])[3]

    def step(at, half):
        columns = slice(half * half_keys, (half + 1) * half_keys)
        block = str_ref[pl.ds(at, BIAS_ROWS), columns]
        for r in range(0, BIAS_ROWS, 2):
            parts = []
            for q in range(2):
                line = jnp.broadcast_to(block[r + q : r + q + 1], (kernels, half_keys))
                z = (line - tab_ref[0]) * tab_ref[1]
                parts.append(jnp.exp2(tab_ref[2] - z * z).astype(BF))
            result = dot_nn(kwt_ref[...], jnp.concatenate(parts, axis=1)) * LOG2E
            out_ref[0, at + r, :, columns] = result[:, :half_keys]
            out_ref[0, at + r + 1, :, columns] = result[:, half_keys:]

    def skipped(at, half):
        columns = slice(half * half_keys, (half + 1) * half_keys)
        out_ref[0, pl.ds(at, BIAS_ROWS), :, columns] = jnp.zeros((BIAS_ROWS, heads, half_keys), F32)

    kernel_steps(span_ref, 0, rows, BIAS_ROWS, step, skipped)


def forward_kernel(
    scale2,
    groups,
    span_ref,
    own_ref,
    other_ref,
    *refs,
):
    token_refs, refs = refs[:14], refs[14:]
    gain_ref, shift_ref, w_ref, select_ref, ones_ref, place_ref, bias_ref, *refs = refs
    att_ref, qaug_ref, lse_ref, kvq_ref, *refs = refs
    qexp_ref, mask_ref, max_ref, sum_ref, acc_ref, lane_ref, both_ref = refs
    step = pl.program_id(0)
    width = groups * SPAN
    tok_ref = token_refs[3]
    rows, model_width = tok_ref.shape
    windows = group_windows(groups, model_width // (groups * GROUP))
    gain, shift = row_of(gain_ref), row_of(shift_ref)

    @pl.when(step == 0)
    def _():
        normed = layer_norm(tok_ref[...].astype(F32), gain, shift).astype(BF)
        query = dot_nn(normed, w_ref[:, :model_width]).astype(BF)
        query = pad_columns(query, select_ref, windows)
        qaug_ref[...] = query
        expand_into(qexp_ref, query, groups)
        max_ref[...] = jnp.full(max_ref.shape, 2.0 * MASKED, F32)
        sum_ref[...] = jnp.zeros(sum_ref.shape, F32)
        acc_ref[...] = jnp.zeros(acc_ref.shape, F32)

    fetch(span_ref, token_refs, both_ref)
    normed = layer_norm(both_ref[...].astype(F32), gain, shift).astype(BF)
    spots = spots_of(span_ref, rows)

    for part in range(3):
        source = (part + 1) % 3 * model_width
        value = dot_nn(normed, w_ref[:, source : source + model_width]).astype(BF)
        value = pad_columns(value, select_ref, windows)
        if part < 2:
            value = value + ones_ref[...].astype(BF)
        for k in range(2):
            kvq_ref[0, spots[k], part * width : (part + 1) * width] = (
                value[k * rows : (k + 1) * rows]
            )
    spread_mask(mask_ref, mask_of(own_ref[...], other_ref[...], False))

    def chunk_step(at, count):
        lines = pl.ds(pl.multiple_of(at * GROUP, HEAD_ROWS * GROUP), count * GROUP)
        mask = mask_ref[pl.ds(at, count)]
        for g in range(groups):
            columns = slice(g * SPAN, (g + 1) * SPAN)
            dots = dot_nt(qexp_ref[g, lines, :], kvq_ref[0, :, columns])
            bias = bias_ref[0, pl.ds(at, count), g * GROUP : (g + 1) * GROUP, :] + mask
            scores = dots * scale2 + bias.reshape(dots.shape)
            old = max_ref[g, lines, :]
            top = jnp.maximum(scores[:, :128], scores[:, 128:])
            new = jnp.maximum(old, jnp.max(top, axis=1, keepdims=True))
            alpha = jnp.exp2(old - new)
            low = jnp.exp2(scores[:, :128] - new)
            high = jnp.exp2(scores[:, 128:] - new)
            max_ref[g, lines, :] = new
            sum_ref[g, lines, :] = sum_ref[g, lines, :] * alpha + (low + high)
            probs = jnp.concatenate([low, high], axis=1).astype(BF)
            values = dot_nn(probs, kvq_ref[0, :, width + g * SPAN : width + (g + 1) * SPAN])
            wide = jnp.concatenate([alpha, alpha], axis=1)
            acc_ref[g, lines, :] = acc_ref[g, lines, :] * wide + values

    head_steps(span_ref, rows, chunk_step)

    @pl.when(step == span_ref[SPAN_LAST, 0] - span_ref[SPAN_FIRST, 0])
    def _():
        lane = lax.broadcasted_iota(jnp.int32, (GROUP, 128), 1)
        head = lax.broadcasted_iota(jnp.int32, (GROUP, 128), 0)

        def finish(i, carry):
            at = pl.multiple_of(i * CHUNK, CHUNK)
            lines = pl.ds(pl.multiple_of(i * CHUNK * GROUP, CHUNK * GROUP), CHUNK * GROUP)
            lanes = jnp.zeros((CHUNK, 128), F32)
            for g in range(groups):
                total = jnp.sum(sum_ref[g, lines, :], axis=1, keepdims=True)
                attended = collapse(acc_ref[g, lines, :] / total)
                att_ref[pl.ds(at, CHUNK), g * SPAN : (g + 1) * SPAN] = attended
                lse = max_ref[g, lines, :] + jnp.log(total) * LOG2E
                own_lane = jnp.where(lane == head + g * GROUP, 1.0, 0.0)
                lanes = lanes + jnp.sum(
                    lse.reshape(CHUNK, GROUP, 128) * own_lane[None], axis=1
                )
            lane_ref[pl.ds(at, CHUNK), :] = lanes
            return carry

        lax.fori_loop(0, rows // CHUNK, finish, 0)
        rest = lane_ref[...] * (-1.0 / scale2)
        query = qaug_ref[...].astype(F32)
        for p in range(PIECES):
            piece = rest.astype(BF)
            rest = rest - piece.astype(F32)
            lse_ref[p] = piece
            query = query + dot_nn(piece, place_ref[p])
        qaug_ref[...] = query.astype(BF)


def query_grad_kernel(
    scale2,
    head_scale,
    groups,
    span_ref,
    own_ref,
    other_ref,
    qaug_ref,
    doaug_ref,
    kv_ref,
    bias_ref,
    select_ref,
    dq_ref,
    ds_ref,
    qexp_ref,
    doexp_ref,
    mask_ref,
    dqacc_ref,
    low_ref,
):
    step = pl.program_id(0)
    width = groups * SPAN
    rows, keys = own_ref.shape[0], other_ref.shape[1]
    windows = group_windows(groups, dq_ref.shape[0] // (groups * GROUP))

    @pl.when(step == 0)
    def _():
        expand_into(qexp_ref, qaug_ref[...], groups)
        expand_into(doexp_ref, doaug_ref[...], groups)
        dqacc_ref[...] = jnp.zeros(dqacc_ref.shape, F32)

    spread_mask(mask_ref, mask_of(own_ref[...], other_ref[...], False))

    def chunk_step(at, count):
        lines = pl.ds(pl.multiple_of(at * GROUP, HEAD_ROWS * GROUP), count * GROUP)
        mask = mask_ref[pl.ds(at, count)]
        waiting = []
        for g in range(groups):
            key_block = kv_ref[0, :, g * SPAN : (g + 1) * SPAN]
            value_block = kv_ref[0, :, width + g * SPAN : width + (g + 1) * SPAN]
            dots = dot_nt(qexp_ref[g, lines, :], key_block)
            grads = dot_nt(doexp_ref[g, lines, :], value_block)
            bias = bias_ref[0, pl.ds(at, count), g * GROUP : (g + 1) * GROUP, :] + mask
            probs = jnp.exp2(dots * scale2 + bias.reshape(dots.shape))
            grad_scores = probs * grads
            dqacc_ref[g, lines, :] += dot_nn(grad_scores.astype(BF), key_block)
            waiting.append(grad_scores.reshape(count, GROUP, keys))
            if len(waiting) == 2:
                ds_ref[0, pl.ds(at, count), (g - 1) * GROUP : (g + 1) * GROUP, :] = (
                    jnp.concatenate(waiting, axis=1).astype(BF)
                )
                waiting = []

    head_steps(span_ref, rows, chunk_step)

    @pl.when(step == span_ref[SPAN_LAST, 0] - span_ref[SPAN_FIRST, 0])
    def _():
        def finish(i, carry):
            at = pl.multiple_of(i * CHUNK, CHUNK)
            lines = pl.ds(pl.multiple_of(i * CHUNK * GROUP, CHUNK * GROUP), CHUNK * GROUP)
            for g in range(groups):
                value = collapse(dqacc_ref[g, lines, :]) * head_scale
                low_ref[pl.ds(at, CHUNK), g * SPAN : (g + 1) * SPAN] = value.astype(BF)
            return carry

        lax.fori_loop(0, rows // CHUNK, finish, 0)
        dq_ref[...] = drop_turned(low_ref[...], select_ref, windows)


def phi_grad_kernel(
    first_row,
    span_ref,
    own_ref,
    other_ref,
    line_ref,
    ds_ref,
    tab_ref,
    kw_ref,
    par_ref,
    small_ref,
    pos_ref,
    str_ref,
    gs_ref,
    own_acc_ref,
    gkw_ref,
    moment_ref,
    type_ref,
):
    step = pl.program_id(0)
    rows, keys = str_ref.shape
    kernels = tab_ref.shape[1]
    heads = gkw_ref.shape[1]
    blocks = pos_ref.shape[0] // 3
    pair_block = 2 * (span_ref[SPAN_CHIP, 0] + span_ref[SPAN_FIRST, 0] + step)

    @pl.when(step == 0)
    def _():
        gkw_ref[...] = jnp.zeros(gkw_ref.shape, F32)
        moment_ref[...] = jnp.zeros(moment_ref.shape, F32)
        own_acc_ref[...] = jnp.zeros(own_acc_ref.shape, F32)
        pos_ref[...] = jnp.zeros(pos_ref.shape, F32)
        type_ref[...] = jnp.zeros(type_ref.shape, F32)

    def add_types(kind, by_scale, by_shift):
        count = type_ref.shape[1]
        onehot = lax.broadcasted_iota(jnp.int32, (count, LANES), 0).astype(F32) == kind
        type_ref[0] += jnp.where(onehot, by_scale, 0.0)
        type_ref[1] += jnp.where(onehot, by_shift, 0.0)

    own, other = own_ref[first_row : first_row + rows, :], other_ref[...]
    str_ref[...] = stretched_of(own, other)[3]

    half_keys = keys // 2

    def pair_step(at, half):
        columns = slice(half * half_keys, (half + 1) * half_keys)
        block = str_ref[pl.ds(at, CHUNK), columns]
        first = second = weights = None
        lines = []
        for r in range(0, CHUNK, 2):
            low = jnp.concatenate([ds_ref[0, at + r + q, :, columns] for q in range(2)], axis=1)
            dphi = dot_nn(kw_ref[...], jnp.concatenate([low] * WEIGHT_PIECES, axis=0))
            phis = []
            for q in range(2):
                away = jnp.broadcast_to(block[r + q : r + q + 1], (kernels, half_keys)) - tab_ref[0]
                phi = jnp.exp2(away * away * tab_ref[3])
                phis.append(phi.astype(BF))
                moved = dphi[:, q * half_keys : (q + 1) * half_keys] * phi * away
                bent = moved * away
                first = moved if first is None else first + moved
                second = bent if second is None else second + bent
                lines.append(jnp.sum(moved, axis=0, keepdims=True))
            part = dot_nt(jnp.concatenate(phis, axis=1), low)
            weights = part if weights is None else weights + part
        moment_ref[0] += first
        moment_ref[1] += second
        gs_ref[pl.ds(at, CHUNK), columns] = jnp.concatenate(lines, axis=0)
        gkw_ref[...] += weights

    def skipped(at, half):
        columns = slice(half * half_keys, (half + 1) * half_keys)
        gs_ref[pl.ds(at, CHUNK), columns] = jnp.zeros((CHUNK, half_keys), F32)

    kernel_steps(span_ref, first_row, rows, CHUNK, pair_step, skipped)

    delta, dist, scales, _ = stretched_of(own, other)
    grad = -gs_ref[...]
    by_scale = grad * dist
    pull = grad * scales / dist
    terms = [pull * delta[0], pull * delta[1], pull * delta[2], by_scale * other[3:4, :], grad]
    for k, term in enumerate(terms):
        own_acc_ref[k] += term[:, :128] + term[:, 128:]
    for half in range(2):
        part = slice(half * LANES, (half + 1) * LANES)
        for k in range(3):
            spot = pl.ds(k * blocks + pair_block + half, 1)
            pos_ref[spot, :] += -jnp.sum(terms[k][:, part], axis=0, keepdims=True)
        add_types(
            other[8:9, part],
            jnp.sum(by_scale[:, part] * own[:, 3:4], axis=0, keepdims=True),
            jnp.sum(grad[:, part], axis=0, keepdims=True),
        )

    @pl.when(step == span_ref[SPAN_LAST, 0] - span_ref[SPAN_FIRST, 0])
    def _():
        lane = lax.broadcasted_iota(jnp.int32, (rows, LANES), 1)
        total = jnp.zeros((rows, LANES), F32)
        for k in range(5):
            column = jnp.sum(own_acc_ref[k], axis=1, keepdims=True)
            total = total + jnp.where(lane == k, column, 0.0)
        rest = [jnp.zeros((count, LANES), F32) for count in (first_row, LANES - first_row - rows)]
        total = jnp.concatenate([x for x in (rest[0], total, rest[1]) if x.shape[0]], axis=0)
        turned = jnp.transpose(total)
        own_block = 2 * (span_ref[SPAN_CHIP, 0] + len(SLOTS[0]) // 2) + span_ref[SPAN_CORE, 0]
        for k in range(3):
            pos_ref[pl.ds(k * blocks + own_block, 1), :] += turned[k : k + 1, :]
        add_types(line_ref[8:9, :], turned[3:4, :], turned[4:5, :])

        par = par_ref[...]
        by_weight = gkw_ref[...] * par[:, heads : heads + 1]
        plain = jnp.sum(by_weight * par[:, :heads], axis=1, keepdims=True)
        by_mean = jnp.sum(moment_ref[0], axis=1, keepdims=True)
        by_width = jnp.sum(moment_ref[1], axis=1, keepdims=True) - plain
        columns = [by_mean, by_width * par[:, heads + 1 : heads + 2]]
        low, high = slice(0, LANES), slice(LANES, 2 * LANES)
        for part in (low, high):
            for k in range(2):
                columns.append(jnp.sum(type_ref[k, part, :], axis=1, keepdims=True))
        lane = lax.broadcasted_iota(jnp.int32, (LANES, LANES), 1)
        wide = jnp.concatenate([by_weight, jnp.zeros((LANES, LANES - heads), F32)], axis=1)
        for k, column in enumerate(columns):
            wide = wide + jnp.where(lane == heads + k, column, 0.0)
        small_ref[...] = jnp.transpose(wide)[: small_ref.shape[0]]


def middle_kernel(
    groups,
    tile,
    flat_ref,
    tok_ref,
    att_ref,
    lse_ref,
    gain_ref,
    shift_ref,
    cot_ref,
    wout_hbm,
    wup_hbm,
    wdown_hbm,
    select_ref,
    place_ref,
    sum_ref,
    into_ref,
    out_ref,
    gmix_ref,
    doaug_ref,
    payload_ref,
    attlow_ref,
    normed_ref,
    mine_ref,
    theirs_ref,
    lngrad_ref,
    wout_ref,
    wup_ref,
    wdown_ref,
    down_ref,
    back_ref,
    wout_sem,
    tile_sems,
):
    rows, model_width = tok_ref.shape
    width = groups * SPAN
    windows = group_windows(groups, model_width // (groups * GROUP))
    tiles = wup_ref.shape[1] // tile
    piece = mine_ref.shape[2]
    core = flat_ref[0] % 2

    def tile_copies(t):
        spot = pl.ds(pl.multiple_of(t * tile, LANES), tile)
        return (
            pltpu.make_async_copy(wup_hbm.at[:, spot], wup_ref.at[:, spot], tile_sems.at[0, t]),
            pltpu.make_async_copy(wdown_hbm.at[spot, :], wdown_ref.at[spot, :], tile_sems.at[1, t]),
        )

    first = pltpu.make_async_copy(wout_hbm, wout_ref, wout_sem)
    first.start()
    for t in range(tiles):
        for copy in tile_copies(t):
            copy.start()

    gain, shift = row_of(gain_ref), row_of(shift_ref)
    cotangent = cot_ref[...]
    attended = att_ref[...]
    attended_low = drop_columns(attended.astype(BF), select_ref, windows)
    attlow_ref[...] = attended_low
    first.wait()
    mixed = tok_ref[...].astype(F32) + dot_nn(attended_low, wout_ref[...])
    normal, slope = norm_parts(mixed)
    normed_ref[...] = (normal * gain + shift).astype(BF)
    down_ref[...] = mixed
    back_ref[...] = jnp.zeros(back_ref.shape, F32)

    def step(t, carry):
        for copy in tile_copies(t):
            copy.wait()
        spot = pl.ds(pl.multiple_of(t * tile, LANES), tile)
        up = dot_nn(normed_ref[...], wup_ref[:, spot])
        grad_hidden = dot_nt(cotangent, wdown_ref[spot, :])
        square = up * up
        bent = jnp.tanh(GELU_SLOPE * (up * (1.0 + GELU_CUBE * square)))
        gate = 0.5 * (1.0 + bent)
        inner = GELU_SLOPE * (1.0 + 3.0 * GELU_CUBE * square)
        hidden = (up * gate).astype(BF)
        grad_up = (grad_hidden * (gate + 0.5 * up * (1.0 - bent * bent) * inner)).astype(BF)
        for kind, value in enumerate((grad_up, hidden)):
            value = jnp.transpose(value.astype(F32)).astype(BF)
            for q in range(tile // piece):
                part = value[q * piece : (q + 1) * piece]
                at = t * (tile // piece // 2) + q // 2

                @pl.when(core == q % 2)
                def _():
                    mine_ref[kind, at] = part

                @pl.when(core != q % 2)
                def _():
                    theirs_ref[kind, at] = part

        down_ref[...] += dot_nn(hidden, wdown_ref[spot, :])
        back_ref[...] += dot_nt(grad_up, wup_ref[:, spot])
        return carry

    lax.fori_loop(0, tiles, step, 0)
    out_ref[...] = down_ref[...].astype(BF)
    back, by_gain, by_shift = norm_back(back_ref[...], normal, slope, gain)
    lngrad_ref[...] = jnp.concatenate([by_gain, by_shift], axis=0)
    grad_mixed = cotangent.astype(F32) + back
    gmix_ref[...] = grad_mixed
    grad_low = grad_mixed.astype(BF)
    grad_attended = dot_nt(grad_low, wout_ref[...]).astype(BF)
    padded = pad_columns(grad_attended, select_ref, windows).astype(F32)
    high, low = split(padded * attended, 2)
    delta = dot_nn(high, sum_ref[...]) + dot_nn(low, sum_ref[...])
    pieces = split(-delta, PIECES)
    tail = jnp.zeros((rows, 2 * LANES), F32)
    for p in range(PIECES):
        padded = padded + dot_nn(pieces[p], place_ref[p])
        tail = tail + dot_nn(lse_ref[p], into_ref[p]) + dot_nn(pieces[p], into_ref[PIECES + p])
    doaug_ref[...] = padded.astype(BF)
    payload_ref[:, :model_width] = grad_low
    payload_ref[:, model_width:] = tail.astype(BF)


def weight_grads_kernel(
    ka_count,
    flat_ref,
    mine_ref,
    came_ref,
    normed_ref,
    normed_came_ref,
    cot_ref,
    cot_came_ref,
    attlow_ref,
    attlow_came_ref,
    payload_ref,
    payload_came_ref,
    up_kept_ref,
    up_sent_ref,
    rest_kept_ref,
    rest_sent_ref,
    product_ref,
):
    flat = flat_ref[0]
    core, bit, side = flat % 2, (flat // 2) % 2, (flat // ka_count) % 2
    model_width = normed_ref.shape[1]
    rows = up_kept_ref.shape[1]
    half = model_width // 2
    slices = up_kept_ref.shape[0] * 2
    out_rows = model_width // ka_count
    normed = jnp.concatenate([normed_ref[...], normed_came_ref[...]], axis=0)
    cotangent = jnp.concatenate([cot_ref[...], cot_came_ref[...]], axis=0)

    def columns(which):
        return pl.ds(pl.multiple_of(which * half, LANES), half)

    def step(m, carry):
        both = jnp.concatenate([mine_ref[0, m], came_ref[0, m]], axis=1)
        value = dot_nn(both, normed).astype(BF)

        @pl.when(m % 2 == bit)
        def _():
            up_kept_ref[m // 2] = value

        @pl.when(m % 2 != bit)
        def _():
            up_sent_ref[m // 2] = value

        both = jnp.concatenate([mine_ref[1, m], came_ref[1, m]], axis=1)
        product_ref[:rows, :] = dot_nn(both, cotangent)
        rest_kept_ref[m, :rows, :] = product_ref[:rows, columns(side)].astype(BF)
        rest_sent_ref[m, :rows, :] = product_ref[:rows, columns(1 - side)].astype(BF)
        return carry

    lax.fori_loop(0, slices, step, 0)
    grads = jnp.concatenate(
        [payload_ref[:, :model_width], payload_came_ref[:, :model_width]], axis=0
    )
    attended = jnp.concatenate([attlow_ref[...], attlow_came_ref[...]], axis=0)
    product_ref[...] = dot_tn(grads, attended)

    def out_step(m, carry):
        spot = pl.ds(pl.multiple_of((2 * m + core) * out_rows, 8), out_rows)
        rest_kept_ref[m, rows:, :] = product_ref[spot, columns(side)].astype(BF)
        rest_sent_ref[m, rows:, :] = product_ref[spot, columns(1 - side)].astype(BF)
        return carry

    lax.fori_loop(0, slices, out_step, 0)


def normal_kernel(tok_ref, gain_ref, shift_ref, out_ref):
    normal, _ = norm_parts(tok_ref[...].astype(F32))
    out_ref[...] = (normal * row_of(gain_ref) + row_of(shift_ref)).astype(BF)


def qkv_grads_kernel(masks, groups, *refs):
    grads_refs, normed_refs, out_ref, norm_ref = refs[:groups], refs[groups:-2], refs[-2], refs[-1]
    columns = out_ref.shape[0]
    lefts, rights, parts = [], [], None
    for ref, group in zip(normed_refs, masks):
        for i, mask in enumerate(group):
            grads = grads_refs[mask // 4][mask % 4]
            lefts.append(grads[:columns])
            rights.append(ref[i])
            part = grads[columns:].astype(F32)
            parts = part if parts is None else parts + part
    total = None
    for i in range(0, len(lefts), 2):
        part = dot_nn(
            jnp.concatenate(lefts[i : i + 2], axis=1), jnp.concatenate(rights[i : i + 2], axis=0)
        )
        total = part if total is None else total + part
    out_ref[...] = total.astype(BF)
    norm_ref[...] = parts


def results_kernel(
    heads,
    types,
    small_rows,
    flat_ref,
    joined_ref,
    first_ref,
    norm_ref,
    weight_ref,
    mean_ref,
    width_ref,
    scale_ref,
    shift_ref,
    pos_ref,
):
    turned = joined_ref[:small_rows, :]
    weight_ref[...] = turned[:heads]
    rows = [turned[heads + k : heads + k + 1, :] for k in range(6)]
    mean_ref[...] = rows[0]
    width_ref[...] = rows[1]
    scale_ref[...] = jnp.concatenate([rows[2], rows[4]], axis=1)[:, :types]
    shift_ref[...] = jnp.concatenate([rows[3], rows[5]], axis=1)[:, :types]
    count = norm_ref.shape[1]
    for k in range(2):
        norm_ref[k] = first_ref[k * count : (k + 1) * count, :]
        norm_ref[2 + k] = joined_ref[small_rows + k * count : small_rows + (k + 1) * count, :]
    first = small_rows + 2 * count
    blocks = (joined_ref.shape[0] - first) // 3
    for k in range(3):
        spot = first + k * blocks + len(SLOTS[0]) // 2 * 2 + flat_ref[0]
        pos_ref[k : k + 1, :] = joined_ref[pl.ds(spot, 1), :]


def first_norm_kernel(
    ka_count,
    flat_ref,
    tok_ref,
    gain_ref,
    dq_ref,
    dkv_ref,
    w_ref,
    gmix_ref,
    grad_ref,
    *refs,
):
    *part_refs, joined_ref = refs
    model_width = tok_ref.shape[1]
    grad = dot_nn(w_ref[:, :model_width], dq_ref[...])
    grad = grad + dot_nn(w_ref[:, model_width:], dkv_ref[...])
    grad = jnp.transpose(grad)
    normal, slope = norm_parts(tok_ref[...].astype(F32))
    back, by_gain, by_shift = norm_back(grad, normal, slope, row_of(gain_ref))
    grad_ref[...] = gmix_ref[...] + back
    lines = [
        row[:, k : k + LANES] for row in (by_gain, by_shift) for k in range(0, model_width, LANES)
    ]
    joined_ref[:model_width, :] = dq_ref[...]
    joined_ref[model_width:, :] = dkv_ref[...]
    here = flat_ref[0] % ka_count
    rows = part_refs[0].shape[1]
    columns = 3 * model_width // ka_count
    lines.append(jnp.zeros((rows - columns - len(lines), LANES), F32))
    lines = jnp.concatenate(lines, axis=0).astype(BF)
    for ref in part_refs:
        for i in range(ka_count // 4):
            ref[i, columns:, :] = lines
    for d in range(ka_count):
        value = joined_ref[d * columns : (d + 1) * columns, :]
        differs = jnp.bitwise_xor(here, d)
        for k, ref in enumerate(part_refs):

            @pl.when(differs % 4 == k)
            def _():
                ref[differs // 4, :columns, :] = value


def regroup_kernel(*refs):
    ins, outs = refs[:4], refs[4:]
    for i, out in enumerate(outs):
        for k, ref in enumerate(ins):
            out[k] = ref[i]


def key_grad_kernel(
    scale2,
    head_scale,
    groups,
    model_width,
    span_ref,
    own_ref,
    other_ref,
    kv_ref,
    q_ref,
    *refs,
):
    payload_refs, refs = refs[:14], refs[14:]
    wout_ref, select_ref, place_ref, bias_ref, dkv_ref, kexp_ref, vexp_ref, *refs = refs
    mask_ref, qb_ref, dob_ref, dk_ref, dv_ref, both_ref, low_ref = refs
    step = pl.program_id(0)
    width = groups * SPAN
    rows = own_ref.shape[0]
    windows = group_windows(groups, model_width // (groups * GROUP))

    @pl.when(step == 0)
    def _():
        expand_into(kexp_ref, kv_ref[0, :, :width], groups)
        expand_into(vexp_ref, kv_ref[0, :, width:], groups)
        dk_ref[...] = jnp.zeros(dk_ref.shape, F32)
        dv_ref[...] = jnp.zeros(dv_ref.shape, F32)

    fetch(span_ref, payload_refs, both_ref)
    payload = both_ref[...]
    tail = payload[:, model_width:]
    grads = dot_nt(payload[:, :model_width], wout_ref[...]).astype(BF)
    grads = pad_columns(grads, select_ref, windows).astype(F32)
    grads = (grads + dot_nn(tail, place_ref[1])).astype(BF)
    shifts = dot_nn(tail, place_ref[0])
    for k, spot in enumerate(spots_of(span_ref, rows)):
        own_part = slice(k * rows, (k + 1) * rows)
        dob_ref[spot, :] = grads[own_part]
        qb_ref[spot, :] = (q_ref[0, spot, :].astype(F32) + shifts[own_part]).astype(BF)
    spread_mask(mask_ref, mask_of(own_ref[...], other_ref[...], True))

    def chunk_step(at, count):
        lines = pl.ds(pl.multiple_of(at * GROUP, HEAD_ROWS * GROUP), count * GROUP)
        mask = mask_ref[pl.ds(at, count)]
        for g in range(groups):
            query_block = qb_ref[:, g * SPAN : (g + 1) * SPAN]
            grad_block = dob_ref[:, g * SPAN : (g + 1) * SPAN]
            dots = dot_nt(kexp_ref[g, lines, :], query_block)
            grads = dot_nt(vexp_ref[g, lines, :], grad_block)
            bias = bias_ref[0, pl.ds(at, count), g * GROUP : (g + 1) * GROUP, :] + mask
            probs = jnp.exp2(dots * scale2 + bias.reshape(dots.shape))
            grad_scores = (probs * grads).astype(BF)
            dk_ref[g, lines, :] += dot_nn(grad_scores, query_block)
            dv_ref[g, lines, :] += dot_nn(probs.astype(BF), grad_block)

    head_steps(span_ref, rows, chunk_step)

    @pl.when(step == span_ref[SPAN_LAST, 0] - span_ref[SPAN_FIRST, 0])
    def _():
        def finish(i, carry):
            at = pl.multiple_of(i * CHUNK, CHUNK)
            lines = pl.ds(pl.multiple_of(i * CHUNK * GROUP, CHUNK * GROUP), CHUNK * GROUP)
            for part, (ref, scale) in enumerate(((dk_ref, head_scale), (dv_ref, 1.0))):
                for g in range(groups):
                    value = collapse(ref[g, lines, :]) * scale
                    low_ref[part, pl.ds(at, CHUNK), g * SPAN : (g + 1) * SPAN] = value.astype(BF)
            return carry

        lax.fori_loop(0, rows // CHUNK, finish, 0)
        for part in range(2):
            dkv_ref[part * model_width : (part + 1) * model_width, :] = drop_turned(
                low_ref[part], select_ref, windows
            )


def fixed(shape):
    return pl.BlockSpec(shape, lambda j, span: (0,) * len(shape), pipeline_mode=pl.Buffered(1))


def pair_at(j, span):
    return jnp.minimum(span[SPAN_FIRST, 0] + j, span[SPAN_LAST, 0])


def moving(shape, rank_at=0, last=0):
    def index(j, span):
        at = [0] * len(shape)
        at[rank_at] = pair_at(j, span)
        if last:
            at[-1] = last
        return tuple(at)

    return pl.BlockSpec(shape, index)


def call(
    kernel, steps, in_specs, out_specs, out_shapes, scratch, flops, name, after=(), carry=(), room=56
):
    extra, given = len(after) + len(carry), len(in_specs)
    single = not isinstance(out_shapes, list)
    if single:
        out_specs, out_shapes = [out_specs], [out_shapes]
    made = len(out_shapes)
    anywhere = pl.BlockSpec(memory_space=pl.ANY)

    def body(span_ref, *refs):
        @pl.when(pl.program_id(0) <= span_ref[SPAN_LAST, 0] - span_ref[SPAN_FIRST, 0])
        def _():
            outs = refs[extra + given : extra + given + made]
            kernel(
                span_ref, *refs[extra : extra + given], *outs, *refs[extra + given + made + len(carry) :]
            )

    inner = pl.pallas_call(
        body,
        grid_spec=pltpu.PrefetchScalarGridSpec(
            num_scalar_prefetch=1,
            grid=(steps,),
            in_specs=[anywhere] * extra + in_specs,
            out_specs=out_specs + [anywhere] * len(carry),
            scratch_shapes=scratch,
        ),
        out_shape=out_shapes + [shape_of(x.shape, x.dtype) for x in carry],
        input_output_aliases={1 + len(after) + k: made + k for k in range(len(carry))},
        compiler_params=pltpu.CompilerParams(
            dimension_semantics=("arbitrary",), vmem_limit_bytes=room * 1024 * 1024
        ),
        cost_estimate=pl.CostEstimate(flops=flops, bytes_accessed=20_000_000, transcendentals=0),
        name=name,
    )

    def run(span, *operands):
        results = inner(span, *after, *carry, *operands)
        return results[0] if single else results

    return run


def shape_of(shape, dtype=F32):
    return jax.ShapeDtypeStruct(shape, dtype)


def once(
    kernel, operands, out_shapes, scratch, flops, name, spaces=(), after=(), carry=(), room=56
):
    spaces = dict(spaces)
    shapes = [*out_shapes, *(shape_of(x.shape, x.dtype) for x in carry)]
    count, extra = len(operands), len(after) + len(carry)
    anywhere = pl.BlockSpec(memory_space=pl.ANY)

    def whole(shape):
        return pl.BlockSpec(shape, lambda j: (0,) * len(shape), pipeline_mode=pl.Buffered(1))

    def body(*refs):
        outs = refs[count + extra : count + extra + len(out_shapes)]
        kernel(*refs[:count], *outs, *refs[count + extra + len(shapes) :])

    results = pl.pallas_call(
        body,
        grid=(1,),
        in_specs=[
            pl.BlockSpec(memory_space=spaces[k]) if k in spaces else whole(x.shape)
            for k, x in enumerate(operands)
        ]
        + [anywhere] * extra,
        out_specs=[whole(x.shape) for x in out_shapes] + [anywhere] * len(carry),
        out_shape=shapes,
        scratch_shapes=scratch,
        input_output_aliases={
            count + len(after) + k: len(out_shapes) + k for k in range(len(carry))
        },
        compiler_params=pltpu.CompilerParams(vmem_limit_bytes=room * 1024 * 1024),
        cost_estimate=pl.CostEstimate(flops=flops, bytes_accessed=5_000_000, transcendentals=0),
        name=name,
    )(*operands, *after, *carry)
    return results


def on_device(
    tokens,
    positions,
    item_of_atom,
    item_lengths,
    atom_types,
    key_mask,
    ln1_gain,
    ln1_bias,
    w_qkv,
    kernel_means,
    kernel_widths,
    kernel_weight,
    type_scale,
    type_shift,
    w_out,
    ln2_gain,
    ln2_bias,
    w_up,
    w_down,
    out_cotangent,
):
    own_rows, model_width = tokens.shape
    assert own_rows == LANES
    kernels, heads = kernel_weight.shape
    head_size = model_width // heads
    head_scale = head_size ** (-0.5)
    scale2 = head_scale * LOG2E
    groups = heads // GROUP
    width = groups * SPAN
    ff_width = w_up.shape[1]
    ka_count = lax.axis_size("ka")
    flat = lax.axis_index("pb") * ka_count + lax.axis_index("ka")
    flat_array = flat.astype(jnp.int32).reshape(1)
    reach = (PROT_LEN + own_rows - 2) // own_rows
    chips = (reach + 1) // 2
    pairs = 2 * chips + 1
    assert pairs == len(SLOTS[0])
    keys = 2 * own_rows
    atoms = positions.shape[1]
    atoms_blocks = atoms // LANES
    types = type_scale.shape[0]
    bits = bits_of("ka") - 1
    up_order = [(0, 1), (1, 2)] + [(bit, 1) for bit in range(3, bits)]
    rest_order = [(bit, 1) for bit in range(bits)]

    window = Window(tokens)
    cotangent_came = core_flip(out_cotangent)
    ln1 = [x.reshape(-1, LANES) for x in (ln1_gain, ln1_bias)]
    ln2 = [x.reshape(-1, LANES) for x in (ln2_gain, ln2_bias)]
    (normed_own,) = once(
        normal_kernel,
        (tokens, *ln1),
        [shape_of(tokens.shape, BF)],
        [],
        1_000_000,
        "first_normal",
        room=16,
    )
    gathered = Gathered(normed_own)

    select = select_table(head_size)
    place = place_table(heads, head_size)
    into_tail, out_of_tail = tail_tables(heads, head_size)
    type_tiles = -(-types // LANES)
    tables = jnp.pad(
        jnp.stack([type_scale, type_shift]), ((0, 0), (0, type_tiles * LANES - types))
    )
    tables = tables.reshape(2, type_tiles, LANES).swapaxes(0, 1).reshape(2 * type_tiles, LANES)
    lengths = jnp.pad(item_lengths, (0, -item_lengths.shape[0] % LANES)).reshape(-1, LANES)
    span, other, own, own_line, tabs, grad_weights, weights_turned, par = once(
        functools.partial(side_kernel, atoms_blocks),
        (
            flat_array,
            positions,
            item_of_atom.reshape(-1, LANES),
            key_mask.reshape(-1, LANES),
            atom_types.reshape(-1, LANES),
            lengths,
            tables,
            kernel_means.reshape(1, LANES),
            kernel_widths.reshape(1, LANES),
            kernel_weight.T,
        ),
        [
            shape_of((SPAN_ROWS, LANES), jnp.int32),
            shape_of((SIDE, pairs * keys)),
            shape_of((own_rows, LANES)),
            shape_of((SIDE, LANES)),
            shape_of((4, kernels, LANES)),
            shape_of((kernels, WEIGHT_PIECES * heads), BF),
            shape_of((heads, kernels), BF),
            shape_of((LANES, LANES)),
        ],
        [],
        1_000_000_000,
        "sides",
        {0: pltpu.SMEM},
    )

    own_spec = fixed((own_rows, LANES))
    other_spec = moving((SIDE, keys), 1)
    bias_spec = moving((1, own_rows, heads, keys))
    bias = call(
        bias_kernel,
        pairs,
        [own_spec, other_spec, fixed((4, kernels, LANES)), fixed((heads, kernels))],
        bias_spec,
        shape_of((pairs, own_rows, heads, keys)),
        [pltpu.VMEM((own_rows, keys), F32)],
        30_000_000_000,
        "pair_bias",
        after=(window.one, window.two, normed_own),
    )(span, own, other, tabs, weights_turned)
    window.middle()
    token_blocks = window.finish()

    expanded = pltpu.VMEM((groups, own_rows * GROUP, SPAN), BF)
    summed = pltpu.VMEM((groups, own_rows * GROUP, SPAN), F32)
    mask_scratch = pltpu.VMEM((own_rows, GROUP, keys), F32)
    line_scratch = pltpu.VMEM((groups, own_rows * GROUP, LANES), F32)
    attended, q_aug, lse_pieces, kvq = call(
        functools.partial(forward_kernel, scale2, groups),
        pairs,
        [own_spec, other_spec]
        + [fixed((own_rows, model_width))] * 14
        + [
            fixed((model_width // LANES, LANES)),
            fixed((model_width // LANES, LANES)),
            fixed((model_width, 3 * model_width)),
            fixed(select.shape),
            fixed((1, width)),
            fixed(place.shape),
            bias_spec,
        ],
        [
            fixed((own_rows, width)),
            fixed((own_rows, width)),
            fixed((PIECES, own_rows, LANES)),
            moving((1, keys, 3 * width)),
        ],
        [
            shape_of((own_rows, width)),
            shape_of((own_rows, width), BF),
            shape_of((PIECES, own_rows, LANES), BF),
            shape_of((pairs, keys, 3 * width), BF),
        ],
        [
            expanded,
            mask_scratch,
            line_scratch,
            line_scratch,
            summed,
            pltpu.VMEM((own_rows, LANES), F32),
            pltpu.VMEM((keys, model_width), BF),
        ],
        25_000_000_000,
        "attention_forward",
        after=(gathered.beside,),
    )(
        span,
        own,
        other,
        *token_blocks,
        *ln1,
        w_qkv,
        select,
        ones_row(heads, head_size),
        place,
        bias,
    )

    far_rows = gathered.far()
    tile = 3 * LANES
    assert ff_width % tile == 0 and tile % (2 * ff_width // ka_count) == 0
    row_shape = shape_of((own_rows, model_width), BF)
    slices = ka_count // 2
    up_rows, out_rows = ff_width // ka_count, model_width // ka_count
    pieces = shape_of((2, slices, up_rows, own_rows), BF)
    block_out, grad_mixed, do_aug, payload, attended_low, normed_second, *parts, ln2_grads = once(
        functools.partial(middle_kernel, groups, tile),
        (
            flat_array,
            tokens,
            attended,
            lse_pieces,
            *ln2,
            out_cotangent,
            w_out,
            w_up,
            w_down,
            select,
            place,
            head_sum_table(heads),
            into_tail,
        ),
        [
            row_shape,
            shape_of((own_rows, model_width)),
            shape_of((own_rows, width), BF),
            shape_of((own_rows, model_width + 2 * LANES), BF),
            row_shape,
            row_shape,
            pieces,
            pieces,
            shape_of((2, model_width)),
        ],
        [
            pltpu.VMEM((model_width, model_width), BF),
            pltpu.VMEM((model_width, ff_width), BF),
            pltpu.VMEM((ff_width, model_width), BF),
            pltpu.VMEM((own_rows, model_width), F32),
            pltpu.VMEM((own_rows, model_width), F32),
            pltpu.SemaphoreType.DMA,
            pltpu.SemaphoreType.DMA((2, ff_width // tile)),
        ],
        10_000_000_000,
        "feed_forward",
        {0: pltpu.SMEM, 7: pl.ANY, 8: pl.ANY, 9: pl.ANY},
        after=tuple(far_rows),
    )
    came = [core_flip(x) for x in (parts[1], normed_second, attended_low, payload)]
    window = Window(payload, came[3])
    gathered.finish()
    half = model_width // 2
    up_kept, up_sent, rest_kept, rest_sent = once(
        functools.partial(weight_grads_kernel, ka_count),
        (
            flat_array,
            parts[0],
            came[0],
            normed_second,
            came[1],
            out_cotangent,
            cotangent_came,
            attended_low,
            came[2],
            payload,
            came[3],
        ),
        [shape_of((slices // 2, up_rows, model_width), BF)] * 2
        + [shape_of((slices, up_rows + out_rows, half), BF)] * 2,
        [pltpu.VMEM((model_width, model_width), F32)],
        5_000_000_000,
        "weight_gradients",
        {0: pltpu.SMEM},
    )
    up_sum = slices_sum(up_kept, up_sent, up_order)
    rest_sum = columns_sum(rest_kept, rest_sent, rest_order)
    rest_sum.cut = up_rows

    dq, grad_scores, window.one, window.two = call(
        functools.partial(query_grad_kernel, scale2, head_scale, groups),
        pairs,
        [
            own_spec,
            other_spec,
            fixed((own_rows, width)),
            fixed((own_rows, width)),
            moving((1, keys, 2 * width)),
            bias_spec,
            fixed(select.shape),
        ],
        [fixed((model_width, own_rows)), moving((1, own_rows, heads, keys))],
        [
            shape_of((model_width, own_rows), BF),
            shape_of((pairs, own_rows, heads, keys), BF),
        ],
        [expanded, expanded, mask_scratch, summed, pltpu.VMEM((own_rows, width), BF)],
        22_000_000_000,
        "query_gradients",
        after=(*up_sum.sent, *rest_sum.sent, window.far),
        carry=(window.one, window.two),
    )(span, own, other, q_aug, do_aug, kvq, bias, select)

    pos_blocks = atoms_blocks + 4 * chips
    small_rows = -(-(heads + 6) // 8) * 8
    small, pos_part = call(
        functools.partial(phi_grad_kernel, 0),
        pairs,
        [
            own_spec,
            other_spec,
            fixed((SIDE, LANES)),
            moving((1, own_rows, heads, keys)),
            fixed((4, kernels, LANES)),
            fixed((kernels, WEIGHT_PIECES * heads)),
            fixed((LANES, LANES)),
        ],
        [fixed((small_rows, LANES)), fixed((3 * pos_blocks, LANES))],
        [shape_of((small_rows, LANES)), shape_of((3 * pos_blocks, LANES))],
        [
            pltpu.VMEM((own_rows, keys), F32),
            pltpu.VMEM((own_rows, keys), F32),
            pltpu.VMEM((5, own_rows, LANES), F32),
            pltpu.VMEM((kernels, heads), F32),
            pltpu.VMEM((2, kernels, LANES), F32),
            pltpu.VMEM((2, 2 * LANES, LANES), F32),
        ],
        40_000_000_000,
        "kernel_gradients",
    )(span, own, other, own_line, grad_scores, tabs, grad_weights, par)
    window.middle()
    payload_blocks = window.finish()
    early_sum = everywhere_sum(
        jnp.concatenate([small, ln2_grads.reshape(-1, LANES), pos_part], axis=0)
    )
    advance([up_sum, rest_sum, early_sum], flat_array, "sums_first", (small,))

    dkv = call(
        functools.partial(key_grad_kernel, scale2, head_scale, groups, model_width),
        pairs,
        [
            own_spec,
            other_spec,
            pl.BlockSpec(
                (1, own_rows, 2 * width),
                lambda j, span: (chips, span[SPAN_CORE, 0], 0),
                pipeline_mode=pl.Buffered(1),
            ),
            moving((1, keys, width), 0, 2),
        ]
        + [fixed((own_rows, model_width + 2 * LANES))] * 14
        + [
            fixed((model_width, model_width)),
            fixed(select.shape),
            fixed(out_of_tail.shape),
            bias_spec,
        ],
        fixed((2 * model_width, own_rows)),
        shape_of((2 * model_width, own_rows), BF),
        [
            expanded,
            expanded,
            mask_scratch,
            pltpu.VMEM((keys, width), BF),
            pltpu.VMEM((keys, width), BF),
            summed,
            summed,
            pltpu.VMEM((keys, model_width + 2 * LANES), BF),
            pltpu.VMEM((2, own_rows, width), BF),
        ],
        28_000_000_000,
        "key_gradients",
        after=(*up_sum.sent, *rest_sum.sent, *early_sum.sent),
    )(span, own, other, kvq, kvq, *payload_blocks, w_out, select, out_of_tail, bias)

    advance([up_sum, rest_sum, early_sum], flat_array, "sums_second", (dkv,))
    qkv_rows = 3 * model_width // ka_count
    norm_count = model_width // LANES
    sent_rows = qkv_rows + -(-2 * norm_count // 16) * 16
    part_shape = shape_of((ka_count // 4, sent_rows, own_rows), BF)
    grad_tokens, stay, to_core, to_chip, to_both = once(
        functools.partial(first_norm_kernel, ka_count),
        (flat_array, tokens, ln1[0], dq, dkv, w_qkv, grad_mixed),
        [shape_of((own_rows, model_width))] + [part_shape] * 4,
        [pltpu.VMEM((3 * model_width, own_rows), BF)],
        2_000_000_000,
        "first_norm",
        {0: pltpu.SMEM},
        after=tuple(early_sum.sent),
    )
    core_stay, core_go = core_flip(to_core), core_flip(to_both)
    chip_own, chip_core = flip_bit(to_chip, "ka", 1), flip_bit(core_go, "ka", 1)
    groups_out = once(
        regroup_kernel,
        (stay, core_stay, chip_own, chip_core),
        [shape_of((4, sent_rows, own_rows), BF)] * (ka_count // 4),
        [],
        1_000_000,
        "regroup",
        room=24,
    )
    advance([up_sum, rest_sum, early_sum], flat_array, "sums_third", (groups_out[0],))
    groups_in = [groups_out[0]] + [
        flip_mask(groups_out[i], "ka", 4 * i) for i in range(1, ka_count // 4)
    ]
    qkv_part, norm_part = once(
        functools.partial(qkv_grads_kernel, gathered.masks(), ka_count // 4),
        (*groups_in, *gathered.arrays()),
        [shape_of((qkv_rows, model_width), BF), shape_of((sent_rows - qkv_rows, LANES))],
        [],
        3_000_000_000,
        "qkv_gradients",
    )
    qkv_sum = Sum(qkv_part, [qkv_part], over("pb"))
    norm_sum = Sum(norm_part, [norm_part], over("pb"))
    advance([up_sum, rest_sum, early_sum], flat_array, "sums_fourth", (qkv_part,))
    sums = [qkv_sum, norm_sum, up_sum, rest_sum, early_sum]
    while any(one.stages for one in sums):
        advance(sums, flat_array, "sums_last")
    joined = early_sum.total
    up_total, rest_total = up_sum.total, rest_sum.total
    norms, by_weight, by_mean, by_width, by_scale, by_shift, grad_positions = once(
        functools.partial(results_kernel, heads, types, small_rows),
        (flat_array, joined, norm_sum.total),
        [
            shape_of((4, norm_count, LANES)),
            shape_of((heads, kernels)),
            shape_of((1, kernels)),
            shape_of((1, kernels)),
            shape_of((1, types)),
            shape_of((1, types)),
            shape_of((3, LANES)),
        ],
        [],
        1_000_000,
        "results",
        {0: pltpu.SMEM},
        room=16,
    )
    qkv_total = qkv_sum.total
    return (
        block_out,
        grad_tokens,
        grad_positions,
        norms[0].reshape(-1),
        norms[1].reshape(-1),
        qkv_total.T,
        by_mean.reshape(-1),
        by_width.reshape(-1),
        by_weight.T,
        by_scale.reshape(-1),
        by_shift.reshape(-1),
        rest_total[1].T,
        norms[2].reshape(-1),
        norms[3].reshape(-1),
        up_total.T,
        rest_total[0],
    )


def solution(mesh):
    rows = P(MESH, None)
    in_specs = (rows,) + (P(),) * 18 + (rows,)
    out_specs = (
        rows,
        rows,
        P(None, MESH),
        P(),
        P(),
        P(None, "ka"),
        P(),
        P(),
        P(),
        P(),
        P(),
        P(None, "ka"),
        P(),
        P(),
        P(None, "ka"),
        P("ka", None),
    )
    return jax.shard_map(
        on_device, mesh=mesh, in_specs=in_specs, out_specs=out_specs, check_vma=False
    )
```

```python
import functools
import math

import jax
import jax.numpy as jnp
import numpy as np
from jax import lax
from jax.experimental import pallas as pl
from jax.experimental.pallas import tpu as pltpu
from jax.sharding import PartitionSpec as P

MOL_TYPES = 128
PROT_LEN = 768
MOL_MEAN = 32

LN_EPS = 1e-05
GELU_SLOPE = math.sqrt(2.0 / math.pi)
GELU_CUBE = 0.044715
MASKED = -1e30
ROOT_TWO_PI = math.sqrt(2.0 * math.pi)
LOG2E = math.log2(math.e)
KAPPA = math.sqrt(0.5 * LOG2E)

PAD = 32
GROUP = 8
SPAN = PAD * GROUP
PIECES = 3
WEIGHT_PIECES = 2
CHUNK = 32
HEAD_ROWS = 64
BIAS_ROWS = 64
FEW = 8
MESH = ("pb", "ka")

BF = jnp.bfloat16
F32 = jnp.float32


def shifted(block, axis, distance):
    devices = range(lax.axis_size(axis))
    route = [(i - distance, i) for i in devices if i - distance in devices]
    return lax.ppermute(block, axis, route)


def core_flip(block):
    devices = range(lax.axis_size(MESH))
    return lax.ppermute(block, MESH, [(i, i ^ 1) for i in devices])


class Window:
    def __init__(self, block, sibling=None):
        devices = range(lax.axis_size(MESH))
        levels = len(devices) // 4

        def of(level, rest):
            return level % levels * 4 + rest

        one, two, far = [], [], []
        for i in devices:
            level, chip, core = i // 4, (i >> 1) & 1, i & 1
            odd = level & 1
            one.append((i, of(level + (-1 if odd else 1), i % 4)))
            two.append((i, of(level + (1 if odd else -1), i % 4)))
            far.append((i, of(level + (2 if chip else -2), (1 - chip) * 2 + core)))
        self.block, self.sibling = block, sibling
        self.one = lax.ppermute(block, MESH, one)
        self.two = lax.ppermute(block, MESH, two)
        self.far = lax.ppermute(block, MESH, far)

    def middle(self):
        self.other_chip = [flip_bit(x, "ka", 1) for x in (self.block, self.one, self.two)]
        return self.other_chip

    def finish(self):
        beside, one, two = self.other_chip
        mine = [self.far, self.one, one, self.block, beside, self.two, two]
        came = [core_flip(x) for x in mine if x is not self.block]
        own = core_flip(self.block) if self.sibling is None else self.sibling
        return mine + came[:3] + [own] + came[3:]


class Gathered:
    def __init__(self, block):
        self.own, self.own_sibling = block, core_flip(block)
        self.beside = flip_bit(block, "ka", 1)

    def far(self):
        mine = jnp.stack([self.own, self.beside])
        self.groups = [
            flip_mask(mine, "ka", mask) for mask in range(4, lax.axis_size("ka"), 4)
        ]
        return self.groups

    def finish(self):
        self.beside_sibling = core_flip(self.beside)
        self.siblings = [core_flip(x) for x in self.groups]

    def arrays(self):
        return [
            *(x[None] for x in (self.own, self.own_sibling, self.beside, self.beside_sibling)),
            *self.groups,
            *self.siblings,
        ]

    def masks(self):
        far = range(4, lax.axis_size("ka"), 4)
        return [
            (0,), (1,), (2,), (3,),
            *((mask, mask + 2) for mask in far),
            *((mask + 1, mask + 3) for mask in far),
        ]


SLOTS = (
    (0, 5, 6, 3, 4, 1, 2),
    (6, 5, 4, 3, 2, 1, 0),
    (0, 1, 2, 3, 4, 5, 6),
    (2, 1, 4, 3, 6, 5, 0),
)
SPAN_FIRST, SPAN_LAST, SPAN_CORE, SPAN_CHIP, SPAN_SLOT = 0, 1, 2, 3, 4
SPAN_LOW = 16
SPAN_HIGH = 32
SPAN_ROWS = 48
LANES = 128
SIDE = 16


def flip_bit(block, axis, bit):
    devices = range(lax.axis_size(axis))
    return lax.ppermute(block, axis, [(i, i ^ (1 << bit)) for i in devices])


def bits_of(axis):
    return (lax.axis_size(axis) - 1).bit_length()


def flip_mask(block, axis, mask):
    devices = range(lax.axis_size(axis))
    return lax.ppermute(block, axis, [(i, i ^ mask) for i in devices])


class Sum:
    def __init__(self, kept, sent, stages, left=()):
        self.kept, self.sent, self.stages, self.left = kept, list(sent), list(stages), list(left)
        self.total, self.cut = None, 0

    def came(self):
        axis, bit, count = self.stages[0][:3]
        partners = range(1, 2**count)
        return [flip_mask(x, axis, p << bit) for x, p in zip(self.sent, partners, strict=True)]

    def plan(self):
        stage = self.stages.pop(0)
        if len(stage) == 4:
            return ("join", self.cut)
        if self.stages and self.stages[0][0] == "ka" and self.left:
            bit, count = self.stages[0][1] - 1, self.stages[0][2]
            self.left = [b for b in self.left if not bit <= b < bit + count]
            below = sum(1 for b in self.left if b < bit)
            return ("part", bit, count, 2 ** (len(self.left) - below), 2**below)
        return ("whole",)


def over(axis, first=0):
    return [(axis, bit, 1) for bit in range(first, bits_of(axis))]


def slices_sum(kept, sent, order):
    stages = [("ka", bit + 1, count) for bit, count in order] + over("pb")
    left = [b for bit, count in order[1:] for b in range(bit, bit + count)]
    return Sum(kept, [sent], stages, left)


def columns_sum(kept, sent, order):
    stages = [("pb", 0, 1)] + [("ka", bit + 1, count) for bit, count in order]
    left = [b for bit, count in order for b in range(bit, bit + count)]
    return Sum(kept, [sent], stages + over("pb", 1) + [("pb", 0, 1, "join")], left)


def everywhere_sum(values):
    return Sum(values, [values], over("ka") + over("pb"))


def stage_kernel(plans, counts, side_bit, flat_ref, *refs):
    flat = flat_ref[0]
    refs = list(refs)
    kept_refs = [refs.pop(0) for _ in plans]
    came_refs = [[refs.pop(0) for _ in range(count)] for count in counts]
    for plan, kept, came in zip(plans, kept_refs, came_refs):

        def total(*at):
            value = kept[at].astype(F32)
            for ref in came:
                value = value + ref[at].astype(F32)
            return value

        out = refs.pop(0)
        if plan[0] == "whole":
            out[...] = total(Ellipsis).astype(out.dtype)
        elif plan[0] == "join":
            half, cut = kept.shape[-1], plan[1]
            side = jnp.right_shift(flat, side_bit) & 1
            for ref, rows in ((out, slice(0, cut)), (refs.pop(0), slice(cut, None))):
                for which, given in ((side, kept), (1 - side, came[0])):
                    spot = pl.ds(pl.multiple_of(which * half, LANES), half)
                    ref[:, spot] = given[rows, :].astype(F32)
        else:
            _, bit, count, above, below = plan
            mine = jnp.right_shift(flat, bit + 1) & (2**count - 1)
            outs = [out] + [refs.pop(0) for _ in range(2**count - 1)]
            for i in range(above):
                for j in range(below):
                    for other, ref in enumerate(outs):
                        group = jnp.bitwise_xor(mine, other)
                        ref[i * below + j] = total((i * 2**count + group) * below + j).astype(BF)


def advance(sums, flat_array, name, after=()):
    sums = [one for one in sums if one.stages]
    if not sums:
        return
    came = [one.came() for one in sums]
    plans, shapes, sizes = [], [], []
    for one in sums:
        plan = one.plan()
        shape, dtype, size = one.kept.shape, one.kept.dtype, 1
        if plan[0] == "join":
            shapes.append(shape_of((plan[1], 2 * shape[1]), F32))
            shape, dtype = (shape[0] - plan[1], 2 * shape[1]), F32
        elif plan[0] == "part":
            shape, size = (plan[3] * plan[4], *shape[1:]), 2 ** plan[2]
        elif not one.stages:
            dtype = F32
        shapes += [shape_of(shape, dtype)] * size
        plans.append(plan)
        sizes.append(2 if plan[0] == "join" else size)
    results = once(
        functools.partial(stage_kernel, plans, [len(x) for x in came], bits_of("ka")),
        (flat_array, *(one.kept for one in sums), *(x for group in came for x in group)),
        shapes,
        [],
        1_000_000_000,
        name,
        {0: pltpu.SMEM},
        after=after,
        room=24,
    )
    results = list(results)
    for one, size, plan in zip(sums, sizes, plans):
        if plan[0] == "join":
            one.total = [results.pop(0) for _ in range(size)]
            continue
        one.kept = results.pop(0)
        one.sent = [results.pop(0) for _ in range(size - 1)] or [one.kept]
        if not one.stages:
            one.total = one.kept
        elif one.kept.ndim == 3 and one.kept.shape[0] == 1 and one.stages[0][0] == "pb":
            one.kept = one.kept.reshape(one.kept.shape[1:])
            one.sent = [one.kept]


def layer_norm(values, ln_gain, ln_shift):
    centre = jnp.mean(values, axis=-1, keepdims=True)
    offsets = values - centre
    spread = jnp.mean(offsets * offsets, axis=-1, keepdims=True)
    return offsets * lax.rsqrt(spread + LN_EPS) * ln_gain + ln_shift


def dot_nn(left, right):
    return lax.dot_general(left, right, (((1,), (0,)), ((), ())), preferred_element_type=F32)


def dot_nt(left, right):
    return lax.dot_general(left, right, (((1,), (1,)), ((), ())), preferred_element_type=F32)


def dot_tn(left, right):
    return lax.dot_general(left, right, (((0,), (0,)), ((), ())), preferred_element_type=F32)


def select_table(head_size):
    column = np.arange(SPAN)
    source = (column // PAD) * head_size + column % PAD
    table = [
        (column[:, None] == (source + off)[None, :]) & (column % PAD < head_size)[None, :]
        for off in (0, 64)
    ]
    return np.stack(table).astype(BF)


def group_windows(groups, head_size):
    out = []
    for g in range(groups):
        start = g * GROUP * head_size
        out.append((start // LANES * LANES, (start % LANES) // 64))
    return out


def place_table(heads, head_size):
    column = np.arange(heads * PAD)
    lane = np.arange(LANES)
    return np.stack(
        [
            (lane[:, None] == (column // PAD)[None, :])
            & (column % PAD == head_size + p)[None, :]
            for p in range(PIECES)
        ]
    ).astype(BF)


def tail_tables(heads, head_size):
    lane, tail = np.arange(LANES), np.arange(2 * LANES)
    into = np.stack(
        [
            (lane[:, None] + p * heads == tail[None, :]) & (lane < heads)[:, None]
            for p in range(2 * PIECES)
        ]
    )
    column = np.arange(heads * PAD)
    piece = column % PAD - head_size
    free = (piece >= 0) & (piece < PIECES)
    lane_of = np.where(free, piece * heads + column // PAD, -1)
    out = np.stack(
        [
            (tail[:, None] == lane_of[None, :]) & free[None, :],
            (tail[:, None] - PIECES * heads == lane_of[None, :]) & free[None, :],
        ]
    )
    return into.astype(BF), out.astype(BF)


def ones_row(heads, head_size):
    column = np.arange(heads * PAD) % PAD
    return ((column >= head_size) & (column < head_size + PIECES)).astype(np.float32)[None]


def head_sum_table(heads):
    column = np.arange(heads * PAD)
    return (column[:, None] // PAD == np.arange(LANES)[None, :]).astype(BF)


def pad_columns(values, select_ref, windows):
    parts = [
        dot_nn(values[:, start : start + SPAN], select_ref[kind]).astype(BF)
        for start, kind in windows
    ]
    return jnp.concatenate(parts, axis=1)


def drop_columns(values, select_ref, windows):
    tiles = {}
    for g, (start, kind) in enumerate(windows):
        part = dot_nt(values[:, g * SPAN : (g + 1) * SPAN], select_ref[kind])
        for k in range(SPAN // LANES):
            tile = part[:, k * LANES : (k + 1) * LANES]
            at = start // LANES + k
            tiles[at] = tiles[at] + tile if at in tiles else tile
    return jnp.concatenate([tiles[at] for at in sorted(tiles)], axis=1).astype(BF)


def drop_turned(values, select_ref, windows):
    tiles = {}
    for g, (start, kind) in enumerate(windows):
        part = dot_nt(select_ref[kind], values[:, g * SPAN : (g + 1) * SPAN])
        for k in range(SPAN // LANES):
            tile = part[k * LANES : (k + 1) * LANES]
            at = start // LANES + k
            tiles[at] = tiles[at] + tile if at in tiles else tile
    return jnp.concatenate([tiles[at] for at in sorted(tiles)], axis=0).astype(BF)


def row_of(ref):
    return jnp.concatenate([ref[k : k + 1, :] for k in range(ref.shape[0])], axis=1)


def split(values, count):
    rest, out = values, []
    for _ in range(count):
        piece = rest.astype(BF)
        rest = rest - piece.astype(F32)
        out.append(piece)
    return out


def norm_parts(values):
    centre = jnp.mean(values, axis=-1, keepdims=True)
    offsets = values - centre
    spread = jnp.mean(offsets * offsets, axis=-1, keepdims=True)
    slope = lax.rsqrt(spread + LN_EPS)
    return offsets * slope, slope


def norm_back(grad, normal, slope, gain):
    inner = grad * gain
    mean = jnp.mean(inner, axis=-1, keepdims=True)
    tilt = jnp.mean(inner * normal, axis=-1, keepdims=True)
    by_gain = jnp.sum(grad * normal, axis=0, keepdims=True)
    by_shift = jnp.sum(grad, axis=0, keepdims=True)
    return slope * (inner - mean - normal * tilt), by_gain, by_shift


def stretched_of(own, other):
    delta = [own[:, i : i + 1] - other[i : i + 1, :] for i in range(3)]
    square = delta[0] * delta[0] + delta[1] * delta[1] + delta[2] * delta[2]
    dist = jnp.sqrt(square + 1.0)
    scales = own[:, 3:4] * other[3:4, :]
    stretched = scales * dist + own[:, 4:5] + other[4:5, :]
    return delta, dist, scales, stretched


def mask_of(own, other, key_is_own):
    same = own[:, 5:6] == other[5:6, :]
    itself = own[:, 7:8] == other[7:8, :]
    is_open = (own[:, 6:7] > 0.5) if key_is_own else (other[6:7, :] > 0.5)
    return jnp.where(same & (is_open | itself), 0.0, MASKED)


def line_atoms(lines):
    line = lax.broadcasted_iota(jnp.int32, (lines, lines // GROUP), 0)
    atom = lax.broadcasted_iota(jnp.int32, (lines, lines // GROUP), 1)
    return jnp.where(line // GROUP == atom, 1.0, 0.0).astype(BF)


def line_heads(lines):
    line = lax.broadcasted_iota(jnp.int32, (lines, SPAN), 0)
    column = lax.broadcasted_iota(jnp.int32, (lines, SPAN), 1)
    return jnp.where(column // PAD == line % GROUP, 1.0, 0.0)


def expand_into(out_ref, padded, groups):
    lines = CHUNK * GROUP
    keep = line_heads(lines).astype(BF)
    spread = line_atoms(lines)
    for g in range(groups):
        for i in range(padded.shape[0] // CHUNK):
            part = padded[i * CHUNK : (i + 1) * CHUNK, g * SPAN : (g + 1) * SPAN]
            out_ref[g, i * lines : (i + 1) * lines, :] = dot_nn(spread, part).astype(BF) * keep


def collapse(values):
    lines = values.shape[0]
    kept = values * line_heads(lines)
    high = kept.astype(BF)
    low = (kept - high.astype(F32)).astype(BF)
    line = lax.broadcasted_iota(jnp.int32, (lines // GROUP, lines), 1)
    atom = lax.broadcasted_iota(jnp.int32, (lines // GROUP, lines), 0)
    gather = jnp.where(line // GROUP == atom, 1.0, 0.0).astype(BF)
    return dot_nn(gather, high) + dot_nn(gather, low)


def fetch(span_ref, refs, out_ref):
    slot = span_ref[SPAN_SLOT + span_ref[SPAN_FIRST, 0] + pl.program_id(0), 0]
    count = len(refs) // 2
    rows = refs[0].shape[0]
    for k in range(count):

        @pl.when(slot == k)
        def _():
            out_ref[:rows] = refs[k][...]
            out_ref[rows:] = refs[count + k][...]


def spots_of(span_ref, rows):
    core = span_ref[SPAN_CORE, 0]
    return [pl.ds(pl.multiple_of(at * rows, rows), rows) for at in (core, 1 - core)]


def spread_mask(mask_ref, mask):
    mask_ref[...] = jnp.broadcast_to(mask[:, None, :], mask_ref.shape)


def reaches(span_ref, first, last, low, high):
    return (span_ref[SPAN_LOW + first, 0] <= high) & (span_ref[SPAN_HIGH + last, 0] >= low)


def head_steps(span_ref, rows, step):
    pair = span_ref[SPAN_FIRST, 0] + pl.program_id(0)
    few = HEAD_ROWS // FEW

    def one(i, carry):
        @pl.when(reaches(span_ref, i * few, i * few + few - 1, 2 * pair, 2 * pair + 1))
        def _():
            step(pl.multiple_of(i * HEAD_ROWS, HEAD_ROWS), HEAD_ROWS)

        return carry

    lax.fori_loop(0, rows // HEAD_ROWS, one, 0)


def kernel_steps(span_ref, first, rows, size, step, skipped):
    pair = span_ref[SPAN_FIRST, 0] + pl.program_id(0)
    few = size // FEW

    def one(i, carry):
        at = pl.multiple_of(i * size, size)
        chunk = first // FEW + i * few
        for half in range(2):
            block = 2 * pair + half
            needed = reaches(span_ref, chunk, chunk + few - 1, block, block)

            @pl.when(needed)
            def _():
                step(at, half)

            @pl.when(jnp.logical_not(needed))
            def _():
                skipped(at, half)

        return carry

    lax.fori_loop(0, rows // size, one, 0)


def side_kernel(
    atoms_blocks,
    flat_ref,
    pos_ref,
    item_ref,
    open_ref,
    type_ref,
    length_ref,
    table_ref,
    means_ref,
    widths_ref,
    kw_ref,
    span_ref,
    other_ref,
    own_ref,
    line_ref,
    tab_ref,
    gw_ref,
    kwt_ref,
    par_ref,
):
    flat = flat_ref[0]
    chips = len(SLOTS[0]) // 2
    first_block = flat // 2 * 2 - 2 * chips
    lane = lax.broadcasted_iota(jnp.int32, (1, LANES), 1)
    tables = []
    for k in range(table_ref.shape[0] // 2):
        rows = split(table_ref[2 * k : 2 * k + 1, :], PIECES)
        rows += split(table_ref[2 * k + 1 : 2 * k + 2, :], PIECES)
        rows += [jnp.zeros((2, LANES), BF)]
        tables.append(jnp.concatenate([row.astype(F32) for row in rows], axis=0).astype(BF))
    flags = [
        jnp.broadcast_to(
            jnp.where(length_ref[k : k + 1, :] > 2 * MOL_MEAN, float(MOL_TYPES), 0.0), (8, LANES)
        ).astype(BF)
        for k in range(length_ref.shape[0])
    ]
    gathered = [[] for _ in range(7)]
    for b in range(other_ref.shape[1] // LANES):
        block = first_block + b
        inside = (block >= 0) & (block < atoms_blocks)
        source = jnp.clip(block, 0, atoms_blocks - 1)
        at = pl.ds(pl.multiple_of(source * LANES, LANES), LANES)
        for k in range(3):
            gathered[k].append(pos_ref[k : k + 1, at])
        gathered[3].append(jnp.where(inside, item_ref[pl.ds(source, 1), :].astype(F32), -1.0))
        gathered[4].append(open_ref[pl.ds(source, 1), :].astype(F32))
        gathered[5].append((block * LANES + lane).astype(F32))
        gathered[6].append(type_ref[pl.ds(source, 1), :].astype(F32))
    rows = [jnp.concatenate(row, axis=1) for row in gathered]
    item, kind = rows[3], rows[6]
    ids = lax.broadcasted_iota(jnp.int32, (LANES, item.shape[1]), 0).astype(F32)
    protein = jnp.zeros_like(kind)
    for k, flag in enumerate(flags):
        onehot = jnp.where(ids + float(k * LANES) == item, 1.0, 0.0).astype(BF)
        protein = protein + dot_nn(flag, onehot)[0:1, :]
    kind = kind + protein
    found = jnp.zeros((8, item.shape[1]), F32)
    for k, table in enumerate(tables):
        onehot = jnp.where(ids + float(k * LANES) == kind, 1.0, 0.0).astype(BF)
        found = found + dot_nn(table, onehot)
    scale = found[0:1] + found[1:2] + found[2:3]
    shift = found[3:4] + found[4:5] + found[5:6]
    rows = [*rows[:3], scale, shift, item, rows[4], rows[5], kind]
    rows.append(jnp.zeros((SIDE - len(rows), item.shape[1]), F32))
    other_ref[...] = jnp.concatenate(rows, axis=0)
    own_at = pl.ds(pl.multiple_of((flat - first_block) * LANES, LANES), LANES)
    line_ref[...] = other_ref[:, own_at]

    line = line_ref[...]
    turned = jnp.transpose(
        jnp.concatenate([line, jnp.zeros((LANES - SIDE, LANES), F32)], axis=0)
    )
    own_ref[...] = turned
    chunks = LANES // FEW
    item_column = jnp.broadcast_to(own_ref[:, 5:6], (LANES, LANES))
    par_ref[...] = item_column
    first_item = par_ref[pl.ds(0, chunks, stride=FEW), :]
    last_item = par_ref[pl.ds(FEW - 1, chunks, stride=FEW), :]

    def count(k, carry):
        row = item_ref[pl.ds(k, 1), :].astype(F32)
        below, upto = carry
        return (
            below + jnp.where(row < first_item, 1.0, 0.0),
            upto + jnp.where(row <= last_item, 1.0, 0.0),
        )

    zero = jnp.zeros((chunks, LANES), F32)
    below, upto = lax.fori_loop(0, atoms_blocks, count, (zero, zero))
    below = jnp.sum(below, axis=1, keepdims=True).astype(jnp.int32)
    upto = jnp.sum(upto, axis=1, keepdims=True).astype(jnp.int32)
    low = jnp.right_shift(below - first_block * LANES, 7)
    high = jnp.right_shift(upto - 1 - first_block * LANES, 7)
    span_ref[SPAN_LOW : SPAN_LOW + chunks, :] = jnp.broadcast_to(low, (chunks, LANES))
    span_ref[SPAN_HIGH : SPAN_HIGH + chunks, :] = jnp.broadcast_to(high, (chunks, LANES))
    row = lax.broadcasted_iota(jnp.int32, (SPAN_LOW, LANES), 0)
    kind = (flat // 2) % 4
    head = jnp.where(row == SPAN_FIRST, jnp.right_shift(low[0:1, :], 1), 0)
    head = head + jnp.where(row == SPAN_LAST, jnp.right_shift(high[chunks - 1 :, :], 1), 0)
    head = head + jnp.where(row == SPAN_CORE, flat % 2, 0)
    head = head + jnp.where(row == SPAN_CHIP, flat // 2, 0)
    for k, slots in enumerate(zip(*SLOTS)):
        slot = sum(jnp.where(kind == which, at, 0) for which, at in enumerate(slots))
        head = head + jnp.where(row == SPAN_SLOT + k, slot, 0)
    span_ref[:SPAN_LOW, :] = head

    def column_of(ref):
        return jnp.transpose(jnp.broadcast_to(ref[...], (LANES, LANES)))

    means, widths = column_of(means_ref), column_of(widths_ref)
    peaks = 1.0 / (ROOT_TWO_PI * widths)
    bend = -(KAPPA * KAPPA) / (widths * widths)
    tab_ref[0] = means
    tab_ref[1] = KAPPA / widths
    tab_ref[2] = LOG2E * jnp.log(peaks)
    tab_ref[3] = bend
    turned_weights = kw_ref[...].astype(F32)
    heads = turned_weights.shape[0]
    filler = jnp.zeros((LANES - heads, LANES), F32)
    wide = jnp.transpose(jnp.concatenate([turned_weights, filler], axis=0))
    weights = wide[:, :heads]
    scaled = weights * (peaks / (widths * widths))[:, :heads]
    gw_ref[...] = jnp.concatenate(split(scaled, WEIGHT_PIECES), axis=1)
    kwt_ref[...] = kw_ref[...]
    lanes = lax.broadcasted_iota(jnp.int32, (LANES, LANES), 1)
    par = wide + jnp.where(lanes == heads, peaks, 0.0)
    par_ref[...] = par + jnp.where(lanes == heads + 1, 1.0 / widths, 0.0)


def bias_kernel(span_ref, own_ref, other_ref, tab_ref, kwt_ref, out_ref, str_ref):
    rows, keys = str_ref.shape
    kernels = tab_ref.shape[1]
    heads = kwt_ref.shape[0]
    half_keys = keys // 2
    str_ref[...] = stretched_of(own_ref[...], other_ref[...])[3]

    def step(at, half):
        columns = slice(half * half_keys, (half + 1) * half_keys)
        block = str_ref[pl.ds(at, BIAS_ROWS), columns]
        for r in range(0, BIAS_ROWS, 2):
            parts = []
            for q in range(2):
                line = jnp.broadcast_to(block[r + q : r + q + 1], (kernels, half_keys))
                z = (line - tab_ref[0]) * tab_ref[1]
                parts.append(jnp.exp2(tab_ref[2] - z * z).astype(BF))
            result = dot_nn(kwt_ref[...], jnp.concatenate(parts, axis=1)) * LOG2E
            out_ref[0, at + r, :, columns] = result[:, :half_keys]
            out_ref[0, at + r + 1, :, columns] = result[:, half_keys:]

    def skipped(at, half):
        columns = slice(half * half_keys, (half + 1) * half_keys)
        out_ref[0, pl.ds(at, BIAS_ROWS), :, columns] = jnp.zeros((BIAS_ROWS, heads, half_keys), F32)

    kernel_steps(span_ref, 0, rows, BIAS_ROWS, step, skipped)


def forward_kernel(
    scale2,
    groups,
    span_ref,
    own_ref,
    other_ref,
    *refs,
):
    token_refs, refs = refs[:14], refs[14:]
    gain_ref, shift_ref, w_ref, select_ref, ones_ref, place_ref, bias_ref, *refs = refs
    att_ref, qaug_ref, lse_ref, kvq_ref, *refs = refs
    qexp_ref, mask_ref, max_ref, sum_ref, acc_ref, lane_ref, both_ref = refs
    step = pl.program_id(0)
    width = groups * SPAN
    tok_ref = token_refs[3]
    rows, model_width = tok_ref.shape
    windows = group_windows(groups, model_width // (groups * GROUP))
    gain, shift = row_of(gain_ref), row_of(shift_ref)

    @pl.when(step == 0)
    def _():
        normed = layer_norm(tok_ref[...].astype(F32), gain, shift).astype(BF)
        query = dot_nn(normed, w_ref[:, :model_width]).astype(BF)
        query = pad_columns(query, select_ref, windows)
        qaug_ref[...] = query
        expand_into(qexp_ref, query, groups)
        max_ref[...] = jnp.full(max_ref.shape, 2.0 * MASKED, F32)
        sum_ref[...] = jnp.zeros(sum_ref.shape, F32)
        acc_ref[...] = jnp.zeros(acc_ref.shape, F32)

    fetch(span_ref, token_refs, both_ref)
    normed = layer_norm(both_ref[...].astype(F32), gain, shift).astype(BF)
    spots = spots_of(span_ref, rows)

    for part in range(3):
        source = (part + 1) % 3 * model_width
        value = dot_nn(normed, w_ref[:, source : source + model_width]).astype(BF)
        value = pad_columns(value, select_ref, windows)
        if part < 2:
            value = value + ones_ref[...].astype(BF)
        for k in range(2):
            kvq_ref[0, spots[k], part * width : (part + 1) * width] = (
                value[k * rows : (k + 1) * rows]
            )
    spread_mask(mask_ref, mask_of(own_ref[...], other_ref[...], False))

    def chunk_step(at, count):
        lines = pl.ds(pl.multiple_of(at * GROUP, HEAD_ROWS * GROUP), count * GROUP)
        mask = mask_ref[pl.ds(at, count)]
        for g in range(groups):
            columns = slice(g * SPAN, (g + 1) * SPAN)
            dots = dot_nt(qexp_ref[g, lines, :], kvq_ref[0, :, columns])
            bias = bias_ref[0, pl.ds(at, count), g * GROUP : (g + 1) * GROUP, :] + mask
            scores = dots * scale2 + bias.reshape(dots.shape)
            old = max_ref[g, lines, :]
            top = jnp.maximum(scores[:, :128], scores[:, 128:])
            new = jnp.maximum(old, jnp.max(top, axis=1, keepdims=True))
            alpha = jnp.exp2(old - new)
            low = jnp.exp2(scores[:, :128] - new)
            high = jnp.exp2(scores[:, 128:] - new)
            max_ref[g, lines, :] = new
            sum_ref[g, lines, :] = sum_ref[g, lines, :] * alpha + (low + high)
            probs = jnp.concatenate([low, high], axis=1).astype(BF)
            values = dot_nn(probs, kvq_ref[0, :, width + g * SPAN : width + (g + 1) * SPAN])
            wide = jnp.concatenate([alpha, alpha], axis=1)
            acc_ref[g, lines, :] = acc_ref[g, lines, :] * wide + values

    head_steps(span_ref, rows, chunk_step)

    @pl.when(step == span_ref[SPAN_LAST, 0] - span_ref[SPAN_FIRST, 0])
    def _():
        lane = lax.broadcasted_iota(jnp.int32, (GROUP, 128), 1)
        head = lax.broadcasted_iota(jnp.int32, (GROUP, 128), 0)

        def finish(i, carry):
            at = pl.multiple_of(i * CHUNK, CHUNK)
            lines = pl.ds(pl.multiple_of(i * CHUNK * GROUP, CHUNK * GROUP), CHUNK * GROUP)
            lanes = jnp.zeros((CHUNK, 128), F32)
            for g in range(groups):
                total = jnp.sum(sum_ref[g, lines, :], axis=1, keepdims=True)
                attended = collapse(acc_ref[g, lines, :] / total)
                att_ref[pl.ds(at, CHUNK), g * SPAN : (g + 1) * SPAN] = attended
                lse = max_ref[g, lines, :] + jnp.log(total) * LOG2E
                own_lane = jnp.where(lane == head + g * GROUP, 1.0, 0.0)
                lanes = lanes + jnp.sum(
                    lse.reshape(CHUNK, GROUP, 128) * own_lane[None], axis=1
                )
            lane_ref[pl.ds(at, CHUNK), :] = lanes
            return carry

        lax.fori_loop(0, rows // CHUNK, finish, 0)
        rest = lane_ref[...] * (-1.0 / scale2)
        query = qaug_ref[...].astype(F32)
        for p in range(PIECES):
            piece = rest.astype(BF)
            rest = rest - piece.astype(F32)
            lse_ref[p] = piece
            query = query + dot_nn(piece, place_ref[p])
        qaug_ref[...] = query.astype(BF)


def query_grad_kernel(
    scale2,
    head_scale,
    groups,
    span_ref,
    own_ref,
    other_ref,
    qaug_ref,
    doaug_ref,
    kv_ref,
    bias_ref,
    select_ref,
    dq_ref,
    ds_ref,
    qexp_ref,
    doexp_ref,
    mask_ref,
    dqacc_ref,
    low_ref,
):
    step = pl.program_id(0)
    width = groups * SPAN
    rows, keys = own_ref.shape[0], other_ref.shape[1]
    windows = group_windows(groups, dq_ref.shape[0] // (groups * GROUP))

    @pl.when(step == 0)
    def _():
        expand_into(qexp_ref, qaug_ref[...], groups)
        expand_into(doexp_ref, doaug_ref[...], groups)
        dqacc_ref[...] = jnp.zeros(dqacc_ref.shape, F32)

    spread_mask(mask_ref, mask_of(own_ref[...], other_ref[...], False))

    def chunk_step(at, count):
        lines = pl.ds(pl.multiple_of(at * GROUP, HEAD_ROWS * GROUP), count * GROUP)
        mask = mask_ref[pl.ds(at, count)]
        waiting = []
        for g in range(groups):
            key_block = kv_ref[0, :, g * SPAN : (g + 1) * SPAN]
            value_block = kv_ref[0, :, width + g * SPAN : width + (g + 1) * SPAN]
            dots = dot_nt(qexp_ref[g, lines, :], key_block)
            grads = dot_nt(doexp_ref[g, lines, :], value_block)
            bias = bias_ref[0, pl.ds(at, count), g * GROUP : (g + 1) * GROUP, :] + mask
            probs = jnp.exp2(dots * scale2 + bias.reshape(dots.shape))
            grad_scores = probs * grads
            dqacc_ref[g, lines, :] += dot_nn(grad_scores.astype(BF), key_block)
            waiting.append(grad_scores.reshape(count, GROUP, keys))
            if len(waiting) == 2:
                ds_ref[0, pl.ds(at, count), (g - 1) * GROUP : (g + 1) * GROUP, :] = (
                    jnp.concatenate(waiting, axis=1).astype(BF)
                )
                waiting = []

    head_steps(span_ref, rows, chunk_step)

    @pl.when(step == span_ref[SPAN_LAST, 0] - span_ref[SPAN_FIRST, 0])
    def _():
        def finish(i, carry):
            at = pl.multiple_of(i * CHUNK, CHUNK)
            lines = pl.ds(pl.multiple_of(i * CHUNK * GROUP, CHUNK * GROUP), CHUNK * GROUP)
            for g in range(groups):
                value = collapse(dqacc_ref[g, lines, :]) * head_scale
                low_ref[pl.ds(at, CHUNK), g * SPAN : (g + 1) * SPAN] = value.astype(BF)
            return carry

        lax.fori_loop(0, rows // CHUNK, finish, 0)
        dq_ref[...] = drop_turned(low_ref[...], select_ref, windows)


def phi_grad_kernel(
    first_row,
    span_ref,
    own_ref,
    other_ref,
    line_ref,
    ds_ref,
    tab_ref,
    kw_ref,
    par_ref,
    small_ref,
    pos_ref,
    str_ref,
    gs_ref,
    own_acc_ref,
    gkw_ref,
    moment_ref,
    type_ref,
):
    step = pl.program_id(0)
    rows, keys = str_ref.shape
    kernels = tab_ref.shape[1]
    heads = gkw_ref.shape[1]
    blocks = pos_ref.shape[0] // 3
    pair_block = 2 * (span_ref[SPAN_CHIP, 0] + span_ref[SPAN_FIRST, 0] + step)

    @pl.when(step == 0)
    def _():
        gkw_ref[...] = jnp.zeros(gkw_ref.shape, F32)
        moment_ref[...] = jnp.zeros(moment_ref.shape, F32)
        own_acc_ref[...] = jnp.zeros(own_acc_ref.shape, F32)
        pos_ref[...] = jnp.zeros(pos_ref.shape, F32)
        type_ref[...] = jnp.zeros(type_ref.shape, F32)

    def add_types(kind, by_scale, by_shift):
        count = type_ref.shape[1]
        onehot = lax.broadcasted_iota(jnp.int32, (count, LANES), 0).astype(F32) == kind
        type_ref[0] += jnp.where(onehot, by_scale, 0.0)
        type_ref[1] += jnp.where(onehot, by_shift, 0.0)

    own, other = own_ref[first_row : first_row + rows, :], other_ref[...]
    str_ref[...] = stretched_of(own, other)[3]

    half_keys = keys // 2

    def pair_step(at, half):
        columns = slice(half * half_keys, (half + 1) * half_keys)
        block = str_ref[pl.ds(at, CHUNK), columns]
        first = second = weights = None
        lines = []
        for r in range(0, CHUNK, 2):
            low = jnp.concatenate([ds_ref[0, at + r + q, :, columns] for q in range(2)], axis=1)
            dphi = dot_nn(kw_ref[...], jnp.concatenate([low] * WEIGHT_PIECES, axis=0))
            phis = []
            for q in range(2):
                away = jnp.broadcast_to(block[r + q : r + q + 1], (kernels, half_keys)) - tab_ref[0]
                phi = jnp.exp2(away * away * tab_ref[3])
                phis.append(phi.astype(BF))
                moved = dphi[:, q * half_keys : (q + 1) * half_keys] * phi * away
                bent = moved * away
                first = moved if first is None else first + moved
                second = bent if second is None else second + bent
                lines.append(jnp.sum(moved, axis=0, keepdims=True))
            part = dot_nt(jnp.concatenate(phis, axis=1), low)
            weights = part if weights is None else weights + part
        moment_ref[0] += first
        moment_ref[1] += second
        gs_ref[pl.ds(at, CHUNK), columns] = jnp.concatenate(lines, axis=0)
        gkw_ref[...] += weights

    def skipped(at, half):
        columns = slice(half * half_keys, (half + 1) * half_keys)
        gs_ref[pl.ds(at, CHUNK), columns] = jnp.zeros((CHUNK, half_keys), F32)

    kernel_steps(span_ref, first_row, rows, CHUNK, pair_step, skipped)

    delta, dist, scales, _ = stretched_of(own, other)
    grad = -gs_ref[...]
    by_scale = grad * dist
    pull = grad * scales / dist
    terms = [pull * delta[0], pull * delta[1], pull * delta[2], by_scale * other[3:4, :], grad]
    for k, term in enumerate(terms):
        own_acc_ref[k] += term[:, :128] + term[:, 128:]
    for half in range(2):
        part = slice(half * LANES, (half + 1) * LANES)
        for k in range(3):
            spot = pl.ds(k * blocks + pair_block + half, 1)
            pos_ref[spot, :] += -jnp.sum(terms[k][:, part], axis=0, keepdims=True)
        add_types(
            other[8:9, part],
            jnp.sum(by_scale[:, part] * own[:, 3:4], axis=0, keepdims=True),
            jnp.sum(grad[:, part], axis=0, keepdims=True),
        )

    @pl.when(step == span_ref[SPAN_LAST, 0] - span_ref[SPAN_FIRST, 0])
    def _():
        lane = lax.broadcasted_iota(jnp.int32, (rows, LANES), 1)
        total = jnp.zeros((rows, LANES), F32)
        for k in range(5):
            column = jnp.sum(own_acc_ref[k], axis=1, keepdims=True)
            total = total + jnp.where(lane == k, column, 0.0)
        rest = [jnp.zeros((count, LANES), F32) for count in (first_row, LANES - first_row - rows)]
        total = jnp.concatenate([x for x in (rest[0], total, rest[1]) if x.shape[0]], axis=0)
        turned = jnp.transpose(total)
        own_block = 2 * (span_ref[SPAN_CHIP, 0] + len(SLOTS[0]) // 2) + span_ref[SPAN_CORE, 0]
        for k in range(3):
            pos_ref[pl.ds(k * blocks + own_block, 1), :] += turned[k : k + 1, :]
        add_types(line_ref[8:9, :], turned[3:4, :], turned[4:5, :])

        par = par_ref[...]
        by_weight = gkw_ref[...] * par[:, heads : heads + 1]
        plain = jnp.sum(by_weight * par[:, :heads], axis=1, keepdims=True)
        by_mean = jnp.sum(moment_ref[0], axis=1, keepdims=True)
        by_width = jnp.sum(moment_ref[1], axis=1, keepdims=True) - plain
        columns = [by_mean, by_width * par[:, heads + 1 : heads + 2]]
        low, high = slice(0, LANES), slice(LANES, 2 * LANES)
        for part in (low, high):
            for k in range(2):
                columns.append(jnp.sum(type_ref[k, part, :], axis=1, keepdims=True))
        lane = lax.broadcasted_iota(jnp.int32, (LANES, LANES), 1)
        wide = jnp.concatenate([by_weight, jnp.zeros((LANES, LANES - heads), F32)], axis=1)
        for k, column in enumerate(columns):
            wide = wide + jnp.where(lane == heads + k, column, 0.0)
        small_ref[...] = jnp.transpose(wide)[: small_ref.shape[0]]


def middle_kernel(
    groups,
    tile,
    flat_ref,
    tok_ref,
    att_ref,
    lse_ref,
    gain_ref,
    shift_ref,
    cot_ref,
    wout_hbm,
    wup_hbm,
    wdown_hbm,
    select_ref,
    place_ref,
    sum_ref,
    into_ref,
    out_ref,
    gmix_ref,
    doaug_ref,
    payload_ref,
    attlow_ref,
    normed_ref,
    mine_ref,
    theirs_ref,
    lngrad_ref,
    wout_ref,
    wup_ref,
    wdown_ref,
    down_ref,
    back_ref,
    wout_sem,
    tile_sems,
):
    rows, model_width = tok_ref.shape
    width = groups * SPAN
    windows = group_windows(groups, model_width // (groups * GROUP))
    tiles = wup_ref.shape[1] // tile
    piece = mine_ref.shape[2]
    core = flat_ref[0] % 2

    def tile_copies(t):
        spot = pl.ds(pl.multiple_of(t * tile, LANES), tile)
        return (
            pltpu.make_async_copy(wup_hbm.at[:, spot], wup_ref.at[:, spot], tile_sems.at[0, t]),
            pltpu.make_async_copy(wdown_hbm.at[spot, :], wdown_ref.at[spot, :], tile_sems.at[1, t]),
        )

    first = pltpu.make_async_copy(wout_hbm, wout_ref, wout_sem)
    first.start()
    for t in range(tiles):
        for copy in tile_copies(t):
            copy.start()

    gain, shift = row_of(gain_ref), row_of(shift_ref)
    cotangent = cot_ref[...]
    attended = att_ref[...]
    attended_low = drop_columns(attended.astype(BF), select_ref, windows)
    attlow_ref[...] = attended_low
    first.wait()
    mixed = tok_ref[...].astype(F32) + dot_nn(attended_low, wout_ref[...])
    normal, slope = norm_parts(mixed)
    normed_ref[...] = (normal * gain + shift).astype(BF)
    down_ref[...] = mixed
    back_ref[...] = jnp.zeros(back_ref.shape, F32)

    def step(t):
        for copy in tile_copies(t):
            copy.wait()
        spot = pl.ds(pl.multiple_of(t * tile, LANES), tile)
        up = dot_nn(normed_ref[...], wup_ref[:, spot])
        grad_hidden = dot_nt(cotangent, wdown_ref[spot, :])
        square = up * up
        bent = jnp.tanh(GELU_SLOPE * (up * (1.0 + GELU_CUBE * square)))
        gate = 0.5 * (1.0 + bent)
        inner = GELU_SLOPE * (1.0 + 3.0 * GELU_CUBE * square)
        hidden = (up * gate).astype(BF)
        grad_up = (grad_hidden * (gate + 0.5 * up * (1.0 - bent * bent) * inner)).astype(BF)
        for kind, value in enumerate((grad_up, hidden)):
            value = jnp.transpose(value.astype(F32)).astype(BF)
            for q in range(tile // piece):
                part = value[q * piece : (q + 1) * piece]
                at = t * (tile // piece // 2) + q // 2

                @pl.when(core == q % 2)
                def _():
                    mine_ref[kind, at] = part

                @pl.when(core != q % 2)
                def _():
                    theirs_ref[kind, at] = part

        down_ref[...] += dot_nn(hidden, wdown_ref[spot, :])
        back_ref[...] += dot_nt(grad_up, wup_ref[:, spot])

    def two_steps(i, carry):
        step(2 * i)
        step(2 * i + 1)
        return carry

    lax.fori_loop(0, tiles // 2, two_steps, 0)
    out_ref[...] = down_ref[...].astype(BF)
    back, by_gain, by_shift = norm_back(back_ref[...], normal, slope, gain)
    lngrad_ref[...] = jnp.concatenate([by_gain, by_shift], axis=0)
    grad_mixed = cotangent.astype(F32) + back
    gmix_ref[...] = grad_mixed
    grad_low = grad_mixed.astype(BF)
    grad_attended = dot_nt(grad_low, wout_ref[...]).astype(BF)
    padded = pad_columns(grad_attended, select_ref, windows).astype(F32)
    high, low = split(padded * attended, 2)
    delta = dot_nn(high, sum_ref[...]) + dot_nn(low, sum_ref[...])
    pieces = split(-delta, PIECES)
    tail = jnp.zeros((rows, 2 * LANES), F32)
    for p in range(PIECES):
        padded = padded + dot_nn(pieces[p], place_ref[p])
        tail = tail + dot_nn(lse_ref[p], into_ref[p]) + dot_nn(pieces[p], into_ref[PIECES + p])
    doaug_ref[...] = padded.astype(BF)
    payload_ref[:, :model_width] = grad_low
    payload_ref[:, model_width:] = tail.astype(BF)


def weight_grads_kernel(
    ka_count,
    flat_ref,
    mine_ref,
    came_ref,
    normed_ref,
    normed_came_ref,
    cot_ref,
    cot_came_ref,
    attlow_ref,
    attlow_came_ref,
    payload_ref,
    payload_came_ref,
    up_kept_ref,
    up_sent_ref,
    rest_kept_ref,
    rest_sent_ref,
    product_ref,
):
    flat = flat_ref[0]
    core, bit, side = flat % 2, (flat // 2) % 2, (flat // ka_count) % 2
    model_width = normed_ref.shape[1]
    rows = up_kept_ref.shape[1]
    half = model_width // 2
    slices = up_kept_ref.shape[0] * 2
    out_rows = model_width // ka_count
    normed = jnp.concatenate([normed_ref[...], normed_came_ref[...]], axis=0)
    cotangent = jnp.concatenate([cot_ref[...], cot_came_ref[...]], axis=0)

    def columns(which):
        return pl.ds(pl.multiple_of(which * half, LANES), half)

    def step(pair, carry):
        for which, ref in ((bit, up_kept_ref), (1 - bit, up_sent_ref)):
            m = 2 * pair + which
            both = jnp.concatenate([mine_ref[0, m], came_ref[0, m]], axis=1)
            ref[pair] = dot_nn(both, normed).astype(BF)
        for k in range(2):
            m = 2 * pair + k
            both = jnp.concatenate([mine_ref[1, m], came_ref[1, m]], axis=1)
            spot = slice(k * rows, (k + 1) * rows)
            product_ref[spot, :] = dot_nn(both, cotangent)
            rest_kept_ref[m, :rows, :] = product_ref[spot, columns(side)].astype(BF)
            rest_sent_ref[m, :rows, :] = product_ref[spot, columns(1 - side)].astype(BF)
        return carry

    lax.fori_loop(0, slices // 2, step, 0)
    grads = jnp.concatenate(
        [payload_ref[:, :model_width], payload_came_ref[:, :model_width]], axis=0
    )
    attended = jnp.concatenate([attlow_ref[...], attlow_came_ref[...]], axis=0)
    product_ref[...] = dot_tn(grads, attended)

    def out_step(m, carry):
        spot = pl.ds(pl.multiple_of((2 * m + core) * out_rows, 8), out_rows)
        rest_kept_ref[m, rows:, :] = product_ref[spot, columns(side)].astype(BF)
        rest_sent_ref[m, rows:, :] = product_ref[spot, columns(1 - side)].astype(BF)
        return carry

    lax.fori_loop(0, slices, out_step, 0)


def normal_kernel(tok_ref, gain_ref, shift_ref, out_ref):
    normal, _ = norm_parts(tok_ref[...].astype(F32))
    out_ref[...] = (normal * row_of(gain_ref) + row_of(shift_ref)).astype(BF)


def qkv_grads_kernel(masks, groups, *refs):
    grads_refs, normed_refs, out_ref, norm_ref = refs[:groups], refs[groups:-2], refs[-2], refs[-1]
    columns = out_ref.shape[0]
    lefts, rights, parts = [], [], None
    for ref, group in zip(normed_refs, masks):
        for i, mask in enumerate(group):
            grads = grads_refs[mask // 4][mask % 4]
            lefts.append(grads[:columns])
            rights.append(ref[i])
            part = grads[columns:].astype(F32)
            parts = part if parts is None else parts + part
    total = None
    for i in range(0, len(lefts), 2):
        part = dot_nn(
            jnp.concatenate(lefts[i : i + 2], axis=1), jnp.concatenate(rights[i : i + 2], axis=0)
        )
        total = part if total is None else total + part
    out_ref[...] = total.astype(BF)
    norm_ref[...] = parts


def results_kernel(
    heads,
    types,
    small_rows,
    flat_ref,
    joined_ref,
    first_ref,
    norm_ref,
    weight_ref,
    mean_ref,
    width_ref,
    scale_ref,
    shift_ref,
    pos_ref,
):
    turned = joined_ref[:small_rows, :]
    weight_ref[...] = turned[:heads]
    rows = [turned[heads + k : heads + k + 1, :] for k in range(6)]
    mean_ref[...] = rows[0]
    width_ref[...] = rows[1]
    scale_ref[...] = jnp.concatenate([rows[2], rows[4]], axis=1)[:, :types]
    shift_ref[...] = jnp.concatenate([rows[3], rows[5]], axis=1)[:, :types]
    count = norm_ref.shape[1]
    for k in range(2):
        norm_ref[k] = first_ref[k * count : (k + 1) * count, :]
        norm_ref[2 + k] = joined_ref[small_rows + k * count : small_rows + (k + 1) * count, :]
    first = small_rows + 2 * count
    blocks = (joined_ref.shape[0] - first) // 3
    for k in range(3):
        spot = first + k * blocks + len(SLOTS[0]) // 2 * 2 + flat_ref[0]
        pos_ref[k : k + 1, :] = joined_ref[pl.ds(spot, 1), :]


def first_norm_kernel(
    ka_count,
    flat_ref,
    tok_ref,
    gain_ref,
    dq_ref,
    dkv_ref,
    w_ref,
    gmix_ref,
    grad_ref,
    *refs,
):
    *part_refs, joined_ref = refs
    model_width = tok_ref.shape[1]
    grad = dot_nn(w_ref[:, :model_width], dq_ref[...])
    grad = grad + dot_nn(w_ref[:, model_width:], dkv_ref[...])
    grad = jnp.transpose(grad)
    normal, slope = norm_parts(tok_ref[...].astype(F32))
    back, by_gain, by_shift = norm_back(grad, normal, slope, row_of(gain_ref))
    grad_ref[...] = gmix_ref[...] + back
    lines = [
        row[:, k : k + LANES] for row in (by_gain, by_shift) for k in range(0, model_width, LANES)
    ]
    joined_ref[:model_width, :] = dq_ref[...]
    joined_ref[model_width:, :] = dkv_ref[...]
    here = flat_ref[0] % ka_count
    rows = part_refs[0].shape[1]
    columns = 3 * model_width // ka_count
    lines.append(jnp.zeros((rows - columns - len(lines), LANES), F32))
    lines = jnp.concatenate(lines, axis=0).astype(BF)
    for ref in part_refs:
        for i in range(ka_count // 4):
            ref[i, columns:, :] = lines
    for d in range(ka_count):
        value = joined_ref[d * columns : (d + 1) * columns, :]
        differs = jnp.bitwise_xor(here, d)
        for k, ref in enumerate(part_refs):

            @pl.when(differs % 4 == k)
            def _():
                ref[differs // 4, :columns, :] = value


def regroup_kernel(*refs):
    ins, outs = refs[:4], refs[4:]
    for i, out in enumerate(outs):
        for k, ref in enumerate(ins):
            out[k] = ref[i]


def key_grad_kernel(
    scale2,
    head_scale,
    groups,
    model_width,
    span_ref,
    own_ref,
    other_ref,
    kv_ref,
    q_ref,
    *refs,
):
    payload_refs, refs = refs[:14], refs[14:]
    wout_ref, select_ref, place_ref, bias_ref, dkv_ref, kexp_ref, vexp_ref, *refs = refs
    mask_ref, qb_ref, dob_ref, dk_ref, dv_ref, both_ref, low_ref = refs
    step = pl.program_id(0)
    width = groups * SPAN
    rows = own_ref.shape[0]
    windows = group_windows(groups, model_width // (groups * GROUP))

    @pl.when(step == 0)
    def _():
        expand_into(kexp_ref, kv_ref[0, :, :width], groups)
        expand_into(vexp_ref, kv_ref[0, :, width:], groups)
        dk_ref[...] = jnp.zeros(dk_ref.shape, F32)
        dv_ref[...] = jnp.zeros(dv_ref.shape, F32)

    fetch(span_ref, payload_refs, both_ref)
    payload = both_ref[...]
    tail = payload[:, model_width:]
    grads = dot_nt(payload[:, :model_width], wout_ref[...]).astype(BF)
    grads = pad_columns(grads, select_ref, windows).astype(F32)
    grads = (grads + dot_nn(tail, place_ref[1])).astype(BF)
    shifts = dot_nn(tail, place_ref[0])
    for k, spot in enumerate(spots_of(span_ref, rows)):
        own_part = slice(k * rows, (k + 1) * rows)
        dob_ref[spot, :] = grads[own_part]
        qb_ref[spot, :] = (q_ref[0, spot, :].astype(F32) + shifts[own_part]).astype(BF)
    spread_mask(mask_ref, mask_of(own_ref[...], other_ref[...], True))

    def chunk_step(at, count):
        lines = pl.ds(pl.multiple_of(at * GROUP, HEAD_ROWS * GROUP), count * GROUP)
        mask = mask_ref[pl.ds(at, count)]
        for g in range(groups):
            query_block = qb_ref[:, g * SPAN : (g + 1) * SPAN]
            grad_block = dob_ref[:, g * SPAN : (g + 1) * SPAN]
            dots = dot_nt(kexp_ref[g, lines, :], query_block)
            grads = dot_nt(vexp_ref[g, lines, :], grad_block)
            bias = bias_ref[0, pl.ds(at, count), g * GROUP : (g + 1) * GROUP, :] + mask
            probs = jnp.exp2(dots * scale2 + bias.reshape(dots.shape))
            grad_scores = (probs * grads).astype(BF)
            dk_ref[g, lines, :] += dot_nn(grad_scores, query_block)
            dv_ref[g, lines, :] += dot_nn(probs.astype(BF), grad_block)

    head_steps(span_ref, rows, chunk_step)

    @pl.when(step == span_ref[SPAN_LAST, 0] - span_ref[SPAN_FIRST, 0])
    def _():
        def finish(i, carry):
            at = pl.multiple_of(i * CHUNK, CHUNK)
            lines = pl.ds(pl.multiple_of(i * CHUNK * GROUP, CHUNK * GROUP), CHUNK * GROUP)
            for part, (ref, scale) in enumerate(((dk_ref, head_scale), (dv_ref, 1.0))):
                for g in range(groups):
                    value = collapse(ref[g, lines, :]) * scale
                    low_ref[part, pl.ds(at, CHUNK), g * SPAN : (g + 1) * SPAN] = value.astype(BF)
            return carry

        lax.fori_loop(0, rows // CHUNK, finish, 0)
        for part in range(2):
            dkv_ref[part * model_width : (part + 1) * model_width, :] = drop_turned(
                low_ref[part], select_ref, windows
            )


def fixed(shape):
    return pl.BlockSpec(shape, lambda j, span: (0,) * len(shape), pipeline_mode=pl.Buffered(1))


def pair_at(j, span):
    return jnp.minimum(span[SPAN_FIRST, 0] + j, span[SPAN_LAST, 0])


def moving(shape, rank_at=0, last=0):
    def index(j, span):
        at = [0] * len(shape)
        at[rank_at] = pair_at(j, span)
        if last:
            at[-1] = last
        return tuple(at)

    return pl.BlockSpec(shape, index)


def call(
    kernel, steps, in_specs, out_specs, out_shapes, scratch, flops, name, after=(), carry=(), room=56
):
    extra, given = len(after) + len(carry), len(in_specs)
    single = not isinstance(out_shapes, list)
    if single:
        out_specs, out_shapes = [out_specs], [out_shapes]
    made = len(out_shapes)
    anywhere = pl.BlockSpec(memory_space=pl.ANY)

    def body(span_ref, *refs):
        @pl.when(pl.program_id(0) <= span_ref[SPAN_LAST, 0] - span_ref[SPAN_FIRST, 0])
        def _():
            outs = refs[extra + given : extra + given + made]
            kernel(
                span_ref, *refs[extra : extra + given], *outs, *refs[extra + given + made + len(carry) :]
            )

    inner = pl.pallas_call(
        body,
        grid_spec=pltpu.PrefetchScalarGridSpec(
            num_scalar_prefetch=1,
            grid=(steps,),
            in_specs=[anywhere] * extra + in_specs,
            out_specs=out_specs + [anywhere] * len(carry),
            scratch_shapes=scratch,
        ),
        out_shape=out_shapes + [shape_of(x.shape, x.dtype) for x in carry],
        input_output_aliases={1 + len(after) + k: made + k for k in range(len(carry))},
        compiler_params=pltpu.CompilerParams(
            dimension_semantics=("arbitrary",), vmem_limit_bytes=room * 1024 * 1024
        ),
        cost_estimate=pl.CostEstimate(flops=flops, bytes_accessed=20_000_000, transcendentals=0),
        name=name,
    )

    def run(span, *operands):
        results = inner(span, *after, *carry, *operands)
        return results[0] if single else results

    return run


def shape_of(shape, dtype=F32):
    return jax.ShapeDtypeStruct(shape, dtype)


def once(
    kernel, operands, out_shapes, scratch, flops, name, spaces=(), after=(), carry=(), room=56
):
    spaces = dict(spaces)
    shapes = [*out_shapes, *(shape_of(x.shape, x.dtype) for x in carry)]
    count, extra = len(operands), len(after) + len(carry)
    anywhere = pl.BlockSpec(memory_space=pl.ANY)

    def whole(shape):
        return pl.BlockSpec(shape, lambda j: (0,) * len(shape), pipeline_mode=pl.Buffered(1))

    def body(*refs):
        outs = refs[count + extra : count + extra + len(out_shapes)]
        kernel(*refs[:count], *outs, *refs[count + extra + len(shapes) :])

    results = pl.pallas_call(
        body,
        grid=(1,),
        in_specs=[
            pl.BlockSpec(memory_space=spaces[k]) if k in spaces else whole(x.shape)
            for k, x in enumerate(operands)
        ]
        + [anywhere] * extra,
        out_specs=[whole(x.shape) for x in out_shapes] + [anywhere] * len(carry),
        out_shape=shapes,
        scratch_shapes=scratch,
        input_output_aliases={
            count + len(after) + k: len(out_shapes) + k for k in range(len(carry))
        },
        compiler_params=pltpu.CompilerParams(vmem_limit_bytes=room * 1024 * 1024),
        cost_estimate=pl.CostEstimate(flops=flops, bytes_accessed=5_000_000, transcendentals=0),
        name=name,
    )(*operands, *after, *carry)
    return results


def on_device(
    tokens,
    positions,
    item_of_atom,
    item_lengths,
    atom_types,
    key_mask,
    ln1_gain,
    ln1_bias,
    w_qkv,
    kernel_means,
    kernel_widths,
    kernel_weight,
    type_scale,
    type_shift,
    w_out,
    ln2_gain,
    ln2_bias,
    w_up,
    w_down,
    out_cotangent,
):
    own_rows, model_width = tokens.shape
    assert own_rows == LANES
    kernels, heads = kernel_weight.shape
    head_size = model_width // heads
    head_scale = head_size ** (-0.5)
    scale2 = head_scale * LOG2E
    groups = heads // GROUP
    width = groups * SPAN
    ff_width = w_up.shape[1]
    ka_count = lax.axis_size("ka")
    flat = lax.axis_index("pb") * ka_count + lax.axis_index("ka")
    flat_array = flat.astype(jnp.int32).reshape(1)
    reach = (PROT_LEN + own_rows - 2) // own_rows
    chips = (reach + 1) // 2
    pairs = 2 * chips + 1
    assert pairs == len(SLOTS[0])
    keys = 2 * own_rows
    atoms = positions.shape[1]
    atoms_blocks = atoms // LANES
    types = type_scale.shape[0]
    bits = bits_of("ka") - 1
    up_order = [(0, 1), (1, 2)] + [(bit, 1) for bit in range(3, bits)]
    rest_order = [(bit, 1) for bit in range(bits)]

    window = Window(tokens)
    cotangent_came = core_flip(out_cotangent)
    ln1 = [x.reshape(-1, LANES) for x in (ln1_gain, ln1_bias)]
    ln2 = [x.reshape(-1, LANES) for x in (ln2_gain, ln2_bias)]
    (normed_own,) = once(
        normal_kernel,
        (tokens, *ln1),
        [shape_of(tokens.shape, BF)],
        [],
        1_000_000,
        "first_normal",
        room=16,
    )
    gathered = Gathered(normed_own)

    select = select_table(head_size)
    place = place_table(heads, head_size)
    into_tail, out_of_tail = tail_tables(heads, head_size)
    type_tiles = -(-types // LANES)
    tables = jnp.pad(
        jnp.stack([type_scale, type_shift]), ((0, 0), (0, type_tiles * LANES - types))
    )
    tables = tables.reshape(2, type_tiles, LANES).swapaxes(0, 1).reshape(2 * type_tiles, LANES)
    lengths = jnp.pad(item_lengths, (0, -item_lengths.shape[0] % LANES)).reshape(-1, LANES)
    span, other, own, own_line, tabs, grad_weights, weights_turned, par = once(
        functools.partial(side_kernel, atoms_blocks),
        (
            flat_array,
            positions,
            item_of_atom.reshape(-1, LANES),
            key_mask.reshape(-1, LANES),
            atom_types.reshape(-1, LANES),
            lengths,
            tables,
            kernel_means.reshape(1, LANES),
            kernel_widths.reshape(1, LANES),
            kernel_weight.T,
        ),
        [
            shape_of((SPAN_ROWS, LANES), jnp.int32),
            shape_of((SIDE, pairs * keys)),
            shape_of((own_rows, LANES)),
            shape_of((SIDE, LANES)),
            shape_of((4, kernels, LANES)),
            shape_of((kernels, WEIGHT_PIECES * heads), BF),
            shape_of((heads, kernels), BF),
            shape_of((LANES, LANES)),
        ],
        [],
        1_000_000_000,
        "sides",
        {0: pltpu.SMEM},
    )

    own_spec = fixed((own_rows, LANES))
    other_spec = moving((SIDE, keys), 1)
    bias_spec = moving((1, own_rows, heads, keys))
    bias = call(
        bias_kernel,
        pairs,
        [own_spec, other_spec, fixed((4, kernels, LANES)), fixed((heads, kernels))],
        bias_spec,
        shape_of((pairs, own_rows, heads, keys)),
        [pltpu.VMEM((own_rows, keys), F32)],
        30_000_000_000,
        "pair_bias",
        after=(window.one, window.two, normed_own),
    )(span, own, other, tabs, weights_turned)
    window.middle()
    token_blocks = window.finish()

    expanded = pltpu.VMEM((groups, own_rows * GROUP, SPAN), BF)
    summed = pltpu.VMEM((groups, own_rows * GROUP, SPAN), F32)
    mask_scratch = pltpu.VMEM((own_rows, GROUP, keys), F32)
    line_scratch = pltpu.VMEM((groups, own_rows * GROUP, LANES), F32)
    attended, q_aug, lse_pieces, kvq = call(
        functools.partial(forward_kernel, scale2, groups),
        pairs,
        [own_spec, other_spec]
        + [fixed((own_rows, model_width))] * 14
        + [
            fixed((model_width // LANES, LANES)),
            fixed((model_width // LANES, LANES)),
            fixed((model_width, 3 * model_width)),
            fixed(select.shape),
            fixed((1, width)),
            fixed(place.shape),
            bias_spec,
        ],
        [
            fixed((own_rows, width)),
            fixed((own_rows, width)),
            fixed((PIECES, own_rows, LANES)),
            moving((1, keys, 3 * width)),
        ],
        [
            shape_of((own_rows, width)),
            shape_of((own_rows, width), BF),
            shape_of((PIECES, own_rows, LANES), BF),
            shape_of((pairs, keys, 3 * width), BF),
        ],
        [
            expanded,
            mask_scratch,
            line_scratch,
            line_scratch,
            summed,
            pltpu.VMEM((own_rows, LANES), F32),
            pltpu.VMEM((keys, model_width), BF),
        ],
        25_000_000_000,
        "attention_forward",
        after=(gathered.beside,),
    )(
        span,
        own,
        other,
        *token_blocks,
        *ln1,
        w_qkv,
        select,
        ones_row(heads, head_size),
        place,
        bias,
    )

    far_rows = gathered.far()
    tile = 3 * LANES
    assert ff_width % tile == 0 and tile % (2 * ff_width // ka_count) == 0
    row_shape = shape_of((own_rows, model_width), BF)
    slices = ka_count // 2
    up_rows, out_rows = ff_width // ka_count, model_width // ka_count
    pieces = shape_of((2, slices, up_rows, own_rows), BF)
    block_out, grad_mixed, do_aug, payload, attended_low, normed_second, *parts, ln2_grads = once(
        functools.partial(middle_kernel, groups, tile),
        (
            flat_array,
            tokens,
            attended,
            lse_pieces,
            *ln2,
            out_cotangent,
            w_out,
            w_up,
            w_down,
            select,
            place,
            head_sum_table(heads),
            into_tail,
        ),
        [
            row_shape,
            shape_of((own_rows, model_width)),
            shape_of((own_rows, width), BF),
            shape_of((own_rows, model_width + 2 * LANES), BF),
            row_shape,
            row_shape,
            pieces,
            pieces,
            shape_of((2, model_width)),
        ],
        [
            pltpu.VMEM((model_width, model_width), BF),
            pltpu.VMEM((model_width, ff_width), BF),
            pltpu.VMEM((ff_width, model_width), BF),
            pltpu.VMEM((own_rows, model_width), F32),
            pltpu.VMEM((own_rows, model_width), F32),
            pltpu.SemaphoreType.DMA,
            pltpu.SemaphoreType.DMA((2, ff_width // tile)),
        ],
        10_000_000_000,
        "feed_forward",
        {0: pltpu.SMEM, 7: pl.ANY, 8: pl.ANY, 9: pl.ANY},
        after=tuple(far_rows),
    )
    came = [core_flip(x) for x in (parts[1], normed_second, attended_low, payload)]
    window = Window(payload, came[3])
    gathered.finish()
    half = model_width // 2
    up_kept, up_sent, rest_kept, rest_sent = once(
        functools.partial(weight_grads_kernel, ka_count),
        (
            flat_array,
            parts[0],
            came[0],
            normed_second,
            came[1],
            out_cotangent,
            cotangent_came,
            attended_low,
            came[2],
            payload,
            came[3],
        ),
        [shape_of((slices // 2, up_rows, model_width), BF)] * 2
        + [shape_of((slices, up_rows + out_rows, half), BF)] * 2,
        [pltpu.VMEM((model_width, model_width), F32)],
        5_000_000_000,
        "weight_gradients",
        {0: pltpu.SMEM},
    )
    up_sum = slices_sum(up_kept, up_sent, up_order)
    rest_sum = columns_sum(rest_kept, rest_sent, rest_order)
    rest_sum.cut = up_rows

    dq, grad_scores, window.one, window.two = call(
        functools.partial(query_grad_kernel, scale2, head_scale, groups),
        pairs,
        [
            own_spec,
            other_spec,
            fixed((own_rows, width)),
            fixed((own_rows, width)),
            moving((1, keys, 2 * width)),
            bias_spec,
            fixed(select.shape),
        ],
        [fixed((model_width, own_rows)), moving((1, own_rows, heads, keys))],
        [
            shape_of((model_width, own_rows), BF),
            shape_of((pairs, own_rows, heads, keys), BF),
        ],
        [expanded, expanded, mask_scratch, summed, pltpu.VMEM((own_rows, width), BF)],
        22_000_000_000,
        "query_gradients",
        after=(*up_sum.sent, *rest_sum.sent, window.far),
        carry=(window.one, window.two),
    )(span, own, other, q_aug, do_aug, kvq, bias, select)

    pos_blocks = atoms_blocks + 4 * chips
    small_rows = -(-(heads + 6) // 8) * 8
    small, pos_part = call(
        functools.partial(phi_grad_kernel, 0),
        pairs,
        [
            own_spec,
            other_spec,
            fixed((SIDE, LANES)),
            moving((1, own_rows, heads, keys)),
            fixed((4, kernels, LANES)),
            fixed((kernels, WEIGHT_PIECES * heads)),
            fixed((LANES, LANES)),
        ],
        [fixed((small_rows, LANES)), fixed((3 * pos_blocks, LANES))],
        [shape_of((small_rows, LANES)), shape_of((3 * pos_blocks, LANES))],
        [
            pltpu.VMEM((own_rows, keys), F32),
            pltpu.VMEM((own_rows, keys), F32),
            pltpu.VMEM((5, own_rows, LANES), F32),
            pltpu.VMEM((kernels, heads), F32),
            pltpu.VMEM((2, kernels, LANES), F32),
            pltpu.VMEM((2, 2 * LANES, LANES), F32),
        ],
        40_000_000_000,
        "kernel_gradients",
    )(span, own, other, own_line, grad_scores, tabs, grad_weights, par)
    window.middle()
    payload_blocks = window.finish()
    early_sum = everywhere_sum(
        jnp.concatenate([small, ln2_grads.reshape(-1, LANES), pos_part], axis=0)
    )
    advance([up_sum, rest_sum, early_sum], flat_array, "sums_first", (small,))

    dkv = call(
        functools.partial(key_grad_kernel, scale2, head_scale, groups, model_width),
        pairs,
        [
            own_spec,
            other_spec,
            pl.BlockSpec(
                (1, own_rows, 2 * width),
                lambda j, span: (chips, span[SPAN_CORE, 0], 0),
                pipeline_mode=pl.Buffered(1),
            ),
            moving((1, keys, width), 0, 2),
        ]
        + [fixed((own_rows, model_width + 2 * LANES))] * 14
        + [
            fixed((model_width, model_width)),
            fixed(select.shape),
            fixed(out_of_tail.shape),
            bias_spec,
        ],
        fixed((2 * model_width, own_rows)),
        shape_of((2 * model_width, own_rows), BF),
        [
            expanded,
            expanded,
            mask_scratch,
            pltpu.VMEM((keys, width), BF),
            pltpu.VMEM((keys, width), BF),
            summed,
            summed,
            pltpu.VMEM((keys, model_width + 2 * LANES), BF),
            pltpu.VMEM((2, own_rows, width), BF),
        ],
        28_000_000_000,
        "key_gradients",
        after=(*up_sum.sent, *rest_sum.sent, *early_sum.sent),
    )(span, own, other, kvq, kvq, *payload_blocks, w_out, select, out_of_tail, bias)

    advance([up_sum, rest_sum, early_sum], flat_array, "sums_second", (dkv,))
    qkv_rows = 3 * model_width // ka_count
    norm_count = model_width // LANES
    sent_rows = qkv_rows + -(-2 * norm_count // 16) * 16
    part_shape = shape_of((ka_count // 4, sent_rows, own_rows), BF)
    grad_tokens, stay, to_core, to_chip, to_both = once(
        functools.partial(first_norm_kernel, ka_count),
        (flat_array, tokens, ln1[0], dq, dkv, w_qkv, grad_mixed),
        [shape_of((own_rows, model_width))] + [part_shape] * 4,
        [pltpu.VMEM((3 * model_width, own_rows), BF)],
        2_000_000_000,
        "first_norm",
        {0: pltpu.SMEM},
        after=tuple(early_sum.sent),
    )
    core_stay, core_go = core_flip(to_core), core_flip(to_both)
    chip_own, chip_core = flip_bit(to_chip, "ka", 1), flip_bit(core_go, "ka", 1)
    groups_out = once(
        regroup_kernel,
        (stay, core_stay, chip_own, chip_core),
        [shape_of((4, sent_rows, own_rows), BF)] * (ka_count // 4),
        [],
        1_000_000,
        "regroup",
        room=24,
    )
    advance([up_sum, rest_sum, early_sum], flat_array, "sums_third", (groups_out[0],))
    groups_in = [groups_out[0]] + [
        flip_mask(groups_out[i], "ka", 4 * i) for i in range(1, ka_count // 4)
    ]
    qkv_part, norm_part = once(
        functools.partial(qkv_grads_kernel, gathered.masks(), ka_count // 4),
        (*groups_in, *gathered.arrays()),
        [shape_of((qkv_rows, model_width), BF), shape_of((sent_rows - qkv_rows, LANES))],
        [],
        3_000_000_000,
        "qkv_gradients",
    )
    qkv_sum = Sum(qkv_part, [qkv_part], over("pb"))
    norm_sum = Sum(norm_part, [norm_part], over("pb"))
    advance([up_sum, rest_sum, early_sum], flat_array, "sums_fourth", (qkv_part,))
    sums = [qkv_sum, norm_sum, up_sum, rest_sum, early_sum]
    while any(one.stages for one in sums):
        advance(sums, flat_array, "sums_last")
    joined = early_sum.total
    up_total, rest_total = up_sum.total, rest_sum.total
    norms, by_weight, by_mean, by_width, by_scale, by_shift, grad_positions = once(
        functools.partial(results_kernel, heads, types, small_rows),
        (flat_array, joined, norm_sum.total),
        [
            shape_of((4, norm_count, LANES)),
            shape_of((heads, kernels)),
            shape_of((1, kernels)),
            shape_of((1, kernels)),
            shape_of((1, types)),
            shape_of((1, types)),
            shape_of((3, LANES)),
        ],
        [],
        1_000_000,
        "results",
        {0: pltpu.SMEM},
        room=16,
    )
    qkv_total = qkv_sum.total
    return (
        block_out,
        grad_tokens,
        grad_positions,
        norms[0].reshape(-1),
        norms[1].reshape(-1),
        qkv_total.T,
        by_mean.reshape(-1),
        by_width.reshape(-1),
        by_weight.T,
        by_scale.reshape(-1),
        by_shift.reshape(-1),
        rest_total[1].T,
        norms[2].reshape(-1),
        norms[3].reshape(-1),
        up_total.T,
        rest_total[0],
    )


def solution(mesh):
    rows = P(MESH, None)
    in_specs = (rows,) + (P(),) * 18 + (rows,)
    out_specs = (
        rows,
        rows,
        P(None, MESH),
        P(),
        P(),
        P(None, "ka"),
        P(),
        P(),
        P(),
        P(),
        P(),
        P(None, "ka"),
        P(),
        P(),
        P(None, "ka"),
        P("ka", None),
    )
    return jax.shard_map(
        on_device, mesh=mesh, in_specs=in_specs, out_specs=out_specs, check_vma=False
    )
```
